32 devices in a mesh: pole: 4 (over y, core), snode: 8 (over z, x).
Axes of the slice: x: 2, y: 2, z: 4, core: 2. Of those that a mesh axis runs over, the one named last changes fastest.
Arguments:
- pivot_inverse: float32 [8, 16, 2, 256, 256], P('pole', 'snode'), as said below
- factor_block: float32 [8, 16, 2, 256, 256], P('pole', 'snode')
- live_width_array: int32 [16], P('snode'), may hold values from 128 to 256, as said below
- pole_weight: float32 [8, 2], P('pole'), may hold values from -4 to 4
Outputs:
- density_diag: float32 [16, 256, 256], P('snode')
- density_off: float32 [16, 256, 256], P('snode')
The draws below stay inside these ranges and needn't reach their ends.
Inputs may be any that keep to these rules, and one draw needn't show every extreme that they name: `live_width_array`: live widths of the supernodes; at least one supernode is 256 wide and one is 128 wide. `pivot_inverse`: symmetric in its last two dimensions with a dominant real diagonal.
All inputs are finite; a program needn't handle non-finite values.
Results may differ from the reference program's by a relative error of at most 0.0003.
Values sent between devices are 32-bit elements; how exact they have to be, the bound alone decides.
No kernel may reach another device: no remote copies, remote signals or barrier semaphores. Data moves between devices by JAX's collectives and lax.ppermute only.
A program may use at most 192 MiB of HBM per device.

```python
import jax
import jax.numpy as jnp
from jax import lax

W = 256
CLUSTER_COUNT = 16
RESIDUE_COUNT = 8


def draw_pivot_inverse(key, part):
    key = jax.random.fold_in(key, 12)
    first, second = jax.random.split(key)
    noise = jax.random.normal(first, (RESIDUE_COUNT, CLUSTER_COUNT, 2, W, W), jnp.float32)
    noise = noise * (0.35 / W ** 0.5)
    symmetric = (noise + jnp.swapaxes(noise, -1, -2)) * 0.7071
    gains = jax.random.uniform(second, (RESIDUE_COUNT, CLUSTER_COUNT, 1, W), jnp.float32, 0.6, 1.4)
    unit_matrix = jnp.eye(W, dtype=jnp.float32)
    diagonal = unit_matrix[None, None, :, :] * gains
    parts_flag = jnp.array([1.0, 0.0], jnp.float32)[None, None, :, None, None]
    return symmetric + parts_flag * diagonal[:, :, None, :, :]


def draw_factor_block(key, part):
    key = jax.random.fold_in(key, 11)
    first, second, third, quartic_coefficient = jax.random.split(key, 4)
    low_rate = 0.3 / CLUSTER_COUNT
    high_rate = 0.08
    noise = jax.random.normal(first, (RESIDUE_COUNT, CLUSTER_COUNT, 2, W, W), jnp.float32)
    noise = noise * (0.15 / W ** 0.5)
    base_rate = jnp.exp(jax.random.uniform(second, (RESIDUE_COUNT, 1, W), jnp.float32, jnp.log(low_rate), jnp.log(high_rate)))
    wobble = jnp.exp(jax.random.uniform(third, (RESIDUE_COUNT, CLUSTER_COUNT, 1), jnp.float32, -0.5, 0.5))
    spike_magnitude = jax.random.uniform(quartic_coefficient, (RESIDUE_COUNT, CLUSTER_COUNT, 1), jnp.float32) < 3.0 / CLUSTER_COUNT
    objective_scalar = jnp.where(spike_magnitude, 0.6, 1.0)
    diagonal_values = jnp.exp(-base_rate * wobble) * objective_scalar
    unit_matrix = jnp.eye(W, dtype=jnp.float32)
    diagonal = unit_matrix[None, None, :, :] * diagonal_values[:, :, None, :]
    parts_flag = jnp.array([1.0, 0.0], jnp.float32)[None, None, :, None, None]
    return noise + parts_flag * diagonal[:, :, None, :, :]


def draw_live_width_array(key, part):
    key = jax.random.fold_in(key, 13)
    first, second, third = jax.random.split(key, 3)
    widths = jax.random.randint(first, (CLUSTER_COUNT,), W // 2, W + 1, jnp.int32)
    widest_width = jax.random.randint(second, (), 0, CLUSTER_COUNT, jnp.int32)
    narrow = (widest_width + 1 + jax.random.randint(third, (), 0, CLUSTER_COUNT - 1, jnp.int32)) % CLUSTER_COUNT
    widths = widths.at[widest_width].set(W)
    widths = widths.at[narrow].set(W // 2)
    return widths


def shard_levels(rng, dims, shards, least, largest):
    gain, own = 1.0, jax.random.fold_in(rng, 6)
    for dim, blocks in shards:
        steps = jnp.exp(jax.random.uniform(jax.random.fold_in(own, dim), (blocks,), jnp.float32, least / len(shards), largest / len(shards)))
        gain = gain * jnp.repeat(steps, dims[dim] // blocks).reshape([-1 if axis == dim else 1 for axis in range(len(dims))])
    return gain


def normal_values(key, extent, scale, bound, pieces=(), kind=jnp.bfloat16):
    entries = scale * jax.random.normal(key, extent, jnp.float32)
    if pieces:
        entries = entries * shard_levels(key, extent, pieces, -0.22, 0.18)
    return jnp.clip(entries, -bound, bound).astype(kind)


def setup_inputs(seed: int = 0) -> dict:
    splits = jax.random.split(jax.random.key(seed), 5)
    return {
        "pivot_inverse": draw_pivot_inverse(jax.random.fold_in(splits[4], 71), 0),
        "factor_block": draw_factor_block(jax.random.fold_in(splits[4], 71), 0),
        "live_width_array": draw_live_width_array(jax.random.fold_in(splits[4], 71), 0),
        "pole_weight": normal_values(splits[3], (RESIDUE_COUNT, 2), 1.0, 4.0, ((0, 4),), jnp.float32),
    }


def multiply_real(left, right):
    return jnp.einsum("...ij,...jk->...ik", left, right, precision=lax.Precision.HIGHEST)


def complex_product(left, right):
    left_real = left[..., 0, :, :]
    leading_imaginary = left[..., 1, :, :]
    right_re = right[..., 0, :, :]
    right_im = right[..., 1, :, :]
    real_part = multiply_real(left_real, right_re) - multiply_real(leading_imaginary, right_im)
    imag_part = multiply_real(left_real, right_im) + multiply_real(leading_imaginary, right_re)
    return jnp.stack([real_part, imag_part], axis=-3)


def transpose_block(block):
    return jnp.swapaxes(block, -1, -2)


def reference(pivot_inverse, factor_block, live_width_array, pole_weight):
    columns = jnp.arange(W, dtype=jnp.int32)
    keep = (columns[None, :] < live_width_array[:, None]).astype(jnp.float32)
    pivot = pivot_inverse * keep[None, :, None, :, None] * keep[None, :, None, None, :]
    factor = factor_block * keep[None, :, None, None, :]

    def one_pole(inputs):
        pole_pivot, pole_factor, weight = inputs

        def proceed_upward(parent, blocks):
            diag_block, link = blocks
            product = complex_product(parent, link)
            inverse = diag_block + complex_product(transpose_block(link), product)
            return inverse, (inverse, -product)

        start = jnp.zeros((2, W, W), jnp.float32)
        _, (reciprocal_matrices, offsets) = lax.scan(proceed_upward, start, (pole_pivot, pole_factor))
        diag_part = weight[0] * reciprocal_matrices[:, 1] + weight[1] * reciprocal_matrices[:, 0]
        off_part = weight[0] * offsets[:, 1] + weight[1] * offsets[:, 0]
        return diag_part, off_part

    diag_terms, off_terms = lax.map(one_pole, (pivot, factor, pole_weight))
    return jnp.sum(diag_terms, axis=0), jnp.sum(off_terms, axis=0)
```

```python
import functools

import jax
import jax.numpy as jnp
from jax import lax
from jax.experimental import pallas as pl
from jax.experimental.pallas import tpu as pltpu
from jax.sharding import PartitionSpec as P

F32 = jnp.float32
BF16 = jnp.bfloat16
AXES = ("pole", "snode")
VMEM_LIMIT = 40 * 1024 * 1024


def halves(value):
    high = value.astype(BF16)
    return high, (value - high.astype(F32)).astype(BF16)


def split_pair(real, imag):
    (rh, rl), (ih, il) = halves(real), halves(imag)
    return rh, ih, rl, il


def dot(left, right):
    return jnp.dot(left, right, preferred_element_type=F32)


def dot3(lh, ll, rh, rl):
    return dot(lh, rh) + (dot(lh, rl) + dot(ll, rh))


def complex_dot(left, right):
    arh, aih, arl, ail = left
    brh, bih, brl, bil = right
    real = dot3(arh, arl, brh, brl) - dot3(aih, ail, bih, bil)
    imag = dot3(arh, arl, bih, bil) + dot3(aih, ail, brh, brl)
    return real, imag


def rows_columns(size):
    return (
        lax.broadcasted_iota(jnp.int32, (size, size), 0),
        lax.broadcasted_iota(jnp.int32, (size, size), 1),
    )


def packed(block):
    half = block.shape[0] // 2
    row, column = rows_columns(half)
    lower = block[half:, half:]
    mixed = jnp.where(row >= column, block[:half, :half], lower)
    diagonal = jnp.sum(jnp.where(row == column, lower, 0.0), axis=0, keepdims=True)
    return jnp.concatenate(
        [block[:half, half:], mixed, jnp.broadcast_to(diagonal, (8, half))], axis=0
    )


def unpacked(value):
    half = value.shape[1]
    row, column = rows_columns(half)
    right, mixed = value[:half], value[half : 2 * half]
    diagonal = value[2 * half : 2 * half + 1]
    turned = mixed.T
    first = jnp.where(row >= column, mixed, turned)
    last = jnp.where(row < column, mixed, jnp.where(row == column, diagonal, turned))
    return jnp.concatenate(
        [jnp.concatenate([first, right], axis=1), jnp.concatenate([right.T, last], axis=1)], axis=0
    )


def unpacked_split(ref):
    return split_pair(unpacked(ref[0]), unpacked(ref[1]))


def load4(ref):
    return tuple(ref[i] for i in range(4))


def store4(ref, parts):
    for i, part in enumerate(parts):
        ref[i] = part


def prepare_kernel(slot, live, weight, pivot, factor, f0s, f0t, gs, gt, g, e, weighted):
    width = pivot.shape[-1]
    row, column = rows_columns(width)
    d, f = [], []
    for k in range(2):
        columns = column < live[k]
        both = jnp.logical_and(row < live[k], columns)
        d.append([jnp.where(both, pivot[0, k, c], 0.0) for c in range(2)])
        f.append([jnp.where(columns, factor[0, k, c], 0.0) for c in range(2)])
    s0, s1 = split_pair(*f[0]), split_pair(*f[1])
    store4(f0s, s0)
    store4(f0t, split_pair(f[0][0].T, f[0][1].T))
    gr, gi = complex_dot(s0, s1)
    g[0], g[1] = gr, gi
    store4(gs, split_pair(gr, gi))
    store4(gt, split_pair(gr.T, gi.T))
    br, bi = complex_dot(split_pair(*d[0]), s1)
    tr, ti = complex_dot(split_pair(f[1][0].T, f[1][1].T), split_pair(br, bi))
    er, ei = d[1][0] + tr, d[1][1] + ti
    e[0], e[1] = packed(er), packed(ei)
    w0, w1 = weight[slot[0], 0], weight[slot[0], 1]
    weighted[0] = packed(w1 * d[0][0] + w0 * d[0][1])
    weighted[1] = packed(w1 * er + w0 * ei)
    b = w1 * br + w0 * bi
    half = width // 2
    weighted_b = jnp.concatenate([b[:, :half], b[:, half:]], axis=0)
    weighted[2] = weighted_b[: width + 8]
    weighted[3, : width - 8] = weighted_b[width + 8 :]


def fold(x, gs, gt, e, out):
    tr, ti = complex_dot(x, load4(gs))
    yr, yi = complex_dot(load4(gt), split_pair(tr, ti))
    out[0] = e[0] + packed(yr)
    out[1] = e[1] + packed(yi)


def step_kernel(active, gs, gt, e, *refs):
    *received, out = refs

    @pl.when(active[0] == 1)
    def _():
        value = received[0][...]
        for other in received[1:]:
            value = value + other[...]
        fold(split_pair(unpacked(value[0]), unpacked(value[1])), gs, gt, e, out)


def pair_kernel(odd, g, e, g_in, e_in, fas, fat, ea, ps, pt, ep):
    is_odd = odd[0] == 1
    ga = [jnp.where(is_odd, g_in[c], g[c]) for c in range(2)]
    gb = [jnp.where(is_odd, g[c], g_in[c]) for c in range(2)]
    low = [jnp.where(is_odd, e_in[c], e[c]) for c in range(2)]
    high = [jnp.where(is_odd, e[c], e_in[c]) for c in range(2)]
    sa, sb = split_pair(*ga), split_pair(*gb)
    store4(fas, sa)
    store4(fat, split_pair(ga[0].T, ga[1].T))
    pr, pi = complex_dot(sa, sb)
    store4(ps, split_pair(pr, pi))
    store4(pt, split_pair(pr.T, pi.T))
    br, bi = complex_dot(split_pair(unpacked(low[0]), unpacked(low[1])), sb)
    tr, ti = complex_dot(split_pair(gb[0].T, gb[1].T), split_pair(br, bi))
    for c, term in enumerate((tr, ti)):
        ea[c] = low[c]
        ep[c] = high[c] + packed(term)


def share_kernel(odd, fas, fat, ea, *refs):
    *received, own, sent, scratch = refs
    value = received[0][...]
    for other in received[1:]:
        value = value + other[...]
    fold(split_pair(unpacked(value[0]), unpacked(value[1])), fas, fat, ea, scratch)
    is_odd = odd[0] == 1
    own[...] = jnp.where(is_odd, scratch[...], value)
    sent[...] = jnp.where(is_odd, value, scratch[...])


def density_kernel(slot, core, weight, x, f0s, f0t, gs, gt, weighted, *refs):
    *before, out = refs
    width = f0s.shape[-1]
    half = width // 2
    tall = width + 8
    w0, w1 = weight[slot[0], 0], weight[slot[0], 1]
    xs = unpacked_split(x)
    pr, pi = complex_dot(xs, load4(f0s))
    qr, qi = complex_dot(xs, load4(gs))
    u, v = w1 * pr + w0 * pi, w0 * pr - w1 * pi
    s, t = w1 * qr + w0 * qi, w0 * qr - w1 * qi
    us, ts = split_pair(u, v), split_pair(s, t)
    f, g = load4(f0t), load4(gt)

    def real_of(left, right):
        return dot3(left[0], left[2], right[0], right[2]) + dot3(left[1], left[3], right[1], right[3])

    def flat(block):
        return jnp.concatenate([block[:, :half], block[:, half:]], axis=0)

    second = flat(real_of(f, ts))
    first_entry, second_entry = core[0], 1 - core[0]

    def put(entry, start, stop, value):
        if before:
            value = value + before[0][entry, start:stop]
        out[entry, start:stop] = value

    put(first_entry, 0, 2 * width, flat(-u))
    put(first_entry, 2 * width, 2 * width + tall, weighted[0] + packed(real_of(f, us)))
    put(second_entry, 0, tall, -(second[:tall] + weighted[2]))
    put(second_entry, tall, 2 * width, -(second[tall:] + weighted[3, : width - 8]))
    put(second_entry, 2 * width, 2 * width + tall, weighted[1] + packed(real_of(g, ts)))


def unpack_kernel(core, mine, theirs, diag, off):
    width = diag.shape[-1]
    half = width // 2
    for source, entry in ((mine, core[0]), (theirs, 1 - core[0])):
        off[entry, :, :half] = source[:width]
        off[entry, :, half:] = source[width : 2 * width]
        diag[entry] = unpacked(source[2 * width :])


SCALAR = pl.BlockSpec(memory_space=pltpu.SMEM)
WHOLE = pl.BlockSpec(memory_space=pltpu.VMEM)


def run(kernel, scalars, arrays, shapes, dots, scratch=()):
    size = sum(a.size * a.dtype.itemsize for a in arrays)
    return pl.pallas_call(
        kernel,
        out_shape=shapes,
        in_specs=[SCALAR] * len(scalars) + [WHOLE] * len(arrays),
        out_specs=[WHOLE] * len(shapes),
        scratch_shapes=list(scratch),
        compiler_params=pltpu.CompilerParams(vmem_limit_bytes=VMEM_LIMIT),
        cost_estimate=pl.CostEstimate(flops=2 * dots * 256**3, bytes_accessed=size, transcendentals=0),
    )(*scalars, *arrays)


def one(value):
    return jnp.asarray(value, jnp.int32).reshape(1)


def prepare(slot, live, weight, pivot, factor):
    width = pivot.shape[-1]
    quarter = (width + 8, width // 2)
    block = (1,) + pivot.shape[1:]
    parts = jax.ShapeDtypeStruct((4, width, width), BF16)
    shapes = [parts] * 4 + [
        jax.ShapeDtypeStruct((2, width, width), F32),
        jax.ShapeDtypeStruct((2,) + quarter, F32),
        jax.ShapeDtypeStruct((4,) + quarter, F32),
    ]
    chosen = pl.BlockSpec(block, lambda i, s, l: (s[0], 0, 0, 0, 0))
    return pl.pallas_call(
        lambda slot, live, weight, pivot, factor, *outs: prepare_kernel(
            slot, live, weight, pivot, factor, *outs
        ),
        out_shape=shapes,
        grid_spec=pltpu.PrefetchScalarGridSpec(
            num_scalar_prefetch=2,
            grid=(1,),
            in_specs=[SCALAR, chosen, chosen],
            out_specs=[pl.BlockSpec(s.shape, lambda i, s_, l, n=len(s.shape): (0,) * n) for s in shapes],
        ),
        compiler_params=pltpu.CompilerParams(vmem_limit_bytes=VMEM_LIMIT),
        cost_estimate=pl.CostEstimate(flops=2 * 36 * width**3, bytes_accessed=6 * 2**20, transcendentals=0),
    )(slot, live, weight, pivot, factor)


def local(pivot, factor, live, weight):
    poles, turns = lax.axis_size("pole"), lax.axis_size("snode")
    rows = turns // 2
    pole, place = lax.axis_index("pole"), lax.axis_index("snode")
    row, odd, core = place // 2, place % 2, pole % 2
    width = pivot.shape[-1]
    quarter = (width + 8, width // 2)
    mirrored = jax.ShapeDtypeStruct((2,) + quarter, F32)
    parts = jax.ShapeDtypeStruct((4, width, width), BF16)

    def at(pole_index, snode_index):
        return pole_index * turns + snode_index

    def host(row_index, pole_index, wave):
        if row_index == 0:
            return 1
        return 2 * row_index + 1 - (pole_index % 2 ^ wave)

    hosted = jnp.where(row == 0, 1 - odd, jnp.where(odd == 1 - core, 0, 1))
    mine, other = one(hosted), one(1 - hosted)
    odd_flag, core_flag = one(odd), one(core)

    swaps = [
        (at(p, s), at(p, s ^ 1)) for p in range(poles) for s in range(2, turns)
    ]
    first = [(at(p, 0), at(p, 1)) for p in range(poles)]

    o_f0s, o_f0t, o_gs, o_gt, o_g, o_e, o_w = prepare(other, live, weight, pivot, factor)
    e_in = lax.ppermute(o_e, AXES, first + swaps)
    m_f0s, m_f0t, m_gs, m_gt, m_g, m_e, m_w = prepare(mine, live, weight, pivot, factor)
    g_in = lax.ppermute(o_g, AXES, swaps)
    e_second = lax.ppermute(m_e, AXES, first)

    starts = one(place == 1)
    (wave_a,) = run(step_kernel, [starts], [m_gs, m_gt, m_e, e_in], [mirrored], 24)
    (wave_b,) = run(step_kernel, [starts], [o_gs, o_gt, o_e, e_second], [mirrored], 24)

    received = []
    if rows > 1:
        received.append(
            lax.ppermute(wave_a, AXES, [(at(p, 1), at(p, host(1, p, 0))) for p in range(poles)])
        )
        received.append(
            lax.ppermute(wave_b, AXES, [(at(p, 1), at(p, host(1, p, 1))) for p in range(poles)])
        )
    fas, fat, ea, ps, pt, ep = run(
        pair_kernel,
        [odd_flag],
        [m_g, m_e, g_in, e_in],
        [parts, parts, mirrored, parts, parts, mirrored],
        36,
    )
    arrived = list(received)
    for turn in range(1, rows - 1):
        (wave,) = run(step_kernel, [one(row == turn)], [ps, pt, ep] + arrived, [mirrored], 24)
        arrived = [
            lax.ppermute(
                wave,
                AXES,
                [
                    (at(p, host(turn, p, w)), at(p, host(turn + 1, p, w)))
                    for p in range(poles)
                    for w in range(2)
                ],
            )
        ]
        received += arrived
    if not received:
        received = [jnp.zeros(mirrored.shape, F32)]
    own, sent = run(
        share_kernel,
        [odd_flag],
        [fas, fat, ea] + received,
        [mirrored, mirrored],
        24,
        [pltpu.VMEM(mirrored.shape, F32)],
    )
    both = [(at(p, s), at(p, s ^ 1)) for p in range(poles) for s in range(turns)]
    shared = lax.ppermute(sent, AXES, both)

    total = jax.ShapeDtypeStruct((2, 3 * width + 8, width // 2), F32)
    (sums,) = run(
        density_kernel, [mine, core_flag, weight], [own, m_f0s, m_f0t, m_gs, m_gt, m_w], [total], 42
    )
    (sums,) = run(
        density_kernel,
        [other, core_flag, weight],
        [shared, o_f0s, o_f0t, o_gs, o_gt, o_w, sums],
        [total],
        42,
    )
    def exchanged(value, distance):
        return lax.ppermute(value, "pole", [(p, p ^ distance) for p in range(poles)])

    kept = sums[0] + exchanged(sums[1], 1)
    distance = 2
    while distance < poles:
        kept = kept + exchanged(kept, distance)
        distance *= 2
    theirs = exchanged(kept, 1)
    full = jax.ShapeDtypeStruct((2, width, width), F32)
    return tuple(run(unpack_kernel, [core_flag], [kept, theirs], [full, full], 0))


def solution(mesh):
    placed = (
        P("pole", "snode", None, None, None),
        P("pole", "snode", None, None, None),
        P("snode"),
        P("pole", None),
    )
    return jax.shard_map(
        local,
        mesh=mesh,
        in_specs=placed,
        out_specs=(P("snode", None, None), P("snode", None, None)),
        check_vma=False,
    )
```

```python
import functools

import jax
import jax.numpy as jnp
from jax import lax
from jax.experimental import pallas as pl
from jax.experimental.pallas import tpu as pltpu
from jax.sharding import PartitionSpec as P

F32 = jnp.float32
BF16 = jnp.bfloat16
AXES = ("pole", "snode")
VMEM_LIMIT = 16 * 1024 * 1024


def halves(value):
    high = value.astype(BF16)
    return high, (value - high.astype(F32)).astype(BF16)


def split_pair(real, imag):
    (rh, rl), (ih, il) = halves(real), halves(imag)
    return rh, ih, rl, il


def dot(left, right):
    return jnp.dot(left, right, preferred_element_type=F32)


def dot3(lh, ll, rh, rl):
    return dot(lh, rh) + (dot(lh, rl) + dot(ll, rh))


def complex_dot(left, right):
    arh, aih, arl, ail = left
    brh, bih, brl, bil = right
    real = dot3(arh, arl, brh, brl) - dot3(aih, ail, bih, bil)
    imag = dot3(arh, arl, bih, bil) + dot3(aih, ail, brh, brl)
    return real, imag


def rows_columns(size):
    return (
        lax.broadcasted_iota(jnp.int32, (size, size), 0),
        lax.broadcasted_iota(jnp.int32, (size, size), 1),
    )


def packed(block):
    half = block.shape[0] // 2
    row, column = rows_columns(half)
    lower = block[half:, half:]
    mixed = jnp.where(row >= column, block[:half, :half], lower)
    diagonal = jnp.sum(jnp.where(row == column, lower, 0.0), axis=0, keepdims=True)
    return jnp.concatenate(
        [block[:half, half:], mixed, jnp.broadcast_to(diagonal, (8, half))], axis=0
    )


def unpacked(value):
    half = value.shape[1]
    row, column = rows_columns(half)
    right, mixed = value[:half], value[half : 2 * half]
    diagonal = value[2 * half : 2 * half + 1]
    turned = mixed.T
    first = jnp.where(row >= column, mixed, turned)
    last = jnp.where(row < column, mixed, jnp.where(row == column, diagonal, turned))
    return jnp.concatenate(
        [jnp.concatenate([first, right], axis=1), jnp.concatenate([right.T, last], axis=1)], axis=0
    )


def unpacked_split(ref):
    return split_pair(unpacked(ref[0]), unpacked(ref[1]))


def load4(ref):
    return tuple(ref[i] for i in range(4))


def store4(ref, parts):
    for i, part in enumerate(parts):
        ref[i] = part


def factor_kernel(slot, live, factor, f0s, f0t, f1s, f1t, gs, gt, g, link, widths, sems):
    width = factor.shape[-1]
    copies = [
        pltpu.make_async_copy(live, widths, sems.at[0]),
        pltpu.make_async_copy(factor.at[slot[0], 0], link.at[0], sems.at[1]),
        pltpu.make_async_copy(factor.at[slot[0], 1], link.at[1], sems.at[2]),
    ]
    for copy in copies:
        copy.start()
    for copy in copies:
        copy.wait()
    _, column = rows_columns(width)
    f = [
        [jnp.where(column < widths[k], link[k, c], 0.0) for c in range(2)] for k in range(2)
    ]
    s0, s1 = split_pair(*f[0]), split_pair(*f[1])
    gr, gi = complex_dot(s0, s1)
    g[0], g[1] = gr, gi
    store4(gs, split_pair(gr, gi))
    store4(gt, split_pair(gr.T, gi.T))
    store4(f0s, s0)
    store4(f0t, split_pair(f[0][0].T, f[0][1].T))
    store4(f1s, s1)
    store4(f1t, split_pair(f[1][0].T, f[1][1].T))


def constant_kernel(slot, live, weight, pivot, f1s, f1t, e, weighted):
    width = pivot.shape[-1]
    row, column = rows_columns(width)
    d = []
    for k in range(2):
        both = jnp.logical_and(row < live[k], column < live[k])
        d.append([jnp.where(both, pivot[slot[0], k, c], 0.0) for c in range(2)])
    br, bi = complex_dot(split_pair(*d[0]), load4(f1s))
    tr, ti = complex_dot(load4(f1t), split_pair(br, bi))
    er, ei = d[1][0] + tr, d[1][1] + ti
    e[0], e[1] = packed(er), packed(ei)
    w0, w1 = weight[slot[0], 0], weight[slot[0], 1]
    weighted[0] = packed(w1 * d[0][0] + w0 * d[0][1])
    weighted[1] = packed(w1 * er + w0 * ei)
    b = w1 * br + w0 * bi
    half = width // 2
    weighted_b = jnp.concatenate([b[:, :half], b[:, half:]], axis=0)
    weighted[2] = weighted_b[: width + 8]
    weighted[3, : width - 8] = weighted_b[width + 8 :]


def fold(x, gs, gt, e, out):
    tr, ti = complex_dot(x, load4(gs))
    yr, yi = complex_dot(load4(gt), split_pair(tr, ti))
    out[0] = e[0] + packed(yr)
    out[1] = e[1] + packed(yi)


def step_kernel(active, gs, gt, e, *refs):
    *received, out = refs

    @pl.when(active[0] == 1)
    def _():
        value = received[0][...]
        for other in received[1:]:
            value = value + other[...]
        fold(split_pair(unpacked(value[0]), unpacked(value[1])), gs, gt, e, out)


def pair_kernel(odd, g, e, g_in, e_first, e_swapped, fas, fat, ea, ps, pt, ep):
    is_odd = odd[0] == 1
    ga = [jnp.where(is_odd, g_in[c], g[c]) for c in range(2)]
    gb = [jnp.where(is_odd, g[c], g_in[c]) for c in range(2)]
    e_in = [e_first[c] + e_swapped[c] for c in range(2)]
    low = [jnp.where(is_odd, e_in[c], e[c]) for c in range(2)]
    high = [jnp.where(is_odd, e[c], e_in[c]) for c in range(2)]
    sa, sb = split_pair(*ga), split_pair(*gb)
    store4(fas, sa)
    store4(fat, split_pair(ga[0].T, ga[1].T))
    pr, pi = complex_dot(sa, sb)
    store4(ps, split_pair(pr, pi))
    store4(pt, split_pair(pr.T, pi.T))
    br, bi = complex_dot(split_pair(unpacked(low[0]), unpacked(low[1])), sb)
    tr, ti = complex_dot(split_pair(gb[0].T, gb[1].T), split_pair(br, bi))
    for c, term in enumerate((tr, ti)):
        ea[c] = low[c]
        ep[c] = high[c] + packed(term)


def share_kernel(odd, fas, fat, ea, *refs):
    *received, own, sent, scratch = refs
    value = received[0][...]
    for other in received[1:]:
        value = value + other[...]
    fold(split_pair(unpacked(value[0]), unpacked(value[1])), fas, fat, ea, scratch)
    is_odd = odd[0] == 1
    own[...] = jnp.where(is_odd, scratch[...], value)
    sent[...] = jnp.where(is_odd, value, scratch[...])


def density_kernel(slot, core, weight, x, f0s, f0t, gs, gt, weighted, *refs):
    *before, out = refs
    width = f0s.shape[-1]
    half = width // 2
    tall = width + 8
    w0, w1 = weight[slot[0], 0], weight[slot[0], 1]
    xs = unpacked_split(x)
    pr, pi = complex_dot(xs, load4(f0s))
    qr, qi = complex_dot(xs, load4(gs))
    u, v = w1 * pr + w0 * pi, w0 * pr - w1 * pi
    s, t = w1 * qr + w0 * qi, w0 * qr - w1 * qi
    us, ts = split_pair(u, v), split_pair(s, t)
    f, g = load4(f0t), load4(gt)

    def real_of(left, right):
        return dot3(left[0], left[2], right[0], right[2]) + dot3(left[1], left[3], right[1], right[3])

    def flat(block):
        return jnp.concatenate([block[:, :half], block[:, half:]], axis=0)

    second = flat(real_of(f, ts))
    first_entry, second_entry = core[0], 1 - core[0]

    def put(entry, start, stop, value):
        if before:
            value = value + before[0][entry, start:stop]
        out[entry, start:stop] = value

    put(first_entry, 0, 2 * width, flat(-u))
    put(first_entry, 2 * width, 2 * width + tall, weighted[0] + packed(real_of(f, us)))
    put(second_entry, 0, tall, -(second[:tall] + weighted[2]))
    put(second_entry, tall, 2 * width, -(second[tall:] + weighted[3, : width - 8]))
    put(second_entry, 2 * width, 2 * width + tall, weighted[1] + packed(real_of(g, ts)))


def unpack_kernel(core, mine, theirs, diag, off):
    width = diag.shape[-1]
    half = width // 2
    for source, entry in ((mine, core[0]), (theirs, 1 - core[0])):
        off[entry, :, :half] = source[:width]
        off[entry, :, half:] = source[width : 2 * width]
        diag[entry] = unpacked(source[2 * width :])


SCALAR = pl.BlockSpec(memory_space=pltpu.SMEM)
WHOLE = pl.BlockSpec(memory_space=pltpu.VMEM)


def run(kernel, scalars, arrays, shapes, dots, scratch=()):
    size = sum(a.size * a.dtype.itemsize for a in arrays)
    return pl.pallas_call(
        kernel,
        out_shape=shapes,
        in_specs=[SCALAR] * len(scalars) + [WHOLE] * len(arrays),
        out_specs=[WHOLE] * len(shapes),
        scratch_shapes=list(scratch),
        compiler_params=pltpu.CompilerParams(vmem_limit_bytes=VMEM_LIMIT),
        cost_estimate=pl.CostEstimate(flops=2 * dots * 256**3, bytes_accessed=size, transcendentals=0),
    )(*scalars, *arrays)


def one(value):
    return jnp.asarray(value, jnp.int32).reshape(1)


def fold_factors(slot, live, factor):
    width = factor.shape[-1]
    parts = jax.ShapeDtypeStruct((4, width, width), BF16)
    shapes = [parts] * 6 + [jax.ShapeDtypeStruct((2, width, width), F32)]
    far = pl.BlockSpec(memory_space=pltpu.HBM)
    return pl.pallas_call(
        factor_kernel,
        out_shape=shapes,
        in_specs=[SCALAR, far, far],
        out_specs=[WHOLE] * len(shapes),
        scratch_shapes=[
            pltpu.VMEM(factor.shape[1:], F32),
            pltpu.SMEM(live.shape, jnp.int32),
            pltpu.SemaphoreType.DMA((3,)),
        ],
        compiler_params=pltpu.CompilerParams(vmem_limit_bytes=VMEM_LIMIT),
        cost_estimate=pl.CostEstimate(flops=24 * width**3, bytes_accessed=2**20, transcendentals=0),
    )(slot, live, factor)


def local(pivot, factor, live, weight):
    poles, turns = lax.axis_size("pole"), lax.axis_size("snode")
    rows = turns // 2
    pole, place = lax.axis_index("pole"), lax.axis_index("snode")
    row, odd, core = place // 2, place % 2, pole % 2
    width = pivot.shape[-1]
    quarter = (width + 8, width // 2)
    mirrored = jax.ShapeDtypeStruct((2,) + quarter, F32)
    parts = jax.ShapeDtypeStruct((4, width, width), BF16)

    def at(pole_index, snode_index):
        return pole_index * turns + snode_index

    def host(row_index, pole_index, wave):
        if row_index == 0:
            return 1
        return 2 * row_index + 1 - (pole_index % 2 ^ wave)

    hosted = jnp.where(row == 0, 1 - odd, jnp.where(odd == 1 - core, 0, 1))
    mine, other = one(hosted), one(1 - hosted)
    odd_flag, core_flag = one(odd), one(core)

    swaps = [(at(p, s), at(p, s ^ 1)) for p in range(poles) for s in range(2, turns)]
    first = [(at(p, 0), at(p, 1)) for p in range(poles)]
    constants = [mirrored, jax.ShapeDtypeStruct((4,) + quarter, F32)]

    factor = pltpu.with_memory_space_constraint(factor, pltpu.HBM)
    far_live = pltpu.with_memory_space_constraint(live, pltpu.HBM)
    o_f0s, o_f0t, o_f1s, o_f1t, o_gs, o_gt, o_g = fold_factors(other, far_live, factor)
    g_in = lax.ppermute(o_g, AXES, swaps)
    o_e, o_w = run(constant_kernel, [other, live, weight], [pivot, o_f1s, o_f1t], constants, 24)
    e_first = lax.ppermute(o_e, AXES, first)
    e_swapped = lax.ppermute(o_e, AXES, swaps)
    m_f0s, m_f0t, m_f1s, m_f1t, m_gs, m_gt, m_g = fold_factors(mine, far_live, factor)
    m_e, m_w = run(constant_kernel, [mine, live, weight], [pivot, m_f1s, m_f1t], constants, 24)
    e_second = lax.ppermute(m_e, AXES, first)

    starts = one(place == 1)
    (wave_a,) = run(step_kernel, [starts], [m_gs, m_gt, m_e, e_first], [mirrored], 24)
    (wave_b,) = run(step_kernel, [starts], [o_gs, o_gt, o_e, e_second], [mirrored], 24)

    received = []
    if rows > 1:
        received.append(
            lax.ppermute(wave_a, AXES, [(at(p, 1), at(p, host(1, p, 0))) for p in range(poles)])
        )
        received.append(
            lax.ppermute(wave_b, AXES, [(at(p, 1), at(p, host(1, p, 1))) for p in range(poles)])
        )
    fas, fat, ea, ps, pt, ep = run(
        pair_kernel,
        [odd_flag],
        [m_g, m_e, g_in, e_first, e_swapped],
        [parts, parts, mirrored, parts, parts, mirrored],
        36,
    )
    arrived = list(received)
    for turn in range(1, rows - 1):
        (wave,) = run(step_kernel, [one(row == turn)], [ps, pt, ep] + arrived, [mirrored], 24)
        arrived = [
            lax.ppermute(
                wave,
                AXES,
                [
                    (at(p, host(turn, p, w)), at(p, host(turn + 1, p, w)))
                    for p in range(poles)
                    for w in range(2)
                ],
            )
        ]
        received += arrived
    if not received:
        received = [jnp.zeros(mirrored.shape, F32)]
    own, sent = run(
        share_kernel,
        [odd_flag],
        [fas, fat, ea] + received,
        [mirrored, mirrored],
        24,
        [pltpu.VMEM(mirrored.shape, F32)],
    )
    both = [(at(p, s), at(p, s ^ 1)) for p in range(poles) for s in range(turns)]
    shared = lax.ppermute(sent, AXES, both)

    total = jax.ShapeDtypeStruct((2, 3 * width + 8, width // 2), F32)
    (sums,) = run(
        density_kernel, [mine, core_flag, weight], [own, m_f0s, m_f0t, m_gs, m_gt, m_w], [total], 42
    )
    (sums,) = run(
        density_kernel,
        [other, core_flag, weight],
        [shared, o_f0s, o_f0t, o_gs, o_gt, o_w, sums],
        [total],
        42,
    )
    def exchanged(value, distance):
        return lax.ppermute(value, "pole", [(p, p ^ distance) for p in range(poles)])

    kept = sums[0] + exchanged(sums[1], 1)
    distance = 2
    while distance < poles:
        kept = kept + exchanged(kept, distance)
        distance *= 2
    theirs = exchanged(kept, 1)
    full = jax.ShapeDtypeStruct((2, width, width), F32)
    return tuple(run(unpack_kernel, [core_flag], [kept, theirs], [full, full], 0))


def solution(mesh):
    placed = (
        P("pole", "snode", None, None, None),
        P("pole", "snode", None, None, None),
        P("snode"),
        P("pole", None),
    )
    return jax.shard_map(
        local,
        mesh=mesh,
        in_specs=placed,
        out_specs=(P("snode", None, None), P("snode", None, None)),
        check_vma=False,
    )
```

```python
import functools

import jax
import jax.numpy as jnp
from jax import lax
from jax.experimental import pallas as pl
from jax.experimental.pallas import tpu as pltpu
from jax.sharding import PartitionSpec as P

F32 = jnp.float32
BF16 = jnp.bfloat16
AXES = ("pole", "snode")
VMEM_LIMIT = 16 * 1024 * 1024


def halves(value):
    high = value.astype(BF16)
    return high, (value - high.astype(F32)).astype(BF16)


def split_pair(real, imag):
    (rh, rl), (ih, il) = halves(real), halves(imag)
    return rh, ih, rl, il


def dot(left, right):
    return jnp.dot(left, right, preferred_element_type=F32)


def dot3(lh, ll, rh, rl):
    return dot(lh, rh) + (dot(lh, rl) + dot(ll, rh))


def complex_dot(left, right):
    arh, aih, arl, ail = left
    brh, bih, brl, bil = right
    real = dot3(arh, arl, brh, brl) - dot3(aih, ail, bih, bil)
    imag = dot3(arh, arl, bih, bil) + dot3(aih, ail, brh, brl)
    return real, imag


def rows_columns(size):
    return (
        lax.broadcasted_iota(jnp.int32, (size, size), 0),
        lax.broadcasted_iota(jnp.int32, (size, size), 1),
    )


def packed(block):
    half = block.shape[0] // 2
    row, column = rows_columns(half)
    lower = block[half:, half:]
    mixed = jnp.where(row >= column, block[:half, :half], lower)
    diagonal = jnp.sum(jnp.where(row == column, lower, 0.0), axis=0, keepdims=True)
    return jnp.concatenate(
        [block[:half, half:], mixed, jnp.broadcast_to(diagonal, (8, half))], axis=0
    )


def unpacked(value):
    half = value.shape[1]
    row, column = rows_columns(half)
    right, mixed = value[:half], value[half : 2 * half]
    diagonal = value[2 * half : 2 * half + 1]
    turned = mixed.T
    first = jnp.where(row >= column, mixed, turned)
    last = jnp.where(row < column, mixed, jnp.where(row == column, diagonal, turned))
    return jnp.concatenate(
        [jnp.concatenate([first, right], axis=1), jnp.concatenate([right.T, last], axis=1)], axis=0
    )


def unpacked_split(ref):
    return split_pair(unpacked(ref[0]), unpacked(ref[1]))


def load4(ref):
    return tuple(ref[i] for i in range(4))


def store4(ref, parts):
    for i, part in enumerate(parts):
        ref[i] = part


def whereabouts():
    place = lax.axis_index("snode")
    return place, lax.rem(place, 2), lax.rem(lax.axis_index("pole"), 2)


def hosted_slot():
    place, odd, core = whereabouts()
    return jnp.where(place < 2, 1 - odd, jnp.where(odd == 1 - core, 0, 1))


def slot_of(hosted):
    return hosted_slot() if hosted else 1 - hosted_slot()


def factor_kernel(hosted, live, factor, f0s, f0t, f1s, f1t, gs, gt, g, link, widths, sems):
    width = factor.shape[-1]
    slot = slot_of(hosted)
    copies = [
        pltpu.make_async_copy(live, widths, sems.at[0]),
        pltpu.make_async_copy(factor.at[slot, 0], link.at[0], sems.at[1]),
        pltpu.make_async_copy(factor.at[slot, 1], link.at[1], sems.at[2]),
    ]
    for copy in copies:
        copy.start()
    for copy in copies:
        copy.wait()
    _, column = rows_columns(width)
    f = [
        [jnp.where(column < widths[k], link[k, c], 0.0) for c in range(2)] for k in range(2)
    ]
    s0, s1 = split_pair(*f[0]), split_pair(*f[1])
    gr, gi = complex_dot(s0, s1)
    g[0], g[1] = gr, gi
    store4(gs, split_pair(gr, gi))
    store4(gt, split_pair(gr.T, gi.T))
    store4(f0s, s0)
    store4(f0t, split_pair(f[0][0].T, f[0][1].T))
    store4(f1s, s1)
    store4(f1t, split_pair(f[1][0].T, f[1][1].T))


def constant_kernel(hosted, live, weight, pivot, f1s, f1t, e, weighted):
    width = pivot.shape[-1]
    slot = slot_of(hosted)
    row, column = rows_columns(width)
    d = []
    for k in range(2):
        both = jnp.logical_and(row < live[k], column < live[k])
        d.append([jnp.where(both, pivot[slot, k, c], 0.0) for c in range(2)])
    br, bi = complex_dot(split_pair(*d[0]), load4(f1s))
    tr, ti = complex_dot(load4(f1t), split_pair(br, bi))
    er, ei = d[1][0] + tr, d[1][1] + ti
    e[0], e[1] = packed(er), packed(ei)
    w0, w1 = weight[slot, 0], weight[slot, 1]
    weighted[0] = packed(w1 * d[0][0] + w0 * d[0][1])
    weighted[1] = packed(w1 * er + w0 * ei)
    b = w1 * br + w0 * bi
    half = width // 2
    weighted_b = jnp.concatenate([b[:, :half], b[:, half:]], axis=0)
    weighted[2] = weighted_b[: width + 8]
    weighted[3, : width - 8] = weighted_b[width + 8 :]


def fold(x, gs, gt, e, out):
    tr, ti = complex_dot(x, load4(gs))
    yr, yi = complex_dot(load4(gt), split_pair(tr, ti))
    out[0] = e[0] + packed(yr)
    out[1] = e[1] + packed(yi)


def step_kernel(active, gs, gt, e, *refs):
    *received, out = refs

    @pl.when(active(whereabouts()[0]))
    def _():
        value = received[0][...]
        for other in received[1:]:
            value = value + other[...]
        fold(split_pair(unpacked(value[0]), unpacked(value[1])), gs, gt, e, out)


def pair_kernel(g, e, g_in, e_first, e_swapped, fas, fat, ea, ps, pt, ep):
    is_odd = whereabouts()[1] == 1
    ga = [jnp.where(is_odd, g_in[c], g[c]) for c in range(2)]
    gb = [jnp.where(is_odd, g[c], g_in[c]) for c in range(2)]
    e_in = [e_first[c] + e_swapped[c] for c in range(2)]
    low = [jnp.where(is_odd, e_in[c], e[c]) for c in range(2)]
    high = [jnp.where(is_odd, e[c], e_in[c]) for c in range(2)]
    sa, sb = split_pair(*ga), split_pair(*gb)
    store4(fas, sa)
    store4(fat, split_pair(ga[0].T, ga[1].T))
    pr, pi = complex_dot(sa, sb)
    store4(ps, split_pair(pr, pi))
    store4(pt, split_pair(pr.T, pi.T))
    br, bi = complex_dot(split_pair(unpacked(low[0]), unpacked(low[1])), sb)
    tr, ti = complex_dot(split_pair(gb[0].T, gb[1].T), split_pair(br, bi))
    for c, term in enumerate((tr, ti)):
        ea[c] = low[c]
        ep[c] = high[c] + packed(term)


def share_kernel(fas, fat, ea, *refs):
    *received, own, sent, scratch = refs
    value = received[0][...]
    for other in received[1:]:
        value = value + other[...]
    fold(split_pair(unpacked(value[0]), unpacked(value[1])), fas, fat, ea, scratch)
    is_odd = whereabouts()[1] == 1
    own[...] = jnp.where(is_odd, scratch[...], value)
    sent[...] = jnp.where(is_odd, value, scratch[...])


def density_kernel(hosted, weight, x, f0s, f0t, gs, gt, weighted, *refs):
    *before, out = refs
    width = f0s.shape[-1]
    half = width // 2
    tall = width + 8
    slot = slot_of(hosted)
    w0, w1 = weight[pl.ds(slot, 1), 0:1], weight[pl.ds(slot, 1), 1:2]
    xs = unpacked_split(x)
    pr, pi = complex_dot(xs, load4(f0s))
    qr, qi = complex_dot(xs, load4(gs))
    u, v = w1 * pr + w0 * pi, w0 * pr - w1 * pi
    s, t = w1 * qr + w0 * qi, w0 * qr - w1 * qi
    us, ts = split_pair(u, v), split_pair(s, t)
    f, g = load4(f0t), load4(gt)

    def real_of(left, right):
        return dot3(left[0], left[2], right[0], right[2]) + dot3(left[1], left[3], right[1], right[3])

    def flat(block):
        return jnp.concatenate([block[:, :half], block[:, half:]], axis=0)

    second = flat(real_of(f, ts))
    core = whereabouts()[2]
    first_entry, second_entry = core, 1 - core

    def put(entry, start, stop, value):
        if before:
            value = value + before[0][entry, start:stop]
        out[entry, start:stop] = value

    put(first_entry, 0, 2 * width, flat(-u))
    put(first_entry, 2 * width, 2 * width + tall, weighted[0] + packed(real_of(f, us)))
    put(second_entry, 0, tall, -(second[:tall] + weighted[2]))
    put(second_entry, tall, 2 * width, -(second[tall:] + weighted[3, : width - 8]))
    put(second_entry, 2 * width, 2 * width + tall, weighted[1] + packed(real_of(g, ts)))


def unpack_kernel(mine, theirs, diag, off):
    core = whereabouts()[2]
    width = diag.shape[-1]
    half = width // 2
    for source, entry in ((mine, core), (theirs, 1 - core)):
        off[entry, :, :half] = source[:width]
        off[entry, :, half:] = source[width : 2 * width]
        diag[entry] = unpacked(source[2 * width :])


SCALAR = pl.BlockSpec(memory_space=pltpu.SMEM)
WHOLE = pl.BlockSpec(memory_space=pltpu.VMEM)


def run(kernel, scalars, arrays, shapes, dots, scratch=()):
    size = sum(a.size * a.dtype.itemsize for a in arrays)
    return pl.pallas_call(
        kernel,
        out_shape=shapes,
        in_specs=[SCALAR] * len(scalars) + [WHOLE] * len(arrays),
        out_specs=[WHOLE] * len(shapes),
        scratch_shapes=list(scratch),
        compiler_params=pltpu.CompilerParams(vmem_limit_bytes=VMEM_LIMIT),
        cost_estimate=pl.CostEstimate(flops=2 * dots * 256**3, bytes_accessed=size, transcendentals=0),
    )(*scalars, *arrays)


def fold_factors(hosted, live, factor):
    width = factor.shape[-1]
    parts = jax.ShapeDtypeStruct((4, width, width), BF16)
    shapes = [parts] * 6 + [jax.ShapeDtypeStruct((2, width, width), F32)]
    far = pl.BlockSpec(memory_space=pltpu.HBM)
    return pl.pallas_call(
        functools.partial(factor_kernel, hosted),
        out_shape=shapes,
        in_specs=[far, far],
        out_specs=[WHOLE] * len(shapes),
        scratch_shapes=[
            pltpu.VMEM(factor.shape[1:], F32),
            pltpu.SMEM(live.shape, jnp.int32),
            pltpu.SemaphoreType.DMA((3,)),
        ],
        compiler_params=pltpu.CompilerParams(vmem_limit_bytes=VMEM_LIMIT),
        cost_estimate=pl.CostEstimate(flops=24 * width**3, bytes_accessed=2**20, transcendentals=0),
    )(live, factor)


def local(pivot, factor, live, weight):
    poles, turns = lax.axis_size("pole"), lax.axis_size("snode")
    rows = turns // 2
    width = pivot.shape[-1]
    quarter = (width + 8, width // 2)
    mirrored = jax.ShapeDtypeStruct((2,) + quarter, F32)
    parts = jax.ShapeDtypeStruct((4, width, width), BF16)

    def at(pole_index, snode_index):
        return pole_index * turns + snode_index

    def host(row_index, pole_index, wave):
        if row_index == 0:
            return 1
        return 2 * row_index + 1 - (pole_index % 2 ^ wave)

    swaps = [(at(p, s), at(p, s ^ 1)) for p in range(poles) for s in range(2, turns)]
    first = [(at(p, 0), at(p, 1)) for p in range(poles)]
    constants = [mirrored, jax.ShapeDtypeStruct((4,) + quarter, F32)]

    factor = pltpu.with_memory_space_constraint(factor, pltpu.HBM)
    far_live = pltpu.with_memory_space_constraint(live, pltpu.HBM)
    o_f0s, o_f0t, o_f1s, o_f1t, o_gs, o_gt, o_g = fold_factors(False, far_live, factor)
    g_in = lax.ppermute(o_g, AXES, swaps)
    o_e, o_w = run(functools.partial(constant_kernel, False), [live, weight], [pivot, o_f1s, o_f1t], constants, 24)
    e_first = lax.ppermute(o_e, AXES, first)
    e_swapped = lax.ppermute(o_e, AXES, swaps)
    m_f0s, m_f0t, m_f1s, m_f1t, m_gs, m_gt, m_g = fold_factors(True, far_live, factor)
    m_e, m_w = run(functools.partial(constant_kernel, True), [live, weight], [pivot, m_f1s, m_f1t], constants, 24)
    e_second = lax.ppermute(m_e, AXES, first)

    starts = functools.partial(step_kernel, lambda place: place == 1)
    (wave_a,) = run(starts, [], [m_gs, m_gt, m_e, e_first], [mirrored], 24)
    (wave_b,) = run(starts, [], [o_gs, o_gt, o_e, e_second], [mirrored], 24)

    received = []
    if rows > 1:
        received.append(
            lax.ppermute(wave_a, AXES, [(at(p, 1), at(p, host(1, p, 0))) for p in range(poles)])
        )
        received.append(
            lax.ppermute(wave_b, AXES, [(at(p, 1), at(p, host(1, p, 1))) for p in range(poles)])
        )
    fas, fat, ea, ps, pt, ep = run(
        pair_kernel,
        [],
        [m_g, m_e, g_in, e_first, e_swapped],
        [parts, parts, mirrored, parts, parts, mirrored],
        36,
    )
    arrived = list(received)
    for turn in range(1, rows - 1):
        active = functools.partial(step_kernel, lambda place, turn=turn: lax.div(place, 2) == turn)
        (wave,) = run(active, [], [ps, pt, ep] + arrived, [mirrored], 24)
        arrived = [
            lax.ppermute(
                wave,
                AXES,
                [
                    (at(p, host(turn, p, w)), at(p, host(turn + 1, p, w)))
                    for p in range(poles)
                    for w in range(2)
                ],
            )
        ]
        received += arrived
    if not received:
        received = [jnp.zeros(mirrored.shape, F32)]
    own, sent = run(
        share_kernel,
        [],
        [fas, fat, ea] + received,
        [mirrored, mirrored],
        24,
        [pltpu.VMEM(mirrored.shape, F32)],
    )
    both = [(at(p, s), at(p, s ^ 1)) for p in range(poles) for s in range(turns)]
    shared = lax.ppermute(sent, AXES, both)

    total = jax.ShapeDtypeStruct((2, 3 * width + 8, width // 2), F32)
    (sums,) = run(
        functools.partial(density_kernel, True), [], [weight, own, m_f0s, m_f0t, m_gs, m_gt, m_w], [total], 42
    )
    (sums,) = run(
        functools.partial(density_kernel, False),
        [],
        [weight, shared, o_f0s, o_f0t, o_gs, o_gt, o_w, sums],
        [total],
        42,
    )
    def exchanged(value, distance):
        return lax.ppermute(value, "pole", [(p, p ^ distance) for p in range(poles)])

    kept = sums[0] + exchanged(sums[1], 1)
    distance = 2
    while distance < poles:
        kept = kept + exchanged(kept, distance)
        distance *= 2
    theirs = exchanged(kept, 1)
    full = jax.ShapeDtypeStruct((2, width, width), F32)
    return tuple(run(unpack_kernel, [], [kept, theirs], [full, full], 0))


def solution(mesh):
    placed = (
        P("pole", "snode", None, None, None),
        P("pole", "snode", None, None, None),
        P("snode"),
        P("pole", None),
    )
    return jax.shard_map(
        local,
        mesh=mesh,
        in_specs=placed,
        out_specs=(P("snode", None, None), P("snode", None, None)),
        check_vma=False,
    )
```

```python
import functools

import jax
import jax.numpy as jnp
from jax import lax
from jax.experimental import pallas as pl
from jax.experimental.pallas import tpu as pltpu
from jax.sharding import PartitionSpec as P

F32 = jnp.float32
BF16 = jnp.bfloat16
AXES = ("pole", "snode")
VMEM_LIMIT = 16 * 1024 * 1024


def halves(value):
    high = value.astype(BF16)
    return high, (value - high.astype(F32)).astype(BF16)


def split_pair(real, imag):
    (rh, rl), (ih, il) = halves(real), halves(imag)
    return rh, ih, rl, il


def dot(left, right):
    return jnp.dot(left, right, preferred_element_type=F32)


def dot3(lh, ll, rh, rl):
    return dot(lh, rh) + (dot(lh, rl) + dot(ll, rh))


def complex_dot(left, right):
    arh, aih, arl, ail = left
    brh, bih, brl, bil = right
    real = dot3(arh, arl, brh, brl) - dot3(aih, ail, bih, bil)
    imag = dot3(arh, arl, bih, bil) + dot3(aih, ail, brh, brl)
    return real, imag


def rows_columns(size):
    return (
        lax.broadcasted_iota(jnp.int32, (size, size), 0),
        lax.broadcasted_iota(jnp.int32, (size, size), 1),
    )


def packed(block):
    half = block.shape[0] // 2
    row, column = rows_columns(half)
    lower = block[half:, half:]
    mixed = jnp.where(row >= column, block[:half, :half], lower)
    diagonal = jnp.sum(jnp.where(row == column, lower, 0.0), axis=0, keepdims=True)
    return jnp.concatenate(
        [block[:half, half:], mixed, jnp.broadcast_to(diagonal, (8, half))], axis=0
    )


def unpacked(value):
    half = value.shape[1]
    row, column = rows_columns(half)
    right, mixed = value[:half], value[half : 2 * half]
    diagonal = value[2 * half : 2 * half + 1]
    turned = mixed.T
    first = jnp.where(row >= column, mixed, turned)
    last = jnp.where(row < column, mixed, jnp.where(row == column, diagonal, turned))
    return jnp.concatenate(
        [jnp.concatenate([first, right], axis=1), jnp.concatenate([right.T, last], axis=1)], axis=0
    )


def unpacked_split(ref):
    return split_pair(unpacked(ref[0]), unpacked(ref[1]))


def load4(ref):
    return tuple(ref[i] for i in range(4))


def store4(ref, parts):
    for i, part in enumerate(parts):
        ref[i] = part


def whereabouts():
    place = lax.axis_index("snode")
    return place, lax.rem(place, 2), lax.rem(lax.axis_index("pole"), 2)


def hosted_slot():
    place, odd, core = whereabouts()
    upper = jnp.where(place < 2, 1, odd)
    return jnp.where(upper == 1 - core, 0, 1)


def slot_of(hosted):
    return hosted_slot() if hosted else 1 - hosted_slot()


def factor_kernel(hosted, live, factor, f0s, f0t, f1s, f1t, gs, gt, g, link, widths, sems):
    width = factor.shape[-1]
    slot = slot_of(hosted)
    copies = [
        pltpu.make_async_copy(live, widths, sems.at[0]),
        pltpu.make_async_copy(factor.at[slot, 0], link.at[0], sems.at[1]),
        pltpu.make_async_copy(factor.at[slot, 1], link.at[1], sems.at[2]),
    ]
    for copy in copies:
        copy.start()
    for copy in copies:
        copy.wait()
    _, column = rows_columns(width)
    f = [
        [jnp.where(column < widths[k], link[k, c], 0.0) for c in range(2)] for k in range(2)
    ]
    s0, s1 = split_pair(*f[0]), split_pair(*f[1])
    gr, gi = complex_dot(s0, s1)
    g[0], g[1] = gr, gi
    store4(gs, split_pair(gr, gi))
    store4(gt, split_pair(gr.T, gi.T))
    store4(f0s, s0)
    store4(f0t, split_pair(f[0][0].T, f[0][1].T))
    store4(f1s, s1)
    store4(f1t, split_pair(f[1][0].T, f[1][1].T))


def constant_kernel(hosted, live, weight, pivot, f1s, f1t, e, weighted):
    width = pivot.shape[-1]
    slot = slot_of(hosted)
    row, column = rows_columns(width)
    d = []
    for k in range(2):
        both = jnp.logical_and(row < live[k], column < live[k])
        d.append([jnp.where(both, pivot[slot, k, c], 0.0) for c in range(2)])
    br, bi = complex_dot(split_pair(*d[0]), load4(f1s))
    tr, ti = complex_dot(load4(f1t), split_pair(br, bi))
    er, ei = d[1][0] + tr, d[1][1] + ti
    e[0], e[1] = packed(er), packed(ei)
    w0, w1 = weight[slot, 0], weight[slot, 1]
    weighted[0] = packed(w1 * d[0][0] + w0 * d[0][1])
    weighted[1] = packed(w1 * er + w0 * ei)
    b = w1 * br + w0 * bi
    half = width // 2
    weighted_b = jnp.concatenate([b[:, :half], b[:, half:]], axis=0)
    weighted[2] = weighted_b[: width + 8]
    weighted[3, : width - 8] = weighted_b[width + 8 :]


def fold(x, gs, gt, e, out):
    tr, ti = complex_dot(x, load4(gs))
    yr, yi = complex_dot(load4(gt), split_pair(tr, ti))
    out[0] = e[0] + packed(yr)
    out[1] = e[1] + packed(yi)


def step_kernel(active, gs, gt, e, *refs):
    *received, out = refs

    @pl.when(active(whereabouts()[0]))
    def _():
        value = received[0][...]
        for other in received[1:]:
            value = value + other[...]
        fold(split_pair(unpacked(value[0]), unpacked(value[1])), gs, gt, e, out)


def pair_kernel(g, e, g_in, e_second, e_swapped, fas, fat, ea, ps, pt, ep):
    is_odd = whereabouts()[1] == 1
    ga = [jnp.where(is_odd, g_in[c], g[c]) for c in range(2)]
    gb = [jnp.where(is_odd, g[c], g_in[c]) for c in range(2)]
    e_in = [e_second[c] + e_swapped[c] for c in range(2)]
    low = [jnp.where(is_odd, e_in[c], e[c]) for c in range(2)]
    high = [jnp.where(is_odd, e[c], e_in[c]) for c in range(2)]
    sa, sb = split_pair(*ga), split_pair(*gb)
    store4(fas, sa)
    store4(fat, split_pair(ga[0].T, ga[1].T))
    pr, pi = complex_dot(sa, sb)
    store4(ps, split_pair(pr, pi))
    store4(pt, split_pair(pr.T, pi.T))
    br, bi = complex_dot(split_pair(unpacked(low[0]), unpacked(low[1])), sb)
    tr, ti = complex_dot(split_pair(gb[0].T, gb[1].T), split_pair(br, bi))
    for c, term in enumerate((tr, ti)):
        ea[c] = low[c]
        ep[c] = high[c] + packed(term)


def share_kernel(fas, fat, ea, *refs):
    *received, own, sent, scratch = refs
    value = received[0][...]
    for other in received[1:]:
        value = value + other[...]
    fold(split_pair(unpacked(value[0]), unpacked(value[1])), fas, fat, ea, scratch)
    is_odd = whereabouts()[1] == 1
    own[...] = jnp.where(is_odd, scratch[...], value)
    sent[...] = jnp.where(is_odd, value, scratch[...])


def flat(block):
    half = block.shape[1] // 2
    return jnp.concatenate([block[:, :half], block[:, half:]], axis=0)


def real_dot(left, right):
    return dot3(left[0], left[2], right[0], right[2]) + dot3(left[1], left[3], right[1], right[3])


def off_values(slot, weight, xs, f0s, f0t, gs, weighted):
    width = f0s.shape[-1]
    w0, w1 = weight[pl.ds(slot, 1), 0:1], weight[pl.ds(slot, 1), 1:2]
    qr, qi = complex_dot(xs, load4(gs))
    ts = split_pair(w1 * qr + w0 * qi, w0 * qr - w1 * qi)
    second = real_dot(load4(f0t), ts)
    pr, pi = complex_dot(xs, load4(f0s))
    u = w1 * pr + w0 * pi
    us = split_pair(u, w0 * pr - w1 * pi)
    constant = jnp.concatenate([weighted[2], weighted[3, : width - 8]], axis=0)
    return -flat(u), -(flat(second) + constant), us, ts


def diag_values(us, ts, f0t, gt, weighted):
    return (
        weighted[0] + packed(real_dot(load4(f0t), us)),
        weighted[1] + packed(real_dot(load4(gt), ts)),
    )


def density_kernel(weight, x, f0s, f0t, gs, gt, weighted, off, diag):
    core = whereabouts()[2]
    first, second, us, ts = off_values(slot_of(True), weight, unpacked_split(x), f0s, f0t, gs, weighted)
    off[core], off[1 - core] = first, second
    diag[core], diag[1 - core] = diag_values(us, ts, f0t, gt, weighted)


def more_off_kernel(weight, x, x_first, f0s, f0t, gs, weighted, before, off, us_out, ts_out):
    core = whereabouts()[2]
    xs = split_pair(unpacked(x[0] + x_first[0]), unpacked(x[1] + x_first[1]))
    first, second, us, ts = off_values(slot_of(False), weight, xs, f0s, f0t, gs, weighted)
    off[core] = first + before[core]
    off[1 - core] = second + before[1 - core]
    store4(us_out, us)
    store4(ts_out, ts)


def more_diag_kernel(us, ts, f0t, gt, weighted, before, diag):
    core = whereabouts()[2]
    first, second = diag_values(load4(us), load4(ts), f0t, gt, weighted)
    diag[core] = first + before[core]
    diag[1 - core] = second + before[1 - core]


def unpack_off_kernel(mine, theirs, off):
    core = whereabouts()[2]
    width = off.shape[-1]
    half = width // 2
    for source, entry in ((mine, core), (theirs, 1 - core)):
        off[entry, :, :half] = source[:width]
        off[entry, :, half:] = source[width:]


def unpack_diag_kernel(mine, theirs, diag):
    core = whereabouts()[2]
    for source, entry in ((mine, core), (theirs, 1 - core)):
        diag[entry] = unpacked(source[...])


SCALAR = pl.BlockSpec(memory_space=pltpu.SMEM)
WHOLE = pl.BlockSpec(memory_space=pltpu.VMEM)


COST = pl.CostEstimate(flops=1, bytes_accessed=1, transcendentals=0)


LONG = pl.CostEstimate(flops=10**11, bytes_accessed=1, transcendentals=0)


def run(kernel, scalars, arrays, shapes, scratch=(), cost=COST):
    return pl.pallas_call(
        kernel,
        out_shape=shapes,
        in_specs=[SCALAR] * len(scalars) + [WHOLE] * len(arrays),
        out_specs=[WHOLE] * len(shapes),
        scratch_shapes=list(scratch),
        compiler_params=pltpu.CompilerParams(vmem_limit_bytes=VMEM_LIMIT),
        cost_estimate=cost,
    )(*scalars, *arrays)


def fold_factors(hosted, live, factor):
    width = factor.shape[-1]
    parts = jax.ShapeDtypeStruct((4, width, width), BF16)
    shapes = [parts] * 6 + [jax.ShapeDtypeStruct((2, width, width), F32)]
    far = pl.BlockSpec(memory_space=pltpu.HBM)
    return pl.pallas_call(
        functools.partial(factor_kernel, hosted),
        out_shape=shapes,
        in_specs=[far, far],
        out_specs=[WHOLE] * len(shapes),
        scratch_shapes=[
            pltpu.VMEM(factor.shape[1:], F32),
            pltpu.SMEM(live.shape, jnp.int32),
            pltpu.SemaphoreType.DMA((3,)),
        ],
        compiler_params=pltpu.CompilerParams(vmem_limit_bytes=VMEM_LIMIT),
        cost_estimate=COST,
    )(live, factor)


def local(pivot, factor, live, weight):
    poles, turns = lax.axis_size("pole"), lax.axis_size("snode")
    rows = turns // 2
    width = pivot.shape[-1]
    quarter = (width + 8, width // 2)
    mirrored = jax.ShapeDtypeStruct((2,) + quarter, F32)
    parts = jax.ShapeDtypeStruct((4, width, width), BF16)

    def at(pole_index, snode_index):
        return pole_index * turns + snode_index

    def hosts(row, pole):
        return at(pole, 2 * row + 1), at(pole, 2 * row)

    swaps = [(at(p, s), at(p, s ^ 1)) for p in range(poles) for s in range(2, turns)]
    first = [(at(p, 0), at(p, 1)) for p in range(poles)]
    back = [(at(p, 1), at(p, 0)) for p in range(poles)]
    constants = [mirrored, jax.ShapeDtypeStruct((4,) + quarter, F32)]
    factor = pltpu.with_memory_space_constraint(factor, pltpu.HBM)
    far_live = pltpu.with_memory_space_constraint(live, pltpu.HBM)

    o_f0s, o_f0t, o_f1s, o_f1t, o_gs, o_gt, o_g = fold_factors(False, far_live, factor)
    g_in = lax.ppermute(o_g, AXES, swaps)
    o_e, o_w = run(
        functools.partial(constant_kernel, False), [live, weight], [pivot, o_f1s, o_f1t], constants
    )
    e_first = lax.ppermute(o_e, AXES, first)
    e_swapped = lax.ppermute(o_e, AXES, swaps)
    m_f0s, m_f0t, m_f1s, m_f1t, m_gs, m_gt, m_g = fold_factors(True, far_live, factor)
    m_e, m_w = run(
        functools.partial(constant_kernel, True), [live, weight], [pivot, m_f1s, m_f1t], constants
    )
    e_second = lax.ppermute(m_e, AXES, first)

    starts = functools.partial(step_kernel, lambda place: place == 1)
    (wave_even,) = run(starts, [], [o_gs, o_gt, o_e, e_first], [mirrored])
    wave_even = lax.ppermute(wave_even, AXES, back)
    (wave_odd,) = run(starts, [], [m_gs, m_gt, m_e, e_second], [mirrored])

    received = []
    if rows > 1:
        received.append(
            lax.ppermute(wave_odd, AXES, [(at(p, 1), at(p, 3)) for p in range(poles)])
        )
        received.append(
            lax.ppermute(wave_even, AXES, [(at(p, 0), at(p, 2)) for p in range(poles)])
        )
    fas, fat, ea, ps, pt, ep = run(
        pair_kernel,
        [],
        [m_g, m_e, g_in, e_second, e_swapped],
        [parts, parts, mirrored, parts, parts, mirrored],
        cost=LONG,
    )
    arrived = list(received)
    for turn in range(1, rows - 1):
        active = functools.partial(step_kernel, lambda place, turn=turn: lax.div(place, 2) == turn)
        (wave,) = run(active, [], [ps, pt, ep] + arrived, [mirrored])
        up = [pair for p in range(poles) for pair in zip(hosts(turn, p), hosts(turn + 1, p))]
        arrived = [lax.ppermute(wave, AXES, up)]
        received += arrived
    if not received:
        received = [jnp.zeros(mirrored.shape, F32)]
    own, sent = run(
        share_kernel,
        [],
        [fas, fat, ea] + received,
        [mirrored, mirrored],
        [pltpu.VMEM(mirrored.shape, F32)],
    )
    shared = lax.ppermute(sent, AXES, swaps)

    offs = jax.ShapeDtypeStruct((2, 2 * width, width // 2), F32)
    diags = jax.ShapeDtypeStruct((2,) + quarter, F32)
    off, diag = run(density_kernel, [], [weight, own, m_f0s, m_f0t, m_gs, m_gt, m_w], [offs, diags])
    off, us, ts = run(
        more_off_kernel,
        [],
        [weight, shared, e_first, o_f0s, o_f0t, o_gs, o_w, off],
        [offs, parts, parts],
    )

    def exchanged(value, distance):
        return lax.ppermute(value, "pole", [(p, p ^ distance) for p in range(poles)])

    def summed(parts):
        kept = parts[0] + exchanged(parts[1], 1)
        distance = 2
        while distance < poles:
            kept = kept + exchanged(kept, distance)
            distance *= 2
        return kept, exchanged(kept, 1)

    full = jax.ShapeDtypeStruct((2, width, width), F32)
    off_sums = summed(off)
    (diag,) = run(more_diag_kernel, [], [us, ts, o_f0t, o_gt, o_w, diag], [diags])
    diag_sums = summed(diag)
    (density_off,) = run(unpack_off_kernel, [], list(off_sums), [full])
    (density_diag,) = run(unpack_diag_kernel, [], list(diag_sums), [full])
    return density_diag, density_off


def solution(mesh):
    placed = (
        P("pole", "snode", None, None, None),
        P("pole", "snode", None, None, None),
        P("snode"),
        P("pole", None),
    )
    return jax.shard_map(
        local,
        mesh=mesh,
        in_specs=placed,
        out_specs=(P("snode", None, None), P("snode", None, None)),
        check_vma=False,
    )
```

```python
import functools

import jax
import jax.numpy as jnp
from jax import lax
from jax.experimental import pallas as pl
from jax.experimental.pallas import tpu as pltpu
from jax.sharding import PartitionSpec as P

F32 = jnp.float32
BF16 = jnp.bfloat16
AXES = ("pole", "snode")
VMEM_LIMIT = 16 * 1024 * 1024


def halves(value):
    high = value.astype(BF16)
    return high, (value - high.astype(F32)).astype(BF16)


def split_pair(real, imag):
    (rh, rl), (ih, il) = halves(real), halves(imag)
    return rh, ih, rl, il


def dot(left, right):
    return jnp.dot(left, right, preferred_element_type=F32)


def dot3(lh, ll, rh, rl):
    return dot(lh, rh) + (dot(lh, rl) + dot(ll, rh))


def complex_dot(left, right):
    arh, aih, arl, ail = left
    brh, bih, brl, bil = right
    real = dot3(arh, arl, brh, brl) - dot3(aih, ail, bih, bil)
    imag = dot3(arh, arl, bih, bil) + dot3(aih, ail, brh, brl)
    return real, imag


def rows_columns(size):
    return (
        lax.broadcasted_iota(jnp.int32, (size, size), 0),
        lax.broadcasted_iota(jnp.int32, (size, size), 1),
    )


def packed(block):
    half = block.shape[0] // 2
    row, column = rows_columns(half)
    lower = block[half:, half:]
    mixed = jnp.where(row >= column, block[:half, :half], lower)
    diagonal = jnp.sum(jnp.where(row == column, lower, 0.0), axis=0, keepdims=True)
    return jnp.concatenate(
        [block[:half, half:], mixed, jnp.broadcast_to(diagonal, (8, half))], axis=0
    )


def unpacked(value):
    half = value.shape[1]
    row, column = rows_columns(half)
    right, mixed = value[:half], value[half : 2 * half]
    diagonal = value[2 * half : 2 * half + 1]
    turned = mixed.T
    first = jnp.where(row >= column, mixed, turned)
    last = jnp.where(row < column, mixed, jnp.where(row == column, diagonal, turned))
    return jnp.concatenate(
        [jnp.concatenate([first, right], axis=1), jnp.concatenate([right.T, last], axis=1)], axis=0
    )


def unpacked_split(ref):
    return split_pair(unpacked(ref[0]), unpacked(ref[1]))


def load4(ref):
    return tuple(ref[i] for i in range(4))


def store4(ref, parts):
    for i, part in enumerate(parts):
        ref[i] = part


def whereabouts():
    place = lax.axis_index("snode")
    return place, lax.rem(place, 2), lax.rem(lax.axis_index("pole"), 2)


def hosted_slot():
    place, odd, core = whereabouts()
    return jnp.where(jnp.logical_and(place > 1, odd == core), 0, 1)


def slot_of(hosted):
    return hosted_slot() if hosted else 1 - hosted_slot()


def constant_kernel(hosted, fetch, live, pivot, factor, weight, *refs):
    width = pivot.shape[-1]
    slot = slot_of(hosted)
    if fetch:
        f1s, e, weighted, blocks, link, widths, weights, sems = refs
        copies = [
            pltpu.make_async_copy(live, widths, sems.at[0]),
            pltpu.make_async_copy(factor.at[slot, 1], link, sems.at[1]),
            pltpu.make_async_copy(pivot.at[slot, 0], blocks.at[0], sems.at[2]),
            pltpu.make_async_copy(pivot.at[slot, 1], blocks.at[1], sems.at[3]),
            pltpu.make_async_copy(weight, weights, sems.at[4]),
        ]
        for copy in copies:
            copy.start()
        copies[0].wait()
        copies[1].wait()
    else:
        _, f1s, e, weighted = refs
        blocks, link, widths, weights, copies = pivot.at[slot], factor.at[slot, 1], live, weight, []
    row, column = rows_columns(width)
    kept = [column < widths[k] for k in range(2)]
    both = [jnp.logical_and(row < widths[k], kept[k]) for k in range(2)]
    f1 = [jnp.where(kept[1], link[c], 0.0) for c in range(2)]
    s1, t1 = split_pair(*f1), split_pair(f1[0].T, f1[1].T)
    store4(f1s, s1)
    for copy in copies[2:]:
        copy.wait()
    d = [[jnp.where(both[k], blocks[k, c], 0.0) for c in range(2)] for k in range(2)]
    br, bi = complex_dot(split_pair(*d[0]), s1)
    tr, ti = complex_dot(t1, split_pair(br, bi))
    er, ei = d[1][0] + tr, d[1][1] + ti
    e[0], e[1] = packed(er), packed(ei)
    w0, w1 = weights[pl.ds(slot, 1), 0:1], weights[pl.ds(slot, 1), 1:2]
    weighted[0] = packed(w1 * d[0][0] + w0 * d[0][1])
    weighted[1] = packed(w1 * er + w0 * ei)
    weighted_b = flat(w1 * br + w0 * bi)
    weighted[2] = weighted_b[: width + 8]
    weighted[3, : width - 8] = weighted_b[width + 8 :]


def factor_kernel(hosted, live, factor, f1s, f0s, f0t, gs, gt, g):
    slot = slot_of(hosted)
    _, column = rows_columns(factor.shape[-1])
    f0 = [jnp.where(column < live[0], factor[slot, 0, c], 0.0) for c in range(2)]
    s0 = split_pair(*f0)
    gr, gi = complex_dot(s0, load4(f1s))
    g[0], g[1] = gr, gi
    store4(gs, split_pair(gr, gi))
    store4(gt, split_pair(gr.T, gi.T))
    store4(f0s, s0)
    store4(f0t, split_pair(f0[0].T, f0[1].T))


def fold(x, gs, gt, e, out):
    tr, ti = complex_dot(x, load4(gs))
    yr, yi = complex_dot(load4(gt), split_pair(tr, ti))
    out[0] = e[0] + packed(yr)
    out[1] = e[1] + packed(yi)


def step_kernel(active, gs, gt, e, *refs):
    *received, out = refs

    @pl.when(active(whereabouts()[0]))
    def _():
        value = received[0][...]
        for other in received[1:]:
            value = value + other[...]
        fold(split_pair(unpacked(value[0]), unpacked(value[1])), gs, gt, e, out)


def pair_kernel(g, e, g_in, e_in, e_second, fas, fat, ea, ps, pt, ep):
    upper = whereabouts()[0] > 1
    is_odd = whereabouts()[1] == 1
    ga = [jnp.where(is_odd, g_in[c], g[c]) for c in range(2)]
    gb = [jnp.where(is_odd, g[c], g_in[c]) for c in range(2)]
    theirs = [jnp.where(upper, e_in[c], e_second[c]) for c in range(2)]
    low = [jnp.where(is_odd, theirs[c], e[c]) for c in range(2)]
    high = [jnp.where(is_odd, e[c], theirs[c]) for c in range(2)]
    sa, sb = split_pair(*ga), split_pair(*gb)
    store4(fas, sa)
    store4(fat, split_pair(ga[0].T, ga[1].T))
    pr, pi = complex_dot(sa, sb)
    store4(ps, split_pair(pr, pi))
    store4(pt, split_pair(pr.T, pi.T))
    br, bi = complex_dot(split_pair(unpacked(low[0]), unpacked(low[1])), sb)
    tr, ti = complex_dot(split_pair(gb[0].T, gb[1].T), split_pair(br, bi))
    for c, term in enumerate((tr, ti)):
        ea[c] = low[c]
        ep[c] = high[c] + packed(term)


def share_kernel(fas, fat, ea, *refs):
    *received, own, sent, scratch = refs
    value = received[0][...]
    for other in received[1:]:
        value = value + other[...]
    value = jnp.where(whereabouts()[0] > 1, value, 0.0)
    fold(split_pair(unpacked(value[0]), unpacked(value[1])), fas, fat, ea, scratch)
    is_odd = whereabouts()[1] == 1
    own[...] = jnp.where(is_odd, scratch[...], value)
    sent[...] = jnp.where(is_odd, value, scratch[...])


def flat(block):
    half = block.shape[1] // 2
    return jnp.concatenate([block[:, :half], block[:, half:]], axis=0)


def real_dot(left, right):
    return dot3(left[0], left[2], right[0], right[2]) + dot3(left[1], left[3], right[1], right[3])


def off_values(slot, weight, xs, f0s, f0t, gs, weighted):
    width = f0s.shape[-1]
    w0, w1 = weight[pl.ds(slot, 1), 0:1], weight[pl.ds(slot, 1), 1:2]
    qr, qi = complex_dot(xs, load4(gs))
    ts = split_pair(w1 * qr + w0 * qi, w0 * qr - w1 * qi)
    second = real_dot(load4(f0t), ts)
    pr, pi = complex_dot(xs, load4(f0s))
    u = w1 * pr + w0 * pi
    us = split_pair(u, w0 * pr - w1 * pi)
    constant = jnp.concatenate([weighted[2], weighted[3, : width - 8]], axis=0)
    return -flat(u), -(flat(second) + constant), us, ts


def diag_values(us, ts, f0t, gt, weighted):
    return (
        weighted[0] + packed(real_dot(load4(f0t), us)),
        weighted[1] + packed(real_dot(load4(gt), ts)),
    )


def density_kernel(weight, x, f0s, f0t, gs, gt, weighted, off, diag):
    core = whereabouts()[2]
    first, second, us, ts = off_values(slot_of(True), weight, unpacked_split(x), f0s, f0t, gs, weighted)
    off[core], off[1 - core] = first, second
    diag[core], diag[1 - core] = diag_values(us, ts, f0t, gt, weighted)


def more_off_kernel(weight, x, x_first, f0s, f0t, gs, weighted, before, off, us_out, ts_out):
    core = whereabouts()[2]
    upper = whereabouts()[0] > 1
    x = [jnp.where(upper, x[c], x_first[c]) for c in range(2)]
    xs = split_pair(unpacked(x[0]), unpacked(x[1]))
    first, second, us, ts = off_values(slot_of(False), weight, xs, f0s, f0t, gs, weighted)
    off[core] = first + before[core]
    off[1 - core] = second + before[1 - core]
    store4(us_out, us)
    store4(ts_out, ts)


def more_diag_kernel(us, ts, f0t, gt, weighted, before, diag):
    core = whereabouts()[2]
    first, second = diag_values(load4(us), load4(ts), f0t, gt, weighted)
    diag[core] = first + before[core]
    diag[1 - core] = second + before[1 - core]


def unpack_off_kernel(mine, theirs, off, done):
    core = whereabouts()[2]
    width = off.shape[-1]
    half = width // 2
    for source, entry in ((mine, core), (theirs, 1 - core)):
        off[entry, :, :half] = source[:width]
        off[entry, :, half:] = source[width:]
    done[...] = jnp.zeros_like(done)


def unpack_diag_kernel(mine, theirs, _, diag):
    core = whereabouts()[2]
    for source, entry in ((mine, core), (theirs, 1 - core)):
        diag[entry] = unpacked(source[...])


SCALAR = pl.BlockSpec(memory_space=pltpu.SMEM)
WHOLE = pl.BlockSpec(memory_space=pltpu.VMEM)


COST = pl.CostEstimate(flops=1, bytes_accessed=1, transcendentals=0)


LONG = pl.CostEstimate(flops=10**11, bytes_accessed=1, transcendentals=0)


def run(kernel, scalars, arrays, shapes, scratch=(), cost=COST, far=()):
    return pl.pallas_call(
        kernel,
        out_shape=shapes,
        in_specs=[SCALAR] * len(scalars)
        + [pl.BlockSpec(memory_space=pltpu.HBM)] * len(far)
        + [WHOLE] * len(arrays),
        out_specs=[WHOLE] * len(shapes),
        scratch_shapes=list(scratch),
        compiler_params=pltpu.CompilerParams(vmem_limit_bytes=VMEM_LIMIT),
        cost_estimate=cost,
    )(*scalars, *far, *arrays)


def local(pivot, factor, live, weight):
    poles, turns = lax.axis_size("pole"), lax.axis_size("snode")
    rows = turns // 2
    width = pivot.shape[-1]
    quarter = (width + 8, width // 2)
    mirrored = jax.ShapeDtypeStruct((2,) + quarter, F32)
    parts = jax.ShapeDtypeStruct((4, width, width), BF16)

    def at(pole_index, snode_index):
        return pole_index * turns + snode_index

    def hosts(row, pole):
        return at(pole, 2 * row + 1), at(pole, 2 * row)

    swaps = [(at(p, s), at(p, s ^ 1)) for p in range(poles) for s in range(2, turns)]
    every = [(at(p, s), at(p, s ^ 1)) for p in range(poles) for s in range(turns)]
    first = [(at(p, 0), at(p, 1)) for p in range(poles)]
    constants = [parts, mirrored, jax.ShapeDtypeStruct((4,) + quarter, F32)]
    factors = [parts, parts, parts, parts, jax.ShapeDtypeStruct((2, width, width), F32)]

    o_f1s, o_e, o_w = run(
        functools.partial(constant_kernel, False, True),
        [],
        [],
        constants,
        [
            pltpu.VMEM(pivot.shape[1:], F32),
            pltpu.VMEM(factor.shape[2:], F32),
            pltpu.SMEM(live.shape, jnp.int32),
            pltpu.VMEM(weight.shape, F32),
            pltpu.SemaphoreType.DMA((5,)),
        ],
        far=[
            pltpu.with_memory_space_constraint(a, pltpu.HBM) for a in (live, pivot, factor, weight)
        ],
    )
    e_in = lax.ppermute(o_e, AXES, first + swaps)
    o_f0s, o_f0t, o_gs, o_gt, o_g = run(
        functools.partial(factor_kernel, False), [live], [factor, o_f1s], factors
    )
    g_in = lax.ppermute(o_g, AXES, swaps)
    m_f1s, m_e, m_w = run(
        functools.partial(constant_kernel, True, False),
        [live],
        [pivot, factor, weight, o_g],
        constants,
    )
    m_f0s, m_f0t, m_gs, m_gt, m_g = run(
        functools.partial(factor_kernel, True), [live], [factor, m_f1s], factors
    )
    e_second = lax.ppermute(m_e, AXES, first)

    starts = functools.partial(step_kernel, lambda place: place == 1)
    received, back = [], []
    for slot, arrays in enumerate(([o_gs, o_gt, o_e, e_in], [m_gs, m_gt, m_e, e_second])):
        (wave,) = run(starts, [], arrays, [mirrored])
        up = [p for p in range(poles) if p % 2 != slot and rows > 1]
        down = [p for p in range(poles) if p % 2 == slot]
        back.append(lax.ppermute(wave, AXES, [(at(p, 1), at(p, 0)) for p in down]))
        received.append(lax.ppermute(wave, AXES, [(at(p, 1), at(p, 3)) for p in up]))
    if rows > 1:
        received.append(
            lax.ppermute(back[0] + back[1], AXES, [(at(p, 0), at(p, 2)) for p in range(poles)])
        )
    fas, fat, ea, ps, pt, ep = run(
        pair_kernel,
        [],
        [m_g, m_e, g_in, e_in, e_second],
        [parts, parts, mirrored, parts, parts, mirrored],
        cost=LONG,
    )
    arrived = list(received)
    for turn in range(1, rows - 1):
        active = functools.partial(step_kernel, lambda place, turn=turn: lax.div(place, 2) == turn)
        (wave,) = run(active, [], [ps, pt, ep] + arrived, [mirrored])
        up = [pair for p in range(poles) for pair in zip(hosts(turn, p), hosts(turn + 1, p))]
        arrived = [lax.ppermute(wave, AXES, up)]
        received += arrived
    own, sent = run(
        share_kernel,
        [],
        [fas, fat, ea] + received,
        [mirrored, mirrored],
        [pltpu.VMEM(mirrored.shape, F32)],
    )
    shared = lax.ppermute(sent, AXES, every)

    offs = jax.ShapeDtypeStruct((2, 2 * width, width // 2), F32)
    diags = jax.ShapeDtypeStruct((2,) + quarter, F32)
    off, diag = run(density_kernel, [], [weight, own, m_f0s, m_f0t, m_gs, m_gt, m_w], [offs, diags])
    off, us, ts = run(
        more_off_kernel,
        [],
        [weight, shared, e_in, o_f0s, o_f0t, o_gs, o_w, off],
        [offs, parts, parts],
    )

    def exchanged(value, distance):
        return lax.ppermute(value, "pole", [(p, p ^ distance) for p in range(poles)])

    def summed(parts):
        kept = parts[0] + exchanged(parts[1], 1)
        distance = 2
        while distance < poles:
            kept = kept + exchanged(kept, distance)
            distance *= 2
        return kept, exchanged(kept, 1)

    full = jax.ShapeDtypeStruct((2, width, width), F32)
    off_sums = summed(off)
    (diag,) = run(more_diag_kernel, [], [us, ts, o_f0t, o_gt, o_w, diag], [diags])
    diag_sums = summed(diag)
    done = jax.ShapeDtypeStruct((8, 128), F32)
    density_off, done = run(unpack_off_kernel, [], list(off_sums), [full, done])
    (density_diag,) = run(unpack_diag_kernel, [], [*diag_sums, done], [full])
    return density_diag, density_off


def solution(mesh):
    placed = (
        P("pole", "snode", None, None, None),
        P("pole", "snode", None, None, None),
        P("snode"),
        P("pole", None),
    )
    return jax.shard_map(
        local,
        mesh=mesh,
        in_specs=placed,
        out_specs=(P("snode", None, None), P("snode", None, None)),
        check_vma=False,
    )
```

```python
import functools

import jax
import jax.numpy as jnp
from jax import lax
from jax.experimental import pallas as pl
from jax.experimental.pallas import tpu as pltpu
from jax.sharding import PartitionSpec as P

F32 = jnp.float32
BF16 = jnp.bfloat16
AXES = ("pole", "snode")
VMEM_LIMIT = 16 * 1024 * 1024


def halves(value):
    high = value.astype(BF16)
    return high, (value - high.astype(F32)).astype(BF16)


def split_pair(real, imag):
    (rh, rl), (ih, il) = halves(real), halves(imag)
    return rh, ih, rl, il


def dot(left, right):
    return jnp.dot(left, right, preferred_element_type=F32)


def dot3(lh, ll, rh, rl):
    return dot(lh, rh) + (dot(lh, rl) + dot(ll, rh))


def complex_dot(left, right):
    arh, aih, arl, ail = left
    brh, bih, brl, bil = right
    real = dot3(arh, arl, brh, brl) - dot3(aih, ail, bih, bil)
    imag = dot3(arh, arl, bih, bil) + dot3(aih, ail, brh, brl)
    return real, imag


def rows_columns(size):
    return (
        lax.broadcasted_iota(jnp.int32, (size, size), 0),
        lax.broadcasted_iota(jnp.int32, (size, size), 1),
    )


def packed(block):
    half = block.shape[0] // 2
    row, column = rows_columns(half)
    lower = block[half:, half:]
    mixed = jnp.where(row >= column, block[:half, :half], lower)
    diagonal = jnp.sum(jnp.where(row == column, lower, 0.0), axis=0, keepdims=True)
    return jnp.concatenate(
        [block[:half, half:], mixed, jnp.broadcast_to(diagonal, (8, half))], axis=0
    )


def unpacked(value):
    half = value.shape[1]
    row, column = rows_columns(half)
    right, mixed = value[:half], value[half : 2 * half]
    diagonal = value[2 * half : 2 * half + 1]
    turned = mixed.T
    first = jnp.where(row >= column, mixed, turned)
    last = jnp.where(row < column, mixed, jnp.where(row == column, diagonal, turned))
    return jnp.concatenate(
        [jnp.concatenate([first, right], axis=1), jnp.concatenate([right.T, last], axis=1)], axis=0
    )


def unpacked_split(ref):
    return split_pair(unpacked(ref[0]), unpacked(ref[1]))


def load4(ref):
    return tuple(ref[i] for i in range(4))


def store4(ref, parts):
    for i, part in enumerate(parts):
        ref[i] = part


def whereabouts():
    place = lax.axis_index("snode")
    return place, lax.rem(place, 2), lax.rem(lax.axis_index("pole"), 2)


def hosted_slot():
    place, odd, _ = whereabouts()
    return jnp.where(place < 2, 0, 1 - odd)


def slot_of(hosted):
    return hosted_slot() if hosted else 1 - hosted_slot()


def constant_kernel(hosted, fetch, live, pivot, factor, weight, *refs):
    width = pivot.shape[-1]
    slot = slot_of(hosted)
    if fetch:
        f1s, e, weighted, blocks, link, widths, weights, sems = refs
        copies = [
            pltpu.make_async_copy(live, widths, sems.at[0]),
            pltpu.make_async_copy(factor.at[slot, 1], link, sems.at[1]),
            pltpu.make_async_copy(pivot.at[slot, 0], blocks.at[0], sems.at[2]),
            pltpu.make_async_copy(pivot.at[slot, 1], blocks.at[1], sems.at[3]),
            pltpu.make_async_copy(weight, weights, sems.at[4]),
        ]
        for copy in copies:
            copy.start()
        copies[0].wait()
        copies[1].wait()
    else:
        _, f1s, e, weighted = refs
        blocks, link, widths, weights, copies = pivot.at[slot], factor.at[slot, 1], live, weight, []
    row, column = rows_columns(width)
    kept = [column < widths[k] for k in range(2)]
    both = [jnp.logical_and(row < widths[k], kept[k]) for k in range(2)]
    f1 = [jnp.where(kept[1], link[c], 0.0) for c in range(2)]
    s1, t1 = split_pair(*f1), split_pair(f1[0].T, f1[1].T)
    store4(f1s, s1)
    for copy in copies[2:]:
        copy.wait()
    d = [[jnp.where(both[k], blocks[k, c], 0.0) for c in range(2)] for k in range(2)]
    br, bi = complex_dot(split_pair(*d[0]), s1)
    tr, ti = complex_dot(t1, split_pair(br, bi))
    er, ei = d[1][0] + tr, d[1][1] + ti
    e[0], e[1] = packed(er), packed(ei)
    w0, w1 = weights[pl.ds(slot, 1), 0:1], weights[pl.ds(slot, 1), 1:2]
    weighted[0] = packed(w1 * d[0][0] + w0 * d[0][1])
    weighted[1] = packed(w1 * er + w0 * ei)
    weighted_b = flat(w1 * br + w0 * bi)
    weighted[2] = weighted_b[: width + 8]
    weighted[3, : width - 8] = weighted_b[width + 8 :]


def factor_kernel(hosted, live, factor, f1s, f0s, f0t, gs, gt, g):
    slot = slot_of(hosted)
    _, column = rows_columns(factor.shape[-1])
    f0 = [jnp.where(column < live[0], factor[slot, 0, c], 0.0) for c in range(2)]
    s0 = split_pair(*f0)
    gr, gi = complex_dot(s0, load4(f1s))
    g[0], g[1] = gr, gi
    store4(gs, split_pair(gr, gi))
    store4(gt, split_pair(gr.T, gi.T))
    store4(f0s, s0)
    store4(f0t, split_pair(f0[0].T, f0[1].T))


def hold_kernel(count, *refs):
    for source, target in zip(refs[:count], refs[-count:]):
        target[...] = source[...]


def fold(x, gs, gt, e, out):
    tr, ti = complex_dot(x, load4(gs))
    yr, yi = complex_dot(load4(gt), split_pair(tr, ti))
    out[0] = e[0] + packed(yr)
    out[1] = e[1] + packed(yi)


def step_kernel(active, gs, gt, e, *refs):
    *received, out = refs

    @pl.when(active(whereabouts()[0]))
    def _():
        value = received[0][...]
        for other in received[1:]:
            value = value + other[...]
        fold(split_pair(unpacked(value[0]), unpacked(value[1])), gs, gt, e, out)


def pair_kernel(g, e, g_in, e_in, e_second, fas, fat, ea, ps, pt, ep):
    upper = whereabouts()[0] > 1
    is_odd = whereabouts()[1] == 1
    ga = [jnp.where(is_odd, g_in[c], g[c]) for c in range(2)]
    gb = [jnp.where(is_odd, g[c], g_in[c]) for c in range(2)]
    theirs = [jnp.where(upper, e_in[c], e_second[c]) for c in range(2)]
    low = [jnp.where(is_odd, theirs[c], e[c]) for c in range(2)]
    high = [jnp.where(is_odd, e[c], theirs[c]) for c in range(2)]
    sa, sb = split_pair(*ga), split_pair(*gb)
    store4(fas, sa)
    store4(fat, split_pair(ga[0].T, ga[1].T))
    pr, pi = complex_dot(sa, sb)
    store4(ps, split_pair(pr, pi))
    store4(pt, split_pair(pr.T, pi.T))
    br, bi = complex_dot(split_pair(unpacked(low[0]), unpacked(low[1])), sb)
    tr, ti = complex_dot(split_pair(gb[0].T, gb[1].T), split_pair(br, bi))
    for c, term in enumerate((tr, ti)):
        ea[c] = low[c]
        ep[c] = high[c] + packed(term)


def share_kernel(fas, fat, ea, *refs):
    *received, own, sent, scratch = refs
    value = received[0][...]
    for other in received[1:]:
        value = value + other[...]
    value = jnp.where(whereabouts()[0] > 1, value, 0.0)
    fold(split_pair(unpacked(value[0]), unpacked(value[1])), fas, fat, ea, scratch)
    is_odd = whereabouts()[1] == 1
    own[...] = jnp.where(is_odd, scratch[...], value)
    sent[...] = jnp.where(is_odd, value, scratch[...])


def flat(block):
    half = block.shape[1] // 2
    return jnp.concatenate([block[:, :half], block[:, half:]], axis=0)


def real_dot(left, right):
    return dot3(left[0], left[2], right[0], right[2]) + dot3(left[1], left[3], right[1], right[3])


def off_values(slot, weight, xs, f0s, f0t, gs, weighted):
    width = f0s.shape[-1]
    w0, w1 = weight[pl.ds(slot, 1), 0:1], weight[pl.ds(slot, 1), 1:2]
    qr, qi = complex_dot(xs, load4(gs))
    ts = split_pair(w1 * qr + w0 * qi, w0 * qr - w1 * qi)
    second = real_dot(load4(f0t), ts)
    pr, pi = complex_dot(xs, load4(f0s))
    u = w1 * pr + w0 * pi
    us = split_pair(u, w0 * pr - w1 * pi)
    constant = jnp.concatenate([weighted[2], weighted[3, : width - 8]], axis=0)
    return -flat(u), -(flat(second) + constant), us, ts


def diag_values(us, ts, f0t, gt, weighted):
    return (
        weighted[0] + packed(real_dot(load4(f0t), us)),
        weighted[1] + packed(real_dot(load4(gt), ts)),
    )


def density_kernel(weight, x, f0s, f0t, gs, gt, weighted, off, diag):
    core = whereabouts()[2]
    first, second, us, ts = off_values(slot_of(True), weight, unpacked_split(x), f0s, f0t, gs, weighted)
    off[core], off[1 - core] = first, second
    diag[core], diag[1 - core] = diag_values(us, ts, f0t, gt, weighted)


def more_off_kernel(weight, x, x_first, f0s, f0t, gs, weighted, before, off, us_out, ts_out):
    core = whereabouts()[2]
    upper = whereabouts()[0] > 1
    x = [jnp.where(upper, x[c], x_first[c]) for c in range(2)]
    xs = split_pair(unpacked(x[0]), unpacked(x[1]))
    first, second, us, ts = off_values(slot_of(False), weight, xs, f0s, f0t, gs, weighted)
    off[core] = first + before[core]
    off[1 - core] = second + before[1 - core]
    store4(us_out, us)
    store4(ts_out, ts)


def more_diag_kernel(us, ts, f0t, gt, weighted, before, diag):
    core = whereabouts()[2]
    first, second = diag_values(load4(us), load4(ts), f0t, gt, weighted)
    diag[core] = first + before[core]
    diag[1 - core] = second + before[1 - core]


def unpack_off_kernel(mine, theirs, off, done):
    core = whereabouts()[2]
    width = off.shape[-1]
    half = width // 2
    for source, entry in ((mine, core), (theirs, 1 - core)):
        off[entry, :, :half] = source[:width]
        off[entry, :, half:] = source[width:]
    done[...] = jnp.zeros_like(done)


def unpack_diag_kernel(mine, theirs, _, diag):
    core = whereabouts()[2]
    for source, entry in ((mine, core), (theirs, 1 - core)):
        diag[entry] = unpacked(source[...])


SCALAR = pl.BlockSpec(memory_space=pltpu.SMEM)
WHOLE = pl.BlockSpec(memory_space=pltpu.VMEM)


COST = pl.CostEstimate(flops=1, bytes_accessed=1, transcendentals=0)


LONG = pl.CostEstimate(flops=10**11, bytes_accessed=1, transcendentals=0)


def run(kernel, scalars, arrays, shapes, scratch=(), cost=COST, far=()):
    return pl.pallas_call(
        kernel,
        out_shape=shapes,
        in_specs=[SCALAR] * len(scalars)
        + [pl.BlockSpec(memory_space=pltpu.HBM)] * len(far)
        + [WHOLE] * len(arrays),
        out_specs=[WHOLE] * len(shapes),
        scratch_shapes=list(scratch),
        compiler_params=pltpu.CompilerParams(vmem_limit_bytes=VMEM_LIMIT),
        cost_estimate=cost,
    )(*scalars, *far, *arrays)


def local(pivot, factor, live, weight):
    poles, turns = lax.axis_size("pole"), lax.axis_size("snode")
    rows = turns // 2
    width = pivot.shape[-1]
    quarter = (width + 8, width // 2)
    mirrored = jax.ShapeDtypeStruct((2,) + quarter, F32)
    parts = jax.ShapeDtypeStruct((4, width, width), BF16)

    def at(pole_index, snode_index):
        return pole_index * turns + snode_index

    def hosts(row, pole):
        return at(pole, 2 * row + 1), at(pole, 2 * row)

    def swaps(core):
        return [(at(p, s), at(p, s ^ 1)) for p in range(core, poles, 2) for s in range(2, turns)]

    def first(core):
        return [(at(p, 0), at(p, 1)) for p in range(core, poles, 2)]

    every = [(at(p, s), at(p, s ^ 1)) for p in range(poles) for s in range(turns)]
    constants = [parts, mirrored, jax.ShapeDtypeStruct((4,) + quarter, F32)]
    factors = [parts, parts, parts, parts, jax.ShapeDtypeStruct((2, width, width), F32)]

    o_f1s, o_e, o_w = run(
        functools.partial(constant_kernel, False, True),
        [],
        [],
        constants,
        [
            pltpu.VMEM(pivot.shape[1:], F32),
            pltpu.VMEM(factor.shape[2:], F32),
            pltpu.SMEM(live.shape, jnp.int32),
            pltpu.VMEM(weight.shape, F32),
            pltpu.SemaphoreType.DMA((5,)),
        ],
        far=[
            pltpu.with_memory_space_constraint(a, pltpu.HBM) for a in (live, pivot, factor, weight)
        ],
    )
    e_in = lax.ppermute(o_e, AXES, first(0) + swaps(0))
    o_f0s, o_f0t, o_gs, o_gt, o_g = run(
        functools.partial(factor_kernel, False), [live], [factor, o_f1s], factors
    )
    g_in = lax.ppermute(o_g, AXES, swaps(0))
    m_f1s, m_e, m_w = run(
        functools.partial(constant_kernel, True, False),
        [live],
        [pivot, factor, weight, o_g],
        constants,
    )
    m_f0s, m_f0t, m_gs, m_gt, m_g = run(
        functools.partial(factor_kernel, True), [live], [factor, m_f1s], factors
    )
    e_second = lax.ppermute(m_e, AXES, first(0))
    e_late, g_late, second_late = run(
        functools.partial(hold_kernel, 3),
        [],
        [o_e, o_g, m_e, e_in, g_in],
        [mirrored, factors[-1], mirrored],
    )
    e_in = e_in + lax.ppermute(e_late, AXES, first(1) + swaps(1))
    g_in = g_in + lax.ppermute(g_late, AXES, swaps(1))
    e_second = e_second + lax.ppermute(second_late, AXES, first(1))

    starts = functools.partial(step_kernel, lambda place: place == 1)
    (wave_even,) = run(starts, [], [o_gs, o_gt, o_e, e_in], [mirrored])
    wave_even = lax.ppermute(wave_even, AXES, [(at(p, 1), at(p, 0)) for p in range(poles)])
    (wave_odd,) = run(starts, [], [m_gs, m_gt, m_e, e_second], [mirrored])
    received = []
    if rows > 1:
        received = [
            lax.ppermute(wave_odd, AXES, [(at(p, 1), at(p, 3)) for p in range(poles)]),
            lax.ppermute(wave_even, AXES, [(at(p, 0), at(p, 2)) for p in range(poles)]),
        ]
    else:
        received = [jnp.zeros(mirrored.shape, F32)]
    fas, fat, ea, ps, pt, ep = run(
        pair_kernel,
        [],
        [m_g, m_e, g_in, e_in, e_second],
        [parts, parts, mirrored, parts, parts, mirrored],
        cost=LONG,
    )
    arrived = list(received)
    for turn in range(1, rows - 1):
        active = functools.partial(step_kernel, lambda place, turn=turn: lax.div(place, 2) == turn)
        (wave,) = run(active, [], [ps, pt, ep] + arrived, [mirrored])
        up = [pair for p in range(poles) for pair in zip(hosts(turn, p), hosts(turn + 1, p))]
        arrived = [lax.ppermute(wave, AXES, up)]
        received += arrived
    own, sent = run(
        share_kernel,
        [],
        [fas, fat, ea] + received,
        [mirrored, mirrored],
        [pltpu.VMEM(mirrored.shape, F32)],
    )
    shared = lax.ppermute(sent, AXES, every)

    offs = jax.ShapeDtypeStruct((2, 2 * width, width // 2), F32)
    diags = jax.ShapeDtypeStruct((2,) + quarter, F32)
    off, diag = run(density_kernel, [], [weight, own, m_f0s, m_f0t, m_gs, m_gt, m_w], [offs, diags])
    off, us, ts = run(
        more_off_kernel,
        [],
        [weight, shared, e_in, o_f0s, o_f0t, o_gs, o_w, off],
        [offs, parts, parts],
    )

    def exchanged(value, distance):
        return lax.ppermute(value, "pole", [(p, p ^ distance) for p in range(poles)])

    def summed(parts):
        kept = parts[0] + exchanged(parts[1], 1)
        distance = 2
        while distance < poles:
            kept = kept + exchanged(kept, distance)
            distance *= 2
        return kept, exchanged(kept, 1)

    full = jax.ShapeDtypeStruct((2, width, width), F32)
    off_sums = summed(off)
    (diag,) = run(more_diag_kernel, [], [us, ts, o_f0t, o_gt, o_w, diag], [diags])
    diag_sums = summed(diag)
    done = jax.ShapeDtypeStruct((8, 128), F32)
    density_off, done = run(unpack_off_kernel, [], list(off_sums), [full, done])
    (density_diag,) = run(unpack_diag_kernel, [], [*diag_sums, done], [full])
    return density_diag, density_off


def solution(mesh):
    placed = (
        P("pole", "snode", None, None, None),
        P("pole", "snode", None, None, None),
        P("snode"),
        P("pole", None),
    )
    return jax.shard_map(
        local,
        mesh=mesh,
        in_specs=placed,
        out_specs=(P("snode", None, None), P("snode", None, None)),
        check_vma=False,
    )
```

```python
import functools

import jax
import jax.numpy as jnp
from jax import lax
from jax.experimental import pallas as pl
from jax.experimental.pallas import tpu as pltpu
from jax.sharding import PartitionSpec as P

F32 = jnp.float32
BF16 = jnp.bfloat16
AXES = ("pole", "snode")
VMEM_LIMIT = 16 * 1024 * 1024


def halves(value):
    high = value.astype(BF16)
    return high, (value - high.astype(F32)).astype(BF16)


def split_pair(real, imag):
    (rh, rl), (ih, il) = halves(real), halves(imag)
    return rh, ih, rl, il


def dot(left, right):
    return jnp.dot(left, right, preferred_element_type=F32)


def dot3(lh, ll, rh, rl):
    return dot(lh, rh) + (dot(lh, rl) + dot(ll, rh))


def complex_dot(left, right):
    arh, aih, arl, ail = left
    brh, bih, brl, bil = right
    real = dot3(arh, arl, brh, brl) - dot3(aih, ail, bih, bil)
    imag = dot3(arh, arl, bih, bil) + dot3(aih, ail, brh, brl)
    return real, imag


def rows_columns(size):
    return (
        lax.broadcasted_iota(jnp.int32, (size, size), 0),
        lax.broadcasted_iota(jnp.int32, (size, size), 1),
    )


def packed(block):
    half = block.shape[0] // 2
    row, column = rows_columns(half)
    lower = block[half:, half:]
    mixed = jnp.where(row >= column, block[:half, :half], lower)
    diagonal = jnp.sum(jnp.where(row == column, lower, 0.0), axis=0, keepdims=True)
    return jnp.concatenate(
        [block[:half, half:], mixed, jnp.broadcast_to(diagonal, (8, half))], axis=0
    )


def unpacked(value):
    half = value.shape[1]
    row, column = rows_columns(half)
    right, mixed = value[:half], value[half : 2 * half]
    diagonal = value[2 * half : 2 * half + 1]
    turned = mixed.T
    first = jnp.where(row >= column, mixed, turned)
    last = jnp.where(row < column, mixed, jnp.where(row == column, diagonal, turned))
    return jnp.concatenate(
        [jnp.concatenate([first, right], axis=1), jnp.concatenate([right.T, last], axis=1)], axis=0
    )


def unpacked_split(ref):
    return split_pair(unpacked(ref[0]), unpacked(ref[1]))


def load4(ref):
    return tuple(ref[i] for i in range(4))


def store4(ref, parts):
    for i, part in enumerate(parts):
        ref[i] = part


def whereabouts():
    place = lax.axis_index("snode")
    return place, lax.rem(place, 2), lax.rem(lax.axis_index("pole"), 2)


def hosted_slot():
    place, odd, _ = whereabouts()
    return jnp.where(place < 2, 0, 1 - odd)


def slot_of(hosted):
    return hosted_slot() if hosted else 1 - hosted_slot()


def constant_kernel(hosted, fetch, live, pivot, factor, weight, *refs):
    width = pivot.shape[-1]
    slot = slot_of(hosted)
    if fetch:
        f1s, e, weighted, blocks, link, widths, weights, sems = refs
        copies = [
            pltpu.make_async_copy(live, widths, sems.at[0]),
            pltpu.make_async_copy(factor.at[slot, 1], link, sems.at[1]),
            pltpu.make_async_copy(pivot.at[slot, 0], blocks.at[0], sems.at[2]),
            pltpu.make_async_copy(pivot.at[slot, 1], blocks.at[1], sems.at[3]),
            pltpu.make_async_copy(weight, weights, sems.at[4]),
        ]
        for copy in copies:
            copy.start()
        copies[0].wait()
        copies[1].wait()
    else:
        _, f1s, e, weighted = refs
        blocks, link, widths, weights, copies = pivot.at[slot], factor.at[slot, 1], live, weight, []
    row, column = rows_columns(width)
    kept = [column < widths[k] for k in range(2)]
    both = [jnp.logical_and(row < widths[k], kept[k]) for k in range(2)]
    f1 = [jnp.where(kept[1], link[c], 0.0) for c in range(2)]
    s1, t1 = split_pair(*f1), split_pair(f1[0].T, f1[1].T)
    store4(f1s, s1)
    for copy in copies[2:]:
        copy.wait()
    d = [[jnp.where(both[k], blocks[k, c], 0.0) for c in range(2)] for k in range(2)]
    br, bi = complex_dot(split_pair(*d[0]), s1)
    tr, ti = complex_dot(t1, split_pair(br, bi))
    er, ei = d[1][0] + tr, d[1][1] + ti
    e[0], e[1] = packed(er), packed(ei)
    w0, w1 = weights[pl.ds(slot, 1), 0:1], weights[pl.ds(slot, 1), 1:2]
    weighted[0] = packed(w1 * d[0][0] + w0 * d[0][1])
    weighted[1] = packed(w1 * er + w0 * ei)
    weighted_b = flat(w1 * br + w0 * bi)
    weighted[2] = weighted_b[: width + 8]
    weighted[3, : width - 8] = weighted_b[width + 8 :]


def factor_kernel(hosted, live, factor, f1s, f0s, f0t, gs, gt, g):
    slot = slot_of(hosted)
    _, column = rows_columns(factor.shape[-1])
    f0 = [jnp.where(column < live[0], factor[slot, 0, c], 0.0) for c in range(2)]
    s0 = split_pair(*f0)
    gr, gi = complex_dot(s0, load4(f1s))
    g[0], g[1] = gr, gi
    store4(gs, split_pair(gr, gi))
    store4(gt, split_pair(gr.T, gi.T))
    store4(f0s, s0)
    store4(f0t, split_pair(f0[0].T, f0[1].T))


def fold(x, gs, gt, e, out):
    tr, ti = complex_dot(x, load4(gs))
    yr, yi = complex_dot(load4(gt), split_pair(tr, ti))
    out[0] = e[0] + packed(yr)
    out[1] = e[1] + packed(yi)


def step_kernel(active, gs, gt, e, *refs):
    *received, out = refs

    @pl.when(active(whereabouts()[0]))
    def _():
        value = received[0][...]
        for other in received[1:]:
            value = value + other[...]
        fold(split_pair(unpacked(value[0]), unpacked(value[1])), gs, gt, e, out)


def pair_kernel(g, e, g_in, e_in, e_second, fas, fat, ea, ps, pt, ep):
    upper = whereabouts()[0] > 1
    is_odd = whereabouts()[1] == 1
    ga = [jnp.where(is_odd, g_in[c], g[c]) for c in range(2)]
    gb = [jnp.where(is_odd, g[c], g_in[c]) for c in range(2)]
    theirs = [jnp.where(upper, e_in[c], e_second[c]) for c in range(2)]
    low = [jnp.where(is_odd, theirs[c], e[c]) for c in range(2)]
    high = [jnp.where(is_odd, e[c], theirs[c]) for c in range(2)]
    sa, sb = split_pair(*ga), split_pair(*gb)
    store4(fas, sa)
    store4(fat, split_pair(ga[0].T, ga[1].T))
    pr, pi = complex_dot(sa, sb)
    store4(ps, split_pair(pr, pi))
    store4(pt, split_pair(pr.T, pi.T))
    br, bi = complex_dot(split_pair(unpacked(low[0]), unpacked(low[1])), sb)
    tr, ti = complex_dot(split_pair(gb[0].T, gb[1].T), split_pair(br, bi))
    for c, term in enumerate((tr, ti)):
        ea[c] = low[c]
        ep[c] = high[c] + packed(term)


def share_kernel(fas, fat, ea, *refs):
    *received, own, sent, scratch = refs
    value = received[0][...]
    for other in received[1:]:
        value = value + other[...]
    value = jnp.where(whereabouts()[0] > 1, value, 0.0)
    fold(split_pair(unpacked(value[0]), unpacked(value[1])), fas, fat, ea, scratch)
    is_odd = whereabouts()[1] == 1
    own[...] = jnp.where(is_odd, scratch[...], value)
    sent[...] = jnp.where(is_odd, value, scratch[...])


def flat(block):
    half = block.shape[1] // 2
    return jnp.concatenate([block[:, :half], block[:, half:]], axis=0)


def real_dot(left, right):
    return dot3(left[0], left[2], right[0], right[2]) + dot3(left[1], left[3], right[1], right[3])


def off_values(slot, weight, xs, f0s, f0t, gs, weighted):
    width = f0s.shape[-1]
    w0, w1 = weight[pl.ds(slot, 1), 0:1], weight[pl.ds(slot, 1), 1:2]
    qr, qi = complex_dot(xs, load4(gs))
    ts = split_pair(w1 * qr + w0 * qi, w0 * qr - w1 * qi)
    second = real_dot(load4(f0t), ts)
    pr, pi = complex_dot(xs, load4(f0s))
    u = w1 * pr + w0 * pi
    us = split_pair(u, w0 * pr - w1 * pi)
    constant = jnp.concatenate([weighted[2], weighted[3, : width - 8]], axis=0)
    return -flat(u), -(flat(second) + constant), us, ts


def diag_values(us, ts, f0t, gt, weighted):
    return (
        weighted[0] + packed(real_dot(load4(f0t), us)),
        weighted[1] + packed(real_dot(load4(gt), ts)),
    )


def density_kernel(weight, x, f0s, f0t, gs, gt, weighted, off, diag):
    core = whereabouts()[2]
    first, second, us, ts = off_values(slot_of(True), weight, unpacked_split(x), f0s, f0t, gs, weighted)
    off[core], off[1 - core] = first, second
    diag[core], diag[1 - core] = diag_values(us, ts, f0t, gt, weighted)


def more_off_kernel(weight, x, x_first, f0s, f0t, gs, weighted, before, off, us_out, ts_out):
    core = whereabouts()[2]
    upper = whereabouts()[0] > 1
    x = [jnp.where(upper, x[c], x_first[c]) for c in range(2)]
    xs = split_pair(unpacked(x[0]), unpacked(x[1]))
    first, second, us, ts = off_values(slot_of(False), weight, xs, f0s, f0t, gs, weighted)
    off[core] = first + before[core]
    off[1 - core] = second + before[1 - core]
    store4(us_out, us)
    store4(ts_out, ts)


def more_diag_kernel(us, ts, f0t, gt, weighted, before, diag):
    core = whereabouts()[2]
    first, second = diag_values(load4(us), load4(ts), f0t, gt, weighted)
    diag[core] = first + before[core]
    diag[1 - core] = second + before[1 - core]


def unpack_off_kernel(mine, theirs, off, done):
    core = whereabouts()[2]
    width = off.shape[-1]
    half = width // 2
    for source, entry in ((mine, core), (theirs, 1 - core)):
        off[entry, :, :half] = source[:width]
        off[entry, :, half:] = source[width:]
    done[...] = jnp.zeros_like(done)


def unpack_diag_kernel(mine, theirs, _, diag):
    core = whereabouts()[2]
    for source, entry in ((mine, core), (theirs, 1 - core)):
        diag[entry] = unpacked(source[...])


SCALAR = pl.BlockSpec(memory_space=pltpu.SMEM)
WHOLE = pl.BlockSpec(memory_space=pltpu.VMEM)


COST = pl.CostEstimate(flops=1, bytes_accessed=1, transcendentals=0)


LONG = pl.CostEstimate(flops=10**11, bytes_accessed=1, transcendentals=0)


def run(kernel, scalars, arrays, shapes, scratch=(), cost=COST, far=()):
    return pl.pallas_call(
        kernel,
        out_shape=shapes,
        in_specs=[SCALAR] * len(scalars)
        + [pl.BlockSpec(memory_space=pltpu.HBM)] * len(far)
        + [WHOLE] * len(arrays),
        out_specs=[WHOLE] * len(shapes),
        scratch_shapes=list(scratch),
        compiler_params=pltpu.CompilerParams(vmem_limit_bytes=VMEM_LIMIT),
        cost_estimate=cost,
    )(*scalars, *far, *arrays)


def local(pivot, factor, live, weight):
    poles, turns = lax.axis_size("pole"), lax.axis_size("snode")
    rows = turns // 2
    width = pivot.shape[-1]
    quarter = (width + 8, width // 2)
    mirrored = jax.ShapeDtypeStruct((2,) + quarter, F32)
    parts = jax.ShapeDtypeStruct((4, width, width), BF16)

    def at(pole_index, snode_index):
        return pole_index * turns + snode_index

    def hosts(row, pole):
        return at(pole, 2 * row + 1), at(pole, 2 * row)

    swaps = [(at(p, s), at(p, s ^ 1)) for p in range(poles) for s in range(2, turns)]
    first = [(at(p, 0), at(p, 1)) for p in range(poles)]
    every = [(at(p, s), at(p, s ^ 1)) for p in range(poles) for s in range(turns)]
    constants = [parts, mirrored, jax.ShapeDtypeStruct((4,) + quarter, F32)]
    factors = [parts, parts, parts, parts, jax.ShapeDtypeStruct((2, width, width), F32)]

    o_f1s, o_e, o_w = run(
        functools.partial(constant_kernel, False, True),
        [],
        [],
        constants,
        [
            pltpu.VMEM(pivot.shape[1:], F32),
            pltpu.VMEM(factor.shape[2:], F32),
            pltpu.SMEM(live.shape, jnp.int32),
            pltpu.VMEM(weight.shape, F32),
            pltpu.SemaphoreType.DMA((5,)),
        ],
        far=[
            pltpu.with_memory_space_constraint(a, pltpu.HBM) for a in (live, pivot, factor, weight)
        ],
    )
    e_in = lax.ppermute(o_e, AXES, first + swaps)
    o_f0s, o_f0t, o_gs, o_gt, o_g = run(
        functools.partial(factor_kernel, False), [live], [factor, o_f1s], factors
    )
    g_in = lax.ppermute(o_g, AXES, swaps)
    m_f1s, m_e, m_w = run(
        functools.partial(constant_kernel, True, False),
        [live],
        [pivot, factor, weight, o_g],
        constants,
    )
    m_f0s, m_f0t, m_gs, m_gt, m_g = run(
        functools.partial(factor_kernel, True), [live], [factor, m_f1s], factors
    )
    e_second = lax.ppermute(m_e, AXES, first)

    starts = functools.partial(step_kernel, lambda place: place == 1)
    (wave_even,) = run(starts, [], [o_gs, o_gt, o_e, e_in], [mirrored])
    wave_even = lax.ppermute(wave_even, AXES, [(at(p, 1), at(p, 0)) for p in range(poles)])
    (wave_odd,) = run(starts, [], [m_gs, m_gt, m_e, e_second], [mirrored])
    received = []
    if rows > 1:
        received = [
            lax.ppermute(wave_odd, AXES, [(at(p, 1), at(p, 3)) for p in range(poles)]),
            lax.ppermute(wave_even, AXES, [(at(p, 0), at(p, 2)) for p in range(poles)]),
        ]
    else:
        received = [jnp.zeros(mirrored.shape, F32)]
    fas, fat, ea, ps, pt, ep = run(
        pair_kernel,
        [],
        [m_g, m_e, g_in, e_in, e_second],
        [parts, parts, mirrored, parts, parts, mirrored],
        cost=LONG,
    )
    arrived = list(received)
    for turn in range(1, rows - 1):
        active = functools.partial(step_kernel, lambda place, turn=turn: lax.div(place, 2) == turn)
        (wave,) = run(active, [], [ps, pt, ep] + arrived, [mirrored])
        up = [pair for p in range(poles) for pair in zip(hosts(turn, p), hosts(turn + 1, p))]
        arrived = [lax.ppermute(wave, AXES, up)]
        received += arrived
    own, sent = run(
        share_kernel,
        [],
        [fas, fat, ea] + received,
        [mirrored, mirrored],
        [pltpu.VMEM(mirrored.shape, F32)],
    )
    shared = lax.ppermute(sent, AXES, every)

    offs = jax.ShapeDtypeStruct((2, 2 * width, width // 2), F32)
    diags = jax.ShapeDtypeStruct((2,) + quarter, F32)
    off, diag = run(density_kernel, [], [weight, own, m_f0s, m_f0t, m_gs, m_gt, m_w], [offs, diags])
    off, us, ts = run(
        more_off_kernel,
        [],
        [weight, shared, e_in, o_f0s, o_f0t, o_gs, o_w, off],
        [offs, parts, parts],
    )

    def exchanged(value, distance):
        return lax.ppermute(value, "pole", [(p, p ^ distance) for p in range(poles)])

    def summed(parts):
        kept = parts[0] + exchanged(parts[1], 1)
        distance = 2
        while distance < poles:
            kept = kept + exchanged(kept, distance)
            distance *= 2
        return kept, exchanged(kept, 1)

    full = jax.ShapeDtypeStruct((2, width, width), F32)
    off_sums = summed(off)
    (diag,) = run(more_diag_kernel, [], [us, ts, o_f0t, o_gt, o_w, diag], [diags])
    diag_sums = summed(diag)
    done = jax.ShapeDtypeStruct((8, 128), F32)
    density_off, done = run(unpack_off_kernel, [], list(off_sums), [full, done])
    (density_diag,) = run(unpack_diag_kernel, [], [*diag_sums, done], [full])
    return density_diag, density_off


def solution(mesh):
    placed = (
        P("pole", "snode", None, None, None),
        P("pole", "snode", None, None, None),
        P("snode"),
        P("pole", None),
    )
    return jax.shard_map(
        local,
        mesh=mesh,
        in_specs=placed,
        out_specs=(P("snode", None, None), P("snode", None, None)),
        check_vma=False,
    )
```

```python
import functools

import jax
import jax.numpy as jnp
from jax import lax
from jax.experimental import pallas as pl
from jax.experimental.pallas import tpu as pltpu
from jax.sharding import PartitionSpec as P

F32 = jnp.float32
BF16 = jnp.bfloat16
AXES = ("pole", "snode")
VMEM_LIMIT = 16 * 1024 * 1024


def halves(value):
    high = value.astype(BF16)
    return high, (value - high.astype(F32)).astype(BF16)


def split_pair(real, imag):
    (rh, rl), (ih, il) = halves(real), halves(imag)
    return rh, ih, rl, il


def dot(left, right):
    return jnp.dot(left, right, preferred_element_type=F32)


def dot3(lh, ll, rh, rl):
    return dot(lh, rh) + (dot(lh, rl) + dot(ll, rh))


def complex_dot(left, right):
    arh, aih, arl, ail = left
    brh, bih, brl, bil = right
    real = dot3(arh, arl, brh, brl) - dot3(aih, ail, bih, bil)
    imag = dot3(arh, arl, bih, bil) + dot3(aih, ail, brh, brl)
    return real, imag


def rows_columns(size):
    return (
        lax.broadcasted_iota(jnp.int32, (size, size), 0),
        lax.broadcasted_iota(jnp.int32, (size, size), 1),
    )


def packed(block):
    half = block.shape[0] // 2
    row, column = rows_columns(half)
    lower = block[half:, half:]
    mixed = jnp.where(row >= column, block[:half, :half], lower)
    diagonal = jnp.sum(jnp.where(row == column, lower, 0.0), axis=0, keepdims=True)
    return jnp.concatenate(
        [block[:half, half:], mixed, jnp.broadcast_to(diagonal, (8, half))], axis=0
    )


def unpacked(value):
    half = value.shape[1]
    row, column = rows_columns(half)
    right, mixed = value[:half], value[half : 2 * half]
    diagonal = value[2 * half : 2 * half + 1]
    turned = mixed.T
    first = jnp.where(row >= column, mixed, turned)
    last = jnp.where(row < column, mixed, jnp.where(row == column, diagonal, turned))
    return jnp.concatenate(
        [jnp.concatenate([first, right], axis=1), jnp.concatenate([right.T, last], axis=1)], axis=0
    )


def unpacked_split(ref):
    return split_pair(unpacked(ref[0]), unpacked(ref[1]))


def load4(ref):
    return tuple(ref[i] for i in range(4))


def store4(ref, parts):
    for i, part in enumerate(parts):
        ref[i] = part


def whereabouts():
    place = lax.axis_index("snode")
    return place, lax.rem(place, 2), lax.rem(lax.axis_index("pole"), 2)


def hosted_slot():
    place, odd, _ = whereabouts()
    return jnp.where(place < 2, 0, 1 - odd)


def slot_of(hosted):
    return hosted_slot() if hosted else 1 - hosted_slot()


def constant_kernel(hosted, fetch, live, pivot, factor, weight, *refs):
    width = pivot.shape[-1]
    slot = slot_of(hosted)
    if fetch:
        f1s, e, weighted, blocks, link, widths, weights, sems = refs
        copies = [
            pltpu.make_async_copy(live, widths, sems.at[0]),
            pltpu.make_async_copy(factor.at[slot, 1], link, sems.at[1]),
            pltpu.make_async_copy(pivot.at[slot, 0], blocks.at[0], sems.at[2]),
            pltpu.make_async_copy(pivot.at[slot, 1], blocks.at[1], sems.at[3]),
            pltpu.make_async_copy(weight, weights, sems.at[4]),
        ]
        for copy in copies:
            copy.start()
        copies[0].wait()
        copies[1].wait()
    else:
        _, f1s, e, weighted = refs
        blocks, link, widths, weights, copies = pivot.at[slot], factor.at[slot, 1], live, weight, []
    row, column = rows_columns(width)
    kept = [column < widths[k] for k in range(2)]
    both = [jnp.logical_and(row < widths[k], kept[k]) for k in range(2)]
    f1 = [jnp.where(kept[1], link[c], 0.0) for c in range(2)]
    s1, t1 = split_pair(*f1), split_pair(f1[0].T, f1[1].T)
    store4(f1s, s1)
    for copy in copies[2:]:
        copy.wait()
    d = [[jnp.where(both[k], blocks[k, c], 0.0) for c in range(2)] for k in range(2)]
    br, bi = complex_dot(split_pair(*d[0]), s1)
    tr, ti = complex_dot(t1, split_pair(br, bi))
    er, ei = d[1][0] + tr, d[1][1] + ti
    e[0], e[1] = packed(er), packed(ei)
    w0, w1 = weights[pl.ds(slot, 1), 0:1], weights[pl.ds(slot, 1), 1:2]
    weighted[0] = packed(w1 * d[0][0] + w0 * d[0][1])
    weighted[1] = packed(w1 * er + w0 * ei)
    weighted_b = flat(w1 * br + w0 * bi)
    weighted[2] = weighted_b[: width + 8]
    weighted[3, : width - 8] = weighted_b[width + 8 :]


def factor_kernel(hosted, count, live, factor, f1s, *refs):
    f0s, f0t, gs, gt, g = refs[count : count + 5]
    slot = slot_of(hosted)
    _, column = rows_columns(factor.shape[-1])
    f0 = [jnp.where(column < live[0], factor[slot, 0, c], 0.0) for c in range(2)]
    s0 = split_pair(*f0)
    gr, gi = complex_dot(s0, load4(f1s))
    g[0], g[1] = gr, gi
    store4(gs, split_pair(gr, gi))
    store4(gt, split_pair(gr.T, gi.T))
    store4(f0s, s0)
    store4(f0t, split_pair(f0[0].T, f0[1].T))
    for source, target in zip(refs[:count], refs[count + 5 :]):
        target[...] = source[...]


def fold(x, gs, gt, e, out):
    tr, ti = complex_dot(x, load4(gs))
    yr, yi = complex_dot(load4(gt), split_pair(tr, ti))
    out[0] = e[0] + packed(yr)
    out[1] = e[1] + packed(yi)


def step_kernel(active, gs, gt, e, *refs):
    *received, out = refs

    @pl.when(active(whereabouts()[0]))
    def _():
        value = received[0][...]
        for other in received[1:]:
            value = value + other[...]
        fold(split_pair(unpacked(value[0]), unpacked(value[1])), gs, gt, e, out)


def pair_kernel(g, e, g_in, e_in, e_second, fas, fat, ea, ps, pt, ep):
    upper = whereabouts()[0] > 1
    is_odd = whereabouts()[1] == 1
    ga = [jnp.where(is_odd, g_in[c], g[c]) for c in range(2)]
    gb = [jnp.where(is_odd, g[c], g_in[c]) for c in range(2)]
    theirs = [jnp.where(upper, e_in[c], e_second[c]) for c in range(2)]
    low = [jnp.where(is_odd, theirs[c], e[c]) for c in range(2)]
    high = [jnp.where(is_odd, e[c], theirs[c]) for c in range(2)]
    sa, sb = split_pair(*ga), split_pair(*gb)
    store4(fas, sa)
    store4(fat, split_pair(ga[0].T, ga[1].T))
    pr, pi = complex_dot(sa, sb)
    store4(ps, split_pair(pr, pi))
    store4(pt, split_pair(pr.T, pi.T))
    br, bi = complex_dot(split_pair(unpacked(low[0]), unpacked(low[1])), sb)
    tr, ti = complex_dot(split_pair(gb[0].T, gb[1].T), split_pair(br, bi))
    for c, term in enumerate((tr, ti)):
        ea[c] = low[c]
        ep[c] = high[c] + packed(term)


def share_kernel(fas, fat, ea, *refs):
    *received, own, sent, scratch = refs
    value = received[0][...]
    for other in received[1:]:
        value = value + other[...]
    value = jnp.where(whereabouts()[0] > 1, value, 0.0)
    fold(split_pair(unpacked(value[0]), unpacked(value[1])), fas, fat, ea, scratch)
    is_odd = whereabouts()[1] == 1
    own[...] = jnp.where(is_odd, scratch[...], value)
    sent[...] = jnp.where(is_odd, value, scratch[...])


def flat(block):
    half = block.shape[1] // 2
    return jnp.concatenate([block[:, :half], block[:, half:]], axis=0)


def real_dot(left, right):
    return dot3(left[0], left[2], right[0], right[2]) + dot3(left[1], left[3], right[1], right[3])


def off_values(slot, weight, xs, f0s, f0t, gs, weighted):
    width = f0s.shape[-1]
    w0, w1 = weight[pl.ds(slot, 1), 0:1], weight[pl.ds(slot, 1), 1:2]
    qr, qi = complex_dot(xs, load4(gs))
    ts = split_pair(w1 * qr + w0 * qi, w0 * qr - w1 * qi)
    second = real_dot(load4(f0t), ts)
    pr, pi = complex_dot(xs, load4(f0s))
    u = w1 * pr + w0 * pi
    us = split_pair(u, w0 * pr - w1 * pi)
    constant = jnp.concatenate([weighted[2], weighted[3, : width - 8]], axis=0)
    return -flat(u), -(flat(second) + constant), us, ts


def diag_values(us, ts, f0t, gt, weighted):
    return (
        weighted[0] + packed(real_dot(load4(f0t), us)),
        weighted[1] + packed(real_dot(load4(gt), ts)),
    )


def density_kernel(weight, x, f0s, f0t, gs, gt, weighted, off, diag):
    core = whereabouts()[2]
    first, second, us, ts = off_values(slot_of(True), weight, unpacked_split(x), f0s, f0t, gs, weighted)
    off[core], off[1 - core] = first, second
    diag[core], diag[1 - core] = diag_values(us, ts, f0t, gt, weighted)


def more_off_kernel(weight, x, x_first, f0s, f0t, gs, weighted, before, off, us_out, ts_out):
    core = whereabouts()[2]
    upper = whereabouts()[0] > 1
    x = [jnp.where(upper, x[c], x_first[c]) for c in range(2)]
    xs = split_pair(unpacked(x[0]), unpacked(x[1]))
    first, second, us, ts = off_values(slot_of(False), weight, xs, f0s, f0t, gs, weighted)
    off[core] = first + before[core]
    off[1 - core] = second + before[1 - core]
    store4(us_out, us)
    store4(ts_out, ts)


def more_diag_kernel(us, ts, f0t, gt, weighted, before, diag):
    core = whereabouts()[2]
    first, second = diag_values(load4(us), load4(ts), f0t, gt, weighted)
    diag[core] = first + before[core]
    diag[1 - core] = second + before[1 - core]


def unpack_off_kernel(mine, theirs, off, done):
    core = whereabouts()[2]
    width = off.shape[-1]
    half = width // 2
    for source, entry in ((mine, core), (theirs, 1 - core)):
        off[entry, :, :half] = source[:width]
        off[entry, :, half:] = source[width:]
    done[...] = jnp.zeros_like(done)


def unpack_diag_kernel(mine, theirs, _, diag):
    core = whereabouts()[2]
    for source, entry in ((mine, core), (theirs, 1 - core)):
        diag[entry] = unpacked(source[...])


SCALAR = pl.BlockSpec(memory_space=pltpu.SMEM)
WHOLE = pl.BlockSpec(memory_space=pltpu.VMEM)


COST = pl.CostEstimate(flops=1, bytes_accessed=1, transcendentals=0)


LONG = pl.CostEstimate(flops=10**11, bytes_accessed=1, transcendentals=0)


def run(kernel, scalars, arrays, shapes, scratch=(), cost=COST, far=()):
    return pl.pallas_call(
        kernel,
        out_shape=shapes,
        in_specs=[SCALAR] * len(scalars)
        + [pl.BlockSpec(memory_space=pltpu.HBM)] * len(far)
        + [WHOLE] * len(arrays),
        out_specs=[WHOLE] * len(shapes),
        scratch_shapes=list(scratch),
        compiler_params=pltpu.CompilerParams(vmem_limit_bytes=VMEM_LIMIT),
        cost_estimate=cost,
    )(*scalars, *far, *arrays)


def local(pivot, factor, live, weight):
    poles, turns = lax.axis_size("pole"), lax.axis_size("snode")
    rows = turns // 2
    width = pivot.shape[-1]
    quarter = (width + 8, width // 2)
    mirrored = jax.ShapeDtypeStruct((2,) + quarter, F32)
    parts = jax.ShapeDtypeStruct((4, width, width), BF16)

    def at(pole_index, snode_index):
        return pole_index * turns + snode_index

    def hosts(row, pole):
        return at(pole, 2 * row + 1), at(pole, 2 * row)

    def swaps(core):
        return [(at(p, s), at(p, s ^ 1)) for p in range(core, poles, 2) for s in range(2, turns)]

    def first(core):
        return [(at(p, 0), at(p, 1)) for p in range(core, poles, 2)]

    every = [(at(p, s), at(p, s ^ 1)) for p in range(poles) for s in range(turns)]
    constants = [parts, mirrored, jax.ShapeDtypeStruct((4,) + quarter, F32)]
    factors = [parts, parts, parts, parts, jax.ShapeDtypeStruct((2, width, width), F32)]

    o_f1s, o_e, o_w = run(
        functools.partial(constant_kernel, False, True),
        [],
        [],
        constants,
        [
            pltpu.VMEM(pivot.shape[1:], F32),
            pltpu.VMEM(factor.shape[2:], F32),
            pltpu.SMEM(live.shape, jnp.int32),
            pltpu.VMEM(weight.shape, F32),
            pltpu.SemaphoreType.DMA((5,)),
        ],
        far=[
            pltpu.with_memory_space_constraint(a, pltpu.HBM) for a in (live, pivot, factor, weight)
        ],
    )
    e_in = lax.ppermute(o_e, AXES, first(1) + swaps(1))
    o_f0s, o_f0t, o_gs, o_gt, o_g, e_late = run(
        functools.partial(factor_kernel, False, 1),
        [live],
        [factor, o_f1s, o_e],
        [*factors, mirrored],
    )
    g_in = lax.ppermute(o_g, AXES, swaps(1))
    e_in = e_in + lax.ppermute(e_late, AXES, first(0) + swaps(0))
    m_f1s, m_e, m_w = run(
        functools.partial(constant_kernel, True, False),
        [live],
        [pivot, factor, weight, o_g],
        constants,
    )
    e_second = lax.ppermute(m_e, AXES, first(1))
    m_f0s, m_f0t, m_gs, m_gt, m_g, g_late, second_late = run(
        functools.partial(factor_kernel, True, 2),
        [live],
        [factor, m_f1s, o_g, m_e],
        [*factors, factors[-1], mirrored],
    )
    g_in = g_in + lax.ppermute(g_late, AXES, swaps(0))
    e_second = e_second + lax.ppermute(second_late, AXES, first(0))

    starts = functools.partial(step_kernel, lambda place: place == 1)
    (wave_even,) = run(starts, [], [o_gs, o_gt, o_e, e_in], [mirrored])
    wave_even = lax.ppermute(wave_even, AXES, [(at(p, 1), at(p, 0)) for p in range(poles)])
    (wave_odd,) = run(starts, [], [m_gs, m_gt, m_e, e_second], [mirrored])
    received = []
    if rows > 1:
        received = [
            lax.ppermute(wave_odd, AXES, [(at(p, 1), at(p, 3)) for p in range(poles)]),
            lax.ppermute(wave_even, AXES, [(at(p, 0), at(p, 2)) for p in range(poles)]),
        ]
    else:
        received = [jnp.zeros(mirrored.shape, F32)]
    fas, fat, ea, ps, pt, ep = run(
        pair_kernel,
        [],
        [m_g, m_e, g_in, e_in, e_second],
        [parts, parts, mirrored, parts, parts, mirrored],
        cost=LONG,
    )
    arrived = list(received)
    for turn in range(1, rows - 1):
        active = functools.partial(step_kernel, lambda place, turn=turn: lax.div(place, 2) == turn)
        (wave,) = run(active, [], [ps, pt, ep] + arrived, [mirrored])
        up = [pair for p in range(poles) for pair in zip(hosts(turn, p), hosts(turn + 1, p))]
        arrived = [lax.ppermute(wave, AXES, up)]
        received += arrived
    own, sent = run(
        share_kernel,
        [],
        [fas, fat, ea] + received,
        [mirrored, mirrored],
        [pltpu.VMEM(mirrored.shape, F32)],
    )
    shared = lax.ppermute(sent, AXES, every)

    offs = jax.ShapeDtypeStruct((2, 2 * width, width // 2), F32)
    diags = jax.ShapeDtypeStruct((2,) + quarter, F32)
    off, diag = run(density_kernel, [], [weight, own, m_f0s, m_f0t, m_gs, m_gt, m_w], [offs, diags])
    off, us, ts = run(
        more_off_kernel,
        [],
        [weight, shared, e_in, o_f0s, o_f0t, o_gs, o_w, off],
        [offs, parts, parts],
    )

    def exchanged(value, distance):
        return lax.ppermute(value, "pole", [(p, p ^ distance) for p in range(poles)])

    def summed(parts):
        kept = parts[0] + exchanged(parts[1], 1)
        distance = 2
        while distance < poles:
            kept = kept + exchanged(kept, distance)
            distance *= 2
        return kept, exchanged(kept, 1)

    full = jax.ShapeDtypeStruct((2, width, width), F32)
    off_sums = summed(off)
    (diag,) = run(more_diag_kernel, [], [us, ts, o_f0t, o_gt, o_w, diag], [diags])
    diag_sums = summed(diag)
    done = jax.ShapeDtypeStruct((8, 128), F32)
    density_off, done = run(unpack_off_kernel, [], list(off_sums), [full, done])
    (density_diag,) = run(unpack_diag_kernel, [], [*diag_sums, done], [full])
    return density_diag, density_off


def solution(mesh):
    placed = (
        P("pole", "snode", None, None, None),
        P("pole", "snode", None, None, None),
        P("snode"),
        P("pole", None),
    )
    return jax.shard_map(
        local,
        mesh=mesh,
        in_specs=placed,
        out_specs=(P("snode", None, None), P("snode", None, None)),
        check_vma=False,
    )
```

```python
import functools

import jax
import jax.numpy as jnp
from jax import lax
from jax.experimental import pallas as pl
from jax.experimental.pallas import tpu as pltpu
from jax.sharding import PartitionSpec as P

F32 = jnp.float32
BF16 = jnp.bfloat16
AXES = ("pole", "snode")
VMEM_LIMIT = 16 * 1024 * 1024


def halves(value):
    high = value.astype(BF16)
    return high, (value - high.astype(F32)).astype(BF16)


def split_pair(real, imag):
    (rh, rl), (ih, il) = halves(real), halves(imag)
    return rh, ih, rl, il


def dot(left, right):
    return jnp.dot(left, right, preferred_element_type=F32)


def dot3(lh, ll, rh, rl):
    return dot(lh, rh) + (dot(lh, rl) + dot(ll, rh))


def complex_dot(left, right):
    arh, aih, arl, ail = left
    brh, bih, brl, bil = right
    real = dot3(arh, arl, brh, brl) - dot3(aih, ail, bih, bil)
    imag = dot3(arh, arl, bih, bil) + dot3(aih, ail, brh, brl)
    return real, imag


def rows_columns(size):
    return (
        lax.broadcasted_iota(jnp.int32, (size, size), 0),
        lax.broadcasted_iota(jnp.int32, (size, size), 1),
    )


def packed(block):
    half = block.shape[0] // 2
    row, column = rows_columns(half)
    lower = block[half:, half:]
    mixed = jnp.where(row >= column, block[:half, :half], lower)
    diagonal = jnp.sum(jnp.where(row == column, lower, 0.0), axis=0, keepdims=True)
    return jnp.concatenate(
        [block[:half, half:], mixed, jnp.broadcast_to(diagonal, (8, half))], axis=0
    )


def unpacked(value):
    half = value.shape[1]
    row, column = rows_columns(half)
    right, mixed = value[:half], value[half : 2 * half]
    diagonal = value[2 * half : 2 * half + 1]
    turned = mixed.T
    first = jnp.where(row >= column, mixed, turned)
    last = jnp.where(row < column, mixed, jnp.where(row == column, diagonal, turned))
    return jnp.concatenate(
        [jnp.concatenate([first, right], axis=1), jnp.concatenate([right.T, last], axis=1)], axis=0
    )


def unpacked_split(ref):
    return split_pair(unpacked(ref[0]), unpacked(ref[1]))


def load4(ref):
    return tuple(ref[i] for i in range(4))


def store4(ref, parts):
    for i, part in enumerate(parts):
        ref[i] = part


def whereabouts():
    place = lax.axis_index("snode")
    return place, lax.rem(place, 2), lax.rem(lax.axis_index("pole"), 2)


def hosted_slot():
    place, odd, core = whereabouts()
    return jnp.where(jnp.logical_and(place < 2, core == 0), 0, 1 - odd)


def slot_of(hosted):
    return hosted_slot() if hosted else 1 - hosted_slot()


def constant_kernel(hosted, fetch, live, pivot, factor, weight, *refs):
    width = pivot.shape[-1]
    slot = slot_of(hosted)
    if fetch:
        f1s, e, weighted, blocks, link, widths, weights, sems = refs
        copies = [
            pltpu.make_async_copy(live, widths, sems.at[0]),
            pltpu.make_async_copy(factor.at[slot, 1], link, sems.at[1]),
            pltpu.make_async_copy(pivot.at[slot, 0], blocks.at[0], sems.at[2]),
            pltpu.make_async_copy(pivot.at[slot, 1], blocks.at[1], sems.at[3]),
            pltpu.make_async_copy(weight, weights, sems.at[4]),
        ]
        for copy in copies:
            copy.start()
        copies[0].wait()
        copies[1].wait()
    else:
        f1s, e, weighted = refs[-3:]
        blocks, link, widths, weights, copies = pivot.at[slot], factor.at[slot, 1], live, weight, []
    row, column = rows_columns(width)
    kept = [column < widths[k] for k in range(2)]
    both = [jnp.logical_and(row < widths[k], kept[k]) for k in range(2)]
    f1 = [jnp.where(kept[1], link[c], 0.0) for c in range(2)]
    s1, t1 = split_pair(*f1), split_pair(f1[0].T, f1[1].T)
    store4(f1s, s1)
    for copy in copies[2:]:
        copy.wait()
    d = [[jnp.where(both[k], blocks[k, c], 0.0) for c in range(2)] for k in range(2)]
    br, bi = complex_dot(split_pair(*d[0]), s1)
    tr, ti = complex_dot(t1, split_pair(br, bi))
    er, ei = d[1][0] + tr, d[1][1] + ti
    e[0], e[1] = packed(er), packed(ei)
    w0, w1 = weights[pl.ds(slot, 1), 0:1], weights[pl.ds(slot, 1), 1:2]
    weighted[0] = packed(w1 * d[0][0] + w0 * d[0][1])
    weighted[1] = packed(w1 * er + w0 * ei)
    weighted_b = flat(w1 * br + w0 * bi)
    weighted[2] = weighted_b[: width + 8]
    weighted[3, : width - 8] = weighted_b[width + 8 :]


def factor_kernel(hosted, live, factor, f1s, passed, *refs):
    f0s, f0t, gs, gt, g, handed = refs[-6:]
    slot = slot_of(hosted)
    _, column = rows_columns(factor.shape[-1])
    f0 = [jnp.where(column < live[0], factor[slot, 0, c], 0.0) for c in range(2)]
    s0 = split_pair(*f0)
    gr, gi = complex_dot(s0, load4(f1s))
    g[0], g[1] = gr, gi
    store4(gs, split_pair(gr, gi))
    store4(gt, split_pair(gr.T, gi.T))
    store4(f0s, s0)
    store4(f0t, split_pair(f0[0].T, f0[1].T))
    handed[...] = passed[...]


def fold(x, gs, gt, e, out):
    tr, ti = complex_dot(x, load4(gs))
    yr, yi = complex_dot(load4(gt), split_pair(tr, ti))
    out[0] = e[0] + packed(yr)
    out[1] = e[1] + packed(yi)


def step_kernel(turn, gs, gt, e, *refs):
    *received, out = refs

    @pl.when(lax.div(whereabouts()[0], 2) == turn)
    def _():
        value = received[0][...]
        for other in received[1:]:
            value = value + other[...]
        fold(split_pair(unpacked(value[0]), unpacked(value[1])), gs, gt, e, out)


def even_start_kernel(gs, gt, e, x, out):
    place, _, core = whereabouts()

    @pl.when(jnp.logical_and(place == 1, core == 0))
    def _():
        fold(unpacked_split(x), gs, gt, e, out)


def odd_start_kernel(gs, gt, e, x_core0, x_core1, out):
    place, _, core = whereabouts()
    for x, its_core in ((x_core0, 0), (x_core1, 1)):

        @pl.when(jnp.logical_and(place == 1, core == its_core))
        def _():
            fold(unpacked_split(x), gs, gt, e, out)


def relay_kernel(back, g, e, x, _, out, gs, gt):
    place, _, core = whereabouts()

    @pl.when(jnp.logical_and(place == 0, core == 0))
    def _():
        out[...] = back[...]

    @pl.when(jnp.logical_and(place == 0, core == 1))
    def _():
        store4(gs, split_pair(g[0], g[1]))
        store4(gt, split_pair(g[0].T, g[1].T))
        fold(unpacked_split(x), gs, gt, e, out)


def pair_kernel(g, e, g_core0, g_core1, e_core0, e_core1, e_second, fas, fat, ea, ps, pt, ep):
    place, odd, core = whereabouts()
    is_odd, first_core = odd == 1, core == 0
    g_in = [jnp.where(first_core, g_core0[c], g_core1[c]) for c in range(2)]
    ga = [jnp.where(is_odd, g_in[c], g[c]) for c in range(2)]
    gb = [jnp.where(is_odd, g[c], g_in[c]) for c in range(2)]
    theirs = [
        jnp.where(first_core, jnp.where(place > 1, e_core0[c], e_second[c]), e_core1[c])
        for c in range(2)
    ]
    low = [jnp.where(is_odd, theirs[c], e[c]) for c in range(2)]
    high = [jnp.where(is_odd, e[c], theirs[c]) for c in range(2)]
    sa, sb = split_pair(*ga), split_pair(*gb)
    store4(fas, sa)
    store4(fat, split_pair(ga[0].T, ga[1].T))
    pr, pi = complex_dot(sa, sb)
    store4(ps, split_pair(pr, pi))
    store4(pt, split_pair(pr.T, pi.T))
    br, bi = complex_dot(split_pair(unpacked(low[0]), unpacked(low[1])), sb)
    tr, ti = complex_dot(split_pair(gb[0].T, gb[1].T), split_pair(br, bi))
    for c, term in enumerate((tr, ti)):
        ea[c] = low[c]
        ep[c] = high[c] + packed(term)


def share_kernel(fas, fat, ea, *refs):
    *received, own, sent, scratch = refs
    value = received[0][...]
    for other in received[1:]:
        value = value + other[...]
    value = jnp.where(whereabouts()[0] > 1, value, 0.0)
    fold(split_pair(unpacked(value[0]), unpacked(value[1])), fas, fat, ea, scratch)
    is_odd = whereabouts()[1] == 1
    own[...] = jnp.where(is_odd, scratch[...], value)
    sent[...] = jnp.where(is_odd, value, scratch[...])


def flat(block):
    half = block.shape[1] // 2
    return jnp.concatenate([block[:, :half], block[:, half:]], axis=0)


def real_dot(left, right):
    return dot3(left[0], left[2], right[0], right[2]) + dot3(left[1], left[3], right[1], right[3])


def off_values(slot, weight, xs, f0s, f0t, gs, weighted):
    width = f0s.shape[-1]
    w0, w1 = weight[pl.ds(slot, 1), 0:1], weight[pl.ds(slot, 1), 1:2]
    qr, qi = complex_dot(xs, load4(gs))
    ts = split_pair(w1 * qr + w0 * qi, w0 * qr - w1 * qi)
    second = real_dot(load4(f0t), ts)
    pr, pi = complex_dot(xs, load4(f0s))
    u = w1 * pr + w0 * pi
    us = split_pair(u, w0 * pr - w1 * pi)
    constant = jnp.concatenate([weighted[2], weighted[3, : width - 8]], axis=0)
    return -flat(u), -(flat(second) + constant), us, ts


def diag_values(us, ts, f0t, gt, weighted):
    return (
        weighted[0] + packed(real_dot(load4(f0t), us)),
        weighted[1] + packed(real_dot(load4(gt), ts)),
    )


def density_kernel(weight, x, f0s, f0t, gs, gt, weighted, off, diag):
    core = whereabouts()[2]
    first, second, us, ts = off_values(slot_of(True), weight, unpacked_split(x), f0s, f0t, gs, weighted)
    off[core], off[1 - core] = first, second
    diag[core], diag[1 - core] = diag_values(us, ts, f0t, gt, weighted)


def more_off_kernel(weight, x, x_first, f0s, f0t, gs, weighted, before, off, us_out, ts_out):
    place, _, core = whereabouts()
    begun = jnp.logical_and(place < 2, core == 0)
    x = [jnp.where(begun, x_first[c], x[c]) for c in range(2)]
    xs = split_pair(unpacked(x[0]), unpacked(x[1]))
    first, second, us, ts = off_values(slot_of(False), weight, xs, f0s, f0t, gs, weighted)
    off[core] = first + before[core]
    off[1 - core] = second + before[1 - core]
    store4(us_out, us)
    store4(ts_out, ts)


def more_diag_kernel(us, ts, f0t, gt, weighted, before, diag):
    core = whereabouts()[2]
    first, second = diag_values(load4(us), load4(ts), f0t, gt, weighted)
    diag[core] = first + before[core]
    diag[1 - core] = second + before[1 - core]


def unpack_off_kernel(mine, theirs, off, done):
    core = whereabouts()[2]
    width = off.shape[-1]
    half = width // 2
    for source, entry in ((mine, core), (theirs, 1 - core)):
        off[entry, :, :half] = source[:width]
        off[entry, :, half:] = source[width:]
    done[...] = jnp.zeros_like(done)


def unpack_diag_kernel(mine, theirs, _, diag):
    core = whereabouts()[2]
    for source, entry in ((mine, core), (theirs, 1 - core)):
        diag[entry] = unpacked(source[...])


SCALAR = pl.BlockSpec(memory_space=pltpu.SMEM)
WHOLE = pl.BlockSpec(memory_space=pltpu.VMEM)


COST = pl.CostEstimate(flops=1, bytes_accessed=1, transcendentals=0)


LONG = pl.CostEstimate(flops=10**11, bytes_accessed=1, transcendentals=0)


def run(kernel, scalars, arrays, shapes, scratch=(), cost=COST, far=()):
    return pl.pallas_call(
        kernel,
        out_shape=shapes,
        in_specs=[SCALAR] * len(scalars)
        + [pl.BlockSpec(memory_space=pltpu.HBM)] * len(far)
        + [WHOLE] * len(arrays),
        out_specs=[WHOLE] * len(shapes),
        scratch_shapes=list(scratch),
        compiler_params=pltpu.CompilerParams(vmem_limit_bytes=VMEM_LIMIT),
        cost_estimate=cost,
    )(*scalars, *far, *arrays)


def local(pivot, factor, live, weight):
    poles, turns = lax.axis_size("pole"), lax.axis_size("snode")
    rows = turns // 2
    width = pivot.shape[-1]
    quarter = (width + 8, width // 2)
    mirrored = jax.ShapeDtypeStruct((2,) + quarter, F32)
    parts = jax.ShapeDtypeStruct((4, width, width), BF16)

    def at(pole_index, snode_index):
        return pole_index * turns + snode_index

    def hosts(row, pole):
        return at(pole, 2 * row + 1), at(pole, 2 * row)

    def swaps(core):
        return [(at(p, s), at(p, s ^ 1)) for p in range(core, poles, 2) for s in range(2, turns)]

    def first(core):
        return [(at(p, 0), at(p, 1)) for p in range(core, poles, 2)]

    every = [(at(p, s), at(p, s ^ 1)) for p in range(poles) for s in range(turns)]
    constants = [parts, mirrored, jax.ShapeDtypeStruct((4,) + quarter, F32)]
    factors = [parts, parts, parts, parts, jax.ShapeDtypeStruct((2, width, width), F32)]

    o_f1s, o_e, o_w = run(
        functools.partial(constant_kernel, False, True),
        [],
        [],
        constants,
        [
            pltpu.VMEM(pivot.shape[1:], F32),
            pltpu.VMEM(factor.shape[2:], F32),
            pltpu.SMEM(live.shape, jnp.int32),
            pltpu.VMEM(weight.shape, F32),
            pltpu.SemaphoreType.DMA((5,)),
        ],
        far=[
            pltpu.with_memory_space_constraint(a, pltpu.HBM) for a in (live, pivot, factor, weight)
        ],
    )
    ahead, behind = range(1, poles, 2), range(0, poles, 2)
    e_core1 = lax.ppermute(o_e, AXES, [(at(p, s), at(p, s ^ 1)) for p in ahead for s in range(turns)])
    o_f0s, o_f0t, o_gs, o_gt, o_g, e_late = run(
        functools.partial(factor_kernel, False),
        [live],
        [factor, o_f1s, o_e],
        [*factors, mirrored],
    )
    g_back = lax.ppermute(o_g, AXES, [(at(p, 1), at(p, 0)) for p in ahead])
    g_core1 = lax.ppermute(o_g, AXES, swaps(1))
    e_core0 = lax.ppermute(e_late, AXES, first(0) + swaps(0))
    m_f1s, m_e, m_w = run(
        functools.partial(constant_kernel, True, False),
        [live],
        [pivot, factor, weight, o_g, e_core1],
        constants,
    )
    m_f0s, m_f0t, m_gs, m_gt, m_g, g_late = run(
        functools.partial(factor_kernel, True),
        [live],
        [factor, m_f1s, o_g, g_back],
        [*factors, factors[-1]],
    )
    e_second = lax.ppermute(m_e, AXES, first(0))
    g_core0 = lax.ppermute(g_late, AXES, swaps(0))

    (wave_even,) = run(even_start_kernel, [], [o_gs, o_gt, o_e, e_core0], [mirrored])
    back = lax.ppermute(wave_even, AXES, [(at(p, 1), at(p, 0)) for p in behind])
    (wave_odd,) = run(odd_start_kernel, [], [m_gs, m_gt, m_e, e_second, e_core1], [mirrored])
    (wave_even,) = run(
        relay_kernel,
        [],
        [back, g_back, e_core1, m_e, wave_odd],
        [mirrored],
        [pltpu.VMEM(parts.shape, BF16)] * 2,
    )
    received = [jnp.zeros(mirrored.shape, F32)]
    if rows > 1:
        received = [
            lax.ppermute(wave_odd, AXES, [(at(p, 1), at(p, 3)) for p in range(poles)]),
            lax.ppermute(wave_even, AXES, [(at(p, 0), at(p, 2)) for p in range(poles)]),
        ]

    fas, fat, ea, ps, pt, ep = run(
        pair_kernel,
        [],
        [m_g, m_e, g_core0, g_core1, e_core0, e_core1, e_second],
        [parts, parts, mirrored, parts, parts, mirrored],
        cost=LONG,
    )
    arrived = list(received)
    for turn in range(1, rows - 1):
        (wave,) = run(
            functools.partial(step_kernel, turn), [], [ps, pt, ep] + arrived, [mirrored]
        )
        up = [pair for p in range(poles) for pair in zip(hosts(turn, p), hosts(turn + 1, p))]
        arrived = [lax.ppermute(wave, AXES, up)]
        received += arrived
    own, sent = run(
        share_kernel,
        [],
        [fas, fat, ea] + received,
        [mirrored, mirrored],
        [pltpu.VMEM(mirrored.shape, F32)],
    )
    shared = lax.ppermute(sent, AXES, every)

    offs = jax.ShapeDtypeStruct((2, 2 * width, width // 2), F32)
    diags = jax.ShapeDtypeStruct((2,) + quarter, F32)
    off, diag = run(density_kernel, [], [weight, own, m_f0s, m_f0t, m_gs, m_gt, m_w], [offs, diags])
    off, us, ts = run(
        more_off_kernel,
        [],
        [weight, shared, e_core0, o_f0s, o_f0t, o_gs, o_w, off],
        [offs, parts, parts],
    )

    def exchanged(value, distance):
        return lax.ppermute(value, "pole", [(p, p ^ distance) for p in range(poles)])

    def summed(parts):
        kept = parts[0] + exchanged(parts[1], 1)
        distance = 2
        while distance < poles:
            kept = kept + exchanged(kept, distance)
            distance *= 2
        return kept, exchanged(kept, 1)

    full = jax.ShapeDtypeStruct((2, width, width), F32)
    off_sums = summed(off)
    (diag,) = run(more_diag_kernel, [], [us, ts, o_f0t, o_gt, o_w, diag], [diags])
    diag_sums = summed(diag)
    done = jax.ShapeDtypeStruct((8, 128), F32)
    density_off, done = run(unpack_off_kernel, [], list(off_sums), [full, done])
    (density_diag,) = run(unpack_diag_kernel, [], [*diag_sums, done], [full])
    return density_diag, density_off


def solution(mesh):
    placed = (
        P("pole", "snode", None, None, None),
        P("pole", "snode", None, None, None),
        P("snode"),
        P("pole", None),
    )
    return jax.shard_map(
        local,
        mesh=mesh,
        in_specs=placed,
        out_specs=(P("snode", None, None), P("snode", None, None)),
        check_vma=False,
    )
```

```python
import functools

import jax
import jax.numpy as jnp
from jax import lax
from jax.experimental import pallas as pl
from jax.experimental.pallas import tpu as pltpu
from jax.sharding import PartitionSpec as P

F32 = jnp.float32
BF16 = jnp.bfloat16
AXES = ("pole", "snode")
VMEM_LIMIT = 16 * 1024 * 1024


def halves(value):
    high = value.astype(BF16)
    return high, (value - high.astype(F32)).astype(BF16)


def split_pair(real, imag):
    (rh, rl), (ih, il) = halves(real), halves(imag)
    return rh, ih, rl, il


def dot(left, right):
    return jnp.dot(left, right, preferred_element_type=F32)


def dot3(lh, ll, rh, rl):
    return dot(lh, rh) + (dot(lh, rl) + dot(ll, rh))


def complex_dot(left, right):
    arh, aih, arl, ail = left
    brh, bih, brl, bil = right
    real = dot3(arh, arl, brh, brl) - dot3(aih, ail, bih, bil)
    imag = dot3(arh, arl, bih, bil) + dot3(aih, ail, brh, brl)
    return real, imag


def rows_columns(size):
    return (
        lax.broadcasted_iota(jnp.int32, (size, size), 0),
        lax.broadcasted_iota(jnp.int32, (size, size), 1),
    )


def packed(block):
    half = block.shape[0] // 2
    row, column = rows_columns(half)
    lower = block[half:, half:]
    mixed = jnp.where(row >= column, block[:half, :half], lower)
    diagonal = jnp.sum(jnp.where(row == column, lower, 0.0), axis=0, keepdims=True)
    return jnp.concatenate(
        [block[:half, half:], mixed, jnp.broadcast_to(diagonal, (8, half))], axis=0
    )


def unpacked(value):
    half = value.shape[1]
    row, column = rows_columns(half)
    right, mixed = value[:half], value[half : 2 * half]
    diagonal = value[2 * half : 2 * half + 1]
    turned = mixed.T
    first = jnp.where(row >= column, mixed, turned)
    last = jnp.where(row < column, mixed, jnp.where(row == column, diagonal, turned))
    return jnp.concatenate(
        [jnp.concatenate([first, right], axis=1), jnp.concatenate([right.T, last], axis=1)], axis=0
    )


def unpacked_split(ref):
    return split_pair(unpacked(ref[0]), unpacked(ref[1]))


def load4(ref):
    return tuple(ref[i] for i in range(4))


def store4(ref, parts):
    for i, part in enumerate(parts):
        ref[i] = part


def whereabouts():
    place = lax.axis_index("snode")
    return place, lax.rem(place, 2), lax.rem(lax.axis_index("pole"), 2)


def hosted_slot():
    place, odd, _ = whereabouts()
    return jnp.where(place < 2, 0, 1 - odd)


def slot_of(hosted):
    return hosted_slot() if hosted else 1 - hosted_slot()


def constant_kernel(hosted, fetch, live, pivot, factor, weight, *refs):
    width = pivot.shape[-1]
    slot = slot_of(hosted)
    if fetch:
        f1s, e, weighted, blocks, link, widths, weights, sems = refs
        copies = [
            pltpu.make_async_copy(live, widths, sems.at[0]),
            pltpu.make_async_copy(factor.at[slot, 1], link, sems.at[1]),
            pltpu.make_async_copy(pivot.at[slot, 0], blocks.at[0], sems.at[2]),
            pltpu.make_async_copy(pivot.at[slot, 1], blocks.at[1], sems.at[3]),
            pltpu.make_async_copy(weight, weights, sems.at[4]),
        ]
        for copy in copies:
            copy.start()
        copies[0].wait()
        copies[1].wait()
    else:
        _, f1s, e, weighted = refs
        blocks, link, widths, weights, copies = pivot.at[slot], factor.at[slot, 1], live, weight, []
    row, column = rows_columns(width)
    kept = [column < widths[k] for k in range(2)]
    both = [jnp.logical_and(row < widths[k], kept[k]) for k in range(2)]
    f1 = [jnp.where(kept[1], link[c], 0.0) for c in range(2)]
    s1, t1 = split_pair(*f1), split_pair(f1[0].T, f1[1].T)
    store4(f1s, s1)
    for copy in copies[2:]:
        copy.wait()
    d = [[jnp.where(both[k], blocks[k, c], 0.0) for c in range(2)] for k in range(2)]
    br, bi = complex_dot(split_pair(*d[0]), s1)
    tr, ti = complex_dot(t1, split_pair(br, bi))
    er, ei = d[1][0] + tr, d[1][1] + ti
    e[0], e[1] = packed(er), packed(ei)
    w0, w1 = weights[pl.ds(slot, 1), 0:1], weights[pl.ds(slot, 1), 1:2]
    weighted[0] = packed(w1 * d[0][0] + w0 * d[0][1])
    weighted[1] = packed(w1 * er + w0 * ei)
    weighted_b = flat(w1 * br + w0 * bi)
    weighted[2] = weighted_b[: width + 8]
    weighted[3, : width - 8] = weighted_b[width + 8 :]


def factor_kernel(hosted, live, factor, f1s, passed, f0s, f0t, gs, gt, g, handed):
    slot = slot_of(hosted)
    _, column = rows_columns(factor.shape[-1])
    f0 = [jnp.where(column < live[0], factor[slot, 0, c], 0.0) for c in range(2)]
    s0 = split_pair(*f0)
    gr, gi = complex_dot(s0, load4(f1s))
    g[0], g[1] = gr, gi
    store4(gs, split_pair(gr, gi))
    store4(gt, split_pair(gr.T, gi.T))
    store4(f0s, s0)
    store4(f0t, split_pair(f0[0].T, f0[1].T))
    handed[...] = passed[...]


def fold(x, gs, gt, e, out):
    tr, ti = complex_dot(x, load4(gs))
    yr, yi = complex_dot(load4(gt), split_pair(tr, ti))
    out[0] = e[0] + packed(yr)
    out[1] = e[1] + packed(yi)


def start_kernel(gs, gt, e, x_core0, x_core1, out):
    place, _, core = whereabouts()
    for x, its_core in ((x_core0, 0), (x_core1, 1)):

        @pl.when(jnp.logical_and(place == 1, core == its_core))
        def _():
            fold(unpacked_split(x), gs, gt, e, out)


def step_kernel(turn, gs, gt, e, *refs):
    *received, out = refs

    @pl.when(lax.div(whereabouts()[0], 2) == turn)
    def _():
        value = received[0][...]
        for other in received[1:]:
            value = value + other[...]
        fold(split_pair(unpacked(value[0]), unpacked(value[1])), gs, gt, e, out)


def pair_kernel(g, e, g_in, e_core0, e_core1, later_core0, later_core1, fas, fat, ea, ps, pt, ep):
    place, odd, core = whereabouts()
    is_odd, first_core, upper = odd == 1, core == 0, place > 1
    ga = [jnp.where(is_odd, g_in[c], g[c]) for c in range(2)]
    gb = [jnp.where(is_odd, g[c], g_in[c]) for c in range(2)]
    theirs = [
        jnp.where(
            upper,
            jnp.where(first_core, e_core0[c], e_core1[c]),
            jnp.where(first_core, later_core0[c], later_core1[c]),
        )
        for c in range(2)
    ]
    low = [jnp.where(is_odd, theirs[c], e[c]) for c in range(2)]
    high = [jnp.where(is_odd, e[c], theirs[c]) for c in range(2)]
    sa, sb = split_pair(*ga), split_pair(*gb)
    store4(fas, sa)
    store4(fat, split_pair(ga[0].T, ga[1].T))
    pr, pi = complex_dot(sa, sb)
    store4(ps, split_pair(pr, pi))
    store4(pt, split_pair(pr.T, pi.T))
    br, bi = complex_dot(split_pair(unpacked(low[0]), unpacked(low[1])), sb)
    tr, ti = complex_dot(split_pair(gb[0].T, gb[1].T), split_pair(br, bi))
    for c, term in enumerate((tr, ti)):
        ea[c] = low[c]
        ep[c] = high[c] + packed(term)


def share_kernel(fas, fat, ea, *refs):
    *received, own, sent, scratch = refs
    value = received[0][...]
    for other in received[1:]:
        value = value + other[...]
    value = jnp.where(whereabouts()[0] > 1, value, 0.0)
    fold(split_pair(unpacked(value[0]), unpacked(value[1])), fas, fat, ea, scratch)
    is_odd = whereabouts()[1] == 1
    own[...] = jnp.where(is_odd, scratch[...], value)
    sent[...] = jnp.where(is_odd, value, scratch[...])


def flat(block):
    half = block.shape[1] // 2
    return jnp.concatenate([block[:, :half], block[:, half:]], axis=0)


def real_dot(left, right):
    return dot3(left[0], left[2], right[0], right[2]) + dot3(left[1], left[3], right[1], right[3])


def off_values(slot, weight, xs, f0s, f0t, gs, weighted):
    width = f0s.shape[-1]
    w0, w1 = weight[pl.ds(slot, 1), 0:1], weight[pl.ds(slot, 1), 1:2]
    qr, qi = complex_dot(xs, load4(gs))
    ts = split_pair(w1 * qr + w0 * qi, w0 * qr - w1 * qi)
    second = real_dot(load4(f0t), ts)
    pr, pi = complex_dot(xs, load4(f0s))
    u = w1 * pr + w0 * pi
    us = split_pair(u, w0 * pr - w1 * pi)
    constant = jnp.concatenate([weighted[2], weighted[3, : width - 8]], axis=0)
    return -flat(u), -(flat(second) + constant), us, ts


def diag_values(us, ts, f0t, gt, weighted):
    return (
        weighted[0] + packed(real_dot(load4(f0t), us)),
        weighted[1] + packed(real_dot(load4(gt), ts)),
    )


def density_kernel(weight, x, f0s, f0t, gs, gt, weighted, off, diag):
    core = whereabouts()[2]
    first, second, us, ts = off_values(slot_of(True), weight, unpacked_split(x), f0s, f0t, gs, weighted)
    off[core], off[1 - core] = first, second
    diag[core], diag[1 - core] = diag_values(us, ts, f0t, gt, weighted)


def more_off_kernel(weight, x, x_core0, x_core1, f0s, f0t, gs, weighted, before, off, us_out, ts_out):
    core = whereabouts()[2]
    upper = whereabouts()[0] > 1
    x = [
        jnp.where(upper, x[c], jnp.where(core == 0, x_core0[c], x_core1[c])) for c in range(2)
    ]
    xs = split_pair(unpacked(x[0]), unpacked(x[1]))
    first, second, us, ts = off_values(slot_of(False), weight, xs, f0s, f0t, gs, weighted)
    off[core] = first + before[core]
    off[1 - core] = second + before[1 - core]
    store4(us_out, us)
    store4(ts_out, ts)


def more_diag_kernel(us, ts, f0t, gt, weighted, before, diag):
    core = whereabouts()[2]
    first, second = diag_values(load4(us), load4(ts), f0t, gt, weighted)
    diag[core] = first + before[core]
    diag[1 - core] = second + before[1 - core]


def unpack_off_kernel(mine, theirs, off, done):
    core = whereabouts()[2]
    width = off.shape[-1]
    half = width // 2
    for source, entry in ((mine, core), (theirs, 1 - core)):
        off[entry, :, :half] = source[:width]
        off[entry, :, half:] = source[width:]
    done[...] = jnp.zeros_like(done)


def unpack_diag_kernel(mine, theirs, _, diag):
    core = whereabouts()[2]
    for source, entry in ((mine, core), (theirs, 1 - core)):
        diag[entry] = unpacked(source[...])


SCALAR = pl.BlockSpec(memory_space=pltpu.SMEM)
WHOLE = pl.BlockSpec(memory_space=pltpu.VMEM)


COST = pl.CostEstimate(flops=1, bytes_accessed=1, transcendentals=0)


LONG = pl.CostEstimate(flops=10**11, bytes_accessed=1, transcendentals=0)


def run(kernel, scalars, arrays, shapes, scratch=(), cost=COST, far=()):
    return pl.pallas_call(
        kernel,
        out_shape=shapes,
        in_specs=[SCALAR] * len(scalars)
        + [pl.BlockSpec(memory_space=pltpu.HBM)] * len(far)
        + [WHOLE] * len(arrays),
        out_specs=[WHOLE] * len(shapes),
        scratch_shapes=list(scratch),
        compiler_params=pltpu.CompilerParams(vmem_limit_bytes=VMEM_LIMIT),
        cost_estimate=cost,
    )(*scalars, *far, *arrays)


def local(pivot, factor, live, weight):
    poles, turns = lax.axis_size("pole"), lax.axis_size("snode")
    rows = turns // 2
    width = pivot.shape[-1]
    quarter = (width + 8, width // 2)
    mirrored = jax.ShapeDtypeStruct((2,) + quarter, F32)
    parts = jax.ShapeDtypeStruct((4, width, width), BF16)

    def at(pole_index, snode_index):
        return pole_index * turns + snode_index

    def hosts(row, pole):
        return at(pole, 2 * row + 1), at(pole, 2 * row)

    swaps = [(at(p, s), at(p, s ^ 1)) for p in range(poles) for s in range(2, turns)]

    def first(core):
        return [(at(p, 0), at(p, 1)) for p in range(core, poles, 2)]

    def swaps_of(core):
        return [(at(p, s), at(p, s ^ 1)) for p in range(core, poles, 2) for s in range(2, turns)]

    every = [(at(p, s), at(p, s ^ 1)) for p in range(poles) for s in range(turns)]
    constants = [parts, mirrored, jax.ShapeDtypeStruct((4,) + quarter, F32)]
    factors = [parts, parts, parts, parts, jax.ShapeDtypeStruct((2, width, width), F32)]

    o_f1s, o_e, o_w = run(
        functools.partial(constant_kernel, False, True),
        [],
        [],
        constants,
        [
            pltpu.VMEM(pivot.shape[1:], F32),
            pltpu.VMEM(factor.shape[2:], F32),
            pltpu.SMEM(live.shape, jnp.int32),
            pltpu.VMEM(weight.shape, F32),
            pltpu.SemaphoreType.DMA((5,)),
        ],
        far=[
            pltpu.with_memory_space_constraint(a, pltpu.HBM) for a in (live, pivot, factor, weight)
        ],
    )
    e_core1 = lax.ppermute(o_e, AXES, first(1) + swaps_of(1))
    o_f0s, o_f0t, o_gs, o_gt, o_g, e_late = run(
        functools.partial(factor_kernel, False), [live], [factor, o_f1s, o_e], [*factors, mirrored]
    )
    e_core0 = lax.ppermute(e_late, AXES, first(0) + swaps_of(0))
    g_in = lax.ppermute(o_g, AXES, swaps)
    m_f1s, m_e, m_w = run(
        functools.partial(constant_kernel, True, False),
        [live],
        [pivot, factor, weight, o_g],
        constants,
    )
    later_core1 = lax.ppermute(m_e, AXES, first(1))
    m_f0s, m_f0t, m_gs, m_gt, m_g, e_late = run(
        functools.partial(factor_kernel, True), [live], [factor, m_f1s, m_e], [*factors, mirrored]
    )
    later_core0 = lax.ppermute(e_late, AXES, first(0))

    (wave_even,) = run(start_kernel, [], [o_gs, o_gt, o_e, e_core0, e_core1], [mirrored])
    wave_even = lax.ppermute(wave_even, AXES, [(at(p, 1), at(p, 0)) for p in range(poles)])
    (wave_odd,) = run(start_kernel, [], [m_gs, m_gt, m_e, later_core0, later_core1], [mirrored])
    received = []
    if rows > 1:
        received = [
            lax.ppermute(wave_odd, AXES, [(at(p, 1), at(p, 3)) for p in range(poles)]),
            lax.ppermute(wave_even, AXES, [(at(p, 0), at(p, 2)) for p in range(poles)]),
        ]
    else:
        received = [jnp.zeros(mirrored.shape, F32)]
    fas, fat, ea, ps, pt, ep = run(
        pair_kernel,
        [],
        [m_g, m_e, g_in, e_core0, e_core1, later_core0, later_core1],
        [parts, parts, mirrored, parts, parts, mirrored],
        cost=LONG,
    )
    arrived = list(received)
    for turn in range(1, rows - 1):
        (wave,) = run(
            functools.partial(step_kernel, turn), [], [ps, pt, ep] + arrived, [mirrored]
        )
        up = [pair for p in range(poles) for pair in zip(hosts(turn, p), hosts(turn + 1, p))]
        arrived = [lax.ppermute(wave, AXES, up)]
        received += arrived
    own, sent = run(
        share_kernel,
        [],
        [fas, fat, ea] + received,
        [mirrored, mirrored],
        [pltpu.VMEM(mirrored.shape, F32)],
    )
    shared = lax.ppermute(sent, AXES, every)

    offs = jax.ShapeDtypeStruct((2, 2 * width, width // 2), F32)
    diags = jax.ShapeDtypeStruct((2,) + quarter, F32)
    off, diag = run(density_kernel, [], [weight, own, m_f0s, m_f0t, m_gs, m_gt, m_w], [offs, diags])
    off, us, ts = run(
        more_off_kernel,
        [],
        [weight, shared, e_core0, e_core1, o_f0s, o_f0t, o_gs, o_w, off],
        [offs, parts, parts],
    )

    def exchanged(value, distance):
        return lax.ppermute(value, "pole", [(p, p ^ distance) for p in range(poles)])

    def summed(parts):
        kept = parts[0] + exchanged(parts[1], 1)
        distance = 2
        while distance < poles:
            kept = kept + exchanged(kept, distance)
            distance *= 2
        return kept, exchanged(kept, 1)

    full = jax.ShapeDtypeStruct((2, width, width), F32)
    off_sums = summed(off)
    (diag,) = run(more_diag_kernel, [], [us, ts, o_f0t, o_gt, o_w, diag], [diags])
    diag_sums = summed(diag)
    done = jax.ShapeDtypeStruct((8, 128), F32)
    density_off, done = run(unpack_off_kernel, [], list(off_sums), [full, done])
    (density_diag,) = run(unpack_diag_kernel, [], [*diag_sums, done], [full])
    return density_diag, density_off


def solution(mesh):
    placed = (
        P("pole", "snode", None, None, None),
        P("pole", "snode", None, None, None),
        P("snode"),
        P("pole", None),
    )
    return jax.shard_map(
        local,
        mesh=mesh,
        in_specs=placed,
        out_specs=(P("snode", None, None), P("snode", None, None)),
        check_vma=False,
    )
```

```python
import functools

import jax
import jax.numpy as jnp
from jax import lax
from jax.experimental import pallas as pl
from jax.experimental.pallas import tpu as pltpu
from jax.sharding import PartitionSpec as P

F32 = jnp.float32
BF16 = jnp.bfloat16
AXES = ("pole", "snode")
VMEM_LIMIT = 16 * 1024 * 1024


def halves(value):
    high = value.astype(BF16)
    return high, (value - high.astype(F32)).astype(BF16)


def split_pair(real, imag):
    (rh, rl), (ih, il) = halves(real), halves(imag)
    return rh, ih, rl, il


def dot(left, right):
    return jnp.dot(left, right, preferred_element_type=F32)


def dot3(lh, ll, rh, rl):
    return dot(lh, rh) + (dot(lh, rl) + dot(ll, rh))


def complex_dot(left, right):
    arh, aih, arl, ail = left
    brh, bih, brl, bil = right
    real = dot3(arh, arl, brh, brl) - dot3(aih, ail, bih, bil)
    imag = dot3(arh, arl, bih, bil) + dot3(aih, ail, brh, brl)
    return real, imag


def rows_columns(size):
    return (
        lax.broadcasted_iota(jnp.int32, (size, size), 0),
        lax.broadcasted_iota(jnp.int32, (size, size), 1),
    )


def packed(block):
    half = block.shape[0] // 2
    row, column = rows_columns(half)
    lower = block[half:, half:]
    mixed = jnp.where(row >= column, block[:half, :half], lower)
    diagonal = jnp.sum(jnp.where(row == column, lower, 0.0), axis=0, keepdims=True)
    return jnp.concatenate(
        [block[:half, half:], mixed, jnp.broadcast_to(diagonal, (8, half))], axis=0
    )


def unpacked(value):
    half = value.shape[1]
    row, column = rows_columns(half)
    right, mixed = value[:half], value[half : 2 * half]
    diagonal = value[2 * half : 2 * half + 1]
    turned = mixed.T
    first = jnp.where(row >= column, mixed, turned)
    last = jnp.where(row < column, mixed, jnp.where(row == column, diagonal, turned))
    return jnp.concatenate(
        [jnp.concatenate([first, right], axis=1), jnp.concatenate([right.T, last], axis=1)], axis=0
    )


def unpacked_split(ref):
    return split_pair(unpacked(ref[0]), unpacked(ref[1]))


def load4(ref):
    return tuple(ref[i] for i in range(4))


def store4(ref, parts):
    for i, part in enumerate(parts):
        ref[i] = part


def whereabouts():
    place = lax.axis_index("snode")
    return place, lax.rem(place, 2), lax.rem(lax.axis_index("pole"), 2)


def hosted_slot():
    place, odd, _ = whereabouts()
    return jnp.where(place < 2, 0, 1 - odd)


def slot_of(hosted):
    return hosted_slot() if hosted else 1 - hosted_slot()


def constants_of(slot, blocks, link, widths, weights, f1s, e, weighted, wait=lambda: None):
    width = blocks.shape[-1]
    row, column = rows_columns(width)
    kept = [column < widths[k] for k in range(2)]
    both = [jnp.logical_and(row < widths[k], kept[k]) for k in range(2)]
    f1 = [jnp.where(kept[1], link[c], 0.0) for c in range(2)]
    s1, t1 = split_pair(*f1), split_pair(f1[0].T, f1[1].T)
    store4(f1s, s1)
    wait()
    d = [[jnp.where(both[k], blocks[k, c], 0.0) for c in range(2)] for k in range(2)]
    br, bi = complex_dot(split_pair(*d[0]), s1)
    tr, ti = complex_dot(t1, split_pair(br, bi))
    er, ei = d[1][0] + tr, d[1][1] + ti
    e[0], e[1] = packed(er), packed(ei)
    w0, w1 = weights[pl.ds(slot, 1), 0:1], weights[pl.ds(slot, 1), 1:2]
    weighted[0] = packed(w1 * d[0][0] + w0 * d[0][1])
    weighted[1] = packed(w1 * er + w0 * ei)
    weighted_b = flat(w1 * br + w0 * bi)
    weighted[2] = weighted_b[: width + 8]
    weighted[3, : width - 8] = weighted_b[width + 8 :]


def fetched_constants(slot, live, pivot, factor, weight, outs, scratch):
    blocks, link, widths, weights, sems = scratch
    copies = [
        pltpu.make_async_copy(live, widths, sems.at[0]),
        pltpu.make_async_copy(factor.at[slot, 1], link, sems.at[1]),
        pltpu.make_async_copy(pivot.at[slot, 0], blocks.at[0], sems.at[2]),
        pltpu.make_async_copy(pivot.at[slot, 1], blocks.at[1], sems.at[3]),
        pltpu.make_async_copy(weight, weights, sems.at[4]),
    ]
    for copy in copies:
        copy.start()
    copies[0].wait()
    copies[1].wait()

    def wait():
        for copy in copies[2:]:
            copy.wait()

    constants_of(slot, blocks, link, widths, weights, *outs, wait)


def root_constant_kernel(live, pivot, factor, weight, *refs):
    @pl.when(whereabouts()[0] == 0)
    def _():
        fetched_constants(slot_of(False), live, pivot, factor, weight, refs[:3], refs[3:])


def first_constant_kernel(live, pivot, factor, weight, *refs):
    made, outs, scratch = refs[:3], refs[3:6], refs[6:]
    place = whereabouts()[0]

    @pl.when(place == 0)
    def _():
        for source, target in zip(made, outs):
            target[...] = source[...]

    @pl.when(place > 0)
    def _():
        fetched_constants(slot_of(False), live, pivot, factor, weight, outs, scratch)


def constant_kernel(live, pivot, factor, weight, _, f1s, e, weighted):
    slot = slot_of(True)
    constants_of(slot, pivot.at[slot], factor.at[slot, 1], live, weight, f1s, e, weighted)


def factor_kernel(hosted, live, factor, f1s, f0s, f0t, gs, gt, g):
    slot = slot_of(hosted)
    _, column = rows_columns(factor.shape[-1])
    f0 = [jnp.where(column < live[0], factor[slot, 0, c], 0.0) for c in range(2)]
    s0 = split_pair(*f0)
    gr, gi = complex_dot(s0, load4(f1s))
    g[0], g[1] = gr, gi
    store4(gs, split_pair(gr, gi))
    store4(gt, split_pair(gr.T, gi.T))
    store4(f0s, s0)
    store4(f0t, split_pair(f0[0].T, f0[1].T))


def fold(x, gs, gt, e, out):
    tr, ti = complex_dot(x, load4(gs))
    yr, yi = complex_dot(load4(gt), split_pair(tr, ti))
    out[0] = e[0] + packed(yr)
    out[1] = e[1] + packed(yi)


def step_kernel(active, gs, gt, e, *refs):
    *received, out = refs

    @pl.when(active(whereabouts()[0]))
    def _():
        value = received[0][...]
        for other in received[1:]:
            value = value + other[...]
        fold(split_pair(unpacked(value[0]), unpacked(value[1])), gs, gt, e, out)


def pair_kernel(g, e, g_in, e_in, e_second, fas, fat, ea, ps, pt, ep):
    upper = whereabouts()[0] > 1
    is_odd = whereabouts()[1] == 1
    ga = [jnp.where(is_odd, g_in[c], g[c]) for c in range(2)]
    gb = [jnp.where(is_odd, g[c], g_in[c]) for c in range(2)]
    theirs = [jnp.where(upper, e_in[c], e_second[c]) for c in range(2)]
    low = [jnp.where(is_odd, theirs[c], e[c]) for c in range(2)]
    high = [jnp.where(is_odd, e[c], theirs[c]) for c in range(2)]
    sa, sb = split_pair(*ga), split_pair(*gb)
    store4(fas, sa)
    store4(fat, split_pair(ga[0].T, ga[1].T))
    pr, pi = complex_dot(sa, sb)
    store4(ps, split_pair(pr, pi))
    store4(pt, split_pair(pr.T, pi.T))
    br, bi = complex_dot(split_pair(unpacked(low[0]), unpacked(low[1])), sb)
    tr, ti = complex_dot(split_pair(gb[0].T, gb[1].T), split_pair(br, bi))
    for c, term in enumerate((tr, ti)):
        ea[c] = low[c]
        ep[c] = high[c] + packed(term)


def share_kernel(fas, fat, ea, *refs):
    *received, own, sent, scratch = refs
    value = received[0][...]
    for other in received[1:]:
        value = value + other[...]
    value = jnp.where(whereabouts()[0] > 1, value, 0.0)
    fold(split_pair(unpacked(value[0]), unpacked(value[1])), fas, fat, ea, scratch)
    is_odd = whereabouts()[1] == 1
    own[...] = jnp.where(is_odd, scratch[...], value)
    sent[...] = jnp.where(is_odd, value, scratch[...])


def flat(block):
    half = block.shape[1] // 2
    return jnp.concatenate([block[:, :half], block[:, half:]], axis=0)


def real_dot(left, right):
    return dot3(left[0], left[2], right[0], right[2]) + dot3(left[1], left[3], right[1], right[3])


def off_values(slot, weight, xs, f0s, f0t, gs, weighted):
    width = f0s.shape[-1]
    w0, w1 = weight[pl.ds(slot, 1), 0:1], weight[pl.ds(slot, 1), 1:2]
    qr, qi = complex_dot(xs, load4(gs))
    ts = split_pair(w1 * qr + w0 * qi, w0 * qr - w1 * qi)
    second = real_dot(load4(f0t), ts)
    pr, pi = complex_dot(xs, load4(f0s))
    u = w1 * pr + w0 * pi
    us = split_pair(u, w0 * pr - w1 * pi)
    constant = jnp.concatenate([weighted[2], weighted[3, : width - 8]], axis=0)
    return -flat(u), -(flat(second) + constant), us, ts


def diag_values(us, ts, f0t, gt, weighted):
    return (
        weighted[0] + packed(real_dot(load4(f0t), us)),
        weighted[1] + packed(real_dot(load4(gt), ts)),
    )


def density_kernel(weight, x, f0s, f0t, gs, gt, weighted, off, diag):
    core = whereabouts()[2]
    first, second, us, ts = off_values(slot_of(True), weight, unpacked_split(x), f0s, f0t, gs, weighted)
    off[core], off[1 - core] = first, second
    diag[core], diag[1 - core] = diag_values(us, ts, f0t, gt, weighted)


def more_off_kernel(weight, x, x_first, f0s, f0t, gs, weighted, before, off, us_out, ts_out):
    core = whereabouts()[2]
    upper = whereabouts()[0] > 1
    x = [jnp.where(upper, x[c], x_first[c]) for c in range(2)]
    xs = split_pair(unpacked(x[0]), unpacked(x[1]))
    first, second, us, ts = off_values(slot_of(False), weight, xs, f0s, f0t, gs, weighted)
    off[core] = first + before[core]
    off[1 - core] = second + before[1 - core]
    store4(us_out, us)
    store4(ts_out, ts)


def more_diag_kernel(us, ts, f0t, gt, weighted, before, diag):
    core = whereabouts()[2]
    first, second = diag_values(load4(us), load4(ts), f0t, gt, weighted)
    diag[core] = first + before[core]
    diag[1 - core] = second + before[1 - core]


def unpack_off_kernel(mine, theirs, off, done):
    core = whereabouts()[2]
    width = off.shape[-1]
    half = width // 2
    for source, entry in ((mine, core), (theirs, 1 - core)):
        off[entry, :, :half] = source[:width]
        off[entry, :, half:] = source[width:]
    done[...] = jnp.zeros_like(done)


def unpack_diag_kernel(mine, theirs, _, diag):
    core = whereabouts()[2]
    for source, entry in ((mine, core), (theirs, 1 - core)):
        diag[entry] = unpacked(source[...])


SCALAR = pl.BlockSpec(memory_space=pltpu.SMEM)
WHOLE = pl.BlockSpec(memory_space=pltpu.VMEM)


COST = pl.CostEstimate(flops=1, bytes_accessed=1, transcendentals=0)


LONG = pl.CostEstimate(flops=10**11, bytes_accessed=1, transcendentals=0)


def run(kernel, scalars, arrays, shapes, scratch=(), cost=COST, far=()):
    return pl.pallas_call(
        kernel,
        out_shape=shapes,
        in_specs=[SCALAR] * len(scalars)
        + [pl.BlockSpec(memory_space=pltpu.HBM)] * len(far)
        + [WHOLE] * len(arrays),
        out_specs=[WHOLE] * len(shapes),
        scratch_shapes=list(scratch),
        compiler_params=pltpu.CompilerParams(vmem_limit_bytes=VMEM_LIMIT),
        cost_estimate=cost,
    )(*scalars, *far, *arrays)


def local(pivot, factor, live, weight):
    poles, turns = lax.axis_size("pole"), lax.axis_size("snode")
    rows = turns // 2
    width = pivot.shape[-1]
    quarter = (width + 8, width // 2)
    mirrored = jax.ShapeDtypeStruct((2,) + quarter, F32)
    parts = jax.ShapeDtypeStruct((4, width, width), BF16)

    def at(pole_index, snode_index):
        return pole_index * turns + snode_index

    def hosts(row, pole):
        return at(pole, 2 * row + 1), at(pole, 2 * row)

    swaps = [(at(p, s), at(p, s ^ 1)) for p in range(poles) for s in range(2, turns)]
    first = [(at(p, 0), at(p, 1)) for p in range(poles)]
    every = [(at(p, s), at(p, s ^ 1)) for p in range(poles) for s in range(turns)]
    constants = [parts, mirrored, jax.ShapeDtypeStruct((4,) + quarter, F32)]
    factors = [parts, parts, parts, parts, jax.ShapeDtypeStruct((2, width, width), F32)]

    scratch = [
        pltpu.VMEM(pivot.shape[1:], F32),
        pltpu.VMEM(factor.shape[2:], F32),
        pltpu.SMEM(live.shape, jnp.int32),
        pltpu.VMEM(weight.shape, F32),
        pltpu.SemaphoreType.DMA((5,)),
    ]
    far = [pltpu.with_memory_space_constraint(a, pltpu.HBM) for a in (live, pivot, factor, weight)]
    made = run(root_constant_kernel, [], [], constants, scratch, far=far)
    e_first = lax.ppermute(made[1], AXES, first)
    o_f1s, o_e, o_w = run(first_constant_kernel, [], made, constants, scratch, far=far)
    e_in = lax.ppermute(o_e, AXES, swaps)
    o_f0s, o_f0t, o_gs, o_gt, o_g = run(
        functools.partial(factor_kernel, False), [live], [factor, o_f1s], factors
    )
    g_in = lax.ppermute(o_g, AXES, swaps)
    m_f1s, m_e, m_w = run(
        constant_kernel,
        [live],
        [pivot, factor, weight, o_g],
        constants,
    )
    m_f0s, m_f0t, m_gs, m_gt, m_g = run(
        functools.partial(factor_kernel, True), [live], [factor, m_f1s], factors
    )
    e_second = lax.ppermute(m_e, AXES, first)

    starts = functools.partial(step_kernel, lambda place: place == 1)
    (wave_even,) = run(starts, [], [o_gs, o_gt, o_e, e_first], [mirrored])
    wave_even = lax.ppermute(wave_even, AXES, [(at(p, 1), at(p, 0)) for p in range(poles)])
    (wave_odd,) = run(starts, [], [m_gs, m_gt, m_e, e_second], [mirrored])
    received = []
    if rows > 1:
        received = [
            lax.ppermute(wave_odd, AXES, [(at(p, 1), at(p, 3)) for p in range(poles)]),
            lax.ppermute(wave_even, AXES, [(at(p, 0), at(p, 2)) for p in range(poles)]),
        ]
    else:
        received = [jnp.zeros(mirrored.shape, F32)]
    fas, fat, ea, ps, pt, ep = run(
        pair_kernel,
        [],
        [m_g, m_e, g_in, e_in, e_second],
        [parts, parts, mirrored, parts, parts, mirrored],
        cost=LONG,
    )
    arrived = list(received)
    for turn in range(1, rows - 1):
        active = functools.partial(step_kernel, lambda place, turn=turn: lax.div(place, 2) == turn)
        (wave,) = run(active, [], [ps, pt, ep] + arrived, [mirrored])
        up = [pair for p in range(poles) for pair in zip(hosts(turn, p), hosts(turn + 1, p))]
        arrived = [lax.ppermute(wave, AXES, up)]
        received += arrived
    own, sent = run(
        share_kernel,
        [],
        [fas, fat, ea] + received,
        [mirrored, mirrored],
        [pltpu.VMEM(mirrored.shape, F32)],
    )
    shared = lax.ppermute(sent, AXES, every)

    offs = jax.ShapeDtypeStruct((2, 2 * width, width // 2), F32)
    diags = jax.ShapeDtypeStruct((2,) + quarter, F32)
    off, diag = run(density_kernel, [], [weight, own, m_f0s, m_f0t, m_gs, m_gt, m_w], [offs, diags])
    off, us, ts = run(
        more_off_kernel,
        [],
        [weight, shared, e_first, o_f0s, o_f0t, o_gs, o_w, off],
        [offs, parts, parts],
    )

    def exchanged(value, distance):
        return lax.ppermute(value, "pole", [(p, p ^ distance) for p in range(poles)])

    def summed(parts):
        kept = parts[0] + exchanged(parts[1], 1)
        distance = 2
        while distance < poles:
            kept = kept + exchanged(kept, distance)
            distance *= 2
        return kept, exchanged(kept, 1)

    full = jax.ShapeDtypeStruct((2, width, width), F32)
    off_sums = summed(off)
    (diag,) = run(more_diag_kernel, [], [us, ts, o_f0t, o_gt, o_w, diag], [diags])
    diag_sums = summed(diag)
    done = jax.ShapeDtypeStruct((8, 128), F32)
    density_off, done = run(unpack_off_kernel, [], list(off_sums), [full, done])
    (density_diag,) = run(unpack_diag_kernel, [], [*diag_sums, done], [full])
    return density_diag, density_off


def solution(mesh):
    placed = (
        P("pole", "snode", None, None, None),
        P("pole", "snode", None, None, None),
        P("snode"),
        P("pole", None),
    )
    return jax.shard_map(
        local,
        mesh=mesh,
        in_specs=placed,
        out_specs=(P("snode", None, None), P("snode", None, None)),
        check_vma=False,
    )
```

```python
import functools

import jax
import jax.numpy as jnp
from jax import lax
from jax.experimental import pallas as pl
from jax.experimental.pallas import tpu as pltpu
from jax.sharding import PartitionSpec as P

F32 = jnp.float32
BF16 = jnp.bfloat16
AXES = ("pole", "snode")
VMEM_LIMIT = 16 * 1024 * 1024


def halves(value):
    high = value.astype(BF16)
    return high, (value - high.astype(F32)).astype(BF16)


def split_pair(real, imag):
    (rh, rl), (ih, il) = halves(real), halves(imag)
    return rh, ih, rl, il


def dot(left, right):
    return jnp.dot(left, right, preferred_element_type=F32)


def dot3(lh, ll, rh, rl):
    return dot(lh, rh) + (dot(lh, rl) + dot(ll, rh))


def complex_dot(left, right):
    arh, aih, arl, ail = left
    brh, bih, brl, bil = right
    real = dot3(arh, arl, brh, brl) - dot3(aih, ail, bih, bil)
    imag = dot3(arh, arl, bih, bil) + dot3(aih, ail, brh, brl)
    return real, imag


def rows_columns(size):
    return (
        lax.broadcasted_iota(jnp.int32, (size, size), 0),
        lax.broadcasted_iota(jnp.int32, (size, size), 1),
    )


def packed(block):
    half = block.shape[0] // 2
    row, column = rows_columns(half)
    lower = block[half:, half:]
    mixed = jnp.where(row >= column, block[:half, :half], lower)
    diagonal = jnp.sum(jnp.where(row == column, lower, 0.0), axis=0, keepdims=True)
    return jnp.concatenate(
        [block[:half, half:], mixed, jnp.broadcast_to(diagonal, (8, half))], axis=0
    )


def unpacked(value):
    half = value.shape[1]
    row, column = rows_columns(half)
    right, mixed = value[:half], value[half : 2 * half]
    diagonal = value[2 * half : 2 * half + 1]
    turned = mixed.T
    first = jnp.where(row >= column, mixed, turned)
    last = jnp.where(row < column, mixed, jnp.where(row == column, diagonal, turned))
    return jnp.concatenate(
        [jnp.concatenate([first, right], axis=1), jnp.concatenate([right.T, last], axis=1)], axis=0
    )


def unpacked_split(ref):
    return split_pair(unpacked(ref[0]), unpacked(ref[1]))


def load4(ref):
    return tuple(ref[i] for i in range(4))


def store4(ref, parts):
    for i, part in enumerate(parts):
        ref[i] = part


def whereabouts():
    place = lax.axis_index("snode")
    return place, lax.rem(place, 2), lax.rem(lax.axis_index("pole"), 2)


def hosted_slot():
    place, odd, _ = whereabouts()
    return jnp.where(place < 2, 0, 1 - odd)


def slot_of(hosted):
    return hosted_slot() if hosted else 1 - hosted_slot()


def constants_of(slot, blocks, link, widths, weights, f1s, e, weighted, wait=lambda: None):
    width = blocks.shape[-1]
    row, column = rows_columns(width)
    kept = [column < widths[k] for k in range(2)]
    both = [jnp.logical_and(row < widths[k], kept[k]) for k in range(2)]
    f1 = [jnp.where(kept[1], link[c], 0.0) for c in range(2)]
    s1, t1 = split_pair(*f1), split_pair(f1[0].T, f1[1].T)
    store4(f1s, s1)
    wait()
    d = [[jnp.where(both[k], blocks[k, c], 0.0) for c in range(2)] for k in range(2)]
    br, bi = complex_dot(split_pair(*d[0]), s1)
    tr, ti = complex_dot(t1, split_pair(br, bi))
    er, ei = d[1][0] + tr, d[1][1] + ti
    e[0], e[1] = packed(er), packed(ei)
    w0, w1 = weights[pl.ds(slot, 1), 0:1], weights[pl.ds(slot, 1), 1:2]
    weighted[0] = packed(w1 * d[0][0] + w0 * d[0][1])
    weighted[1] = packed(w1 * er + w0 * ei)
    weighted_b = flat(w1 * br + w0 * bi)
    weighted[2] = weighted_b[: width + 8]
    weighted[3, : width - 8] = weighted_b[width + 8 :]


def fetched_constants(slot, live, pivot, factor, weight, outs, scratch):
    blocks, link, widths, weights, sems = scratch
    copies = [
        pltpu.make_async_copy(live, widths, sems.at[0]),
        pltpu.make_async_copy(factor.at[slot, 1], link, sems.at[1]),
        pltpu.make_async_copy(pivot.at[slot, 0], blocks.at[0], sems.at[2]),
        pltpu.make_async_copy(pivot.at[slot, 1], blocks.at[1], sems.at[3]),
        pltpu.make_async_copy(weight, weights, sems.at[4]),
    ]
    for copy in copies:
        copy.start()
    copies[0].wait()
    copies[1].wait()

    def wait():
        for copy in copies[2:]:
            copy.wait()

    constants_of(slot, blocks, link, widths, weights, *outs, wait)


def root_constant_kernel(live, pivot, factor, weight, *refs):
    @pl.when(whereabouts()[0] == 0)
    def _():
        fetched_constants(slot_of(False), live, pivot, factor, weight, refs[:3], refs[3:])


def first_constant_kernel(live, pivot, factor, weight, *refs):
    made, outs, scratch = refs[:3], refs[3:6], refs[6:]
    place = whereabouts()[0]

    @pl.when(place == 0)
    def _():
        for source, target in zip(made, outs):
            target[...] = source[...]

    @pl.when(place > 0)
    def _():
        fetched_constants(slot_of(False), live, pivot, factor, weight, outs, scratch)


def constant_kernel(live, pivot, factor, weight, _, f1s, e, weighted):
    slot = slot_of(True)
    constants_of(slot, pivot.at[slot], factor.at[slot, 1], live, weight, f1s, e, weighted)


def factor_kernel(hosted, live, factor, f1s, f0s, f0t, gs, gt, g):
    slot = slot_of(hosted)
    _, column = rows_columns(factor.shape[-1])
    f0 = [jnp.where(column < live[0], factor[slot, 0, c], 0.0) for c in range(2)]
    s0 = split_pair(*f0)
    gr, gi = complex_dot(s0, load4(f1s))
    g[0], g[1] = gr, gi
    store4(gs, split_pair(gr, gi))
    store4(gt, split_pair(gr.T, gi.T))
    store4(f0s, s0)
    store4(f0t, split_pair(f0[0].T, f0[1].T))


def fold(x, gs, gt, e, out):
    tr, ti = complex_dot(x, load4(gs))
    yr, yi = complex_dot(load4(gt), split_pair(tr, ti))
    out[0] = e[0] + packed(yr)
    out[1] = e[1] + packed(yi)


def step_kernel(active, gs, gt, e, *refs):
    *received, out = refs

    @pl.when(active(whereabouts()[0]))
    def _():
        value = received[0][...]
        for other in received[1:]:
            value = value + other[...]
        fold(split_pair(unpacked(value[0]), unpacked(value[1])), gs, gt, e, out)


def pair_kernel(g, e, g_in, e_in, e_second, fas, fat, ea, ps, pt, ep):
    upper = whereabouts()[0] > 1
    is_odd = whereabouts()[1] == 1
    ga = [jnp.where(is_odd, g_in[c], g[c]) for c in range(2)]
    gb = [jnp.where(is_odd, g[c], g_in[c]) for c in range(2)]
    theirs = [jnp.where(upper, e_in[c], e_second[c]) for c in range(2)]
    low = [jnp.where(is_odd, theirs[c], e[c]) for c in range(2)]
    high = [jnp.where(is_odd, e[c], theirs[c]) for c in range(2)]
    sa, sb = split_pair(*ga), split_pair(*gb)
    store4(fas, sa)
    store4(fat, split_pair(ga[0].T, ga[1].T))
    pr, pi = complex_dot(sa, sb)
    store4(ps, split_pair(pr, pi))
    store4(pt, split_pair(pr.T, pi.T))
    br, bi = complex_dot(split_pair(unpacked(low[0]), unpacked(low[1])), sb)
    tr, ti = complex_dot(split_pair(gb[0].T, gb[1].T), split_pair(br, bi))
    for c, term in enumerate((tr, ti)):
        ea[c] = low[c]
        ep[c] = high[c] + packed(term)


def share_kernel(fas, fat, ea, *refs):
    *received, own, sent, scratch = refs
    value = received[0][...]
    for other in received[1:]:
        value = value + other[...]
    value = jnp.where(whereabouts()[0] > 1, value, 0.0)
    fold(split_pair(unpacked(value[0]), unpacked(value[1])), fas, fat, ea, scratch)
    is_odd = whereabouts()[1] == 1
    own[...] = jnp.where(is_odd, scratch[...], value)
    sent[...] = jnp.where(is_odd, value, scratch[...])


def flat(block):
    half = block.shape[1] // 2
    return jnp.concatenate([block[:, :half], block[:, half:]], axis=0)


def real_dot(left, right):
    return dot3(left[0], left[2], right[0], right[2]) + dot3(left[1], left[3], right[1], right[3])


def off_values(slot, weight, xs, f0s, f0t, gs, weighted):
    width = f0s.shape[-1]
    w0, w1 = weight[pl.ds(slot, 1), 0:1], weight[pl.ds(slot, 1), 1:2]
    qr, qi = complex_dot(xs, load4(gs))
    ts = split_pair(w1 * qr + w0 * qi, w0 * qr - w1 * qi)
    second = real_dot(load4(f0t), ts)
    pr, pi = complex_dot(xs, load4(f0s))
    u = w1 * pr + w0 * pi
    us = split_pair(u, w0 * pr - w1 * pi)
    constant = jnp.concatenate([weighted[2], weighted[3, : width - 8]], axis=0)
    return -flat(u), -(flat(second) + constant), us, ts


def diag_values(us, ts, f0t, gt, weighted):
    return (
        weighted[0] + packed(real_dot(load4(f0t), us)),
        weighted[1] + packed(real_dot(load4(gt), ts)),
    )


def density_kernel(weight, x, f0s, f0t, gs, gt, weighted, off, diag):
    core = whereabouts()[2]
    first, second, us, ts = off_values(slot_of(True), weight, unpacked_split(x), f0s, f0t, gs, weighted)
    off[core], off[1 - core] = first, second
    diag[core], diag[1 - core] = diag_values(us, ts, f0t, gt, weighted)


def more_off_kernel(weight, x, x_first, f0s, f0t, gs, weighted, before, off, us_out, ts_out):
    core = whereabouts()[2]
    upper = whereabouts()[0] > 1
    x = [jnp.where(upper, x[c], x_first[c]) for c in range(2)]
    xs = split_pair(unpacked(x[0]), unpacked(x[1]))
    first, second, us, ts = off_values(slot_of(False), weight, xs, f0s, f0t, gs, weighted)
    off[core] = first + before[core]
    off[1 - core] = second + before[1 - core]
    store4(us_out, us)
    store4(ts_out, ts)


def more_diag_kernel(us, ts, f0t, gt, weighted, before, diag):
    core = whereabouts()[2]
    first, second = diag_values(load4(us), load4(ts), f0t, gt, weighted)
    diag[core] = first + before[core]
    diag[1 - core] = second + before[1 - core]


def unpack_off_kernel(mine, theirs, off, done):
    core = whereabouts()[2]
    width = off.shape[-1]
    half = width // 2
    for source, entry in ((mine, core), (theirs, 1 - core)):
        off[entry, :, :half] = source[:width]
        off[entry, :, half:] = source[width:]
    done[...] = jnp.zeros_like(done)


def unpack_diag_kernel(mine, theirs, _, diag):
    core = whereabouts()[2]
    for source, entry in ((mine, core), (theirs, 1 - core)):
        diag[entry] = unpacked(source[...])


SCALAR = pl.BlockSpec(memory_space=pltpu.SMEM)
WHOLE = pl.BlockSpec(memory_space=pltpu.VMEM)


COST = pl.CostEstimate(flops=1, bytes_accessed=1, transcendentals=0)


LONG = pl.CostEstimate(flops=10**11, bytes_accessed=1, transcendentals=0)


def run(kernel, scalars, arrays, shapes, scratch=(), cost=COST, far=()):
    return pl.pallas_call(
        kernel,
        out_shape=shapes,
        in_specs=[SCALAR] * len(scalars)
        + [pl.BlockSpec(memory_space=pltpu.HBM)] * len(far)
        + [WHOLE] * len(arrays),
        out_specs=[WHOLE] * len(shapes),
        scratch_shapes=list(scratch),
        compiler_params=pltpu.CompilerParams(vmem_limit_bytes=VMEM_LIMIT),
        cost_estimate=cost,
    )(*scalars, *far, *arrays)


def local(pivot, factor, live, weight):
    poles, turns = lax.axis_size("pole"), lax.axis_size("snode")
    rows = turns // 2
    width = pivot.shape[-1]
    quarter = (width + 8, width // 2)
    mirrored = jax.ShapeDtypeStruct((2,) + quarter, F32)
    parts = jax.ShapeDtypeStruct((4, width, width), BF16)

    def at(pole_index, snode_index):
        return pole_index * turns + snode_index

    def hosts(row, pole):
        return at(pole, 2 * row + 1), at(pole, 2 * row)

    swaps = [(at(p, s), at(p, s ^ 1)) for p in range(poles) for s in range(2, turns)]
    first = [(at(p, 0), at(p, 1)) for p in range(poles)]
    every = [(at(p, s), at(p, s ^ 1)) for p in range(poles) for s in range(turns)]
    constants = [parts, mirrored, jax.ShapeDtypeStruct((4,) + quarter, F32)]
    factors = [parts, parts, parts, parts, jax.ShapeDtypeStruct((2, width, width), F32)]

    scratch = [
        pltpu.VMEM(pivot.shape[1:], F32),
        pltpu.VMEM(factor.shape[2:], F32),
        pltpu.SMEM(live.shape, jnp.int32),
        pltpu.VMEM(weight.shape, F32),
        pltpu.SemaphoreType.DMA((5,)),
    ]
    far = [pltpu.with_memory_space_constraint(a, pltpu.HBM) for a in (live, pivot, factor, weight)]
    made = run(root_constant_kernel, [], [], constants, scratch, far=far)
    e_first = lax.ppermute(made[1], AXES, first)
    o_f1s, o_e, o_w = run(first_constant_kernel, [], made, constants, scratch, far=far)
    e_in = lax.ppermute(o_e, AXES, swaps)
    o_f0s, o_f0t, o_gs, o_gt, o_g = run(
        functools.partial(factor_kernel, False), [live], [factor, o_f1s], factors
    )
    g_in = lax.ppermute(o_g, AXES, swaps)
    m_f1s, m_e, m_w = run(
        constant_kernel,
        [live],
        [pivot, factor, weight, o_g],
        constants,
    )
    m_f0s, m_f0t, m_gs, m_gt, m_g = run(
        functools.partial(factor_kernel, True), [live], [factor, m_f1s], factors
    )
    e_second = lax.ppermute(m_e, AXES, first)

    starts = functools.partial(step_kernel, lambda place: place == 1)
    (wave_even,) = run(starts, [], [o_gs, o_gt, o_e, e_first, e_in], [mirrored])
    wave_even = lax.ppermute(wave_even, AXES, [(at(p, 1), at(p, 0)) for p in range(poles)])
    (wave_odd,) = run(starts, [], [m_gs, m_gt, m_e, e_second], [mirrored])
    received = []
    if rows > 1:
        received = [
            lax.ppermute(wave_odd, AXES, [(at(p, 1), at(p, 3)) for p in range(poles)]),
            lax.ppermute(wave_even, AXES, [(at(p, 0), at(p, 2)) for p in range(poles)]),
        ]
    else:
        received = [jnp.zeros(mirrored.shape, F32)]
    fas, fat, ea, ps, pt, ep = run(
        pair_kernel,
        [],
        [m_g, m_e, g_in, e_in, e_second],
        [parts, parts, mirrored, parts, parts, mirrored],
        cost=LONG,
    )
    arrived = list(received)
    for turn in range(1, rows - 1):
        active = functools.partial(step_kernel, lambda place, turn=turn: lax.div(place, 2) == turn)
        (wave,) = run(active, [], [ps, pt, ep] + arrived, [mirrored])
        up = [pair for p in range(poles) for pair in zip(hosts(turn, p), hosts(turn + 1, p))]
        arrived = [lax.ppermute(wave, AXES, up)]
        received += arrived
    own, sent = run(
        share_kernel,
        [],
        [fas, fat, ea] + received,
        [mirrored, mirrored],
        [pltpu.VMEM(mirrored.shape, F32)],
    )
    shared = lax.ppermute(sent, AXES, every)

    offs = jax.ShapeDtypeStruct((2, 2 * width, width // 2), F32)
    diags = jax.ShapeDtypeStruct((2,) + quarter, F32)
    off, diag = run(density_kernel, [], [weight, own, m_f0s, m_f0t, m_gs, m_gt, m_w], [offs, diags])
    off, us, ts = run(
        more_off_kernel,
        [],
        [weight, shared, e_first, o_f0s, o_f0t, o_gs, o_w, off],
        [offs, parts, parts],
    )

    def exchanged(value, distance):
        return lax.ppermute(value, "pole", [(p, p ^ distance) for p in range(poles)])

    def summed(parts):
        kept = parts[0] + exchanged(parts[1], 1)
        distance = 2
        while distance < poles:
            kept = kept + exchanged(kept, distance)
            distance *= 2
        return kept, exchanged(kept, 1)

    full = jax.ShapeDtypeStruct((2, width, width), F32)
    off_sums = summed(off)
    (diag,) = run(more_diag_kernel, [], [us, ts, o_f0t, o_gt, o_w, diag], [diags])
    diag_sums = summed(diag)
    done = jax.ShapeDtypeStruct((8, 128), F32)
    density_off, done = run(unpack_off_kernel, [], list(off_sums), [full, done])
    (density_diag,) = run(unpack_diag_kernel, [], [*diag_sums, done], [full])
    return density_diag, density_off


def solution(mesh):
    placed = (
        P("pole", "snode", None, None, None),
        P("pole", "snode", None, None, None),
        P("snode"),
        P("pole", None),
    )
    return jax.shard_map(
        local,
        mesh=mesh,
        in_specs=placed,
        out_specs=(P("snode", None, None), P("snode", None, None)),
        check_vma=False,
    )
```

```python
import functools

import jax
import jax.numpy as jnp
from jax import lax
from jax.experimental import pallas as pl
from jax.experimental.pallas import tpu as pltpu
from jax.sharding import PartitionSpec as P

F32 = jnp.float32
BF16 = jnp.bfloat16
AXES = ("pole", "snode")
VMEM_LIMIT = 16 * 1024 * 1024


def halves(value):
    high = value.astype(BF16)
    return high, (value - high.astype(F32)).astype(BF16)


def split_pair(real, imag):
    (rh, rl), (ih, il) = halves(real), halves(imag)
    return rh, ih, rl, il


def dot(left, right):
    return jnp.dot(left, right, preferred_element_type=F32)


def dot3(lh, ll, rh, rl):
    return dot(lh, rh) + (dot(lh, rl) + dot(ll, rh))


def complex_dot(left, right):
    arh, aih, arl, ail = left
    brh, bih, brl, bil = right
    real = dot3(arh, arl, brh, brl) - dot3(aih, ail, bih, bil)
    imag = dot3(arh, arl, bih, bil) + dot3(aih, ail, brh, brl)
    return real, imag


def rows_columns(size):
    return (
        lax.broadcasted_iota(jnp.int32, (size, size), 0),
        lax.broadcasted_iota(jnp.int32, (size, size), 1),
    )


def packed(block):
    half = block.shape[0] // 2
    row, column = rows_columns(half)
    lower = block[half:, half:]
    mixed = jnp.where(row >= column, block[:half, :half], lower)
    diagonal = jnp.sum(jnp.where(row == column, lower, 0.0), axis=0, keepdims=True)
    return jnp.concatenate(
        [block[:half, half:], mixed, jnp.broadcast_to(diagonal, (8, half))], axis=0
    )


def unpacked(value):
    half = value.shape[1]
    row, column = rows_columns(half)
    right, mixed = value[:half], value[half : 2 * half]
    diagonal = value[2 * half : 2 * half + 1]
    turned = mixed.T
    first = jnp.where(row >= column, mixed, turned)
    last = jnp.where(row < column, mixed, jnp.where(row == column, diagonal, turned))
    return jnp.concatenate(
        [jnp.concatenate([first, right], axis=1), jnp.concatenate([right.T, last], axis=1)], axis=0
    )


def unpacked_split(ref):
    return split_pair(unpacked(ref[0]), unpacked(ref[1]))


def load4(ref):
    return tuple(ref[i] for i in range(4))


def store4(ref, parts):
    for i, part in enumerate(parts):
        ref[i] = part


def whereabouts():
    place = lax.axis_index("snode")
    return place, lax.rem(place, 2), lax.rem(lax.axis_index("pole"), 2)


def hosted_slot():
    place, odd, _ = whereabouts()
    return jnp.where(place < 2, 0, 1 - odd)


def slot_of(hosted):
    return hosted_slot() if hosted else 1 - hosted_slot()


def constants_of(slot, blocks, link, widths, weights, f1s, e, weighted, wait=lambda: None):
    width = blocks.shape[-1]
    row, column = rows_columns(width)
    kept = [column < widths[k] for k in range(2)]
    both = [jnp.logical_and(row < widths[k], kept[k]) for k in range(2)]
    f1 = [jnp.where(kept[1], link[c], 0.0) for c in range(2)]
    s1, t1 = split_pair(*f1), split_pair(f1[0].T, f1[1].T)
    store4(f1s, s1)
    wait()
    d = [[jnp.where(both[k], blocks[k, c], 0.0) for c in range(2)] for k in range(2)]
    br, bi = complex_dot(split_pair(*d[0]), s1)
    tr, ti = complex_dot(t1, split_pair(br, bi))
    er, ei = d[1][0] + tr, d[1][1] + ti
    e[0], e[1] = packed(er), packed(ei)
    w0, w1 = weights[pl.ds(slot, 1), 0:1], weights[pl.ds(slot, 1), 1:2]
    weighted[0] = packed(w1 * d[0][0] + w0 * d[0][1])
    weighted[1] = packed(w1 * er + w0 * ei)
    weighted_b = flat(w1 * br + w0 * bi)
    weighted[2] = weighted_b[: width + 8]
    weighted[3, : width - 8] = weighted_b[width + 8 :]


def fetched_constants(slot, live, pivot, factor, weight, outs, scratch):
    blocks, link, widths, weights, sems = scratch
    copies = [
        pltpu.make_async_copy(live, widths, sems.at[0]),
        pltpu.make_async_copy(factor.at[slot, 1], link, sems.at[1]),
        pltpu.make_async_copy(pivot.at[slot, 0], blocks.at[0], sems.at[2]),
        pltpu.make_async_copy(pivot.at[slot, 1], blocks.at[1], sems.at[3]),
        pltpu.make_async_copy(weight, weights, sems.at[4]),
    ]
    for copy in copies:
        copy.start()
    copies[0].wait()
    copies[1].wait()

    def wait():
        for copy in copies[2:]:
            copy.wait()

    constants_of(slot, blocks, link, widths, weights, *outs, wait)


def sent_constant_kernel(live, pivot, factor, weight, *refs):
    @pl.when(whereabouts()[0] != 1)
    def _():
        fetched_constants(slot_of(False), live, pivot, factor, weight, refs[:3], refs[3:])


def first_constant_kernel(live, pivot, factor, weight, *refs):
    made, outs, scratch = refs[:3], refs[3:6], refs[6:]
    place = whereabouts()[0]

    @pl.when(place != 1)
    def _():
        for source, target in zip(made, outs):
            target[...] = source[...]

    @pl.when(place == 1)
    def _():
        fetched_constants(slot_of(False), live, pivot, factor, weight, outs, scratch)


def constant_kernel(live, pivot, factor, weight, _, f1s, e, weighted):
    slot = slot_of(True)
    constants_of(slot, pivot.at[slot], factor.at[slot, 1], live, weight, f1s, e, weighted)


def factor_kernel(hosted, live, factor, f1s, f0s, f0t, gs, gt, g):
    slot = slot_of(hosted)
    _, column = rows_columns(factor.shape[-1])
    f0 = [jnp.where(column < live[0], factor[slot, 0, c], 0.0) for c in range(2)]
    s0 = split_pair(*f0)
    gr, gi = complex_dot(s0, load4(f1s))
    g[0], g[1] = gr, gi
    store4(gs, split_pair(gr, gi))
    store4(gt, split_pair(gr.T, gi.T))
    store4(f0s, s0)
    store4(f0t, split_pair(f0[0].T, f0[1].T))


def fold(x, gs, gt, e, out):
    tr, ti = complex_dot(x, load4(gs))
    yr, yi = complex_dot(load4(gt), split_pair(tr, ti))
    out[0] = e[0] + packed(yr)
    out[1] = e[1] + packed(yi)


def step_kernel(active, gs, gt, e, *refs):
    *received, out = refs

    @pl.when(active(whereabouts()[0]))
    def _():
        value = received[0][...]
        for other in received[1:]:
            value = value + other[...]
        fold(split_pair(unpacked(value[0]), unpacked(value[1])), gs, gt, e, out)


def pair_kernel(g, e, g_in, e_in, e_second, fas, fat, ea, ps, pt, ep):
    upper = whereabouts()[0] > 1
    is_odd = whereabouts()[1] == 1
    ga = [jnp.where(is_odd, g_in[c], g[c]) for c in range(2)]
    gb = [jnp.where(is_odd, g[c], g_in[c]) for c in range(2)]
    theirs = [jnp.where(upper, e_in[c], e_second[c]) for c in range(2)]
    low = [jnp.where(is_odd, theirs[c], e[c]) for c in range(2)]
    high = [jnp.where(is_odd, e[c], theirs[c]) for c in range(2)]
    sa, sb = split_pair(*ga), split_pair(*gb)
    store4(fas, sa)
    store4(fat, split_pair(ga[0].T, ga[1].T))
    pr, pi = complex_dot(sa, sb)
    store4(ps, split_pair(pr, pi))
    store4(pt, split_pair(pr.T, pi.T))
    br, bi = complex_dot(split_pair(unpacked(low[0]), unpacked(low[1])), sb)
    tr, ti = complex_dot(split_pair(gb[0].T, gb[1].T), split_pair(br, bi))
    for c, term in enumerate((tr, ti)):
        ea[c] = low[c]
        ep[c] = high[c] + packed(term)


def share_kernel(fas, fat, ea, *refs):
    *received, own, sent, scratch = refs
    value = received[0][...]
    for other in received[1:]:
        value = value + other[...]
    value = jnp.where(whereabouts()[0] > 1, value, 0.0)
    fold(split_pair(unpacked(value[0]), unpacked(value[1])), fas, fat, ea, scratch)
    is_odd = whereabouts()[1] == 1
    own[...] = jnp.where(is_odd, scratch[...], value)
    sent[...] = jnp.where(is_odd, value, scratch[...])


def flat(block):
    half = block.shape[1] // 2
    return jnp.concatenate([block[:, :half], block[:, half:]], axis=0)


def real_dot(left, right):
    return dot3(left[0], left[2], right[0], right[2]) + dot3(left[1], left[3], right[1], right[3])


def off_values(slot, weight, xs, f0s, f0t, gs, weighted):
    width = f0s.shape[-1]
    w0, w1 = weight[pl.ds(slot, 1), 0:1], weight[pl.ds(slot, 1), 1:2]
    qr, qi = complex_dot(xs, load4(gs))
    ts = split_pair(w1 * qr + w0 * qi, w0 * qr - w1 * qi)
    second = real_dot(load4(f0t), ts)
    pr, pi = complex_dot(xs, load4(f0s))
    u = w1 * pr + w0 * pi
    us = split_pair(u, w0 * pr - w1 * pi)
    constant = jnp.concatenate([weighted[2], weighted[3, : width - 8]], axis=0)
    return -flat(u), -(flat(second) + constant), us, ts


def diag_values(us, ts, f0t, gt, weighted):
    return (
        weighted[0] + packed(real_dot(load4(f0t), us)),
        weighted[1] + packed(real_dot(load4(gt), ts)),
    )


def density_kernel(weight, x, f0s, f0t, gs, gt, weighted, off, diag):
    core = whereabouts()[2]
    first, second, us, ts = off_values(slot_of(True), weight, unpacked_split(x), f0s, f0t, gs, weighted)
    off[core], off[1 - core] = first, second
    diag[core], diag[1 - core] = diag_values(us, ts, f0t, gt, weighted)


def more_off_kernel(weight, x, x_first, f0s, f0t, gs, weighted, before, off, us_out, ts_out):
    core = whereabouts()[2]
    upper = whereabouts()[0] > 1
    x = [jnp.where(upper, x[c], x_first[c]) for c in range(2)]
    xs = split_pair(unpacked(x[0]), unpacked(x[1]))
    first, second, us, ts = off_values(slot_of(False), weight, xs, f0s, f0t, gs, weighted)
    off[core] = first + before[core]
    off[1 - core] = second + before[1 - core]
    store4(us_out, us)
    store4(ts_out, ts)


def more_diag_kernel(us, ts, f0t, gt, weighted, before, diag):
    core = whereabouts()[2]
    first, second = diag_values(load4(us), load4(ts), f0t, gt, weighted)
    diag[core] = first + before[core]
    diag[1 - core] = second + before[1 - core]


def unpack_off_kernel(mine, theirs, off, done):
    core = whereabouts()[2]
    width = off.shape[-1]
    half = width // 2
    for source, entry in ((mine, core), (theirs, 1 - core)):
        off[entry, :, :half] = source[:width]
        off[entry, :, half:] = source[width:]
    done[...] = jnp.zeros_like(done)


def unpack_diag_kernel(mine, theirs, _, diag):
    core = whereabouts()[2]
    for source, entry in ((mine, core), (theirs, 1 - core)):
        diag[entry] = unpacked(source[...])


SCALAR = pl.BlockSpec(memory_space=pltpu.SMEM)
WHOLE = pl.BlockSpec(memory_space=pltpu.VMEM)


COST = pl.CostEstimate(flops=1, bytes_accessed=1, transcendentals=0)


LONG = pl.CostEstimate(flops=10**11, bytes_accessed=1, transcendentals=0)


def run(kernel, scalars, arrays, shapes, scratch=(), cost=COST, far=()):
    return pl.pallas_call(
        kernel,
        out_shape=shapes,
        in_specs=[SCALAR] * len(scalars)
        + [pl.BlockSpec(memory_space=pltpu.HBM)] * len(far)
        + [WHOLE] * len(arrays),
        out_specs=[WHOLE] * len(shapes),
        scratch_shapes=list(scratch),
        compiler_params=pltpu.CompilerParams(vmem_limit_bytes=VMEM_LIMIT),
        cost_estimate=cost,
    )(*scalars, *far, *arrays)


def local(pivot, factor, live, weight):
    poles, turns = lax.axis_size("pole"), lax.axis_size("snode")
    rows = turns // 2
    width = pivot.shape[-1]
    quarter = (width + 8, width // 2)
    mirrored = jax.ShapeDtypeStruct((2,) + quarter, F32)
    parts = jax.ShapeDtypeStruct((4, width, width), BF16)

    def at(pole_index, snode_index):
        return pole_index * turns + snode_index

    def hosts(row, pole):
        return at(pole, 2 * row + 1), at(pole, 2 * row)

    swaps = [(at(p, s), at(p, s ^ 1)) for p in range(poles) for s in range(2, turns)]
    first = [(at(p, 0), at(p, 1)) for p in range(poles)]
    every = [(at(p, s), at(p, s ^ 1)) for p in range(poles) for s in range(turns)]
    constants = [parts, mirrored, jax.ShapeDtypeStruct((4,) + quarter, F32)]
    factors = [parts, parts, parts, parts, jax.ShapeDtypeStruct((2, width, width), F32)]

    scratch = [
        pltpu.VMEM(pivot.shape[1:], F32),
        pltpu.VMEM(factor.shape[2:], F32),
        pltpu.SMEM(live.shape, jnp.int32),
        pltpu.VMEM(weight.shape, F32),
        pltpu.SemaphoreType.DMA((5,)),
    ]
    far = [pltpu.with_memory_space_constraint(a, pltpu.HBM) for a in (live, pivot, factor, weight)]
    made = run(sent_constant_kernel, [], [], constants, scratch, far=far)
    e_in = lax.ppermute(made[1], AXES, first + swaps)
    o_f1s, o_e, o_w = run(first_constant_kernel, [], made, constants, scratch, far=far)
    o_f0s, o_f0t, o_gs, o_gt, o_g = run(
        functools.partial(factor_kernel, False), [live], [factor, o_f1s], factors
    )
    g_in = lax.ppermute(o_g, AXES, swaps)
    m_f1s, m_e, m_w = run(
        constant_kernel,
        [live],
        [pivot, factor, weight, o_g],
        constants,
    )
    m_f0s, m_f0t, m_gs, m_gt, m_g = run(
        functools.partial(factor_kernel, True), [live], [factor, m_f1s], factors
    )
    e_second = lax.ppermute(m_e, AXES, first)

    starts = functools.partial(step_kernel, lambda place: place == 1)
    (wave_even,) = run(starts, [], [o_gs, o_gt, o_e, e_in], [mirrored])
    wave_even = lax.ppermute(wave_even, AXES, [(at(p, 1), at(p, 0)) for p in range(poles)])
    (wave_odd,) = run(starts, [], [m_gs, m_gt, m_e, e_second], [mirrored])
    received = []
    if rows > 1:
        received = [
            lax.ppermute(wave_odd, AXES, [(at(p, 1), at(p, 3)) for p in range(poles)]),
            lax.ppermute(wave_even, AXES, [(at(p, 0), at(p, 2)) for p in range(poles)]),
        ]
    else:
        received = [jnp.zeros(mirrored.shape, F32)]
    fas, fat, ea, ps, pt, ep = run(
        pair_kernel,
        [],
        [m_g, m_e, g_in, e_in, e_second],
        [parts, parts, mirrored, parts, parts, mirrored],
        cost=LONG,
    )
    arrived = list(received)
    for turn in range(1, rows - 1):
        active = functools.partial(step_kernel, lambda place, turn=turn: lax.div(place, 2) == turn)
        (wave,) = run(active, [], [ps, pt, ep] + arrived, [mirrored])
        up = [pair for p in range(poles) for pair in zip(hosts(turn, p), hosts(turn + 1, p))]
        arrived = [lax.ppermute(wave, AXES, up)]
        received += arrived
    own, sent = run(
        share_kernel,
        [],
        [fas, fat, ea] + received,
        [mirrored, mirrored],
        [pltpu.VMEM(mirrored.shape, F32)],
    )
    shared = lax.ppermute(sent, AXES, every)

    offs = jax.ShapeDtypeStruct((2, 2 * width, width // 2), F32)
    diags = jax.ShapeDtypeStruct((2,) + quarter, F32)
    off, diag = run(density_kernel, [], [weight, own, m_f0s, m_f0t, m_gs, m_gt, m_w], [offs, diags])
    off, us, ts = run(
        more_off_kernel,
        [],
        [weight, shared, e_in, o_f0s, o_f0t, o_gs, o_w, off],
        [offs, parts, parts],
    )

    def exchanged(value, distance):
        return lax.ppermute(value, "pole", [(p, p ^ distance) for p in range(poles)])

    def summed(parts):
        kept = parts[0] + exchanged(parts[1], 1)
        distance = 2
        while distance < poles:
            kept = kept + exchanged(kept, distance)
            distance *= 2
        return kept, exchanged(kept, 1)

    full = jax.ShapeDtypeStruct((2, width, width), F32)
    off_sums = summed(off)
    (diag,) = run(more_diag_kernel, [], [us, ts, o_f0t, o_gt, o_w, diag], [diags])
    diag_sums = summed(diag)
    done = jax.ShapeDtypeStruct((8, 128), F32)
    density_off, done = run(unpack_off_kernel, [], list(off_sums), [full, done])
    (density_diag,) = run(unpack_diag_kernel, [], [*diag_sums, done], [full])
    return density_diag, density_off


def solution(mesh):
    placed = (
        P("pole", "snode", None, None, None),
        P("pole", "snode", None, None, None),
        P("snode"),
        P("pole", None),
    )
    return jax.shard_map(
        local,
        mesh=mesh,
        in_specs=placed,
        out_specs=(P("snode", None, None), P("snode", None, None)),
        check_vma=False,
    )
```

```python
import functools

import jax
import jax.numpy as jnp
from jax import lax
from jax.experimental import pallas as pl
from jax.experimental.pallas import tpu as pltpu
from jax.sharding import PartitionSpec as P

F32 = jnp.float32
BF16 = jnp.bfloat16
AXES = ("pole", "snode")
VMEM_LIMIT = 16 * 1024 * 1024


def halves(value):
    high = value.astype(BF16)
    return high, (value - high.astype(F32)).astype(BF16)


def split_pair(real, imag):
    (rh, rl), (ih, il) = halves(real), halves(imag)
    return rh, ih, rl, il


def deep_dot(left, right):
    return jnp.dot(
        jnp.concatenate(left, axis=1), jnp.concatenate(right, axis=0), preferred_element_type=F32
    )


def complex_dot(left, right):
    arh, aih, arl, ail = left
    brh, bih, brl, bil = right
    blocks = [arh, arh, arl, aih, aih, ail]
    real = deep_dot(blocks, [brh, brl, brh, -bih, -bil, -bih])
    imag = deep_dot(blocks, [bih, bil, bih, brh, brl, brh])
    return real, imag


def rows_columns(size):
    return (
        lax.broadcasted_iota(jnp.int32, (size, size), 0),
        lax.broadcasted_iota(jnp.int32, (size, size), 1),
    )


def packed(block):
    half = block.shape[0] // 2
    row, column = rows_columns(half)
    lower = block[half:, half:]
    mixed = jnp.where(row >= column, block[:half, :half], lower)
    diagonal = jnp.sum(jnp.where(row == column, lower, 0.0), axis=0, keepdims=True)
    return jnp.concatenate(
        [block[:half, half:], mixed, jnp.broadcast_to(diagonal, (8, half))], axis=0
    )


def unpacked(value):
    half = value.shape[1]
    row, column = rows_columns(half)
    right, mixed = value[:half], value[half : 2 * half]
    diagonal = value[2 * half : 2 * half + 1]
    turned = mixed.T
    first = jnp.where(row >= column, mixed, turned)
    last = jnp.where(row < column, mixed, jnp.where(row == column, diagonal, turned))
    return jnp.concatenate(
        [jnp.concatenate([first, right], axis=1), jnp.concatenate([right.T, last], axis=1)], axis=0
    )


def unpacked_split(ref):
    return split_pair(unpacked(ref[0]), unpacked(ref[1]))


def load4(ref):
    return tuple(ref[i] for i in range(4))


def store4(ref, parts):
    for i, part in enumerate(parts):
        ref[i] = part


def whereabouts():
    place = lax.axis_index("snode")
    return place, lax.rem(place, 2), lax.rem(lax.axis_index("pole"), 2)


def hosted_slot():
    place, odd, _ = whereabouts()
    return jnp.where(place < 2, 0, 1 - odd)


def slot_of(hosted):
    return hosted_slot() if hosted else 1 - hosted_slot()


def constants_of(slot, blocks, link, widths, weights, f1s, e, weighted, *_, wait=lambda: None):
    width = blocks.shape[-1]
    row, column = rows_columns(width)
    kept = [column < widths[k] for k in range(2)]
    both = [jnp.logical_and(row < widths[k], kept[k]) for k in range(2)]
    f1 = [jnp.where(kept[1], link[c], 0.0) for c in range(2)]
    s1, t1 = split_pair(*f1), split_pair(f1[0].T, f1[1].T)
    store4(f1s, s1)
    wait()
    d = [[jnp.where(both[k], blocks[k, c], 0.0) for c in range(2)] for k in range(2)]
    br, bi = complex_dot(split_pair(*d[0]), s1)
    tr, ti = complex_dot(t1, split_pair(br, bi))
    er, ei = d[1][0] + tr, d[1][1] + ti
    e[0], e[1] = packed(er), packed(ei)
    w0, w1 = weights[pl.ds(slot, 1), 0:1], weights[pl.ds(slot, 1), 1:2]
    weighted[0] = packed(w1 * d[0][0] + w0 * d[0][1])
    weighted[1] = packed(w1 * er + w0 * ei)
    weighted_b = flat(w1 * br + w0 * bi)
    weighted[2] = weighted_b[: width + 8]
    weighted[3, : width - 8] = weighted_b[width + 8 :]


def fetched_constants(slot, live, pivot, factor, weight, outs, scratch):
    blocks, link, widths, weights, sems = scratch
    first_factor = pltpu.make_async_copy(factor.at[slot, 0], outs[3], sems.at[5])
    copies = [
        pltpu.make_async_copy(live, widths, sems.at[0]),
        pltpu.make_async_copy(factor.at[slot, 1], link, sems.at[1]),
        pltpu.make_async_copy(pivot.at[slot, 0], blocks.at[0], sems.at[2]),
        pltpu.make_async_copy(pivot.at[slot, 1], blocks.at[1], sems.at[3]),
        pltpu.make_async_copy(weight, weights, sems.at[4]),
    ]
    for copy in copies:
        copy.start()
    first_factor.start()
    copies[0].wait()
    copies[1].wait()

    def wait():
        for copy in copies[2:]:
            copy.wait()

    constants_of(slot, blocks, link, widths, weights, *outs, wait=wait)
    first_factor.wait()


def sent_constant_kernel(live, pivot, factor, weight, *refs):
    @pl.when(whereabouts()[0] != 1)
    def _():
        fetched_constants(slot_of(False), live, pivot, factor, weight, refs[:4], refs[4:])


def first_constant_kernel(live, pivot, factor, weight, *refs):
    made, outs, scratch = refs[:4], refs[4:8], refs[8:]
    place = whereabouts()[0]

    @pl.when(place != 1)
    def _():
        for source, target in zip(made, outs):
            target[...] = source[...]

    @pl.when(place == 1)
    def _():
        fetched_constants(slot_of(False), live, pivot, factor, weight, outs, scratch)


def constant_kernel(live, pivot, factor, weight, _, f1s, e, weighted, first_factor):
    slot = slot_of(True)
    first_factor[...] = factor[slot, 0]
    constants_of(slot, pivot.at[slot], factor.at[slot, 1], live, weight, f1s, e, weighted)


def factor_kernel(live, factor, f1s, f0s, f0t, gs, gt, g):
    _, column = rows_columns(factor.shape[-1])
    f0 = [jnp.where(column < live[0], factor[c], 0.0) for c in range(2)]
    s0 = split_pair(*f0)
    gr, gi = complex_dot(s0, load4(f1s))
    g[0], g[1] = gr, gi
    store4(gs, split_pair(gr, gi))
    store4(gt, split_pair(gr.T, gi.T))
    store4(f0s, s0)
    store4(f0t, split_pair(f0[0].T, f0[1].T))


def fold(x, gs, gt, e, out):
    tr, ti = complex_dot(x, load4(gs))
    yr, yi = complex_dot(load4(gt), split_pair(tr, ti))
    out[0] = e[0] + packed(yr)
    out[1] = e[1] + packed(yi)


def step_kernel(active, gs, gt, e, *refs):
    *received, out = refs

    @pl.when(active(whereabouts()[0]))
    def _():
        value = received[0][...]
        for other in received[1:]:
            value = value + other[...]
        fold(split_pair(unpacked(value[0]), unpacked(value[1])), gs, gt, e, out)


def pair_kernel(g, e, g_in, e_in, e_second, fas, fat, ea, ps, pt, ep):
    upper = whereabouts()[0] > 1
    is_odd = whereabouts()[1] == 1
    ga = [jnp.where(is_odd, g_in[c], g[c]) for c in range(2)]
    gb = [jnp.where(is_odd, g[c], g_in[c]) for c in range(2)]
    theirs = [jnp.where(upper, e_in[c], e_second[c]) for c in range(2)]
    low = [jnp.where(is_odd, theirs[c], e[c]) for c in range(2)]
    high = [jnp.where(is_odd, e[c], theirs[c]) for c in range(2)]
    sa, sb = split_pair(*ga), split_pair(*gb)
    store4(fas, sa)
    store4(fat, split_pair(ga[0].T, ga[1].T))
    pr, pi = complex_dot(sa, sb)
    store4(ps, split_pair(pr, pi))
    store4(pt, split_pair(pr.T, pi.T))
    br, bi = complex_dot(split_pair(unpacked(low[0]), unpacked(low[1])), sb)
    tr, ti = complex_dot(split_pair(gb[0].T, gb[1].T), split_pair(br, bi))
    for c, term in enumerate((tr, ti)):
        ea[c] = low[c]
        ep[c] = high[c] + packed(term)


def share_kernel(fas, fat, ea, *refs):
    *received, own, sent, scratch = refs
    value = received[0][...]
    for other in received[1:]:
        value = value + other[...]
    value = jnp.where(whereabouts()[0] > 1, value, 0.0)
    fold(split_pair(unpacked(value[0]), unpacked(value[1])), fas, fat, ea, scratch)
    is_odd = whereabouts()[1] == 1
    own[...] = jnp.where(is_odd, scratch[...], value)
    sent[...] = jnp.where(is_odd, value, scratch[...])


def flat(block):
    half = block.shape[1] // 2
    return jnp.concatenate([block[:, :half], block[:, half:]], axis=0)


def real_dot(left, right):
    arh, aih, arl, ail = left
    brh, bih, brl, bil = right
    return deep_dot([arh, arh, arl, aih, aih, ail], [brh, brl, brh, bih, bil, bih])


def off_values(slot, weight, xs, f0s, f0t, gs, weighted):
    width = f0s.shape[-1]
    w0, w1 = weight[pl.ds(slot, 1), 0:1], weight[pl.ds(slot, 1), 1:2]
    qr, qi = complex_dot(xs, load4(gs))
    ts = split_pair(w1 * qr + w0 * qi, w0 * qr - w1 * qi)
    second = real_dot(load4(f0t), ts)
    pr, pi = complex_dot(xs, load4(f0s))
    u = w1 * pr + w0 * pi
    us = split_pair(u, w0 * pr - w1 * pi)
    constant = jnp.concatenate([weighted[2], weighted[3, : width - 8]], axis=0)
    return -flat(u), -(flat(second) + constant), us, ts


def diag_values(us, ts, f0t, gt, weighted):
    return (
        weighted[0] + packed(real_dot(load4(f0t), us)),
        weighted[1] + packed(real_dot(load4(gt), ts)),
    )


def density_kernel(weight, x, f0s, f0t, gs, gt, weighted, off, diag):
    core = whereabouts()[2]
    first, second, us, ts = off_values(slot_of(True), weight, unpacked_split(x), f0s, f0t, gs, weighted)
    off[core], off[1 - core] = first, second
    diag[core], diag[1 - core] = diag_values(us, ts, f0t, gt, weighted)


def more_off_kernel(weight, x, x_first, f0s, f0t, gs, weighted, before, off, us_out, ts_out):
    core = whereabouts()[2]
    upper = whereabouts()[0] > 1
    x = [jnp.where(upper, x[c], x_first[c]) for c in range(2)]
    xs = split_pair(unpacked(x[0]), unpacked(x[1]))
    first, second, us, ts = off_values(slot_of(False), weight, xs, f0s, f0t, gs, weighted)
    off[core] = first + before[core]
    off[1 - core] = second + before[1 - core]
    store4(us_out, us)
    store4(ts_out, ts)


def more_diag_kernel(us, ts, f0t, gt, weighted, before, diag):
    core = whereabouts()[2]
    first, second = diag_values(load4(us), load4(ts), f0t, gt, weighted)
    diag[core] = first + before[core]
    diag[1 - core] = second + before[1 - core]


def unpack_off_kernel(mine, theirs, off, done):
    core = whereabouts()[2]
    width = off.shape[-1]
    half = width // 2
    for source, entry in ((mine, core), (theirs, 1 - core)):
        off[entry, :, :half] = source[:width]
        off[entry, :, half:] = source[width:]
    done[...] = jnp.zeros_like(done)


def unpack_diag_kernel(mine, theirs, _, diag):
    core = whereabouts()[2]
    for source, entry in ((mine, core), (theirs, 1 - core)):
        diag[entry] = unpacked(source[...])


SCALAR = pl.BlockSpec(memory_space=pltpu.SMEM)
WHOLE = pl.BlockSpec(memory_space=pltpu.VMEM)


COST = pl.CostEstimate(flops=1, bytes_accessed=1, transcendentals=0)


LONG = pl.CostEstimate(flops=10**11, bytes_accessed=1, transcendentals=0)


def run(kernel, scalars, arrays, shapes, scratch=(), cost=COST, far=()):
    return pl.pallas_call(
        kernel,
        out_shape=shapes,
        in_specs=[SCALAR] * len(scalars)
        + [pl.BlockSpec(memory_space=pltpu.HBM)] * len(far)
        + [WHOLE] * len(arrays),
        out_specs=[WHOLE] * len(shapes),
        scratch_shapes=list(scratch),
        compiler_params=pltpu.CompilerParams(vmem_limit_bytes=VMEM_LIMIT),
        cost_estimate=cost,
    )(*scalars, *far, *arrays)


def local(pivot, factor, live, weight):
    poles, turns = lax.axis_size("pole"), lax.axis_size("snode")
    rows = turns // 2
    width = pivot.shape[-1]
    quarter = (width + 8, width // 2)
    mirrored = jax.ShapeDtypeStruct((2,) + quarter, F32)
    parts = jax.ShapeDtypeStruct((4, width, width), BF16)

    def at(pole_index, snode_index):
        return pole_index * turns + snode_index

    def hosts(row, pole):
        return at(pole, 2 * row + 1), at(pole, 2 * row)

    swaps = [(at(p, s), at(p, s ^ 1)) for p in range(poles) for s in range(2, turns)]
    first = [(at(p, 0), at(p, 1)) for p in range(poles)]
    every = [(at(p, s), at(p, s ^ 1)) for p in range(poles) for s in range(turns)]
    raw = jax.ShapeDtypeStruct((2, width, width), F32)
    constants = [parts, mirrored, jax.ShapeDtypeStruct((4,) + quarter, F32), raw]
    factors = [parts, parts, parts, parts, raw]

    scratch = [
        pltpu.VMEM(pivot.shape[1:], F32),
        pltpu.VMEM(factor.shape[2:], F32),
        pltpu.SMEM(live.shape, jnp.int32),
        pltpu.VMEM(weight.shape, F32),
        pltpu.SemaphoreType.DMA((6,)),
    ]
    far = [pltpu.with_memory_space_constraint(a, pltpu.HBM) for a in (live, pivot, factor, weight)]
    made = run(sent_constant_kernel, [], [], constants, scratch, far=far)
    e_in = lax.ppermute(made[1], AXES, first + swaps)
    o_f1s, o_e, o_w, o_f0 = run(first_constant_kernel, [], made, constants, scratch, far=far)
    o_f0s, o_f0t, o_gs, o_gt, o_g = run(
        factor_kernel, [live], [o_f0, o_f1s], factors
    )
    g_in = lax.ppermute(o_g, AXES, swaps)
    m_f1s, m_e, m_w, m_f0 = run(
        constant_kernel,
        [live],
        [pivot, factor, weight, o_g],
        constants,
    )
    m_f0s, m_f0t, m_gs, m_gt, m_g = run(
        factor_kernel, [live], [m_f0, m_f1s], factors
    )
    e_second = lax.ppermute(m_e, AXES, first)

    starts = functools.partial(step_kernel, lambda place: place == 1)
    (wave_even,) = run(starts, [], [o_gs, o_gt, o_e, e_in], [mirrored])
    wave_even = lax.ppermute(wave_even, AXES, [(at(p, 1), at(p, 0)) for p in range(poles)])
    (wave_odd,) = run(starts, [], [m_gs, m_gt, m_e, e_second], [mirrored])
    received = []
    if rows > 1:
        received = [
            lax.ppermute(wave_odd, AXES, [(at(p, 1), at(p, 3)) for p in range(poles)]),
            lax.ppermute(wave_even, AXES, [(at(p, 0), at(p, 2)) for p in range(poles)]),
        ]
    else:
        received = [jnp.zeros(mirrored.shape, F32)]
    fas, fat, ea, ps, pt, ep = run(
        pair_kernel,
        [],
        [m_g, m_e, g_in, e_in, e_second],
        [parts, parts, mirrored, parts, parts, mirrored],
        cost=LONG,
    )
    arrived = list(received)
    for turn in range(1, rows - 1):
        active = functools.partial(step_kernel, lambda place, turn=turn: lax.div(place, 2) == turn)
        (wave,) = run(active, [], [ps, pt, ep] + arrived, [mirrored])
        up = [pair for p in range(poles) for pair in zip(hosts(turn, p), hosts(turn + 1, p))]
        arrived = [lax.ppermute(wave, AXES, up)]
        received += arrived
    own, sent = run(
        share_kernel,
        [],
        [fas, fat, ea] + received,
        [mirrored, mirrored],
        [pltpu.VMEM(mirrored.shape, F32)],
    )
    shared = lax.ppermute(sent, AXES, every)

    offs = jax.ShapeDtypeStruct((2, 2 * width, width // 2), F32)
    diags = jax.ShapeDtypeStruct((2,) + quarter, F32)
    off, diag = run(density_kernel, [], [weight, own, m_f0s, m_f0t, m_gs, m_gt, m_w], [offs, diags])
    off, us, ts = run(
        more_off_kernel,
        [],
        [weight, shared, e_in, o_f0s, o_f0t, o_gs, o_w, off],
        [offs, parts, parts],
    )

    def exchanged(value, distance):
        return lax.ppermute(value, "pole", [(p, p ^ distance) for p in range(poles)])

    def summed(parts):
        kept = parts[0] + exchanged(parts[1], 1)
        distance = 2
        while distance < poles:
            kept = kept + exchanged(kept, distance)
            distance *= 2
        return kept, exchanged(kept, 1)

    full = jax.ShapeDtypeStruct((2, width, width), F32)
    off_sums = summed(off)
    (diag,) = run(more_diag_kernel, [], [us, ts, o_f0t, o_gt, o_w, diag], [diags])
    diag_sums = summed(diag)
    done = jax.ShapeDtypeStruct((8, 128), F32)
    density_off, done = run(unpack_off_kernel, [], list(off_sums), [full, done])
    (density_diag,) = run(unpack_diag_kernel, [], [*diag_sums, done], [full])
    return density_diag, density_off


def solution(mesh):
    placed = (
        P("pole", "snode", None, None, None),
        P("pole", "snode", None, None, None),
        P("snode"),
        P("pole", None),
    )
    return jax.shard_map(
        local,
        mesh=mesh,
        in_specs=placed,
        out_specs=(P("snode", None, None), P("snode", None, None)),
        check_vma=False,
    )
```

```python
import functools

import jax
import jax.numpy as jnp
from jax import lax
from jax.experimental import pallas as pl
from jax.experimental.pallas import tpu as pltpu
from jax.sharding import PartitionSpec as P

F32 = jnp.float32
BF16 = jnp.bfloat16
AXES = ("pole", "snode")
VMEM_LIMIT = 16 * 1024 * 1024


def halves(value):
    high = value.astype(BF16)
    return high, (value - high.astype(F32)).astype(BF16)


def split_pair(real, imag):
    (rh, rl), (ih, il) = halves(real), halves(imag)
    return rh, ih, rl, il


def deep_dot(left, right):
    return jnp.dot(
        jnp.concatenate(left, axis=1), jnp.concatenate(right, axis=0), preferred_element_type=F32
    )


def dot(left, right):
    return jnp.dot(left, right, preferred_element_type=F32)


def dot3(lh, ll, rh, rl):
    return dot(lh, rh) + (dot(lh, rl) + dot(ll, rh))


def wide_dot(left, right):
    arh, aih, arl, ail = left
    brh, bih, brl, bil = right
    real = dot3(arh, arl, brh, brl) - dot3(aih, ail, bih, bil)
    imag = dot3(arh, arl, bih, bil) + dot3(aih, ail, brh, brl)
    return real, imag


def complex_dot(left, right):
    arh, aih, arl, ail = left
    brh, bih, brl, bil = right
    blocks = [arh, arh, arl, aih, aih, ail]
    real = deep_dot(blocks, [brh, brl, brh, -bih, -bil, -bih])
    imag = deep_dot(blocks, [bih, bil, bih, brh, brl, brh])
    return real, imag


def rows_columns(size):
    return (
        lax.broadcasted_iota(jnp.int32, (size, size), 0),
        lax.broadcasted_iota(jnp.int32, (size, size), 1),
    )


def packed(block):
    half = block.shape[0] // 2
    row, column = rows_columns(half)
    lower = block[half:, half:]
    mixed = jnp.where(row >= column, block[:half, :half], lower)
    diagonal = jnp.sum(jnp.where(row == column, lower, 0.0), axis=0, keepdims=True)
    return jnp.concatenate(
        [block[:half, half:], mixed, jnp.broadcast_to(diagonal, (8, half))], axis=0
    )


def unpacked(value):
    half = value.shape[1]
    row, column = rows_columns(half)
    right, mixed = value[:half], value[half : 2 * half]
    diagonal = value[2 * half : 2 * half + 1]
    turned = mixed.T
    first = jnp.where(row >= column, mixed, turned)
    last = jnp.where(row < column, mixed, jnp.where(row == column, diagonal, turned))
    return jnp.concatenate(
        [jnp.concatenate([first, right], axis=1), jnp.concatenate([right.T, last], axis=1)], axis=0
    )


def unpacked_split(ref):
    return split_pair(unpacked(ref[0]), unpacked(ref[1]))


def load4(ref):
    return tuple(ref[i] for i in range(4))


def store4(ref, parts):
    for i, part in enumerate(parts):
        ref[i] = part


def whereabouts():
    place = lax.axis_index("snode")
    return place, lax.rem(place, 2), lax.rem(lax.axis_index("pole"), 2)


def hosted_slot():
    place, odd, _ = whereabouts()
    return jnp.where(place < 2, 0, 1 - odd)


def slot_of(hosted):
    return hosted_slot() if hosted else 1 - hosted_slot()


def constants_of(slot, blocks, link, widths, weights, f1s, e, weighted, *_, wait=lambda: None):
    width = blocks.shape[-1]
    row, column = rows_columns(width)
    kept = [column < widths[k] for k in range(2)]
    both = [jnp.logical_and(row < widths[k], kept[k]) for k in range(2)]
    f1 = [jnp.where(kept[1], link[c], 0.0) for c in range(2)]
    s1, t1 = split_pair(*f1), split_pair(f1[0].T, f1[1].T)
    store4(f1s, s1)
    wait()
    d = [[jnp.where(both[k], blocks[k, c], 0.0) for c in range(2)] for k in range(2)]
    br, bi = complex_dot(split_pair(*d[0]), s1)
    tr, ti = complex_dot(t1, split_pair(br, bi))
    er, ei = d[1][0] + tr, d[1][1] + ti
    e[0], e[1] = packed(er), packed(ei)
    w0, w1 = weights[pl.ds(slot, 1), 0:1], weights[pl.ds(slot, 1), 1:2]
    weighted[0] = packed(w1 * d[0][0] + w0 * d[0][1])
    weighted[1] = packed(w1 * er + w0 * ei)
    weighted_b = flat(w1 * br + w0 * bi)
    weighted[2] = weighted_b[: width + 8]
    weighted[3, : width - 8] = weighted_b[width + 8 :]


def fetched_constants(slot, live, pivot, factor, weight, outs, scratch):
    blocks, link, widths, weights, sems = scratch
    first_factor = pltpu.make_async_copy(factor.at[slot, 0], outs[3], sems.at[5])
    copies = [
        pltpu.make_async_copy(live, widths, sems.at[0]),
        pltpu.make_async_copy(factor.at[slot, 1], link, sems.at[1]),
        pltpu.make_async_copy(pivot.at[slot, 0], blocks.at[0], sems.at[2]),
        pltpu.make_async_copy(pivot.at[slot, 1], blocks.at[1], sems.at[3]),
        pltpu.make_async_copy(weight, weights, sems.at[4]),
    ]
    for copy in copies:
        copy.start()
    first_factor.start()
    copies[0].wait()
    copies[1].wait()

    def wait():
        for copy in copies[2:]:
            copy.wait()

    constants_of(slot, blocks, link, widths, weights, *outs, wait=wait)
    first_factor.wait()


def sent_constant_kernel(live, pivot, factor, weight, *refs):
    @pl.when(whereabouts()[0] != 1)
    def _():
        fetched_constants(slot_of(False), live, pivot, factor, weight, refs[:4], refs[4:])


def first_constant_kernel(live, pivot, factor, weight, *refs):
    made, outs, scratch = refs[:4], refs[4:8], refs[8:]
    place = whereabouts()[0]

    @pl.when(place != 1)
    def _():
        for source, target in zip(made, outs):
            target[...] = source[...]

    @pl.when(place == 1)
    def _():
        fetched_constants(slot_of(False), live, pivot, factor, weight, outs, scratch)


def second_constants(live, pivot, factor, weight, f1s, e, weighted, first_factor):
    slot = slot_of(True)
    first_factor[...] = factor[slot, 0]
    constants_of(slot, pivot.at[slot], factor.at[slot, 1], live, weight, f1s, e, weighted)


def sent_second_kernel(live, pivot, factor, weight, _, *outs):
    @pl.when(whereabouts()[0] != 1)
    def _():
        second_constants(live, pivot, factor, weight, *outs)


def second_constant_kernel(live, pivot, factor, weight, *refs):
    made, outs = refs[:4], refs[4:]
    place = whereabouts()[0]

    @pl.when(place != 1)
    def _():
        for source, target in zip(made, outs):
            target[...] = source[...]

    @pl.when(place == 1)
    def _():
        second_constants(live, pivot, factor, weight, *outs)


def factor_kernel(live, factor, f1s, f0s, f0t, gs, gt, g):
    _, column = rows_columns(factor.shape[-1])
    f0 = [jnp.where(column < live[0], factor[c], 0.0) for c in range(2)]
    s0 = split_pair(*f0)
    gr, gi = complex_dot(s0, load4(f1s))
    g[0], g[1] = gr, gi
    store4(gs, split_pair(gr, gi))
    store4(gt, split_pair(gr.T, gi.T))
    store4(f0s, s0)
    store4(f0t, split_pair(f0[0].T, f0[1].T))


def fold(x, gs, gt, e, out):
    tr, ti = complex_dot(x, load4(gs))
    yr, yi = complex_dot(load4(gt), split_pair(tr, ti))
    out[0] = e[0] + packed(yr)
    out[1] = e[1] + packed(yi)


def step_kernel(active, gs, gt, e, *refs):
    *received, out = refs

    @pl.when(active(whereabouts()[0]))
    def _():
        value = received[0][...]
        for other in received[1:]:
            value = value + other[...]
        fold(split_pair(unpacked(value[0]), unpacked(value[1])), gs, gt, e, out)


def pair_kernel(g, e, g_in, e_in, e_second, fas, fat, ea, ps, pt, ep):
    upper = whereabouts()[0] > 1
    is_odd = whereabouts()[1] == 1
    ga = [jnp.where(is_odd, g_in[c], g[c]) for c in range(2)]
    gb = [jnp.where(is_odd, g[c], g_in[c]) for c in range(2)]
    theirs = [jnp.where(upper, e_in[c], e_second[c]) for c in range(2)]
    low = [jnp.where(is_odd, theirs[c], e[c]) for c in range(2)]
    high = [jnp.where(is_odd, e[c], theirs[c]) for c in range(2)]
    sa, sb = split_pair(*ga), split_pair(*gb)
    store4(fas, sa)
    store4(fat, split_pair(ga[0].T, ga[1].T))
    pr, pi = complex_dot(sa, sb)
    store4(ps, split_pair(pr, pi))
    store4(pt, split_pair(pr.T, pi.T))
    br, bi = complex_dot(split_pair(unpacked(low[0]), unpacked(low[1])), sb)
    tr, ti = complex_dot(split_pair(gb[0].T, gb[1].T), split_pair(br, bi))
    for c, term in enumerate((tr, ti)):
        ea[c] = low[c]
        ep[c] = high[c] + packed(term)


def share_kernel(fas, fat, ea, *refs):
    *received, own, sent, scratch = refs
    value = received[0][...]
    for other in received[1:]:
        value = value + other[...]
    value = jnp.where(whereabouts()[0] > 1, value, 0.0)
    fold(split_pair(unpacked(value[0]), unpacked(value[1])), fas, fat, ea, scratch)
    is_odd = whereabouts()[1] == 1
    own[...] = jnp.where(is_odd, scratch[...], value)
    sent[...] = jnp.where(is_odd, value, scratch[...])


def flat(block):
    half = block.shape[1] // 2
    return jnp.concatenate([block[:, :half], block[:, half:]], axis=0)


def real_dot(left, right):
    return dot3(left[0], left[2], right[0], right[2]) + dot3(left[1], left[3], right[1], right[3])


def off_values(slot, weight, xs, f0s, f0t, gs, weighted):
    width = f0s.shape[-1]
    w0, w1 = weight[pl.ds(slot, 1), 0:1], weight[pl.ds(slot, 1), 1:2]
    qr, qi = wide_dot(xs, load4(gs))
    ts = split_pair(w1 * qr + w0 * qi, w0 * qr - w1 * qi)
    second = real_dot(load4(f0t), ts)
    pr, pi = wide_dot(xs, load4(f0s))
    u = w1 * pr + w0 * pi
    us = split_pair(u, w0 * pr - w1 * pi)
    constant = jnp.concatenate([weighted[2], weighted[3, : width - 8]], axis=0)
    return -flat(u), -(flat(second) + constant), us, ts


def diag_values(us, ts, f0t, gt, weighted):
    return (
        weighted[0] + packed(real_dot(load4(f0t), us)),
        weighted[1] + packed(real_dot(load4(gt), ts)),
    )


def density_kernel(weight, x, f0s, f0t, gs, gt, weighted, off, diag):
    core = whereabouts()[2]
    first, second, us, ts = off_values(slot_of(True), weight, unpacked_split(x), f0s, f0t, gs, weighted)
    off[core], off[1 - core] = first, second
    diag[core], diag[1 - core] = diag_values(us, ts, f0t, gt, weighted)


def more_off_kernel(weight, x, x_first, f0s, f0t, gs, weighted, before, off, us_out, ts_out):
    core = whereabouts()[2]
    upper = whereabouts()[0] > 1
    x = [jnp.where(upper, x[c], x_first[c]) for c in range(2)]
    xs = split_pair(unpacked(x[0]), unpacked(x[1]))
    first, second, us, ts = off_values(slot_of(False), weight, xs, f0s, f0t, gs, weighted)
    off[core] = first + before[core]
    off[1 - core] = second + before[1 - core]
    store4(us_out, us)
    store4(ts_out, ts)


def more_diag_kernel(us, ts, f0t, gt, weighted, before, diag):
    core = whereabouts()[2]
    first, second = diag_values(load4(us), load4(ts), f0t, gt, weighted)
    diag[core] = first + before[core]
    diag[1 - core] = second + before[1 - core]


def unpack_off_kernel(mine, theirs, off, done):
    core = whereabouts()[2]
    width = off.shape[-1]
    half = width // 2
    for source, entry in ((mine, core), (theirs, 1 - core)):
        off[entry, :, :half] = source[:width]
        off[entry, :, half:] = source[width:]
    done[...] = jnp.zeros_like(done)


def unpack_diag_kernel(mine, theirs, _, diag):
    core = whereabouts()[2]
    for source, entry in ((mine, core), (theirs, 1 - core)):
        diag[entry] = unpacked(source[...])


SCALAR = pl.BlockSpec(memory_space=pltpu.SMEM)
WHOLE = pl.BlockSpec(memory_space=pltpu.VMEM)


COST = pl.CostEstimate(flops=1, bytes_accessed=1, transcendentals=0)


LONG = pl.CostEstimate(flops=10**11, bytes_accessed=1, transcendentals=0)


def run(kernel, scalars, arrays, shapes, scratch=(), cost=COST, far=()):
    return pl.pallas_call(
        kernel,
        out_shape=shapes,
        in_specs=[SCALAR] * len(scalars)
        + [pl.BlockSpec(memory_space=pltpu.HBM)] * len(far)
        + [WHOLE] * len(arrays),
        out_specs=[WHOLE] * len(shapes),
        scratch_shapes=list(scratch),
        compiler_params=pltpu.CompilerParams(vmem_limit_bytes=VMEM_LIMIT),
        cost_estimate=cost,
    )(*scalars, *far, *arrays)


def local(pivot, factor, live, weight):
    poles, turns = lax.axis_size("pole"), lax.axis_size("snode")
    rows = turns // 2
    width = pivot.shape[-1]
    quarter = (width + 8, width // 2)
    mirrored = jax.ShapeDtypeStruct((2,) + quarter, F32)
    parts = jax.ShapeDtypeStruct((4, width, width), BF16)

    def at(pole_index, snode_index):
        return pole_index * turns + snode_index

    def hosts(row, pole):
        return at(pole, 2 * row + 1), at(pole, 2 * row)

    swaps = [(at(p, s), at(p, s ^ 1)) for p in range(poles) for s in range(2, turns)]
    first = [(at(p, 0), at(p, 1)) for p in range(poles)]
    every = [(at(p, s), at(p, s ^ 1)) for p in range(poles) for s in range(turns)]
    raw = jax.ShapeDtypeStruct((2, width, width), F32)
    constants = [parts, mirrored, jax.ShapeDtypeStruct((4,) + quarter, F32), raw]
    factors = [parts, parts, parts, parts, raw]

    scratch = [
        pltpu.VMEM(pivot.shape[1:], F32),
        pltpu.VMEM(factor.shape[2:], F32),
        pltpu.SMEM(live.shape, jnp.int32),
        pltpu.VMEM(weight.shape, F32),
        pltpu.SemaphoreType.DMA((6,)),
    ]
    far = [pltpu.with_memory_space_constraint(a, pltpu.HBM) for a in (live, pivot, factor, weight)]
    made = run(sent_constant_kernel, [], [], constants, scratch, far=far)
    e_in = lax.ppermute(made[1], AXES, first + swaps)
    o_f1s, o_e, o_w, o_f0 = run(first_constant_kernel, [], made, constants, scratch, far=far)
    o_f0s, o_f0t, o_gs, o_gt, o_g = run(
        factor_kernel, [live], [o_f0, o_f1s], factors
    )
    g_in = lax.ppermute(o_g, AXES, swaps)
    made = run(sent_second_kernel, [live], [pivot, factor, weight, o_g], constants)
    e_second = lax.ppermute(made[1], AXES, first)
    m_f1s, m_e, m_w, m_f0 = run(
        second_constant_kernel, [live], [pivot, factor, weight, *made], constants
    )
    m_f0s, m_f0t, m_gs, m_gt, m_g = run(
        factor_kernel, [live], [m_f0, m_f1s], factors
    )
    starts = functools.partial(step_kernel, lambda place: place == 1)
    (wave_even,) = run(starts, [], [o_gs, o_gt, o_e, e_in], [mirrored])
    wave_even = lax.ppermute(wave_even, AXES, [(at(p, 1), at(p, 0)) for p in range(poles)])
    (wave_odd,) = run(starts, [], [m_gs, m_gt, m_e, e_second], [mirrored])
    received = []
    if rows > 1:
        received = [
            lax.ppermute(wave_odd, AXES, [(at(p, 1), at(p, 3)) for p in range(poles)]),
            lax.ppermute(wave_even, AXES, [(at(p, 0), at(p, 2)) for p in range(poles)]),
        ]
    else:
        received = [jnp.zeros(mirrored.shape, F32)]
    fas, fat, ea, ps, pt, ep = run(
        pair_kernel,
        [],
        [m_g, m_e, g_in, e_in, e_second],
        [parts, parts, mirrored, parts, parts, mirrored],
        cost=LONG,
    )
    arrived = list(received)
    for turn in range(1, rows - 1):
        active = functools.partial(step_kernel, lambda place, turn=turn: lax.div(place, 2) == turn)
        (wave,) = run(active, [], [ps, pt, ep] + arrived, [mirrored])
        up = [pair for p in range(poles) for pair in zip(hosts(turn, p), hosts(turn + 1, p))]
        arrived = [lax.ppermute(wave, AXES, up)]
        received += arrived
    own, sent = run(
        share_kernel,
        [],
        [fas, fat, ea] + received,
        [mirrored, mirrored],
        [pltpu.VMEM(mirrored.shape, F32)],
    )
    shared = lax.ppermute(sent, AXES, every)

    offs = jax.ShapeDtypeStruct((2, 2 * width, width // 2), F32)
    diags = jax.ShapeDtypeStruct((2,) + quarter, F32)
    off, diag = run(density_kernel, [], [weight, own, m_f0s, m_f0t, m_gs, m_gt, m_w], [offs, diags])
    off, us, ts = run(
        more_off_kernel,
        [],
        [weight, shared, e_in, o_f0s, o_f0t, o_gs, o_w, off],
        [offs, parts, parts],
    )

    def exchanged(value, distance):
        return lax.ppermute(value, "pole", [(p, p ^ distance) for p in range(poles)])

    def summed(parts):
        kept = parts[0] + exchanged(parts[1], 1)
        distance = 2
        while distance < poles:
            kept = kept + exchanged(kept, distance)
            distance *= 2
        return kept, exchanged(kept, 1)

    full = jax.ShapeDtypeStruct((2, width, width), F32)
    off_sums = summed(off)
    (diag,) = run(more_diag_kernel, [], [us, ts, o_f0t, o_gt, o_w, diag], [diags])
    diag_sums = summed(diag)
    done = jax.ShapeDtypeStruct((8, 128), F32)
    density_off, done = run(unpack_off_kernel, [], list(off_sums), [full, done])
    (density_diag,) = run(unpack_diag_kernel, [], [*diag_sums, done], [full])
    return density_diag, density_off


def solution(mesh):
    placed = (
        P("pole", "snode", None, None, None),
        P("pole", "snode", None, None, None),
        P("snode"),
        P("pole", None),
    )
    return jax.shard_map(
        local,
        mesh=mesh,
        in_specs=placed,
        out_specs=(P("snode", None, None), P("snode", None, None)),
        check_vma=False,
    )
```

```python
import functools

import jax
import jax.numpy as jnp
from jax import lax
from jax.experimental import pallas as pl
from jax.experimental.pallas import tpu as pltpu
from jax.sharding import PartitionSpec as P

F32 = jnp.float32
BF16 = jnp.bfloat16
AXES = ("pole", "snode")
VMEM_LIMIT = 16 * 1024 * 1024


def halves(value):
    high = value.astype(BF16)
    return high, (value - high.astype(F32)).astype(BF16)


def split_pair(real, imag):
    (rh, rl), (ih, il) = halves(real), halves(imag)
    return rh, ih, rl, il


def deep_dot(left, right):
    return jnp.dot(
        jnp.concatenate(left, axis=1), jnp.concatenate(right, axis=0), preferred_element_type=F32
    )


def dot(left, right):
    return jnp.dot(left, right, preferred_element_type=F32)


def dot3(lh, ll, rh, rl):
    return dot(lh, rh) + (dot(lh, rl) + dot(ll, rh))


def wide_dot(left, right):
    arh, aih, arl, ail = left
    brh, bih, brl, bil = right
    real = dot3(arh, arl, brh, brl) - dot3(aih, ail, bih, bil)
    imag = dot3(arh, arl, bih, bil) + dot3(aih, ail, brh, brl)
    return real, imag


def complex_dot(left, right):
    arh, aih, arl, ail = left
    brh, bih, brl, bil = right
    blocks = [arh, arh, arl, aih, aih, ail]
    real = deep_dot(blocks, [brh, brl, brh, -bih, -bil, -bih])
    imag = deep_dot(blocks, [bih, bil, bih, brh, brl, brh])
    return real, imag


def rows_columns(size):
    return (
        lax.broadcasted_iota(jnp.int32, (size, size), 0),
        lax.broadcasted_iota(jnp.int32, (size, size), 1),
    )


def packed(block):
    half = block.shape[0] // 2
    row, column = rows_columns(half)
    lower = block[half:, half:]
    mixed = jnp.where(row >= column, block[:half, :half], lower)
    diagonal = jnp.sum(jnp.where(row == column, lower, 0.0), axis=0, keepdims=True)
    return jnp.concatenate(
        [block[:half, half:], mixed, jnp.broadcast_to(diagonal, (8, half))], axis=0
    )


def unpacked(value):
    half = value.shape[1]
    row, column = rows_columns(half)
    right, mixed = value[:half], value[half : 2 * half]
    diagonal = value[2 * half : 2 * half + 1]
    turned = mixed.T
    first = jnp.where(row >= column, mixed, turned)
    last = jnp.where(row < column, mixed, jnp.where(row == column, diagonal, turned))
    return jnp.concatenate(
        [jnp.concatenate([first, right], axis=1), jnp.concatenate([right.T, last], axis=1)], axis=0
    )


def unpacked_split(ref):
    return split_pair(unpacked(ref[0]), unpacked(ref[1]))


def load4(ref):
    return tuple(ref[i] for i in range(4))


def store4(ref, parts):
    for i, part in enumerate(parts):
        ref[i] = part


def whereabouts():
    place = lax.axis_index("snode")
    return place, lax.rem(place, 2), lax.rem(lax.axis_index("pole"), 2)


def hosted_slot():
    place, odd, _ = whereabouts()
    return jnp.where(place < 2, 0, 1 - odd)


def slot_of(hosted):
    return hosted_slot() if hosted else 1 - hosted_slot()


def constants_of(slot, blocks, link, widths, weights, f1s, e, weighted, *_, wait=lambda: None):
    width = blocks.shape[-1]
    row, column = rows_columns(width)
    kept = [column < widths[k] for k in range(2)]
    both = [jnp.logical_and(row < widths[k], kept[k]) for k in range(2)]
    f1 = [jnp.where(kept[1], link[c], 0.0) for c in range(2)]
    s1, t1 = split_pair(*f1), split_pair(f1[0].T, f1[1].T)
    store4(f1s, s1)
    wait()
    d = [[jnp.where(both[k], blocks[k, c], 0.0) for c in range(2)] for k in range(2)]
    br, bi = complex_dot(split_pair(*d[0]), s1)
    tr, ti = complex_dot(t1, split_pair(br, bi))
    er, ei = d[1][0] + tr, d[1][1] + ti
    e[0], e[1] = packed(er), packed(ei)
    w0, w1 = weights[pl.ds(slot, 1), 0:1], weights[pl.ds(slot, 1), 1:2]
    weighted[0] = packed(w1 * d[0][0] + w0 * d[0][1])
    weighted[1] = packed(w1 * er + w0 * ei)
    weighted_b = flat(w1 * br + w0 * bi)
    weighted[2] = weighted_b[: width + 8]
    weighted[3, : width - 8] = weighted_b[width + 8 :]


def fetched_constants(slot, live, pivot, factor, weight, outs, scratch):
    blocks, link, widths, weights, sems = scratch
    first_factor = pltpu.make_async_copy(factor.at[slot, 0], outs[3], sems.at[5])
    copies = [
        pltpu.make_async_copy(live, widths, sems.at[0]),
        pltpu.make_async_copy(factor.at[slot, 1], link, sems.at[1]),
        pltpu.make_async_copy(pivot.at[slot, 0], blocks.at[0], sems.at[2]),
        pltpu.make_async_copy(pivot.at[slot, 1], blocks.at[1], sems.at[3]),
        pltpu.make_async_copy(weight, weights, sems.at[4]),
    ]
    for copy in copies:
        copy.start()
    first_factor.start()
    copies[0].wait()
    copies[1].wait()

    def wait():
        for copy in copies[2:]:
            copy.wait()

    constants_of(slot, blocks, link, widths, weights, *outs, wait=wait)
    first_factor.wait()


def sent_constant_kernel(live, pivot, factor, weight, *refs):
    outs, second, scratch = refs[:4], refs[4:8], refs[8:]
    place, _, core = whereabouts()

    @pl.when(jnp.logical_and(place != 1, core == 0))
    def _():
        fetched_constants(slot_of(True), live, pivot, factor, weight, second, scratch)

    @pl.when(place != 1)
    def _():
        fetched_constants(slot_of(False), live, pivot, factor, weight, outs, scratch)


def first_constant_kernel(live, pivot, factor, weight, *refs):
    made, outs, scratch = refs[:4], refs[4:8], refs[8:]
    place = whereabouts()[0]

    @pl.when(place != 1)
    def _():
        for source, target in zip(made, outs):
            target[...] = source[...]

    @pl.when(place == 1)
    def _():
        fetched_constants(slot_of(False), live, pivot, factor, weight, outs, scratch)


def second_constants(live, pivot, factor, weight, f1s, e, weighted, first_factor):
    slot = slot_of(True)
    first_factor[...] = factor[slot, 0]
    constants_of(slot, pivot.at[slot], factor.at[slot, 1], live, weight, f1s, e, weighted)


def sent_second_kernel(live, pivot, factor, weight, _, *refs):
    made, outs = refs[:4], refs[4:]
    place, _, core = whereabouts()

    @pl.when(core == 0)
    def _():
        for source, target in zip(made, outs):
            target[...] = source[...]

    @pl.when(jnp.logical_and(place != 1, core == 1))
    def _():
        second_constants(live, pivot, factor, weight, *outs)


def second_constant_kernel(live, pivot, factor, weight, *refs):
    made, outs = refs[:4], refs[4:]
    place = whereabouts()[0]

    @pl.when(place != 1)
    def _():
        for source, target in zip(made, outs):
            target[...] = source[...]

    @pl.when(place == 1)
    def _():
        second_constants(live, pivot, factor, weight, *outs)


def factor_kernel(live, factor, f1s, f0s, f0t, gs, gt, g):
    _, column = rows_columns(factor.shape[-1])
    f0 = [jnp.where(column < live[0], factor[c], 0.0) for c in range(2)]
    s0 = split_pair(*f0)
    gr, gi = complex_dot(s0, load4(f1s))
    g[0], g[1] = gr, gi
    store4(gs, split_pair(gr, gi))
    store4(gt, split_pair(gr.T, gi.T))
    store4(f0s, s0)
    store4(f0t, split_pair(f0[0].T, f0[1].T))


def fold(x, gs, gt, e, out):
    tr, ti = complex_dot(x, load4(gs))
    yr, yi = complex_dot(load4(gt), split_pair(tr, ti))
    out[0] = e[0] + packed(yr)
    out[1] = e[1] + packed(yi)


def step_kernel(active, gs, gt, e, *refs):
    *received, out = refs

    @pl.when(active(whereabouts()[0]))
    def _():
        value = received[0][...]
        for other in received[1:]:
            value = value + other[...]
        fold(split_pair(unpacked(value[0]), unpacked(value[1])), gs, gt, e, out)


def pair_kernel(g, e, g_in, e_in, e_second, fas, fat, ea, ps, pt, ep):
    upper = whereabouts()[0] > 1
    is_odd = whereabouts()[1] == 1
    ga = [jnp.where(is_odd, g_in[c], g[c]) for c in range(2)]
    gb = [jnp.where(is_odd, g[c], g_in[c]) for c in range(2)]
    theirs = [jnp.where(upper, e_in[c], e_second[c]) for c in range(2)]
    low = [jnp.where(is_odd, theirs[c], e[c]) for c in range(2)]
    high = [jnp.where(is_odd, e[c], theirs[c]) for c in range(2)]
    sa, sb = split_pair(*ga), split_pair(*gb)
    store4(fas, sa)
    store4(fat, split_pair(ga[0].T, ga[1].T))
    pr, pi = complex_dot(sa, sb)
    store4(ps, split_pair(pr, pi))
    store4(pt, split_pair(pr.T, pi.T))
    br, bi = complex_dot(split_pair(unpacked(low[0]), unpacked(low[1])), sb)
    tr, ti = complex_dot(split_pair(gb[0].T, gb[1].T), split_pair(br, bi))
    for c, term in enumerate((tr, ti)):
        ea[c] = low[c]
        ep[c] = high[c] + packed(term)


def share_kernel(fas, fat, ea, *refs):
    *received, own, sent, scratch = refs
    value = received[0][...]
    for other in received[1:]:
        value = value + other[...]
    value = jnp.where(whereabouts()[0] > 1, value, 0.0)
    fold(split_pair(unpacked(value[0]), unpacked(value[1])), fas, fat, ea, scratch)
    is_odd = whereabouts()[1] == 1
    own[...] = jnp.where(is_odd, scratch[...], value)
    sent[...] = jnp.where(is_odd, value, scratch[...])


def flat(block):
    half = block.shape[1] // 2
    return jnp.concatenate([block[:, :half], block[:, half:]], axis=0)


def real_dot(left, right):
    return dot3(left[0], left[2], right[0], right[2]) + dot3(left[1], left[3], right[1], right[3])


def off_values(slot, weight, xs, f0s, f0t, gs, weighted):
    width = f0s.shape[-1]
    w0, w1 = weight[pl.ds(slot, 1), 0:1], weight[pl.ds(slot, 1), 1:2]
    qr, qi = wide_dot(xs, load4(gs))
    ts = split_pair(w1 * qr + w0 * qi, w0 * qr - w1 * qi)
    second = real_dot(load4(f0t), ts)
    pr, pi = wide_dot(xs, load4(f0s))
    u = w1 * pr + w0 * pi
    us = split_pair(u, w0 * pr - w1 * pi)
    constant = jnp.concatenate([weighted[2], weighted[3, : width - 8]], axis=0)
    return -flat(u), -(flat(second) + constant), us, ts


def diag_values(us, ts, f0t, gt, weighted):
    return (
        weighted[0] + packed(real_dot(load4(f0t), us)),
        weighted[1] + packed(real_dot(load4(gt), ts)),
    )


def density_kernel(weight, x, f0s, f0t, gs, gt, weighted, off, diag):
    core = whereabouts()[2]
    first, second, us, ts = off_values(slot_of(True), weight, unpacked_split(x), f0s, f0t, gs, weighted)
    off[core], off[1 - core] = first, second
    diag[core], diag[1 - core] = diag_values(us, ts, f0t, gt, weighted)


def more_off_kernel(weight, x, x_first, f0s, f0t, gs, weighted, before, off, us_out, ts_out):
    core = whereabouts()[2]
    upper = whereabouts()[0] > 1
    x = [jnp.where(upper, x[c], x_first[c]) for c in range(2)]
    xs = split_pair(unpacked(x[0]), unpacked(x[1]))
    first, second, us, ts = off_values(slot_of(False), weight, xs, f0s, f0t, gs, weighted)
    off[core] = first + before[core]
    off[1 - core] = second + before[1 - core]
    store4(us_out, us)
    store4(ts_out, ts)


def more_diag_kernel(us, ts, f0t, gt, weighted, before, diag):
    core = whereabouts()[2]
    first, second = diag_values(load4(us), load4(ts), f0t, gt, weighted)
    diag[core] = first + before[core]
    diag[1 - core] = second + before[1 - core]


def unpack_off_kernel(mine, theirs, off, done):
    core = whereabouts()[2]
    width = off.shape[-1]
    half = width // 2
    for source, entry in ((mine, core), (theirs, 1 - core)):
        off[entry, :, :half] = source[:width]
        off[entry, :, half:] = source[width:]
    done[...] = jnp.zeros_like(done)


def unpack_diag_kernel(mine, theirs, _, diag):
    core = whereabouts()[2]
    for source, entry in ((mine, core), (theirs, 1 - core)):
        diag[entry] = unpacked(source[...])


SCALAR = pl.BlockSpec(memory_space=pltpu.SMEM)
WHOLE = pl.BlockSpec(memory_space=pltpu.VMEM)


COST = pl.CostEstimate(flops=1, bytes_accessed=1, transcendentals=0)


LONG = pl.CostEstimate(flops=10**11, bytes_accessed=1, transcendentals=0)


def run(kernel, scalars, arrays, shapes, scratch=(), cost=COST, far=()):
    return pl.pallas_call(
        kernel,
        out_shape=shapes,
        in_specs=[SCALAR] * len(scalars)
        + [pl.BlockSpec(memory_space=pltpu.HBM)] * len(far)
        + [WHOLE] * len(arrays),
        out_specs=[WHOLE] * len(shapes),
        scratch_shapes=list(scratch),
        compiler_params=pltpu.CompilerParams(vmem_limit_bytes=VMEM_LIMIT),
        cost_estimate=cost,
    )(*scalars, *far, *arrays)


def local(pivot, factor, live, weight):
    poles, turns = lax.axis_size("pole"), lax.axis_size("snode")
    rows = turns // 2
    width = pivot.shape[-1]
    quarter = (width + 8, width // 2)
    mirrored = jax.ShapeDtypeStruct((2,) + quarter, F32)
    parts = jax.ShapeDtypeStruct((4, width, width), BF16)

    def at(pole_index, snode_index):
        return pole_index * turns + snode_index

    def hosts(row, pole):
        return at(pole, 2 * row + 1), at(pole, 2 * row)

    swaps = [(at(p, s), at(p, s ^ 1)) for p in range(poles) for s in range(2, turns)]
    first = [(at(p, 0), at(p, 1)) for p in range(poles)]
    every = [(at(p, s), at(p, s ^ 1)) for p in range(poles) for s in range(turns)]
    raw = jax.ShapeDtypeStruct((2, width, width), F32)
    constants = [parts, mirrored, jax.ShapeDtypeStruct((4,) + quarter, F32), raw]
    factors = [parts, parts, parts, parts, raw]

    scratch = [
        pltpu.VMEM(pivot.shape[1:], F32),
        pltpu.VMEM(factor.shape[2:], F32),
        pltpu.SMEM(live.shape, jnp.int32),
        pltpu.VMEM(weight.shape, F32),
        pltpu.SemaphoreType.DMA((6,)),
    ]
    far = [pltpu.with_memory_space_constraint(a, pltpu.HBM) for a in (live, pivot, factor, weight)]
    made = run(sent_constant_kernel, [], [], constants * 2, scratch, far=far)
    made, second = made[:4], made[4:]
    e_in = lax.ppermute(made[1], AXES, first + swaps)
    o_f1s, o_e, o_w, o_f0 = run(first_constant_kernel, [], made, constants, scratch, far=far)
    o_f0s, o_f0t, o_gs, o_gt, o_g = run(
        factor_kernel, [live], [o_f0, o_f1s], factors
    )
    g_in = lax.ppermute(o_g, AXES, swaps)
    made = run(sent_second_kernel, [live], [pivot, factor, weight, o_g, *second], constants)
    e_second = lax.ppermute(made[1], AXES, first)
    m_f1s, m_e, m_w, m_f0 = run(
        second_constant_kernel, [live], [pivot, factor, weight, *made], constants
    )
    m_f0s, m_f0t, m_gs, m_gt, m_g = run(
        factor_kernel, [live], [m_f0, m_f1s], factors
    )
    starts = functools.partial(step_kernel, lambda place: place == 1)
    (wave_even,) = run(starts, [], [o_gs, o_gt, o_e, e_in], [mirrored])
    wave_even = lax.ppermute(wave_even, AXES, [(at(p, 1), at(p, 0)) for p in range(poles)])
    (wave_odd,) = run(starts, [], [m_gs, m_gt, m_e, e_second], [mirrored])
    received = []
    if rows > 1:
        received = [
            lax.ppermute(wave_odd, AXES, [(at(p, 1), at(p, 3)) for p in range(poles)]),
            lax.ppermute(wave_even, AXES, [(at(p, 0), at(p, 2)) for p in range(poles)]),
        ]
    else:
        received = [jnp.zeros(mirrored.shape, F32)]
    fas, fat, ea, ps, pt, ep = run(
        pair_kernel,
        [],
        [m_g, m_e, g_in, e_in, e_second],
        [parts, parts, mirrored, parts, parts, mirrored],
        cost=LONG,
    )
    arrived = list(received)
    for turn in range(1, rows - 1):
        active = functools.partial(step_kernel, lambda place, turn=turn: lax.div(place, 2) == turn)
        (wave,) = run(active, [], [ps, pt, ep] + arrived, [mirrored])
        up = [pair for p in range(poles) for pair in zip(hosts(turn, p), hosts(turn + 1, p))]
        arrived = [lax.ppermute(wave, AXES, up)]
        received += arrived
    own, sent = run(
        share_kernel,
        [],
        [fas, fat, ea] + received,
        [mirrored, mirrored],
        [pltpu.VMEM(mirrored.shape, F32)],
    )
    shared = lax.ppermute(sent, AXES, every)

    offs = jax.ShapeDtypeStruct((2, 2 * width, width // 2), F32)
    diags = jax.ShapeDtypeStruct((2,) + quarter, F32)
    off, diag = run(density_kernel, [], [weight, own, m_f0s, m_f0t, m_gs, m_gt, m_w], [offs, diags])
    off, us, ts = run(
        more_off_kernel,
        [],
        [weight, shared, e_in, o_f0s, o_f0t, o_gs, o_w, off],
        [offs, parts, parts],
    )

    def exchanged(value, distance):
        return lax.ppermute(value, "pole", [(p, p ^ distance) for p in range(poles)])

    def summed(parts):
        kept = parts[0] + exchanged(parts[1], 1)
        distance = 2
        while distance < poles:
            kept = kept + exchanged(kept, distance)
            distance *= 2
        return kept, exchanged(kept, 1)

    full = jax.ShapeDtypeStruct((2, width, width), F32)
    off_sums = summed(off)
    (diag,) = run(more_diag_kernel, [], [us, ts, o_f0t, o_gt, o_w, diag], [diags])
    diag_sums = summed(diag)
    done = jax.ShapeDtypeStruct((8, 128), F32)
    density_off, done = run(unpack_off_kernel, [], list(off_sums), [full, done])
    (density_diag,) = run(unpack_diag_kernel, [], [*diag_sums, done], [full])
    return density_diag, density_off


def solution(mesh):
    placed = (
        P("pole", "snode", None, None, None),
        P("pole", "snode", None, None, None),
        P("snode"),
        P("pole", None),
    )
    return jax.shard_map(
        local,
        mesh=mesh,
        in_specs=placed,
        out_specs=(P("snode", None, None), P("snode", None, None)),
        check_vma=False,
    )
```

```python
import functools

import jax
import jax.numpy as jnp
from jax import lax
from jax.experimental import pallas as pl
from jax.experimental.pallas import tpu as pltpu
from jax.sharding import PartitionSpec as P

F32 = jnp.float32
BF16 = jnp.bfloat16
AXES = ("pole", "snode")
VMEM_LIMIT = 16 * 1024 * 1024


def halves(value):
    high = value.astype(BF16)
    return high, (value - high.astype(F32)).astype(BF16)


def split_pair(real, imag):
    (rh, rl), (ih, il) = halves(real), halves(imag)
    return rh, ih, rl, il


def deep_dot(left, right):
    return jnp.dot(
        jnp.concatenate(left, axis=1), jnp.concatenate(right, axis=0), preferred_element_type=F32
    )


def dot(left, right):
    return jnp.dot(left, right, preferred_element_type=F32)


def dot3(lh, ll, rh, rl):
    return dot(lh, rh) + (dot(lh, rl) + dot(ll, rh))


def wide_dot(left, right):
    arh, aih, arl, ail = left
    brh, bih, brl, bil = right
    real = dot3(arh, arl, brh, brl) - dot3(aih, ail, bih, bil)
    imag = dot3(arh, arl, bih, bil) + dot3(aih, ail, brh, brl)
    return real, imag


def complex_dot(left, right):
    arh, aih, arl, ail = left
    brh, bih, brl, bil = right
    blocks = [arh, arh, arl, aih, aih, ail]
    real = deep_dot(blocks, [brh, brl, brh, -bih, -bil, -bih])
    imag = deep_dot(blocks, [bih, bil, bih, brh, brl, brh])
    return real, imag


def rows_columns(size):
    return (
        lax.broadcasted_iota(jnp.int32, (size, size), 0),
        lax.broadcasted_iota(jnp.int32, (size, size), 1),
    )


def packed(block):
    half = block.shape[0] // 2
    row, column = rows_columns(half)
    lower = block[half:, half:]
    mixed = jnp.where(row >= column, block[:half, :half], lower)
    diagonal = jnp.sum(jnp.where(row == column, lower, 0.0), axis=0, keepdims=True)
    return jnp.concatenate(
        [block[:half, half:], mixed, jnp.broadcast_to(diagonal, (8, half))], axis=0
    )


def unpacked(value):
    half = value.shape[1]
    row, column = rows_columns(half)
    right, mixed = value[:half], value[half : 2 * half]
    diagonal = value[2 * half : 2 * half + 1]
    turned = mixed.T
    first = jnp.where(row >= column, mixed, turned)
    last = jnp.where(row < column, mixed, jnp.where(row == column, diagonal, turned))
    return jnp.concatenate(
        [jnp.concatenate([first, right], axis=1), jnp.concatenate([right.T, last], axis=1)], axis=0
    )


def unpacked_split(ref):
    return split_pair(unpacked(ref[0]), unpacked(ref[1]))


def load4(ref):
    return tuple(ref[i] for i in range(4))


def store4(ref, parts):
    for i, part in enumerate(parts):
        ref[i] = part


def whereabouts():
    place = lax.axis_index("snode")
    return place, lax.rem(place, 2), lax.rem(lax.axis_index("pole"), 2)


def hosted_slot():
    place, odd, _ = whereabouts()
    return jnp.where(place < 2, 0, 1 - odd)


def slot_of(hosted):
    return hosted_slot() if hosted else 1 - hosted_slot()


def constants_of(slot, blocks, link, widths, weights, f1s, e, weighted, *_, wait=lambda: None):
    width = blocks.shape[-1]
    row, column = rows_columns(width)
    kept = [column < widths[k] for k in range(2)]
    both = [jnp.logical_and(row < widths[k], kept[k]) for k in range(2)]
    f1 = [jnp.where(kept[1], link[c], 0.0) for c in range(2)]
    s1, t1 = split_pair(*f1), split_pair(f1[0].T, f1[1].T)
    store4(f1s, s1)
    wait()
    d = [[jnp.where(both[k], blocks[k, c], 0.0) for c in range(2)] for k in range(2)]
    br, bi = complex_dot(split_pair(*d[0]), s1)
    tr, ti = complex_dot(t1, split_pair(br, bi))
    er, ei = d[1][0] + tr, d[1][1] + ti
    e[0], e[1] = packed(er), packed(ei)
    w0, w1 = weights[pl.ds(slot, 1), 0:1], weights[pl.ds(slot, 1), 1:2]
    weighted[0] = packed(w1 * d[0][0] + w0 * d[0][1])
    weighted[1] = packed(w1 * er + w0 * ei)
    weighted_b = flat(w1 * br + w0 * bi)
    weighted[2] = weighted_b[: width + 8]
    weighted[3, : width - 8] = weighted_b[width + 8 :]


def fetched_constants(slot, live, pivot, factor, weight, outs, scratch):
    blocks, link, widths, weights, sems = scratch
    first_factor = pltpu.make_async_copy(factor.at[slot, 0], outs[3], sems.at[5])
    copies = [
        pltpu.make_async_copy(live, widths, sems.at[0]),
        pltpu.make_async_copy(factor.at[slot, 1], link, sems.at[1]),
        pltpu.make_async_copy(pivot.at[slot, 0], blocks.at[0], sems.at[2]),
        pltpu.make_async_copy(pivot.at[slot, 1], blocks.at[1], sems.at[3]),
        pltpu.make_async_copy(weight, weights, sems.at[4]),
    ]
    for copy in copies:
        copy.start()
    first_factor.start()
    copies[0].wait()
    copies[1].wait()

    def wait():
        for copy in copies[2:]:
            copy.wait()

    constants_of(slot, blocks, link, widths, weights, *outs, wait=wait)
    first_factor.wait()


def sent_constant_kernel(live, pivot, factor, weight, *refs):
    outs, second, scratch = refs[:4], refs[4:8], refs[8:]
    place, _, core = whereabouts()

    @pl.when(jnp.logical_and(place != 1, core == 0))
    def _():
        fetched_constants(slot_of(True), live, pivot, factor, weight, second, scratch)

    @pl.when(place != 1)
    def _():
        fetched_constants(slot_of(False), live, pivot, factor, weight, outs, scratch)


def first_constant_kernel(live, pivot, factor, weight, *refs):
    made, outs, scratch = refs[:4], refs[4:8], refs[8:]
    place = whereabouts()[0]

    @pl.when(place != 1)
    def _():
        for source, target in zip(made, outs):
            target[...] = source[...]

    @pl.when(place == 1)
    def _():
        fetched_constants(slot_of(False), live, pivot, factor, weight, outs, scratch)


def second_constants(live, pivot, factor, weight, f1s, e, weighted, first_factor):
    slot = slot_of(True)
    first_factor[...] = factor[slot, 0]
    constants_of(slot, pivot.at[slot], factor.at[slot, 1], live, weight, f1s, e, weighted)


def sent_second_kernel(live, pivot, factor, weight, _, *refs):
    made, outs = refs[:4], refs[4:]
    place, _, core = whereabouts()

    @pl.when(core == 0)
    def _():
        for source, target in zip(made, outs):
            target[...] = source[...]

    @pl.when(jnp.logical_and(place != 1, core == 1))
    def _():
        second_constants(live, pivot, factor, weight, *outs)


def second_constant_kernel(live, pivot, factor, weight, *refs):
    made, outs = refs[:4], refs[4:]
    place = whereabouts()[0]

    @pl.when(place != 1)
    def _():
        for source, target in zip(made, outs):
            target[...] = source[...]

    @pl.when(place == 1)
    def _():
        second_constants(live, pivot, factor, weight, *outs)


def factor_kernel(live, factor, f1s, f0s, f0t, gs, gt, g):
    _, column = rows_columns(factor.shape[-1])
    f0 = [jnp.where(column < live[0], factor[c], 0.0) for c in range(2)]
    s0 = split_pair(*f0)
    gr, gi = complex_dot(s0, load4(f1s))
    g[0], g[1] = gr, gi
    store4(gs, split_pair(gr, gi))
    store4(gt, split_pair(gr.T, gi.T))
    store4(f0s, s0)
    store4(f0t, split_pair(f0[0].T, f0[1].T))


def fold(x, gs, gt, e, out):
    tr, ti = complex_dot(x, load4(gs))
    yr, yi = complex_dot(load4(gt), split_pair(tr, ti))
    out[0] = e[0] + packed(yr)
    out[1] = e[1] + packed(yi)


def step_kernel(active, gs, gt, e, *refs):
    *received, out = refs

    @pl.when(active(whereabouts()[0]))
    def _():
        value = received[0][...]
        for other in received[1:]:
            value = value + other[...]
        fold(split_pair(unpacked(value[0]), unpacked(value[1])), gs, gt, e, out)


def pair_kernel(g, e, g_in, e_in, e_second, fas, fat, ea, ps, pt, ep):
    upper = whereabouts()[0] > 1
    is_odd = whereabouts()[1] == 1
    ga = [jnp.where(is_odd, g_in[c], g[c]) for c in range(2)]
    gb = [jnp.where(is_odd, g[c], g_in[c]) for c in range(2)]
    theirs = [jnp.where(upper, e_in[c], e_second[c]) for c in range(2)]
    low = [jnp.where(is_odd, theirs[c], e[c]) for c in range(2)]
    high = [jnp.where(is_odd, e[c], theirs[c]) for c in range(2)]
    sa, sb = split_pair(*ga), split_pair(*gb)
    store4(fas, sa)
    store4(fat, split_pair(ga[0].T, ga[1].T))
    pr, pi = complex_dot(sa, sb)
    store4(ps, split_pair(pr, pi))
    store4(pt, split_pair(pr.T, pi.T))
    br, bi = complex_dot(split_pair(unpacked(low[0]), unpacked(low[1])), sb)
    tr, ti = complex_dot(split_pair(gb[0].T, gb[1].T), split_pair(br, bi))
    for c, term in enumerate((tr, ti)):
        ea[c] = low[c]
        ep[c] = high[c] + packed(term)


def share_kernel(fas, fat, ea, *refs):
    *received, own, sent, scratch = refs
    value = received[0][...]
    for other in received[1:]:
        value = value + other[...]
    value = jnp.where(whereabouts()[0] > 1, value, 0.0)
    fold(split_pair(unpacked(value[0]), unpacked(value[1])), fas, fat, ea, scratch)
    is_odd = whereabouts()[1] == 1
    own[...] = jnp.where(is_odd, scratch[...], value)
    sent[...] = jnp.where(is_odd, value, scratch[...])


def flat(block):
    half = block.shape[1] // 2
    return jnp.concatenate([block[:, :half], block[:, half:]], axis=0)


def real_dot(left, right):
    return dot3(left[0], left[2], right[0], right[2]) + dot3(left[1], left[3], right[1], right[3])


def off_values(slot, weight, xs, f0s, f0t, gs, weighted):
    width = f0s.shape[-1]
    w0, w1 = weight[pl.ds(slot, 1), 0:1], weight[pl.ds(slot, 1), 1:2]
    qr, qi = wide_dot(xs, load4(gs))
    ts = split_pair(w1 * qr + w0 * qi, w0 * qr - w1 * qi)
    second = real_dot(load4(f0t), ts)
    pr, pi = wide_dot(xs, load4(f0s))
    u = w1 * pr + w0 * pi
    us = split_pair(u, w0 * pr - w1 * pi)
    constant = jnp.concatenate([weighted[2], weighted[3, : width - 8]], axis=0)
    return -flat(u), -(flat(second) + constant), us, ts


def diag_values(us, ts, f0t, gt, weighted):
    return (
        weighted[0] + packed(real_dot(load4(f0t), us)),
        weighted[1] + packed(real_dot(load4(gt), ts)),
    )


def density_kernel(weight, x, f0s, f0t, gs, gt, weighted, off, diag):
    core = whereabouts()[2]
    first, second, us, ts = off_values(slot_of(True), weight, unpacked_split(x), f0s, f0t, gs, weighted)
    off[core], off[1 - core] = first, second
    diag[core], diag[1 - core] = diag_values(us, ts, f0t, gt, weighted)


def entering(x, x_first):
    place = whereabouts()[0]
    upper = place > 1
    x = [jnp.where(upper, x[c], x_first[c]) for c in range(2)]
    return split_pair(unpacked(x[0]), unpacked(x[1]))


def more_ahead_kernel(weight, x, x_first, f0s, f0t, gs, gt, weighted, off, diag, kept, sent):
    rows = off.shape[1]

    @pl.when(whereabouts()[2] == 1)
    def _():
        xs = entering(x, x_first)
        first, second, us, ts = off_values(slot_of(False), weight, xs, f0s, f0t, gs, weighted)
        sent[:rows] = first + off[1]
        kept[:rows] = second + off[0]
        first, second = diag_values(us, ts, f0t, gt, weighted)
        sent[rows:] = first + diag[1]
        kept[rows:] = second + diag[0]


def more_off_kernel(weight, x, x_first, f0s, f0t, gs, weighted, before, kept, sent, us_out, ts_out):
    @pl.when(whereabouts()[2] == 0)
    def _():
        xs = entering(x, x_first)
        first, second, us, ts = off_values(slot_of(False), weight, xs, f0s, f0t, gs, weighted)
        kept[...] = first + before[0]
        sent[...] = second + before[1]
        store4(us_out, us)
        store4(ts_out, ts)


def more_diag_kernel(us, ts, f0t, gt, weighted, off_kept, off_sent, before, from1, kept, sent):
    rows = off_kept.shape[0]

    @pl.when(whereabouts()[2] == 0)
    def _():
        first, second = diag_values(load4(us), load4(ts), f0t, gt, weighted)
        kept[:rows] = off_kept[...] + from1[:rows]
        sent[:rows] = off_sent[...]
        kept[rows:] = first + before[0] + from1[rows:]
        sent[rows:] = second + before[1]


def add_kernel(ours, theirs, _, out):
    out[...] = ours[...] + theirs[...]


def unpack_kernel(entry, ours, theirs, *refs):
    diag, off, block, other, sems = refs[-5:]
    width = block.shape[-1]
    half = width // 2
    core = whereabouts()[2]
    for source, here in ((ours, core == entry), (theirs, core != entry)):

        @pl.when(here)
        def _():
            other[:, :half] = source[:width]
            other[:, half:] = source[width : 2 * width]
            block[...] = unpacked(source[2 * width :])

    copies = [
        pltpu.make_async_copy(block, diag.at[entry], sems.at[0]),
        pltpu.make_async_copy(other, off.at[entry], sems.at[1]),
    ]
    for copy in copies:
        copy.start()
    for copy in copies:
        copy.wait()


SCALAR = pl.BlockSpec(memory_space=pltpu.SMEM)
WHOLE = pl.BlockSpec(memory_space=pltpu.VMEM)


COST = pl.CostEstimate(flops=1, bytes_accessed=1, transcendentals=0)


LONG = pl.CostEstimate(flops=10**11, bytes_accessed=1, transcendentals=0)


def run(kernel, scalars, arrays, shapes, scratch=(), cost=COST, far=()):
    return pl.pallas_call(
        kernel,
        out_shape=shapes,
        in_specs=[SCALAR] * len(scalars)
        + [pl.BlockSpec(memory_space=pltpu.HBM)] * len(far)
        + [WHOLE] * len(arrays),
        out_specs=[WHOLE] * len(shapes),
        scratch_shapes=list(scratch),
        compiler_params=pltpu.CompilerParams(vmem_limit_bytes=VMEM_LIMIT),
        cost_estimate=cost,
    )(*scalars, *far, *arrays)


def local(pivot, factor, live, weight):
    poles, turns = lax.axis_size("pole"), lax.axis_size("snode")
    rows = turns // 2
    width = pivot.shape[-1]
    quarter = (width + 8, width // 2)
    mirrored = jax.ShapeDtypeStruct((2,) + quarter, F32)
    parts = jax.ShapeDtypeStruct((4, width, width), BF16)

    def at(pole_index, snode_index):
        return pole_index * turns + snode_index

    def hosts(row, pole):
        return at(pole, 2 * row + 1), at(pole, 2 * row)

    swaps = [(at(p, s), at(p, s ^ 1)) for p in range(poles) for s in range(2, turns)]
    first = [(at(p, 0), at(p, 1)) for p in range(poles)]
    every = [(at(p, s), at(p, s ^ 1)) for p in range(poles) for s in range(turns)]
    raw = jax.ShapeDtypeStruct((2, width, width), F32)
    constants = [parts, mirrored, jax.ShapeDtypeStruct((4,) + quarter, F32), raw]
    factors = [parts, parts, parts, parts, raw]

    scratch = [
        pltpu.VMEM(pivot.shape[1:], F32),
        pltpu.VMEM(factor.shape[2:], F32),
        pltpu.SMEM(live.shape, jnp.int32),
        pltpu.VMEM(weight.shape, F32),
        pltpu.SemaphoreType.DMA((6,)),
    ]
    far = [pltpu.with_memory_space_constraint(a, pltpu.HBM) for a in (live, pivot, factor, weight)]
    made = run(sent_constant_kernel, [], [], constants * 2, scratch, far=far)
    made, second = made[:4], made[4:]
    e_in = lax.ppermute(made[1], AXES, first + swaps)
    o_f1s, o_e, o_w, o_f0 = run(first_constant_kernel, [], made, constants, scratch, far=far)
    o_f0s, o_f0t, o_gs, o_gt, o_g = run(
        factor_kernel, [live], [o_f0, o_f1s], factors
    )
    g_in = lax.ppermute(o_g, AXES, swaps)
    made = run(sent_second_kernel, [live], [pivot, factor, weight, o_g, *second], constants)
    e_second = lax.ppermute(made[1], AXES, first)
    m_f1s, m_e, m_w, m_f0 = run(
        second_constant_kernel, [live], [pivot, factor, weight, *made], constants
    )
    m_f0s, m_f0t, m_gs, m_gt, m_g = run(
        factor_kernel, [live], [m_f0, m_f1s], factors
    )
    starts = functools.partial(step_kernel, lambda place: place == 1)
    (wave_even,) = run(starts, [], [o_gs, o_gt, o_e, e_in], [mirrored])
    wave_even = lax.ppermute(wave_even, AXES, [(at(p, 1), at(p, 0)) for p in range(poles)])
    (wave_odd,) = run(starts, [], [m_gs, m_gt, m_e, e_second], [mirrored])
    received = []
    if rows > 1:
        received = [
            lax.ppermute(wave_odd, AXES, [(at(p, 1), at(p, 3)) for p in range(poles)]),
            lax.ppermute(wave_even, AXES, [(at(p, 0), at(p, 2)) for p in range(poles)]),
        ]
    else:
        received = [jnp.zeros(mirrored.shape, F32)]
    fas, fat, ea, ps, pt, ep = run(
        pair_kernel,
        [],
        [m_g, m_e, g_in, e_in, e_second],
        [parts, parts, mirrored, parts, parts, mirrored],
        cost=LONG,
    )
    arrived = list(received)
    for turn in range(1, rows - 1):
        active = functools.partial(step_kernel, lambda place, turn=turn: lax.div(place, 2) == turn)
        (wave,) = run(active, [], [ps, pt, ep] + arrived, [mirrored])
        up = [pair for p in range(poles) for pair in zip(hosts(turn, p), hosts(turn + 1, p))]
        arrived = [lax.ppermute(wave, AXES, up)]
        received += arrived
    own, sent = run(
        share_kernel,
        [],
        [fas, fat, ea] + received,
        [mirrored, mirrored],
        [pltpu.VMEM(mirrored.shape, F32)],
    )
    shared = lax.ppermute(sent, AXES, every)

    offs = jax.ShapeDtypeStruct((2, 2 * width, width // 2), F32)
    diags = jax.ShapeDtypeStruct((2,) + quarter, F32)
    off, diag = run(density_kernel, [], [weight, own, m_f0s, m_f0t, m_gs, m_gt, m_w], [offs, diags])
    flat_off = jax.ShapeDtypeStruct(offs.shape[1:], F32)
    both = jax.ShapeDtypeStruct((offs.shape[1] + quarter[0], quarter[1]), F32)

    def to_core(core, value):
        return lax.ppermute(value, "pole", [(p ^ 1, p) for p in range(core, poles, 2)])

    kept1, sent1 = run(
        more_ahead_kernel,
        [],
        [weight, shared, e_in, o_f0s, o_f0t, o_gs, o_gt, o_w, off, diag],
        [both, both],
    )
    from1 = to_core(0, sent1)
    off_kept, off_sent, us, ts = run(
        more_off_kernel,
        [],
        [weight, shared, e_in, o_f0s, o_f0t, o_gs, o_w, off],
        [flat_off, flat_off, parts, parts],
    )
    kept0, sent0 = run(
        more_diag_kernel,
        [],
        [us, ts, o_f0t, o_gt, o_w, off_kept, off_sent, diag, from1],
        [both, both],
    )

    def over_poles(value, core):
        distance, other = 2, jnp.zeros_like(value)
        while distance < poles:
            other = lax.ppermute(value, "pole", [(p, p ^ distance) for p in range(core, poles, 2)])
            distance *= 2
            if distance < poles:
                value = value + other
        return value, other

    from0 = to_core(1, sent0)
    kept0, other0 = over_poles(kept0, 0)
    (total0,) = run(add_kernel, [], [kept0, other0, other0], [both])
    (kept1,) = run(add_kernel, [], [kept1, from0, other0], [both])
    theirs0 = to_core(1, total0)
    kept1, other1 = over_poles(kept1, 1)
    (total1,) = run(add_kernel, [], [kept1, other1, other1], [both])
    theirs1 = to_core(0, total1)

    anywhere = pl.BlockSpec(memory_space=pl.ANY)
    outs = [jax.ShapeDtypeStruct((2, width, width), F32)] * 2
    for entry, ours, theirs in ((0, total0, theirs0), (1, total1, theirs1)):
        written = [] if entry == 0 else list(outs)
        outs = pl.pallas_call(
            functools.partial(unpack_kernel, entry),
            out_shape=[jax.ShapeDtypeStruct((2, width, width), F32)] * 2,
            in_specs=[WHOLE] * 2 + [anywhere] * len(written),
            out_specs=[anywhere] * 2,
            scratch_shapes=[pltpu.VMEM((width, width), F32)] * 2 + [pltpu.SemaphoreType.DMA((2,))],
            input_output_aliases={2: 0, 3: 1} if written else {},
            compiler_params=pltpu.CompilerParams(vmem_limit_bytes=VMEM_LIMIT),
            cost_estimate=COST,
        )(ours, theirs, *written)
    return tuple(outs)


def solution(mesh):
    placed = (
        P("pole", "snode", None, None, None),
        P("pole", "snode", None, None, None),
        P("snode"),
        P("pole", None),
    )
    return jax.shard_map(
        local,
        mesh=mesh,
        in_specs=placed,
        out_specs=(P("snode", None, None), P("snode", None, None)),
        check_vma=False,
    )
```

```python
import functools

import jax
import jax.numpy as jnp
from jax import lax
from jax.experimental import pallas as pl
from jax.experimental.pallas import tpu as pltpu
from jax.sharding import PartitionSpec as P

F32 = jnp.float32
BF16 = jnp.bfloat16
AXES = ("pole", "snode")
VMEM_LIMIT = 16 * 1024 * 1024


def halves(value):
    high = value.astype(BF16)
    return high, (value - high.astype(F32)).astype(BF16)


def split_pair(real, imag):
    (rh, rl), (ih, il) = halves(real), halves(imag)
    return rh, ih, rl, il


def deep_dot(left, right):
    return jnp.dot(
        jnp.concatenate(left, axis=1), jnp.concatenate(right, axis=0), preferred_element_type=F32
    )


def dot(left, right):
    return jnp.dot(left, right, preferred_element_type=F32)


def dot3(lh, ll, rh, rl):
    return dot(lh, rh) + (dot(lh, rl) + dot(ll, rh))


def wide_dot(left, right):
    arh, aih, arl, ail = left
    brh, bih, brl, bil = right
    real = dot3(arh, arl, brh, brl) - dot3(aih, ail, bih, bil)
    imag = dot3(arh, arl, bih, bil) + dot3(aih, ail, brh, brl)
    return real, imag


def complex_dot(left, right):
    arh, aih, arl, ail = left
    brh, bih, brl, bil = right
    blocks = [arh, arh, arl, aih, aih, ail]
    real = deep_dot(blocks, [brh, brl, brh, -bih, -bil, -bih])
    imag = deep_dot(blocks, [bih, bil, bih, brh, brl, brh])
    return real, imag


def rows_columns(size):
    return (
        lax.broadcasted_iota(jnp.int32, (size, size), 0),
        lax.broadcasted_iota(jnp.int32, (size, size), 1),
    )


def packed(block):
    half = block.shape[0] // 2
    row, column = rows_columns(half)
    lower = block[half:, half:]
    mixed = jnp.where(row >= column, block[:half, :half], lower)
    diagonal = jnp.sum(jnp.where(row == column, lower, 0.0), axis=0, keepdims=True)
    return jnp.concatenate(
        [block[:half, half:], mixed, jnp.broadcast_to(diagonal, (8, half))], axis=0
    )


def unpacked(value):
    half = value.shape[1]
    row, column = rows_columns(half)
    right, mixed = value[:half], value[half : 2 * half]
    diagonal = value[2 * half : 2 * half + 1]
    turned = mixed.T
    first = jnp.where(row >= column, mixed, turned)
    last = jnp.where(row < column, mixed, jnp.where(row == column, diagonal, turned))
    return jnp.concatenate(
        [jnp.concatenate([first, right], axis=1), jnp.concatenate([right.T, last], axis=1)], axis=0
    )


def unpacked_split(ref):
    return split_pair(unpacked(ref[0]), unpacked(ref[1]))


def load4(ref):
    return tuple(ref[i] for i in range(4))


def store4(ref, parts):
    for i, part in enumerate(parts):
        ref[i] = part


def whereabouts():
    place = lax.axis_index("snode")
    return place, lax.rem(place, 2), lax.rem(lax.axis_index("pole"), 2)


def hosted_slot():
    place, odd, _ = whereabouts()
    return jnp.where(place < 2, 0, 1 - odd)


def slot_of(hosted):
    return hosted_slot() if hosted else 1 - hosted_slot()


def constants_of(slot, blocks, link, widths, weights, f1s, e, weighted, *_, wait=lambda: None):
    width = blocks.shape[-1]
    row, column = rows_columns(width)
    kept = [column < widths[k] for k in range(2)]
    both = [jnp.logical_and(row < widths[k], kept[k]) for k in range(2)]
    f1 = [jnp.where(kept[1], link[c], 0.0) for c in range(2)]
    s1, t1 = split_pair(*f1), split_pair(f1[0].T, f1[1].T)
    store4(f1s, s1)
    wait()
    d = [[jnp.where(both[k], blocks[k, c], 0.0) for c in range(2)] for k in range(2)]
    br, bi = complex_dot(split_pair(*d[0]), s1)
    tr, ti = complex_dot(t1, split_pair(br, bi))
    er, ei = d[1][0] + tr, d[1][1] + ti
    e[0], e[1] = packed(er), packed(ei)
    w0, w1 = weights[pl.ds(slot, 1), 0:1], weights[pl.ds(slot, 1), 1:2]
    weighted[0] = packed(w1 * d[0][0] + w0 * d[0][1])
    weighted[1] = packed(w1 * er + w0 * ei)
    weighted_b = flat(w1 * br + w0 * bi)
    weighted[2] = weighted_b[: width + 8]
    weighted[3, : width - 8] = weighted_b[width + 8 :]


def fetched_constants(slot, live, pivot, factor, weight, outs, scratch):
    blocks, link, widths, weights, sems = scratch
    first_factor = pltpu.make_async_copy(factor.at[slot, 0], outs[3], sems.at[5])
    copies = [
        pltpu.make_async_copy(live, widths, sems.at[0]),
        pltpu.make_async_copy(factor.at[slot, 1], link, sems.at[1]),
        pltpu.make_async_copy(pivot.at[slot, 0], blocks.at[0], sems.at[2]),
        pltpu.make_async_copy(pivot.at[slot, 1], blocks.at[1], sems.at[3]),
        pltpu.make_async_copy(weight, weights, sems.at[4]),
    ]
    for copy in copies:
        copy.start()
    first_factor.start()
    copies[0].wait()
    copies[1].wait()

    def wait():
        for copy in copies[2:]:
            copy.wait()

    constants_of(slot, blocks, link, widths, weights, *outs, wait=wait)
    first_factor.wait()


def sent_constant_kernel(live, pivot, factor, weight, *refs):
    outs, second, scratch = refs[:4], refs[4:8], refs[8:]
    place, _, core = whereabouts()

    @pl.when(jnp.logical_and(place != 1, core == 0))
    def _():
        fetched_constants(slot_of(True), live, pivot, factor, weight, second, scratch)

    @pl.when(place != 1)
    def _():
        fetched_constants(slot_of(False), live, pivot, factor, weight, outs, scratch)


def first_constant_kernel(live, pivot, factor, weight, *refs):
    made, outs, scratch = refs[:4], refs[4:8], refs[8:]
    place = whereabouts()[0]

    @pl.when(place != 1)
    def _():
        for source, target in zip(made, outs):
            target[...] = source[...]

    @pl.when(place == 1)
    def _():
        fetched_constants(slot_of(False), live, pivot, factor, weight, outs, scratch)


def second_constants(live, pivot, factor, weight, f1s, e, weighted, first_factor):
    slot = slot_of(True)
    first_factor[...] = factor[slot, 0]
    constants_of(slot, pivot.at[slot], factor.at[slot, 1], live, weight, f1s, e, weighted)


def sent_second_kernel(live, pivot, factor, weight, _, *refs):
    made, outs = refs[:4], refs[4:]
    place, _, core = whereabouts()

    @pl.when(core == 0)
    def _():
        for source, target in zip(made, outs):
            target[...] = source[...]

    @pl.when(jnp.logical_and(place != 1, core == 1))
    def _():
        second_constants(live, pivot, factor, weight, *outs)


def second_constant_kernel(live, pivot, factor, weight, *refs):
    made, outs = refs[:4], refs[4:]
    place = whereabouts()[0]

    @pl.when(place != 1)
    def _():
        for source, target in zip(made, outs):
            target[...] = source[...]

    @pl.when(place == 1)
    def _():
        second_constants(live, pivot, factor, weight, *outs)


def factor_kernel(live, factor, f1s, f0s, f0t, gs, gt, g):
    _, column = rows_columns(factor.shape[-1])
    f0 = [jnp.where(column < live[0], factor[c], 0.0) for c in range(2)]
    s0 = split_pair(*f0)
    gr, gi = complex_dot(s0, load4(f1s))
    g[0], g[1] = gr, gi
    store4(gs, split_pair(gr, gi))
    store4(gt, split_pair(gr.T, gi.T))
    store4(f0s, s0)
    store4(f0t, split_pair(f0[0].T, f0[1].T))


def fold(x, gs, gt, e, out):
    tr, ti = complex_dot(x, load4(gs))
    yr, yi = complex_dot(load4(gt), split_pair(tr, ti))
    out[0] = e[0] + packed(yr)
    out[1] = e[1] + packed(yi)


def start_kernel(gs, gt, e, x, out):
    @pl.when(whereabouts()[0] == 1)
    def _():
        fold(unpacked_split(x), gs, gt, e, out)


def choose(row, odd, up, relay, later, out):
    @pl.when(row == 0)
    def _():
        out[...] = jnp.zeros_like(out)

    @pl.when(jnp.logical_and(row == 1, odd == 1))
    def _():
        out[...] = up[...]

    @pl.when(jnp.logical_and(row == 1, odd == 0))
    def _():
        out[...] = relay[...]

    for turn, ref in enumerate(later, 2):

        @pl.when(row == turn)
        def _():
            out[...] = ref[...]


def second_row_kernel(gs, gt, e, up, relay, out):
    place, odd, _ = whereabouts()
    for value, column in ((relay, 0), (up, 1)):

        @pl.when(jnp.logical_and(lax.div(place, 2) == 1, odd == column))
        def _():
            fold(unpacked_split(value), gs, gt, e, out)


def step_kernel(turn, gs, gt, e, x, out):
    @pl.when(lax.div(whereabouts()[0], 2) == turn)
    def _():
        fold(unpacked_split(x), gs, gt, e, out)


def pair_kernel(g, e, g_in, e_in, e_second, fas, fat, ea, ps, pt, ep):
    upper = whereabouts()[0] > 1
    is_odd = whereabouts()[1] == 1
    ga = [jnp.where(is_odd, g_in[c], g[c]) for c in range(2)]
    gb = [jnp.where(is_odd, g[c], g_in[c]) for c in range(2)]
    theirs = [jnp.where(upper, e_in[c], e_second[c]) for c in range(2)]
    low = [jnp.where(is_odd, theirs[c], e[c]) for c in range(2)]
    high = [jnp.where(is_odd, e[c], theirs[c]) for c in range(2)]
    sa, sb = split_pair(*ga), split_pair(*gb)
    store4(fas, sa)
    store4(fat, split_pair(ga[0].T, ga[1].T))
    pr, pi = complex_dot(sa, sb)
    store4(ps, split_pair(pr, pi))
    store4(pt, split_pair(pr.T, pi.T))
    br, bi = complex_dot(split_pair(unpacked(low[0]), unpacked(low[1])), sb)
    tr, ti = complex_dot(split_pair(gb[0].T, gb[1].T), split_pair(br, bi))
    for c, term in enumerate((tr, ti)):
        ea[c] = low[c]
        ep[c] = high[c] + packed(term)


def share_kernel(fas, fat, ea, up, relay, *refs):
    *later, own, sent, value, scratch = refs
    place, odd, _ = whereabouts()
    choose(lax.div(place, 2), odd, up, relay, later, value)
    fold(unpacked_split(value), fas, fat, ea, scratch)
    is_odd = odd == 1
    own[...] = jnp.where(is_odd, scratch[...], value[...])
    sent[...] = jnp.where(is_odd, value[...], scratch[...])


def flat(block):
    half = block.shape[1] // 2
    return jnp.concatenate([block[:, :half], block[:, half:]], axis=0)


def real_dot(left, right):
    return dot3(left[0], left[2], right[0], right[2]) + dot3(left[1], left[3], right[1], right[3])


def off_values(slot, weight, xs, f0s, f0t, gs, weighted):
    width = f0s.shape[-1]
    w0, w1 = weight[pl.ds(slot, 1), 0:1], weight[pl.ds(slot, 1), 1:2]
    qr, qi = wide_dot(xs, load4(gs))
    ts = split_pair(w1 * qr + w0 * qi, w0 * qr - w1 * qi)
    second = real_dot(load4(f0t), ts)
    pr, pi = wide_dot(xs, load4(f0s))
    u = w1 * pr + w0 * pi
    us = split_pair(u, w0 * pr - w1 * pi)
    constant = jnp.concatenate([weighted[2], weighted[3, : width - 8]], axis=0)
    return -flat(u), -(flat(second) + constant), us, ts


def diag_values(us, ts, f0t, gt, weighted):
    return (
        weighted[0] + packed(real_dot(load4(f0t), us)),
        weighted[1] + packed(real_dot(load4(gt), ts)),
    )


def density_kernel(weight, x, f0s, f0t, gs, gt, weighted, off, diag):
    core = whereabouts()[2]
    first, second, us, ts = off_values(slot_of(True), weight, unpacked_split(x), f0s, f0t, gs, weighted)
    off[core], off[1 - core] = first, second
    diag[core], diag[1 - core] = diag_values(us, ts, f0t, gt, weighted)


def more_off_kernel(weight, x, x_first, f0s, f0t, gs, weighted, before, off, us_out, ts_out):
    core = whereabouts()[2]
    place = whereabouts()[0]
    x = [
        jnp.where(place > 1, x[c], jnp.where(place == 1, x_first[c], 0.0)) for c in range(2)
    ]
    xs = split_pair(unpacked(x[0]), unpacked(x[1]))
    first, second, us, ts = off_values(slot_of(False), weight, xs, f0s, f0t, gs, weighted)
    off[core] = first + before[core]
    off[1 - core] = second + before[1 - core]
    store4(us_out, us)
    store4(ts_out, ts)


def more_diag_kernel(us, ts, f0t, gt, weighted, before, diag):
    core = whereabouts()[2]
    first, second = diag_values(load4(us), load4(ts), f0t, gt, weighted)
    diag[core] = first + before[core]
    diag[1 - core] = second + before[1 - core]


def unpack_off_kernel(mine, theirs, off, done):
    core = whereabouts()[2]
    width = off.shape[-1]
    half = width // 2
    for source, entry in ((mine, core), (theirs, 1 - core)):
        off[entry, :, :half] = source[:width]
        off[entry, :, half:] = source[width:]
    done[...] = jnp.zeros_like(done)


def unpack_diag_kernel(mine, theirs, _, diag):
    core = whereabouts()[2]
    for source, entry in ((mine, core), (theirs, 1 - core)):
        diag[entry] = unpacked(source[...])


SCALAR = pl.BlockSpec(memory_space=pltpu.SMEM)
WHOLE = pl.BlockSpec(memory_space=pltpu.VMEM)


COST = pl.CostEstimate(flops=1, bytes_accessed=1, transcendentals=0)


LONG = pl.CostEstimate(flops=10**11, bytes_accessed=1, transcendentals=0)


def run(kernel, scalars, arrays, shapes, scratch=(), cost=COST, far=()):
    return pl.pallas_call(
        kernel,
        out_shape=shapes,
        in_specs=[SCALAR] * len(scalars)
        + [pl.BlockSpec(memory_space=pltpu.HBM)] * len(far)
        + [WHOLE] * len(arrays),
        out_specs=[WHOLE] * len(shapes),
        scratch_shapes=list(scratch),
        compiler_params=pltpu.CompilerParams(vmem_limit_bytes=VMEM_LIMIT),
        cost_estimate=cost,
    )(*scalars, *far, *arrays)


def local(pivot, factor, live, weight):
    poles, turns = lax.axis_size("pole"), lax.axis_size("snode")
    rows = turns // 2
    width = pivot.shape[-1]
    quarter = (width + 8, width // 2)
    mirrored = jax.ShapeDtypeStruct((2,) + quarter, F32)
    parts = jax.ShapeDtypeStruct((4, width, width), BF16)

    def at(pole_index, snode_index):
        return pole_index * turns + snode_index

    def permuted(value, pairs):
        partner = dict(pairs) | {t: s for s, t in pairs}
        return lax.ppermute(
            value,
            AXES,
            [(at(p, s), at(p, partner.get(s, s))) for p in range(poles) for s in range(turns)],
        )

    neighbours = [(s, s + 1) for s in range(0, turns, 2)]

    raw = jax.ShapeDtypeStruct((2, width, width), F32)
    constants = [parts, mirrored, jax.ShapeDtypeStruct((4,) + quarter, F32), raw]
    factors = [parts, parts, parts, parts, raw]

    scratch = [
        pltpu.VMEM(pivot.shape[1:], F32),
        pltpu.VMEM(factor.shape[2:], F32),
        pltpu.SMEM(live.shape, jnp.int32),
        pltpu.VMEM(weight.shape, F32),
        pltpu.SemaphoreType.DMA((6,)),
    ]
    far = [pltpu.with_memory_space_constraint(a, pltpu.HBM) for a in (live, pivot, factor, weight)]
    made = run(sent_constant_kernel, [], [], constants * 2, scratch, far=far)
    made, second = made[:4], made[4:]
    e_in = permuted(made[1], neighbours)
    o_f1s, o_e, o_w, o_f0 = run(first_constant_kernel, [], made, constants, scratch, far=far)
    o_f0s, o_f0t, o_gs, o_gt, o_g = run(
        factor_kernel, [live], [o_f0, o_f1s], factors
    )
    g_in = permuted(o_g, neighbours[1:])
    made = run(sent_second_kernel, [live], [pivot, factor, weight, o_g, *second], constants)
    e_second = permuted(made[1], neighbours[:1])
    m_f1s, m_e, m_w, m_f0 = run(
        second_constant_kernel, [live], [pivot, factor, weight, *made], constants
    )
    m_f0s, m_f0t, m_gs, m_gt, m_g = run(
        factor_kernel, [live], [m_f0, m_f1s], factors
    )
    (wave_even,) = run(start_kernel, [], [o_gs, o_gt, o_e, e_in], [mirrored])
    wave_even = permuted(wave_even, neighbours[:1])
    (wave_odd,) = run(start_kernel, [], [m_gs, m_gt, m_e, e_second], [mirrored])
    up = permuted(wave_odd, [(1, 3)])
    relay = permuted(wave_even, [(0, 2)])
    fas, fat, ea, ps, pt, ep = run(
        pair_kernel,
        [],
        [m_g, m_e, g_in, e_in, e_second],
        [parts, parts, mirrored, parts, parts, mirrored],
        cost=LONG,
    )
    later = []
    for turn in range(1, rows - 1):
        if turn == 1:
            (wave,) = run(second_row_kernel, [], [ps, pt, ep, up, relay], [mirrored])
        else:
            step = functools.partial(step_kernel, turn)
            (wave,) = run(step, [], [ps, pt, ep, later[-1]], [mirrored])
        here = 2 * turn
        later.append(permuted(wave, [(here, here + 2), (here + 1, here + 3)]))
    own, sent = run(
        share_kernel,
        [],
        [fas, fat, ea, up, relay, *later],
        [mirrored, mirrored],
        [pltpu.VMEM(mirrored.shape, F32)] * 2,
    )
    shared = permuted(sent, neighbours)

    offs = jax.ShapeDtypeStruct((2, 2 * width, width // 2), F32)
    diags = jax.ShapeDtypeStruct((2,) + quarter, F32)
    off, diag = run(density_kernel, [], [weight, own, m_f0s, m_f0t, m_gs, m_gt, m_w], [offs, diags])
    off, us, ts = run(
        more_off_kernel,
        [],
        [weight, shared, e_in, o_f0s, o_f0t, o_gs, o_w, off],
        [offs, parts, parts],
    )

    def exchanged(value, distance):
        return lax.ppermute(value, "pole", [(p, p ^ distance) for p in range(poles)])

    def summed(parts):
        kept = parts[0] + exchanged(parts[1], 1)
        distance = 2
        while distance < poles:
            kept = kept + exchanged(kept, distance)
            distance *= 2
        return kept, exchanged(kept, 1)

    full = jax.ShapeDtypeStruct((2, width, width), F32)
    off_sums = summed(off)
    (diag,) = run(more_diag_kernel, [], [us, ts, o_f0t, o_gt, o_w, diag], [diags])
    diag_sums = summed(diag)
    done = jax.ShapeDtypeStruct((8, 128), F32)
    density_off, done = run(unpack_off_kernel, [], list(off_sums), [full, done])
    (density_diag,) = run(unpack_diag_kernel, [], [*diag_sums, done], [full])
    return density_diag, density_off


def solution(mesh):
    placed = (
        P("pole", "snode", None, None, None),
        P("pole", "snode", None, None, None),
        P("snode"),
        P("pole", None),
    )
    return jax.shard_map(
        local,
        mesh=mesh,
        in_specs=placed,
        out_specs=(P("snode", None, None), P("snode", None, None)),
        check_vma=False,
    )
```

```python
import functools

import jax
import jax.numpy as jnp
from jax import lax
from jax.experimental import pallas as pl
from jax.experimental.pallas import tpu as pltpu
from jax.sharding import PartitionSpec as P

F32 = jnp.float32
BF16 = jnp.bfloat16
AXES = ("pole", "snode")
VMEM_LIMIT = 16 * 1024 * 1024


def halves(value):
    high = value.astype(BF16)
    return high, (value - high.astype(F32)).astype(BF16)


def split_pair(real, imag):
    (rh, rl), (ih, il) = halves(real), halves(imag)
    return rh, ih, rl, il


def deep_dot(left, right):
    return jnp.dot(
        jnp.concatenate(left, axis=1), jnp.concatenate(right, axis=0), preferred_element_type=F32
    )


def dot(left, right):
    return jnp.dot(left, right, preferred_element_type=F32)


def dot3(lh, ll, rh, rl):
    return dot(lh, rh) + (dot(lh, rl) + dot(ll, rh))


def wide_dot(left, right):
    arh, aih, arl, ail = left
    brh, bih, brl, bil = right
    real = dot3(arh, arl, brh, brl) - dot3(aih, ail, bih, bil)
    imag = dot3(arh, arl, bih, bil) + dot3(aih, ail, brh, brl)
    return real, imag


def complex_dot(left, right):
    arh, aih, arl, ail = left
    brh, bih, brl, bil = right
    blocks = [arh, arh, arl, aih, aih, ail]
    real = deep_dot(blocks, [brh, brl, brh, -bih, -bil, -bih])
    imag = deep_dot(blocks, [bih, bil, bih, brh, brl, brh])
    return real, imag


def rows_columns(size):
    return (
        lax.broadcasted_iota(jnp.int32, (size, size), 0),
        lax.broadcasted_iota(jnp.int32, (size, size), 1),
    )


def packed(block):
    half = block.shape[0] // 2
    row, column = rows_columns(half)
    lower = block[half:, half:]
    mixed = jnp.where(row >= column, block[:half, :half], lower)
    diagonal = jnp.sum(jnp.where(row == column, lower, 0.0), axis=0, keepdims=True)
    return jnp.concatenate(
        [block[:half, half:], mixed, jnp.broadcast_to(diagonal, (8, half))], axis=0
    )


def unpacked(value):
    half = value.shape[1]
    row, column = rows_columns(half)
    right, mixed = value[:half], value[half : 2 * half]
    diagonal = value[2 * half : 2 * half + 1]
    turned = mixed.T
    first = jnp.where(row >= column, mixed, turned)
    last = jnp.where(row < column, mixed, jnp.where(row == column, diagonal, turned))
    return jnp.concatenate(
        [jnp.concatenate([first, right], axis=1), jnp.concatenate([right.T, last], axis=1)], axis=0
    )


def unpacked_split(ref):
    return split_pair(unpacked(ref[0]), unpacked(ref[1]))


def load4(ref):
    return tuple(ref[i] for i in range(4))


def store4(ref, parts):
    for i, part in enumerate(parts):
        ref[i] = part


def whereabouts():
    place = lax.axis_index("snode")
    return place, lax.rem(place, 2), lax.rem(lax.axis_index("pole"), 2)


def hosted_slot():
    place, odd, _ = whereabouts()
    return jnp.where(place < 2, 0, 1 - odd)


def slot_of(hosted):
    return hosted_slot() if hosted else 1 - hosted_slot()


def constants_of(slot, blocks, link, widths, weights, f1s, e, weighted, *_, wait=lambda: None):
    width = blocks.shape[-1]
    row, column = rows_columns(width)
    kept = [column < widths[k] for k in range(2)]
    both = [jnp.logical_and(row < widths[k], kept[k]) for k in range(2)]
    f1 = [jnp.where(kept[1], link[c], 0.0) for c in range(2)]
    s1, t1 = split_pair(*f1), split_pair(f1[0].T, f1[1].T)
    store4(f1s, s1)
    wait()
    d = [[jnp.where(both[k], blocks[k, c], 0.0) for c in range(2)] for k in range(2)]
    br, bi = complex_dot(split_pair(*d[0]), s1)
    tr, ti = complex_dot(t1, split_pair(br, bi))
    er, ei = d[1][0] + tr, d[1][1] + ti
    e[0], e[1] = packed(er), packed(ei)
    w0, w1 = weights[pl.ds(slot, 1), 0:1], weights[pl.ds(slot, 1), 1:2]
    weighted[0] = packed(w1 * d[0][0] + w0 * d[0][1])
    weighted[1] = packed(w1 * er + w0 * ei)
    weighted_b = flat(w1 * br + w0 * bi)
    weighted[2] = weighted_b[: width + 8]
    weighted[3, : width - 8] = weighted_b[width + 8 :]


def fetched_constants(slot, live, pivot, factor, weight, outs, scratch):
    blocks, link, widths, weights, sems = scratch
    first_factor = pltpu.make_async_copy(factor.at[slot, 0], outs[3], sems.at[5])
    copies = [
        pltpu.make_async_copy(live, widths, sems.at[0]),
        pltpu.make_async_copy(factor.at[slot, 1], link, sems.at[1]),
        pltpu.make_async_copy(pivot.at[slot, 0], blocks.at[0], sems.at[2]),
        pltpu.make_async_copy(pivot.at[slot, 1], blocks.at[1], sems.at[3]),
        pltpu.make_async_copy(weight, weights, sems.at[4]),
    ]
    for copy in copies:
        copy.start()
    first_factor.start()
    copies[0].wait()
    copies[1].wait()

    def wait():
        for copy in copies[2:]:
            copy.wait()

    constants_of(slot, blocks, link, widths, weights, *outs, wait=wait)
    first_factor.wait()


def sent_constant_kernel(live, pivot, factor, weight, *refs):
    outs, second, scratch = refs[:4], refs[4:8], refs[8:]
    place, _, core = whereabouts()

    @pl.when(jnp.logical_and(place != 1, core == 0))
    def _():
        fetched_constants(slot_of(True), live, pivot, factor, weight, second, scratch)

    @pl.when(place != 1)
    def _():
        fetched_constants(slot_of(False), live, pivot, factor, weight, outs, scratch)


def first_constant_kernel(live, pivot, factor, weight, *refs):
    made, outs, scratch = refs[:4], refs[4:8], refs[8:]
    place = whereabouts()[0]

    @pl.when(place != 1)
    def _():
        for source, target in zip(made, outs):
            target[...] = source[...]

    @pl.when(place == 1)
    def _():
        fetched_constants(slot_of(False), live, pivot, factor, weight, outs, scratch)


def second_constants(live, pivot, factor, weight, f1s, e, weighted, first_factor):
    slot = slot_of(True)
    first_factor[...] = factor[slot, 0]
    constants_of(slot, pivot.at[slot], factor.at[slot, 1], live, weight, f1s, e, weighted)


def sent_second_kernel(live, pivot, factor, weight, _, *refs):
    made, outs = refs[:4], refs[4:]
    place, _, core = whereabouts()

    @pl.when(core == 0)
    def _():
        for source, target in zip(made, outs):
            target[...] = source[...]

    @pl.when(jnp.logical_and(place != 1, core == 1))
    def _():
        second_constants(live, pivot, factor, weight, *outs)


def second_constant_kernel(live, pivot, factor, weight, *refs):
    made, outs = refs[:4], refs[4:]
    place = whereabouts()[0]

    @pl.when(place != 1)
    def _():
        for source, target in zip(made, outs):
            target[...] = source[...]

    @pl.when(place == 1)
    def _():
        second_constants(live, pivot, factor, weight, *outs)


def factor_kernel(live, factor, f1s, f0s, f0t, gs, gt, g):
    _, column = rows_columns(factor.shape[-1])
    f0 = [jnp.where(column < live[0], factor[c], 0.0) for c in range(2)]
    s0 = split_pair(*f0)
    gr, gi = complex_dot(s0, load4(f1s))
    g[0], g[1] = gr, gi
    store4(gs, split_pair(gr, gi))
    store4(gt, split_pair(gr.T, gi.T))
    store4(f0s, s0)
    store4(f0t, split_pair(f0[0].T, f0[1].T))


def fold(x, gs, gt, e, out):
    tr, ti = complex_dot(x, load4(gs))
    yr, yi = complex_dot(load4(gt), split_pair(tr, ti))
    out[0] = e[0] + packed(yr)
    out[1] = e[1] + packed(yi)


def step_kernel(active, gs, gt, e, *refs):
    *received, out = refs

    @pl.when(active(whereabouts()[0]))
    def _():
        value = received[0][...]
        for other in received[1:]:
            value = value + other[...]
        fold(split_pair(unpacked(value[0]), unpacked(value[1])), gs, gt, e, out)


def pair_kernel(g, e, g_in, e_in, e_second, fas, fat, ea, ps, pt, ep):
    upper = whereabouts()[0] > 1
    is_odd = whereabouts()[1] == 1
    ga = [jnp.where(is_odd, g_in[c], g[c]) for c in range(2)]
    gb = [jnp.where(is_odd, g[c], g_in[c]) for c in range(2)]
    theirs = [jnp.where(upper, e_in[c], e_second[c]) for c in range(2)]
    low = [jnp.where(is_odd, theirs[c], e[c]) for c in range(2)]
    high = [jnp.where(is_odd, e[c], theirs[c]) for c in range(2)]
    sa, sb = split_pair(*ga), split_pair(*gb)
    store4(fas, sa)
    store4(fat, split_pair(ga[0].T, ga[1].T))
    pr, pi = complex_dot(sa, sb)
    store4(ps, split_pair(pr, pi))
    store4(pt, split_pair(pr.T, pi.T))
    br, bi = complex_dot(split_pair(unpacked(low[0]), unpacked(low[1])), sb)
    tr, ti = complex_dot(split_pair(gb[0].T, gb[1].T), split_pair(br, bi))
    for c, term in enumerate((tr, ti)):
        ea[c] = low[c]
        ep[c] = high[c] + packed(term)


def share_kernel(fas, fat, ea, *refs):
    *received, own, sent, scratch = refs
    value = received[0][...]
    for other in received[1:]:
        value = value + other[...]
    value = jnp.where(whereabouts()[0] > 1, value, 0.0)
    fold(split_pair(unpacked(value[0]), unpacked(value[1])), fas, fat, ea, scratch)
    is_odd = whereabouts()[1] == 1
    own[...] = jnp.where(is_odd, scratch[...], value)
    sent[...] = jnp.where(is_odd, value, scratch[...])


def flat(block):
    half = block.shape[1] // 2
    return jnp.concatenate([block[:, :half], block[:, half:]], axis=0)


def real_dot(left, right):
    return dot3(left[0], left[2], right[0], right[2]) + dot3(left[1], left[3], right[1], right[3])


def off_values(slot, weight, xs, f0s, f0t, gs, weighted):
    width = f0s.shape[-1]
    w0, w1 = weight[pl.ds(slot, 1), 0:1], weight[pl.ds(slot, 1), 1:2]
    qr, qi = wide_dot(xs, load4(gs))
    ts = split_pair(w1 * qr + w0 * qi, w0 * qr - w1 * qi)
    second = real_dot(load4(f0t), ts)
    pr, pi = wide_dot(xs, load4(f0s))
    u = w1 * pr + w0 * pi
    us = split_pair(u, w0 * pr - w1 * pi)
    constant = jnp.concatenate([weighted[2], weighted[3, : width - 8]], axis=0)
    return -flat(u), -(flat(second) + constant), us, ts


def diag_values(us, ts, f0t, gt, weighted):
    return (
        weighted[0] + packed(real_dot(load4(f0t), us)),
        weighted[1] + packed(real_dot(load4(gt), ts)),
    )


def density_kernel(weight, x, f0s, f0t, gs, gt, weighted, off, diag):
    core = whereabouts()[2]
    first, second, us, ts = off_values(slot_of(True), weight, unpacked_split(x), f0s, f0t, gs, weighted)
    off[core], off[1 - core] = first, second
    diag[core], diag[1 - core] = diag_values(us, ts, f0t, gt, weighted)


def more_off_kernel(weight, x, x_first, f0s, f0t, gs, weighted, before, off, us_out, ts_out):
    core = whereabouts()[2]
    place = whereabouts()[0]
    x = [
        jnp.where(place > 1, x[c], jnp.where(place == 1, x_first[c], 0.0)) for c in range(2)
    ]
    xs = split_pair(unpacked(x[0]), unpacked(x[1]))
    first, second, us, ts = off_values(slot_of(False), weight, xs, f0s, f0t, gs, weighted)
    off[core] = first + before[core]
    off[1 - core] = second + before[1 - core]
    store4(us_out, us)
    store4(ts_out, ts)


def more_diag_kernel(us, ts, f0t, gt, weighted, before, diag):
    core = whereabouts()[2]
    first, second = diag_values(load4(us), load4(ts), f0t, gt, weighted)
    diag[core] = first + before[core]
    diag[1 - core] = second + before[1 - core]


def unpack_off_kernel(mine, theirs, off, done):
    core = whereabouts()[2]
    width = off.shape[-1]
    half = width // 2
    for source, entry in ((mine, core), (theirs, 1 - core)):
        off[entry, :, :half] = source[:width]
        off[entry, :, half:] = source[width:]
    done[...] = jnp.zeros_like(done)


def unpack_diag_kernel(mine, theirs, _, diag):
    core = whereabouts()[2]
    for source, entry in ((mine, core), (theirs, 1 - core)):
        diag[entry] = unpacked(source[...])


SCALAR = pl.BlockSpec(memory_space=pltpu.SMEM)
WHOLE = pl.BlockSpec(memory_space=pltpu.VMEM)


COST = pl.CostEstimate(flops=1, bytes_accessed=1, transcendentals=0)


LONG = pl.CostEstimate(flops=10**11, bytes_accessed=1, transcendentals=0)


def run(kernel, scalars, arrays, shapes, scratch=(), cost=COST, far=()):
    return pl.pallas_call(
        kernel,
        out_shape=shapes,
        in_specs=[SCALAR] * len(scalars)
        + [pl.BlockSpec(memory_space=pltpu.HBM)] * len(far)
        + [WHOLE] * len(arrays),
        out_specs=[WHOLE] * len(shapes),
        scratch_shapes=list(scratch),
        compiler_params=pltpu.CompilerParams(vmem_limit_bytes=VMEM_LIMIT),
        cost_estimate=cost,
    )(*scalars, *far, *arrays)


def local(pivot, factor, live, weight):
    poles, turns = lax.axis_size("pole"), lax.axis_size("snode")
    rows = turns // 2
    width = pivot.shape[-1]
    quarter = (width + 8, width // 2)
    mirrored = jax.ShapeDtypeStruct((2,) + quarter, F32)
    parts = jax.ShapeDtypeStruct((4, width, width), BF16)

    def at(pole_index, snode_index):
        return pole_index * turns + snode_index

    def hosts(row, pole):
        return at(pole, 2 * row + 1), at(pole, 2 * row)

    swaps = [(at(p, s), at(p, s ^ 1)) for p in range(poles) for s in range(2, turns)]
    first = [(at(p, 0), at(p, 1)) for p in range(poles)]
    every = [(at(p, s), at(p, s ^ 1)) for p in range(poles) for s in range(turns)]
    raw = jax.ShapeDtypeStruct((2, width, width), F32)
    constants = [parts, mirrored, jax.ShapeDtypeStruct((4,) + quarter, F32), raw]
    factors = [parts, parts, parts, parts, raw]

    scratch = [
        pltpu.VMEM(pivot.shape[1:], F32),
        pltpu.VMEM(factor.shape[2:], F32),
        pltpu.SMEM(live.shape, jnp.int32),
        pltpu.VMEM(weight.shape, F32),
        pltpu.SemaphoreType.DMA((6,)),
    ]
    far = [pltpu.with_memory_space_constraint(a, pltpu.HBM) for a in (live, pivot, factor, weight)]
    made = run(sent_constant_kernel, [], [], constants * 2, scratch, far=far)
    made, second = made[:4], made[4:]
    e_in = lax.ppermute(made[1], AXES, every)
    o_f1s, o_e, o_w, o_f0 = run(first_constant_kernel, [], made, constants, scratch, far=far)
    o_f0s, o_f0t, o_gs, o_gt, o_g = run(
        factor_kernel, [live], [o_f0, o_f1s], factors
    )
    g_in = lax.ppermute(o_g, AXES, swaps)
    made = run(sent_second_kernel, [live], [pivot, factor, weight, o_g, *second], constants)
    e_second = lax.ppermute(made[1], AXES, first)
    m_f1s, m_e, m_w, m_f0 = run(
        second_constant_kernel, [live], [pivot, factor, weight, *made], constants
    )
    m_f0s, m_f0t, m_gs, m_gt, m_g = run(
        factor_kernel, [live], [m_f0, m_f1s], factors
    )
    starts = functools.partial(step_kernel, lambda place: place == 1)
    (wave_even,) = run(starts, [], [o_gs, o_gt, o_e, e_in], [mirrored])
    wave_even = lax.ppermute(wave_even, AXES, [(at(p, 1), at(p, 0)) for p in range(poles)])
    (wave_odd,) = run(starts, [], [m_gs, m_gt, m_e, e_second], [mirrored])
    received = []
    if rows > 1:
        received = [
            lax.ppermute(wave_odd, AXES, [(at(p, 1), at(p, 3)) for p in range(poles)]),
            lax.ppermute(wave_even, AXES, [(at(p, 0), at(p, 2)) for p in range(poles)]),
        ]
    else:
        received = [jnp.zeros(mirrored.shape, F32)]
    fas, fat, ea, ps, pt, ep = run(
        pair_kernel,
        [],
        [m_g, m_e, g_in, e_in, e_second],
        [parts, parts, mirrored, parts, parts, mirrored],
        cost=LONG,
    )
    arrived = list(received)
    for turn in range(1, rows - 1):
        active = functools.partial(step_kernel, lambda place, turn=turn: lax.div(place, 2) == turn)
        (wave,) = run(active, [], [ps, pt, ep] + arrived, [mirrored])
        up = [pair for p in range(poles) for pair in zip(hosts(turn, p), hosts(turn + 1, p))]
        arrived = [lax.ppermute(wave, AXES, up)]
        received += arrived
    own, sent = run(
        share_kernel,
        [],
        [fas, fat, ea] + received,
        [mirrored, mirrored],
        [pltpu.VMEM(mirrored.shape, F32)],
    )
    shared = lax.ppermute(sent, AXES, every)

    offs = jax.ShapeDtypeStruct((2, 2 * width, width // 2), F32)
    diags = jax.ShapeDtypeStruct((2,) + quarter, F32)
    off, diag = run(density_kernel, [], [weight, own, m_f0s, m_f0t, m_gs, m_gt, m_w], [offs, diags])
    off, us, ts = run(
        more_off_kernel,
        [],
        [weight, shared, e_in, o_f0s, o_f0t, o_gs, o_w, off],
        [offs, parts, parts],
    )

    def exchanged(value, distance):
        return lax.ppermute(value, "pole", [(p, p ^ distance) for p in range(poles)])

    def summed(parts):
        kept = parts[0] + exchanged(parts[1], 1)
        distance = 2
        while distance < poles:
            kept = kept + exchanged(kept, distance)
            distance *= 2
        return kept, exchanged(kept, 1)

    full = jax.ShapeDtypeStruct((2, width, width), F32)
    off_sums = summed(off)
    (diag,) = run(more_diag_kernel, [], [us, ts, o_f0t, o_gt, o_w, diag], [diags])
    diag_sums = summed(diag)
    done = jax.ShapeDtypeStruct((8, 128), F32)
    density_off, done = run(unpack_off_kernel, [], list(off_sums), [full, done])
    (density_diag,) = run(unpack_diag_kernel, [], [*diag_sums, done], [full])
    return density_diag, density_off


def solution(mesh):
    placed = (
        P("pole", "snode", None, None, None),
        P("pole", "snode", None, None, None),
        P("snode"),
        P("pole", None),
    )
    return jax.shard_map(
        local,
        mesh=mesh,
        in_specs=placed,
        out_specs=(P("snode", None, None), P("snode", None, None)),
        check_vma=False,
    )
```

```python
import functools

import jax
import jax.numpy as jnp
from jax import lax
from jax.experimental import pallas as pl
from jax.experimental.pallas import tpu as pltpu
from jax.sharding import PartitionSpec as P

F32 = jnp.float32
BF16 = jnp.bfloat16
AXES = ("pole", "snode")
VMEM_LIMIT = 16 * 1024 * 1024


def halves(value):
    high = value.astype(BF16)
    return high, (value - high.astype(F32)).astype(BF16)


def split_pair(real, imag):
    (rh, rl), (ih, il) = halves(real), halves(imag)
    return rh, ih, rl, il


def deep_dot(left, right):
    return jnp.dot(
        jnp.concatenate(left, axis=1), jnp.concatenate(right, axis=0), preferred_element_type=F32
    )


def dot(left, right):
    return jnp.dot(left, right, preferred_element_type=F32)


def dot3(lh, ll, rh, rl):
    return dot(lh, rh) + (dot(lh, rl) + dot(ll, rh))


def wide_dot(left, right):
    arh, aih, arl, ail = left
    brh, bih, brl, bil = right
    real = dot3(arh, arl, brh, brl) - dot3(aih, ail, bih, bil)
    imag = dot3(arh, arl, bih, bil) + dot3(aih, ail, brh, brl)
    return real, imag


def complex_dot(left, right):
    arh, aih, arl, ail = left
    brh, bih, brl, bil = right
    blocks = [arh, arh, arl, aih, aih, ail]
    real = deep_dot(blocks, [brh, brl, brh, -bih, -bil, -bih])
    imag = deep_dot(blocks, [bih, bil, bih, brh, brl, brh])
    return real, imag


def rows_columns(size):
    return (
        lax.broadcasted_iota(jnp.int32, (size, size), 0),
        lax.broadcasted_iota(jnp.int32, (size, size), 1),
    )


def packed(block):
    half = block.shape[0] // 2
    row, column = rows_columns(half)
    lower = block[half:, half:]
    mixed = jnp.where(row >= column, block[:half, :half], lower)
    diagonal = jnp.sum(jnp.where(row == column, lower, 0.0), axis=0, keepdims=True)
    return jnp.concatenate(
        [block[:half, half:], mixed, jnp.broadcast_to(diagonal, (8, half))], axis=0
    )


def unpacked(value):
    half = value.shape[1]
    row, column = rows_columns(half)
    right, mixed = value[:half], value[half : 2 * half]
    diagonal = value[2 * half : 2 * half + 1]
    turned = mixed.T
    first = jnp.where(row >= column, mixed, turned)
    last = jnp.where(row < column, mixed, jnp.where(row == column, diagonal, turned))
    return jnp.concatenate(
        [jnp.concatenate([first, right], axis=1), jnp.concatenate([right.T, last], axis=1)], axis=0
    )


def unpacked_split(ref):
    return split_pair(unpacked(ref[0]), unpacked(ref[1]))


def load4(ref):
    return tuple(ref[i] for i in range(4))


def store4(ref, parts):
    for i, part in enumerate(parts):
        ref[i] = part


def whereabouts():
    place = lax.axis_index("snode")
    return place, lax.rem(place, 2), lax.rem(lax.axis_index("pole"), 2)


def hosted_slot():
    place, odd, _ = whereabouts()
    return jnp.where(place < 2, 0, 1 - odd)


def slot_of(hosted):
    return hosted_slot() if hosted else 1 - hosted_slot()


def constants_of(slot, blocks, link, widths, weights, f1s, e, weighted, *_, wait=lambda: None):
    width = blocks.shape[-1]
    row, column = rows_columns(width)
    kept = [column < widths[k] for k in range(2)]
    both = [jnp.logical_and(row < widths[k], kept[k]) for k in range(2)]
    f1 = [jnp.where(kept[1], link[c], 0.0) for c in range(2)]
    s1, t1 = split_pair(*f1), split_pair(f1[0].T, f1[1].T)
    store4(f1s, s1)
    wait()
    d = [[jnp.where(both[k], blocks[k, c], 0.0) for c in range(2)] for k in range(2)]
    br, bi = complex_dot(split_pair(*d[0]), s1)
    tr, ti = complex_dot(t1, split_pair(br, bi))
    er, ei = d[1][0] + tr, d[1][1] + ti
    e[0], e[1] = packed(er), packed(ei)
    w0, w1 = weights[pl.ds(slot, 1), 0:1], weights[pl.ds(slot, 1), 1:2]
    weighted[0] = packed(w1 * d[0][0] + w0 * d[0][1])
    weighted[1] = packed(w1 * er + w0 * ei)
    weighted_b = flat(w1 * br + w0 * bi)
    weighted[2] = weighted_b[: width + 8]
    weighted[3, : width - 8] = weighted_b[width + 8 :]


def fetched_constants(slot, live, pivot, factor, weight, outs, scratch):
    blocks, link, widths, weights, sems = scratch
    first_factor = pltpu.make_async_copy(factor.at[slot, 0], outs[3], sems.at[5])
    copies = [
        pltpu.make_async_copy(live, widths, sems.at[0]),
        pltpu.make_async_copy(factor.at[slot, 1], link, sems.at[1]),
        pltpu.make_async_copy(pivot.at[slot, 0], blocks.at[0], sems.at[2]),
        pltpu.make_async_copy(pivot.at[slot, 1], blocks.at[1], sems.at[3]),
        pltpu.make_async_copy(weight, weights, sems.at[4]),
    ]
    for copy in copies:
        copy.start()
    first_factor.start()
    copies[0].wait()
    copies[1].wait()

    def wait():
        for copy in copies[2:]:
            copy.wait()

    constants_of(slot, blocks, link, widths, weights, *outs, wait=wait)
    first_factor.wait()


def sent_constant_kernel(live, pivot, factor, weight, *refs):
    outs, second, scratch = refs[:4], refs[4:8], refs[8:]
    place, _, core = whereabouts()

    @pl.when(jnp.logical_and(place != 1, core == 0))
    def _():
        fetched_constants(slot_of(True), live, pivot, factor, weight, second, scratch)

    @pl.when(place != 1)
    def _():
        fetched_constants(slot_of(False), live, pivot, factor, weight, outs, scratch)


def first_constant_kernel(live, pivot, factor, weight, *refs):
    made, outs, scratch = refs[:4], refs[4:8], refs[8:]
    place = whereabouts()[0]

    @pl.when(place != 1)
    def _():
        for source, target in zip(made, outs):
            target[...] = source[...]

    @pl.when(place == 1)
    def _():
        fetched_constants(slot_of(False), live, pivot, factor, weight, outs, scratch)


def second_constants(live, pivot, factor, weight, f1s, e, weighted, first_factor):
    slot = slot_of(True)
    first_factor[...] = factor[slot, 0]
    constants_of(slot, pivot.at[slot], factor.at[slot, 1], live, weight, f1s, e, weighted)


def sent_second_kernel(live, pivot, factor, weight, _, *refs):
    made, outs = refs[:4], refs[4:]
    place, _, core = whereabouts()

    @pl.when(core == 0)
    def _():
        for source, target in zip(made, outs):
            target[...] = source[...]

    @pl.when(jnp.logical_and(place != 1, core == 1))
    def _():
        second_constants(live, pivot, factor, weight, *outs)


def second_constant_kernel(live, pivot, factor, weight, *refs):
    made, outs = refs[:4], refs[4:]
    place = whereabouts()[0]

    @pl.when(place != 1)
    def _():
        for source, target in zip(made, outs):
            target[...] = source[...]

    @pl.when(place == 1)
    def _():
        second_constants(live, pivot, factor, weight, *outs)


def factor_kernel(live, factor, f1s, f0s, f0t, gs, gt, g):
    _, column = rows_columns(factor.shape[-1])
    f0 = [jnp.where(column < live[0], factor[c], 0.0) for c in range(2)]
    s0 = split_pair(*f0)
    gr, gi = complex_dot(s0, load4(f1s))
    g[0], g[1] = gr, gi
    store4(gs, split_pair(gr, gi))
    store4(gt, split_pair(gr.T, gi.T))
    store4(f0s, s0)
    store4(f0t, split_pair(f0[0].T, f0[1].T))


def fold(x, gs, gt, e, out):
    tr, ti = complex_dot(x, load4(gs))
    yr, yi = complex_dot(load4(gt), split_pair(tr, ti))
    out[0] = e[0] + packed(yr)
    out[1] = e[1] + packed(yi)


def step_kernel(active, gs, gt, e, *refs):
    *received, out = refs

    @pl.when(active(whereabouts()[0]))
    def _():
        value = received[0][...]
        for other in received[1:]:
            value = value + other[...]
        fold(split_pair(unpacked(value[0]), unpacked(value[1])), gs, gt, e, out)


def pair_kernel(g, e, g_in, e_in, e_second, fas, fat, ea, ps, pt, ep):
    upper = whereabouts()[0] > 1
    is_odd = whereabouts()[1] == 1
    ga = [jnp.where(is_odd, g_in[c], g[c]) for c in range(2)]
    gb = [jnp.where(is_odd, g[c], g_in[c]) for c in range(2)]
    theirs = [jnp.where(upper, e_in[c], e_second[c]) for c in range(2)]
    low = [jnp.where(is_odd, theirs[c], e[c]) for c in range(2)]
    high = [jnp.where(is_odd, e[c], theirs[c]) for c in range(2)]
    sa, sb = split_pair(*ga), split_pair(*gb)
    store4(fas, sa)
    store4(fat, split_pair(ga[0].T, ga[1].T))
    pr, pi = complex_dot(sa, sb)
    store4(ps, split_pair(pr, pi))
    store4(pt, split_pair(pr.T, pi.T))
    br, bi = complex_dot(split_pair(unpacked(low[0]), unpacked(low[1])), sb)
    tr, ti = complex_dot(split_pair(gb[0].T, gb[1].T), split_pair(br, bi))
    for c, term in enumerate((tr, ti)):
        ea[c] = low[c]
        ep[c] = high[c] + packed(term)


def share_kernel(fas, fat, ea, *refs):
    *received, own, sent, scratch = refs
    value = received[0][...]
    for other in received[1:]:
        value = value + other[...]
    value = jnp.where(whereabouts()[0] > 1, value, 0.0)
    fold(split_pair(unpacked(value[0]), unpacked(value[1])), fas, fat, ea, scratch)
    is_odd = whereabouts()[1] == 1
    own[...] = jnp.where(is_odd, scratch[...], value)
    sent[...] = jnp.where(is_odd, value, scratch[...])


def flat(block):
    half = block.shape[1] // 2
    return jnp.concatenate([block[:, :half], block[:, half:]], axis=0)


def real_dot(left, right):
    return dot3(left[0], left[2], right[0], right[2]) + dot3(left[1], left[3], right[1], right[3])


def off_values(slot, weight, xs, f0s, f0t, gs, weighted):
    width = f0s.shape[-1]
    w0, w1 = weight[pl.ds(slot, 1), 0:1], weight[pl.ds(slot, 1), 1:2]
    qr, qi = wide_dot(xs, load4(gs))
    ts = split_pair(w1 * qr + w0 * qi, w0 * qr - w1 * qi)
    second = real_dot(load4(f0t), ts)
    pr, pi = wide_dot(xs, load4(f0s))
    u = w1 * pr + w0 * pi
    us = split_pair(u, w0 * pr - w1 * pi)
    constant = jnp.concatenate([weighted[2], weighted[3, : width - 8]], axis=0)
    return -flat(u), -(flat(second) + constant), us, ts


def diag_values(us, ts, f0t, gt, weighted):
    return (
        weighted[0] + packed(real_dot(load4(f0t), us)),
        weighted[1] + packed(real_dot(load4(gt), ts)),
    )


def density_kernel(weight, x, f0s, f0t, gs, gt, weighted, off, diag):
    core = whereabouts()[2]
    first, second, us, ts = off_values(slot_of(True), weight, unpacked_split(x), f0s, f0t, gs, weighted)
    off[core], off[1 - core] = first, second
    diag[core], diag[1 - core] = diag_values(us, ts, f0t, gt, weighted)


def more_off_kernel(weight, x, x_first, f0s, f0t, gs, weighted, before, off, us_out, ts_out):
    core = whereabouts()[2]
    place = whereabouts()[0]
    x = [
        jnp.where(place > 1, x[c], jnp.where(place == 1, x_first[c], 0.0)) for c in range(2)
    ]
    xs = split_pair(unpacked(x[0]), unpacked(x[1]))
    first, second, us, ts = off_values(slot_of(False), weight, xs, f0s, f0t, gs, weighted)
    off[core] = first + before[core]
    off[1 - core] = second + before[1 - core]
    store4(us_out, us)
    store4(ts_out, ts)


def more_diag_kernel(us, ts, f0t, gt, weighted, before, diag):
    core = whereabouts()[2]
    first, second = diag_values(load4(us), load4(ts), f0t, gt, weighted)
    diag[core] = first + before[core]
    diag[1 - core] = second + before[1 - core]


def unpack_off_kernel(mine, theirs, off, done):
    core = whereabouts()[2]
    width = off.shape[-1]
    half = width // 2
    for source, entry in ((mine, core), (theirs, 1 - core)):
        off[entry, :, :half] = source[:width]
        off[entry, :, half:] = source[width:]
    done[...] = jnp.zeros_like(done)


def unpack_diag_kernel(mine, theirs, _, diag):
    core = whereabouts()[2]
    for source, entry in ((mine, core), (theirs, 1 - core)):
        diag[entry] = unpacked(source[...])


SCALAR = pl.BlockSpec(memory_space=pltpu.SMEM)
WHOLE = pl.BlockSpec(memory_space=pltpu.VMEM)


COST = pl.CostEstimate(flops=1, bytes_accessed=1, transcendentals=0)


LONG = pl.CostEstimate(flops=10**11, bytes_accessed=1, transcendentals=0)


def run(kernel, scalars, arrays, shapes, scratch=(), cost=COST, far=()):
    return pl.pallas_call(
        kernel,
        out_shape=shapes,
        in_specs=[SCALAR] * len(scalars)
        + [pl.BlockSpec(memory_space=pltpu.HBM)] * len(far)
        + [WHOLE] * len(arrays),
        out_specs=[WHOLE] * len(shapes),
        scratch_shapes=list(scratch),
        compiler_params=pltpu.CompilerParams(vmem_limit_bytes=VMEM_LIMIT),
        cost_estimate=cost,
    )(*scalars, *far, *arrays)


def local(pivot, factor, live, weight):
    poles, turns = lax.axis_size("pole"), lax.axis_size("snode")
    rows = turns // 2
    width = pivot.shape[-1]
    quarter = (width + 8, width // 2)
    mirrored = jax.ShapeDtypeStruct((2,) + quarter, F32)
    parts = jax.ShapeDtypeStruct((4, width, width), BF16)

    def at(pole_index, snode_index):
        return pole_index * turns + snode_index

    def hosts(row, pole):
        return at(pole, 2 * row + 1), at(pole, 2 * row)

    swaps = [(at(p, s), at(p, s ^ 1)) for p in range(poles) for s in range(2, turns)]
    first = [(at(p, 0), at(p, 1)) for p in range(poles)]
    every = [(at(p, s), at(p, s ^ 1)) for p in range(poles) for s in range(turns)]
    raw = jax.ShapeDtypeStruct((2, width, width), F32)
    constants = [parts, mirrored, jax.ShapeDtypeStruct((4,) + quarter, F32), raw]
    factors = [parts, parts, parts, parts, raw]

    scratch = [
        pltpu.VMEM(pivot.shape[1:], F32),
        pltpu.VMEM(factor.shape[2:], F32),
        pltpu.SMEM(live.shape, jnp.int32),
        pltpu.VMEM(weight.shape, F32),
        pltpu.SemaphoreType.DMA((6,)),
    ]
    far = [pltpu.with_memory_space_constraint(a, pltpu.HBM) for a in (live, pivot, factor, weight)]
    made = run(sent_constant_kernel, [], [], constants * 2, scratch, far=far)
    made, second = made[:4], made[4:]
    crossed = [(at(p, 1), at(p ^ 1, 0)) for p in range(poles)]
    e_in = lax.ppermute(made[1], AXES, first + crossed + swaps)
    o_f1s, o_e, o_w, o_f0 = run(first_constant_kernel, [], made, constants, scratch, far=far)
    o_f0s, o_f0t, o_gs, o_gt, o_g = run(
        factor_kernel, [live], [o_f0, o_f1s], factors
    )
    g_in = lax.ppermute(o_g, AXES, swaps)
    made = run(sent_second_kernel, [live], [pivot, factor, weight, o_g, *second], constants)
    e_second = lax.ppermute(made[1], AXES, first)
    m_f1s, m_e, m_w, m_f0 = run(
        second_constant_kernel, [live], [pivot, factor, weight, *made], constants
    )
    m_f0s, m_f0t, m_gs, m_gt, m_g = run(
        factor_kernel, [live], [m_f0, m_f1s], factors
    )
    starts = functools.partial(step_kernel, lambda place: place == 1)
    (wave_even,) = run(starts, [], [o_gs, o_gt, o_e, e_in], [mirrored])
    wave_even = lax.ppermute(wave_even, AXES, [(at(p, 1), at(p, 0)) for p in range(poles)])
    (wave_odd,) = run(starts, [], [m_gs, m_gt, m_e, e_second], [mirrored])
    received = []
    if rows > 1:
        received = [
            lax.ppermute(wave_odd, AXES, [(at(p, 1), at(p, 3)) for p in range(poles)]),
            lax.ppermute(wave_even, AXES, [(at(p, 0), at(p, 2)) for p in range(poles)]),
        ]
    else:
        received = [jnp.zeros(mirrored.shape, F32)]
    fas, fat, ea, ps, pt, ep = run(
        pair_kernel,
        [],
        [m_g, m_e, g_in, e_in, e_second],
        [parts, parts, mirrored, parts, parts, mirrored],
        cost=LONG,
    )
    arrived = list(received)
    for turn in range(1, rows - 1):
        active = functools.partial(step_kernel, lambda place, turn=turn: lax.div(place, 2) == turn)
        (wave,) = run(active, [], [ps, pt, ep] + arrived, [mirrored])
        up = [pair for p in range(poles) for pair in zip(hosts(turn, p), hosts(turn + 1, p))]
        arrived = [lax.ppermute(wave, AXES, up)]
        received += arrived
    own, sent = run(
        share_kernel,
        [],
        [fas, fat, ea] + received,
        [mirrored, mirrored],
        [pltpu.VMEM(mirrored.shape, F32)],
    )
    shared = lax.ppermute(sent, AXES, every)

    offs = jax.ShapeDtypeStruct((2, 2 * width, width // 2), F32)
    diags = jax.ShapeDtypeStruct((2,) + quarter, F32)
    off, diag = run(density_kernel, [], [weight, own, m_f0s, m_f0t, m_gs, m_gt, m_w], [offs, diags])
    off, us, ts = run(
        more_off_kernel,
        [],
        [weight, shared, e_in, o_f0s, o_f0t, o_gs, o_w, off],
        [offs, parts, parts],
    )

    def exchanged(value, distance):
        return lax.ppermute(value, "pole", [(p, p ^ distance) for p in range(poles)])

    def summed(parts):
        kept = parts[0] + exchanged(parts[1], 1)
        distance = 2
        while distance < poles:
            kept = kept + exchanged(kept, distance)
            distance *= 2
        return kept, exchanged(kept, 1)

    full = jax.ShapeDtypeStruct((2, width, width), F32)
    off_sums = summed(off)
    (diag,) = run(more_diag_kernel, [], [us, ts, o_f0t, o_gt, o_w, diag], [diags])
    diag_sums = summed(diag)
    done = jax.ShapeDtypeStruct((8, 128), F32)
    density_off, done = run(unpack_off_kernel, [], list(off_sums), [full, done])
    (density_diag,) = run(unpack_diag_kernel, [], [*diag_sums, done], [full])
    return density_diag, density_off


def solution(mesh):
    placed = (
        P("pole", "snode", None, None, None),
        P("pole", "snode", None, None, None),
        P("snode"),
        P("pole", None),
    )
    return jax.shard_map(
        local,
        mesh=mesh,
        in_specs=placed,
        out_specs=(P("snode", None, None), P("snode", None, None)),
        check_vma=False,
    )
```

```python
import functools

import jax
import jax.numpy as jnp
from jax import lax
from jax.experimental import pallas as pl
from jax.experimental.pallas import tpu as pltpu
from jax.sharding import PartitionSpec as P

F32 = jnp.float32
BF16 = jnp.bfloat16
AXES = ("pole", "snode")
VMEM_LIMIT = 16 * 1024 * 1024


def halves(value):
    high = value.astype(BF16)
    return high, (value - high.astype(F32)).astype(BF16)


def split_pair(real, imag):
    (rh, rl), (ih, il) = halves(real), halves(imag)
    return rh, ih, rl, il


def deep_dot(left, right):
    return jnp.dot(
        jnp.concatenate(left, axis=1), jnp.concatenate(right, axis=0), preferred_element_type=F32
    )


def dot(left, right):
    return jnp.dot(left, right, preferred_element_type=F32)


def dot3(lh, ll, rh, rl):
    return dot(lh, rh) + (dot(lh, rl) + dot(ll, rh))


def wide_dot(left, right):
    arh, aih, arl, ail = left
    brh, bih, brl, bil = right
    real = dot3(arh, arl, brh, brl) - dot3(aih, ail, bih, bil)
    imag = dot3(arh, arl, bih, bil) + dot3(aih, ail, brh, brl)
    return real, imag


def complex_dot(left, right):
    arh, aih, arl, ail = left
    brh, bih, brl, bil = right
    blocks = [arh, arh, arl, aih, aih, ail]
    real = deep_dot(blocks, [brh, brl, brh, -bih, -bil, -bih])
    imag = deep_dot(blocks, [bih, bil, bih, brh, brl, brh])
    return real, imag


def rows_columns(size):
    return (
        lax.broadcasted_iota(jnp.int32, (size, size), 0),
        lax.broadcasted_iota(jnp.int32, (size, size), 1),
    )


def packed(block):
    half = block.shape[0] // 2
    row, column = rows_columns(half)
    lower = block[half:, half:]
    mixed = jnp.where(row >= column, block[:half, :half], lower)
    diagonal = jnp.sum(jnp.where(row == column, lower, 0.0), axis=0, keepdims=True)
    return jnp.concatenate(
        [block[:half, half:], mixed, jnp.broadcast_to(diagonal, (8, half))], axis=0
    )


def unpacked(value):
    half = value.shape[1]
    row, column = rows_columns(half)
    right, mixed = value[:half], value[half : 2 * half]
    diagonal = value[2 * half : 2 * half + 1]
    turned = mixed.T
    first = jnp.where(row >= column, mixed, turned)
    last = jnp.where(row < column, mixed, jnp.where(row == column, diagonal, turned))
    return jnp.concatenate(
        [jnp.concatenate([first, right], axis=1), jnp.concatenate([right.T, last], axis=1)], axis=0
    )


def unpacked_split(ref):
    return split_pair(unpacked(ref[0]), unpacked(ref[1]))


def load4(ref):
    return tuple(ref[i] for i in range(4))


def store4(ref, parts):
    for i, part in enumerate(parts):
        ref[i] = part


def whereabouts():
    place = lax.axis_index("snode")
    return place, lax.rem(place, 2), lax.rem(lax.axis_index("pole"), 2)


def hosted_slot():
    place, odd, _ = whereabouts()
    return jnp.where(place < 2, 0, 1 - odd)


def slot_of(hosted):
    return hosted_slot() if hosted else 1 - hosted_slot()


def constants_of(slot, blocks, link, widths, weights, f1s, e, weighted, *_, wait=lambda: None):
    width = blocks.shape[-1]
    row, column = rows_columns(width)
    kept = [column < widths[k] for k in range(2)]
    both = [jnp.logical_and(row < widths[k], kept[k]) for k in range(2)]
    f1 = [jnp.where(kept[1], link[c], 0.0) for c in range(2)]
    s1, t1 = split_pair(*f1), split_pair(f1[0].T, f1[1].T)
    store4(f1s, s1)
    wait()
    d = [[jnp.where(both[k], blocks[k, c], 0.0) for c in range(2)] for k in range(2)]
    br, bi = complex_dot(split_pair(*d[0]), s1)
    tr, ti = complex_dot(t1, split_pair(br, bi))
    er, ei = d[1][0] + tr, d[1][1] + ti
    e[0], e[1] = packed(er), packed(ei)
    w0, w1 = weights[pl.ds(slot, 1), 0:1], weights[pl.ds(slot, 1), 1:2]
    weighted[0] = packed(w1 * d[0][0] + w0 * d[0][1])
    weighted[1] = packed(w1 * er + w0 * ei)
    weighted_b = flat(w1 * br + w0 * bi)
    weighted[2] = weighted_b[: width + 8]
    weighted[3, : width - 8] = weighted_b[width + 8 :]


def fetched_constants(slot, live, pivot, factor, weight, outs, scratch):
    blocks, link, widths, weights, sems = scratch
    first_factor = pltpu.make_async_copy(factor.at[slot, 0], outs[3], sems.at[5])
    copies = [
        pltpu.make_async_copy(live, widths, sems.at[0]),
        pltpu.make_async_copy(factor.at[slot, 1], link, sems.at[1]),
        pltpu.make_async_copy(pivot.at[slot, 0], blocks.at[0], sems.at[2]),
        pltpu.make_async_copy(pivot.at[slot, 1], blocks.at[1], sems.at[3]),
        pltpu.make_async_copy(weight, weights, sems.at[4]),
    ]
    for copy in copies:
        copy.start()
    first_factor.start()
    copies[0].wait()
    copies[1].wait()

    def wait():
        for copy in copies[2:]:
            copy.wait()

    constants_of(slot, blocks, link, widths, weights, *outs, wait=wait)
    first_factor.wait()


def sent_constant_kernel(live, pivot, factor, weight, *refs):
    outs, second, scratch = refs[:4], refs[4:8], refs[8:]
    place, _, core = whereabouts()

    @pl.when(jnp.logical_and(place != 1, core == 0))
    def _():
        fetched_constants(slot_of(True), live, pivot, factor, weight, second, scratch)

    @pl.when(jnp.logical_or(place != 1, core == 0))
    def _():
        fetched_constants(slot_of(False), live, pivot, factor, weight, outs, scratch)


def first_constant_kernel(live, pivot, factor, weight, *refs):
    made, outs, scratch = refs[:4], refs[4:8], refs[8:]
    place, _, core = whereabouts()
    late = jnp.logical_and(place == 1, core == 1)

    @pl.when(jnp.logical_not(late))
    def _():
        for source, target in zip(made, outs):
            target[...] = source[...]

    @pl.when(late)
    def _():
        fetched_constants(slot_of(False), live, pivot, factor, weight, outs, scratch)


def second_constants(live, pivot, factor, weight, f1s, e, weighted, first_factor):
    slot = slot_of(True)
    first_factor[...] = factor[slot, 0]
    constants_of(slot, pivot.at[slot], factor.at[slot, 1], live, weight, f1s, e, weighted)


def sent_second_kernel(live, pivot, factor, weight, _, *refs):
    made, outs = refs[:4], refs[4:]
    place, _, core = whereabouts()

    @pl.when(core == 0)
    def _():
        for source, target in zip(made, outs):
            target[...] = source[...]

    @pl.when(jnp.logical_and(place != 1, core == 1))
    def _():
        second_constants(live, pivot, factor, weight, *outs)


def second_constant_kernel(live, pivot, factor, weight, *refs):
    made, outs = refs[:4], refs[4:]
    place = whereabouts()[0]

    @pl.when(place != 1)
    def _():
        for source, target in zip(made, outs):
            target[...] = source[...]

    @pl.when(place == 1)
    def _():
        second_constants(live, pivot, factor, weight, *outs)


def factor_kernel(live, factor, f1s, f0s, f0t, gs, gt, g):
    _, column = rows_columns(factor.shape[-1])
    f0 = [jnp.where(column < live[0], factor[c], 0.0) for c in range(2)]
    s0 = split_pair(*f0)
    gr, gi = complex_dot(s0, load4(f1s))
    g[0], g[1] = gr, gi
    store4(gs, split_pair(gr, gi))
    store4(gt, split_pair(gr.T, gi.T))
    store4(f0s, s0)
    store4(f0t, split_pair(f0[0].T, f0[1].T))


def fold(x, gs, gt, e, out):
    tr, ti = complex_dot(x, load4(gs))
    yr, yi = complex_dot(load4(gt), split_pair(tr, ti))
    out[0] = e[0] + packed(yr)
    out[1] = e[1] + packed(yi)


def step_kernel(active, gs, gt, e, *refs):
    *received, out = refs

    @pl.when(active(whereabouts()[0]))
    def _():
        value = received[0][...]
        for other in received[1:]:
            value = value + other[...]
        fold(split_pair(unpacked(value[0]), unpacked(value[1])), gs, gt, e, out)


def pair_kernel(g, e, g_in, e_in, e_second, fas, fat, ea, ps, pt, ep):
    upper = whereabouts()[0] > 1
    is_odd = whereabouts()[1] == 1
    ga = [jnp.where(is_odd, g_in[c], g[c]) for c in range(2)]
    gb = [jnp.where(is_odd, g[c], g_in[c]) for c in range(2)]
    theirs = [jnp.where(upper, e_in[c], e_second[c]) for c in range(2)]
    low = [jnp.where(is_odd, theirs[c], e[c]) for c in range(2)]
    high = [jnp.where(is_odd, e[c], theirs[c]) for c in range(2)]
    sa, sb = split_pair(*ga), split_pair(*gb)
    store4(fas, sa)
    store4(fat, split_pair(ga[0].T, ga[1].T))
    pr, pi = complex_dot(sa, sb)
    store4(ps, split_pair(pr, pi))
    store4(pt, split_pair(pr.T, pi.T))
    br, bi = complex_dot(split_pair(unpacked(low[0]), unpacked(low[1])), sb)
    tr, ti = complex_dot(split_pair(gb[0].T, gb[1].T), split_pair(br, bi))
    for c, term in enumerate((tr, ti)):
        ea[c] = low[c]
        ep[c] = high[c] + packed(term)


def share_kernel(fas, fat, ea, *refs):
    *received, own, sent, scratch = refs
    value = received[0][...]
    for other in received[1:]:
        value = value + other[...]
    value = jnp.where(whereabouts()[0] > 1, value, 0.0)
    fold(split_pair(unpacked(value[0]), unpacked(value[1])), fas, fat, ea, scratch)
    is_odd = whereabouts()[1] == 1
    own[...] = jnp.where(is_odd, scratch[...], value)
    sent[...] = jnp.where(is_odd, value, scratch[...])


def flat(block):
    half = block.shape[1] // 2
    return jnp.concatenate([block[:, :half], block[:, half:]], axis=0)


def real_dot(left, right):
    return dot3(left[0], left[2], right[0], right[2]) + dot3(left[1], left[3], right[1], right[3])


def off_values(slot, weight, xs, f0s, f0t, gs, weighted):
    width = f0s.shape[-1]
    w0, w1 = weight[pl.ds(slot, 1), 0:1], weight[pl.ds(slot, 1), 1:2]
    qr, qi = wide_dot(xs, load4(gs))
    ts = split_pair(w1 * qr + w0 * qi, w0 * qr - w1 * qi)
    second = real_dot(load4(f0t), ts)
    pr, pi = wide_dot(xs, load4(f0s))
    u = w1 * pr + w0 * pi
    us = split_pair(u, w0 * pr - w1 * pi)
    constant = jnp.concatenate([weighted[2], weighted[3, : width - 8]], axis=0)
    return -flat(u), -(flat(second) + constant), us, ts


def diag_values(us, ts, f0t, gt, weighted):
    return (
        weighted[0] + packed(real_dot(load4(f0t), us)),
        weighted[1] + packed(real_dot(load4(gt), ts)),
    )


def density_kernel(weight, x, f0s, f0t, gs, gt, weighted, off, diag):
    core = whereabouts()[2]
    first, second, us, ts = off_values(slot_of(True), weight, unpacked_split(x), f0s, f0t, gs, weighted)
    off[core], off[1 - core] = first, second
    diag[core], diag[1 - core] = diag_values(us, ts, f0t, gt, weighted)


def more_off_kernel(weight, x, x_first, f0s, f0t, gs, weighted, before, off, us_out, ts_out):
    core = whereabouts()[2]
    place = whereabouts()[0]
    x = [
        jnp.where(place > 1, x[c], jnp.where(place == 1, x_first[c], 0.0)) for c in range(2)
    ]
    xs = split_pair(unpacked(x[0]), unpacked(x[1]))
    first, second, us, ts = off_values(slot_of(False), weight, xs, f0s, f0t, gs, weighted)
    off[core] = first + before[core]
    off[1 - core] = second + before[1 - core]
    store4(us_out, us)
    store4(ts_out, ts)


def more_diag_kernel(us, ts, f0t, gt, weighted, before, diag):
    core = whereabouts()[2]
    first, second = diag_values(load4(us), load4(ts), f0t, gt, weighted)
    diag[core] = first + before[core]
    diag[1 - core] = second + before[1 - core]


def unpack_off_kernel(mine, theirs, off, done):
    core = whereabouts()[2]
    width = off.shape[-1]
    half = width // 2
    for source, entry in ((mine, core), (theirs, 1 - core)):
        off[entry, :, :half] = source[:width]
        off[entry, :, half:] = source[width:]
    done[...] = jnp.zeros_like(done)


def unpack_diag_kernel(mine, theirs, _, diag):
    core = whereabouts()[2]
    for source, entry in ((mine, core), (theirs, 1 - core)):
        diag[entry] = unpacked(source[...])


SCALAR = pl.BlockSpec(memory_space=pltpu.SMEM)
WHOLE = pl.BlockSpec(memory_space=pltpu.VMEM)


COST = pl.CostEstimate(flops=1, bytes_accessed=1, transcendentals=0)


LONG = pl.CostEstimate(flops=10**11, bytes_accessed=1, transcendentals=0)


def run(kernel, scalars, arrays, shapes, scratch=(), cost=COST, far=()):
    return pl.pallas_call(
        kernel,
        out_shape=shapes,
        in_specs=[SCALAR] * len(scalars)
        + [pl.BlockSpec(memory_space=pltpu.HBM)] * len(far)
        + [WHOLE] * len(arrays),
        out_specs=[WHOLE] * len(shapes),
        scratch_shapes=list(scratch),
        compiler_params=pltpu.CompilerParams(vmem_limit_bytes=VMEM_LIMIT),
        cost_estimate=cost,
    )(*scalars, *far, *arrays)


def local(pivot, factor, live, weight):
    poles, turns = lax.axis_size("pole"), lax.axis_size("snode")
    rows = turns // 2
    width = pivot.shape[-1]
    quarter = (width + 8, width // 2)
    mirrored = jax.ShapeDtypeStruct((2,) + quarter, F32)
    parts = jax.ShapeDtypeStruct((4, width, width), BF16)

    def at(pole_index, snode_index):
        return pole_index * turns + snode_index

    def hosts(row, pole):
        return at(pole, 2 * row + 1), at(pole, 2 * row)

    swaps = [(at(p, s), at(p, s ^ 1)) for p in range(poles) for s in range(2, turns)]
    first = [(at(p, 0), at(p, 1)) for p in range(poles)]
    every = [(at(p, s), at(p, s ^ 1)) for p in range(poles) for s in range(turns)]
    raw = jax.ShapeDtypeStruct((2, width, width), F32)
    constants = [parts, mirrored, jax.ShapeDtypeStruct((4,) + quarter, F32), raw]
    factors = [parts, parts, parts, parts, raw]

    scratch = [
        pltpu.VMEM(pivot.shape[1:], F32),
        pltpu.VMEM(factor.shape[2:], F32),
        pltpu.SMEM(live.shape, jnp.int32),
        pltpu.VMEM(weight.shape, F32),
        pltpu.SemaphoreType.DMA((6,)),
    ]
    far = [pltpu.with_memory_space_constraint(a, pltpu.HBM) for a in (live, pivot, factor, weight)]
    made = run(sent_constant_kernel, [], [], constants * 2, scratch, far=far)
    made, second = made[:4], made[4:]
    e_in = lax.ppermute(made[1], AXES, every)
    o_f1s, o_e, o_w, o_f0 = run(first_constant_kernel, [], made, constants, scratch, far=far)
    o_f0s, o_f0t, o_gs, o_gt, o_g = run(
        factor_kernel, [live], [o_f0, o_f1s], factors
    )
    g_in = lax.ppermute(o_g, AXES, swaps)
    made = run(sent_second_kernel, [live], [pivot, factor, weight, o_g, *second], constants)
    e_second = lax.ppermute(made[1], AXES, first)
    m_f1s, m_e, m_w, m_f0 = run(
        second_constant_kernel, [live], [pivot, factor, weight, *made], constants
    )
    m_f0s, m_f0t, m_gs, m_gt, m_g = run(
        factor_kernel, [live], [m_f0, m_f1s], factors
    )
    starts = functools.partial(step_kernel, lambda place: place == 1)
    (wave_even,) = run(starts, [], [o_gs, o_gt, o_e, e_in], [mirrored])
    wave_even = lax.ppermute(wave_even, AXES, [(at(p, 1), at(p, 0)) for p in range(poles)])
    (wave_odd,) = run(starts, [], [m_gs, m_gt, m_e, e_second], [mirrored])
    received = []
    if rows > 1:
        received = [
            lax.ppermute(wave_odd, AXES, [(at(p, 1), at(p, 3)) for p in range(poles)]),
            lax.ppermute(wave_even, AXES, [(at(p, 0), at(p, 2)) for p in range(poles)]),
        ]
    else:
        received = [jnp.zeros(mirrored.shape, F32)]
    fas, fat, ea, ps, pt, ep = run(
        pair_kernel,
        [],
        [m_g, m_e, g_in, e_in, e_second],
        [parts, parts, mirrored, parts, parts, mirrored],
        cost=LONG,
    )
    arrived = list(received)
    for turn in range(1, rows - 1):
        active = functools.partial(step_kernel, lambda place, turn=turn: lax.div(place, 2) == turn)
        (wave,) = run(active, [], [ps, pt, ep] + arrived, [mirrored])
        up = [pair for p in range(poles) for pair in zip(hosts(turn, p), hosts(turn + 1, p))]
        arrived = [lax.ppermute(wave, AXES, up)]
        received += arrived
    own, sent = run(
        share_kernel,
        [],
        [fas, fat, ea] + received,
        [mirrored, mirrored],
        [pltpu.VMEM(mirrored.shape, F32)],
    )
    shared = lax.ppermute(sent, AXES, every)

    offs = jax.ShapeDtypeStruct((2, 2 * width, width // 2), F32)
    diags = jax.ShapeDtypeStruct((2,) + quarter, F32)
    off, diag = run(density_kernel, [], [weight, own, m_f0s, m_f0t, m_gs, m_gt, m_w], [offs, diags])
    off, us, ts = run(
        more_off_kernel,
        [],
        [weight, shared, e_in, o_f0s, o_f0t, o_gs, o_w, off],
        [offs, parts, parts],
    )

    def exchanged(value, distance):
        return lax.ppermute(value, "pole", [(p, p ^ distance) for p in range(poles)])

    def summed(parts):
        kept = parts[0] + exchanged(parts[1], 1)
        distance = 2
        while distance < poles:
            kept = kept + exchanged(kept, distance)
            distance *= 2
        return kept, exchanged(kept, 1)

    full = jax.ShapeDtypeStruct((2, width, width), F32)
    off_sums = summed(off)
    (diag,) = run(more_diag_kernel, [], [us, ts, o_f0t, o_gt, o_w, diag], [diags])
    diag_sums = summed(diag)
    done = jax.ShapeDtypeStruct((8, 128), F32)
    density_off, done = run(unpack_off_kernel, [], list(off_sums), [full, done])
    (density_diag,) = run(unpack_diag_kernel, [], [*diag_sums, done], [full])
    return density_diag, density_off


def solution(mesh):
    placed = (
        P("pole", "snode", None, None, None),
        P("pole", "snode", None, None, None),
        P("snode"),
        P("pole", None),
    )
    return jax.shard_map(
        local,
        mesh=mesh,
        in_specs=placed,
        out_specs=(P("snode", None, None), P("snode", None, None)),
        check_vma=False,
    )
```

```python
import functools

import jax
import jax.numpy as jnp
from jax import lax
from jax.experimental import pallas as pl
from jax.experimental.pallas import tpu as pltpu
from jax.sharding import PartitionSpec as P

F32 = jnp.float32
BF16 = jnp.bfloat16
AXES = ("pole", "snode")
VMEM_LIMIT = 16 * 1024 * 1024


def halves(value):
    high = value.astype(BF16)
    return high, (value - high.astype(F32)).astype(BF16)


def split_pair(real, imag):
    (rh, rl), (ih, il) = halves(real), halves(imag)
    return rh, ih, rl, il


def deep_dot(left, right):
    return jnp.dot(
        jnp.concatenate(left, axis=1), jnp.concatenate(right, axis=0), preferred_element_type=F32
    )


def dot(left, right):
    return jnp.dot(left, right, preferred_element_type=F32)


def dot3(lh, ll, rh, rl):
    return dot(lh, rh) + (dot(lh, rl) + dot(ll, rh))


def wide_dot(left, right):
    arh, aih, arl, ail = left
    brh, bih, brl, bil = right
    real = dot3(arh, arl, brh, brl) - dot3(aih, ail, bih, bil)
    imag = dot3(arh, arl, bih, bil) + dot3(aih, ail, brh, brl)
    return real, imag


def complex_dot(left, right):
    arh, aih, arl, ail = left
    brh, bih, brl, bil = right
    blocks = [arh, arh, arl, aih, aih, ail]
    real = deep_dot(blocks, [brh, brl, brh, -bih, -bil, -bih])
    imag = deep_dot(blocks, [bih, bil, bih, brh, brl, brh])
    return real, imag


def rows_columns(size):
    return (
        lax.broadcasted_iota(jnp.int32, (size, size), 0),
        lax.broadcasted_iota(jnp.int32, (size, size), 1),
    )


def packed(block):
    half = block.shape[0] // 2
    row, column = rows_columns(half)
    lower = block[half:, half:]
    mixed = jnp.where(row >= column, block[:half, :half], lower)
    diagonal = jnp.sum(jnp.where(row == column, lower, 0.0), axis=0, keepdims=True)
    return jnp.concatenate(
        [block[:half, half:], mixed, jnp.broadcast_to(diagonal, (8, half))], axis=0
    )


def unpacked(value):
    half = value.shape[1]
    row, column = rows_columns(half)
    right, mixed = value[:half], value[half : 2 * half]
    diagonal = value[2 * half : 2 * half + 1]
    turned = mixed.T
    first = jnp.where(row >= column, mixed, turned)
    last = jnp.where(row < column, mixed, jnp.where(row == column, diagonal, turned))
    return jnp.concatenate(
        [jnp.concatenate([first, right], axis=1), jnp.concatenate([right.T, last], axis=1)], axis=0
    )


def unpacked_split(ref):
    return split_pair(unpacked(ref[0]), unpacked(ref[1]))


def load4(ref):
    return tuple(ref[i] for i in range(4))


def store4(ref, parts):
    for i, part in enumerate(parts):
        ref[i] = part


def whereabouts():
    place = lax.axis_index("snode")
    return place, lax.rem(place, 2), lax.rem(lax.axis_index("pole"), 2)


def hosted_slot():
    place, odd, _ = whereabouts()
    return jnp.where(place < 2, 0, 1 - odd)


def slot_of(hosted):
    return hosted_slot() if hosted else 1 - hosted_slot()


def constants_of(slot, blocks, link, widths, weights, f1s, e, weighted, *_, wait=lambda: None):
    width = blocks.shape[-1]
    row, column = rows_columns(width)
    kept = [column < widths[k] for k in range(2)]
    both = [jnp.logical_and(row < widths[k], kept[k]) for k in range(2)]
    f1 = [jnp.where(kept[1], link[c], 0.0) for c in range(2)]
    s1, t1 = split_pair(*f1), split_pair(f1[0].T, f1[1].T)
    store4(f1s, s1)
    wait()
    d = [[jnp.where(both[k], blocks[k, c], 0.0) for c in range(2)] for k in range(2)]
    br, bi = complex_dot(split_pair(*d[0]), s1)
    tr, ti = complex_dot(t1, split_pair(br, bi))
    er, ei = d[1][0] + tr, d[1][1] + ti
    e[0], e[1] = packed(er), packed(ei)
    w0, w1 = weights[pl.ds(slot, 1), 0:1], weights[pl.ds(slot, 1), 1:2]
    weighted[0] = packed(w1 * d[0][0] + w0 * d[0][1])
    weighted[1] = packed(w1 * er + w0 * ei)
    weighted_b = flat(w1 * br + w0 * bi)
    weighted[2] = weighted_b[: width + 8]
    weighted[3, : width - 8] = weighted_b[width + 8 :]


def fetched_constants(slot, live, pivot, factor, weight, outs, scratch):
    blocks, link, widths, weights, sems = scratch
    first_factor = pltpu.make_async_copy(factor.at[slot, 0], outs[3], sems.at[5])
    copies = [
        pltpu.make_async_copy(live, widths, sems.at[0]),
        pltpu.make_async_copy(factor.at[slot, 1], link, sems.at[1]),
        pltpu.make_async_copy(pivot.at[slot, 0], blocks.at[0], sems.at[2]),
        pltpu.make_async_copy(pivot.at[slot, 1], blocks.at[1], sems.at[3]),
        pltpu.make_async_copy(weight, weights, sems.at[4]),
    ]
    for copy in copies:
        copy.start()
    first_factor.start()
    copies[0].wait()
    copies[1].wait()

    def wait():
        for copy in copies[2:]:
            copy.wait()

    constants_of(slot, blocks, link, widths, weights, *outs, wait=wait)
    first_factor.wait()


def sent_constant_kernel(live, pivot, factor, weight, *refs):
    outs, second, scratch = refs[:4], refs[4:8], refs[8:]
    place, _, core = whereabouts()

    @pl.when(jnp.logical_and(place != 1, core == 0))
    def _():
        fetched_constants(slot_of(True), live, pivot, factor, weight, second, scratch)

    @pl.when(jnp.logical_or(place != 1, core == 0))
    def _():
        fetched_constants(slot_of(False), live, pivot, factor, weight, outs, scratch)


def first_constant_kernel(live, pivot, factor, weight, *refs):
    made, outs, scratch = refs[:4], refs[4:8], refs[8:]
    place, _, core = whereabouts()
    late = jnp.logical_and(place == 1, core == 1)

    @pl.when(jnp.logical_not(late))
    def _():
        for source, target in zip(made, outs):
            target[...] = source[...]

    @pl.when(late)
    def _():
        fetched_constants(slot_of(False), live, pivot, factor, weight, outs, scratch)


def second_constants(live, pivot, factor, weight, f1s, e, weighted, first_factor):
    slot = slot_of(True)
    first_factor[...] = factor[slot, 0]
    constants_of(slot, pivot.at[slot], factor.at[slot, 1], live, weight, f1s, e, weighted)


def sent_second_kernel(live, pivot, factor, weight, _, *refs):
    made, outs = refs[:4], refs[4:]
    place, _, core = whereabouts()

    @pl.when(core == 0)
    def _():
        for source, target in zip(made, outs):
            target[...] = source[...]

    @pl.when(jnp.logical_and(place != 1, core == 1))
    def _():
        second_constants(live, pivot, factor, weight, *outs)


def second_constant_kernel(live, pivot, factor, weight, *refs):
    made, outs = refs[:4], refs[4:]
    place = whereabouts()[0]

    @pl.when(place != 1)
    def _():
        for source, target in zip(made, outs):
            target[...] = source[...]

    @pl.when(place == 1)
    def _():
        second_constants(live, pivot, factor, weight, *outs)


def factor_kernel(live, factor, f1s, f0s, f0t, gs, gt, g):
    _, column = rows_columns(factor.shape[-1])
    f0 = [jnp.where(column < live[0], factor[c], 0.0) for c in range(2)]
    s0 = split_pair(*f0)
    gr, gi = complex_dot(s0, load4(f1s))
    g[0], g[1] = gr, gi
    store4(gs, split_pair(gr, gi))
    store4(gt, split_pair(gr.T, gi.T))
    store4(f0s, s0)
    store4(f0t, split_pair(f0[0].T, f0[1].T))


def fold(x, gs, gt, e, out):
    tr, ti = complex_dot(x, load4(gs))
    yr, yi = complex_dot(load4(gt), split_pair(tr, ti))
    out[0] = e[0] + packed(yr)
    out[1] = e[1] + packed(yi)


def step_kernel(active, gs, gt, e, *refs):
    *received, out = refs

    @pl.when(active(whereabouts()[0]))
    def _():
        value = received[0][...]
        for other in received[1:]:
            value = value + other[...]
        fold(split_pair(unpacked(value[0]), unpacked(value[1])), gs, gt, e, out)


def pair_kernel(g, e, g_in, e_in, e_second, fas, fat, ea, ps, pt, ep):
    upper = whereabouts()[0] > 1
    is_odd = whereabouts()[1] == 1
    ga = [jnp.where(is_odd, g_in[c], g[c]) for c in range(2)]
    gb = [jnp.where(is_odd, g[c], g_in[c]) for c in range(2)]
    theirs = [jnp.where(upper, e_in[c], e_second[c]) for c in range(2)]
    low = [jnp.where(is_odd, theirs[c], e[c]) for c in range(2)]
    high = [jnp.where(is_odd, e[c], theirs[c]) for c in range(2)]
    sa, sb = split_pair(*ga), split_pair(*gb)
    store4(fas, sa)
    store4(fat, split_pair(ga[0].T, ga[1].T))
    pr, pi = complex_dot(sa, sb)
    store4(ps, split_pair(pr, pi))
    store4(pt, split_pair(pr.T, pi.T))
    br, bi = complex_dot(split_pair(unpacked(low[0]), unpacked(low[1])), sb)
    tr, ti = complex_dot(split_pair(gb[0].T, gb[1].T), split_pair(br, bi))
    for c, term in enumerate((tr, ti)):
        ea[c] = low[c]
        ep[c] = high[c] + packed(term)


def sum_kernel(*refs):
    *parts, out = refs
    value = parts[0][...]
    for part in parts[1:]:
        value = value + part[...]
    out[...] = value


def share_kernel(fas, fat, ea, *refs):
    *received, own, sent, scratch = refs
    value = received[0][...]
    for other in received[1:]:
        value = value + other[...]
    value = jnp.where(whereabouts()[0] > 1, value, 0.0)
    fold(split_pair(unpacked(value[0]), unpacked(value[1])), fas, fat, ea, scratch)
    is_odd = whereabouts()[1] == 1
    own[...] = jnp.where(is_odd, scratch[...], value)
    sent[...] = jnp.where(is_odd, value, scratch[...])


def flat(block):
    half = block.shape[1] // 2
    return jnp.concatenate([block[:, :half], block[:, half:]], axis=0)


def real_dot(left, right):
    return dot3(left[0], left[2], right[0], right[2]) + dot3(left[1], left[3], right[1], right[3])


def off_values(slot, weight, xs, f0s, f0t, gs, weighted):
    width = f0s.shape[-1]
    w0, w1 = weight[pl.ds(slot, 1), 0:1], weight[pl.ds(slot, 1), 1:2]
    qr, qi = wide_dot(xs, load4(gs))
    ts = split_pair(w1 * qr + w0 * qi, w0 * qr - w1 * qi)
    second = real_dot(load4(f0t), ts)
    pr, pi = wide_dot(xs, load4(f0s))
    u = w1 * pr + w0 * pi
    us = split_pair(u, w0 * pr - w1 * pi)
    constant = jnp.concatenate([weighted[2], weighted[3, : width - 8]], axis=0)
    return -flat(u), -(flat(second) + constant), us, ts


def diag_values(us, ts, f0t, gt, weighted):
    return (
        weighted[0] + packed(real_dot(load4(f0t), us)),
        weighted[1] + packed(real_dot(load4(gt), ts)),
    )


def density_kernel(weight, x, f0s, f0t, gs, gt, weighted, _, off, diag):
    core = whereabouts()[2]
    first, second, us, ts = off_values(slot_of(True), weight, unpacked_split(x), f0s, f0t, gs, weighted)
    off[core], off[1 - core] = first, second
    diag[core], diag[1 - core] = diag_values(us, ts, f0t, gt, weighted)


def more_off_kernel(weight, x_even, x_odd, x_first, f0s, f0t, gs, weighted, before, off, us_out, ts_out):
    core = whereabouts()[2]
    place = whereabouts()[0]
    x = [
        jnp.where(place > 1, x_even[c] + x_odd[c], jnp.where(place == 1, x_first[c], 0.0))
        for c in range(2)
    ]
    xs = split_pair(unpacked(x[0]), unpacked(x[1]))
    first, second, us, ts = off_values(slot_of(False), weight, xs, f0s, f0t, gs, weighted)
    off[core] = first + before[core]
    off[1 - core] = second + before[1 - core]
    store4(us_out, us)
    store4(ts_out, ts)


def more_diag_kernel(us, ts, f0t, gt, weighted, before, diag):
    core = whereabouts()[2]
    first, second = diag_values(load4(us), load4(ts), f0t, gt, weighted)
    diag[core] = first + before[core]
    diag[1 - core] = second + before[1 - core]


def unpack_off_kernel(mine, theirs, off, done):
    core = whereabouts()[2]
    width = off.shape[-1]
    half = width // 2
    for source, entry in ((mine, core), (theirs, 1 - core)):
        off[entry, :, :half] = source[:width]
        off[entry, :, half:] = source[width:]
    done[...] = jnp.zeros_like(done)


def unpack_diag_kernel(mine, theirs, _, diag):
    core = whereabouts()[2]
    for source, entry in ((mine, core), (theirs, 1 - core)):
        diag[entry] = unpacked(source[...])


SCALAR = pl.BlockSpec(memory_space=pltpu.SMEM)
WHOLE = pl.BlockSpec(memory_space=pltpu.VMEM)


COST = pl.CostEstimate(flops=1, bytes_accessed=1, transcendentals=0)


LONG = pl.CostEstimate(flops=10**11, bytes_accessed=1, transcendentals=0)


def run(kernel, scalars, arrays, shapes, scratch=(), cost=COST, far=()):
    return pl.pallas_call(
        kernel,
        out_shape=shapes,
        in_specs=[SCALAR] * len(scalars)
        + [pl.BlockSpec(memory_space=pltpu.HBM)] * len(far)
        + [WHOLE] * len(arrays),
        out_specs=[WHOLE] * len(shapes),
        scratch_shapes=list(scratch),
        compiler_params=pltpu.CompilerParams(vmem_limit_bytes=VMEM_LIMIT),
        cost_estimate=cost,
    )(*scalars, *far, *arrays)


def local(pivot, factor, live, weight):
    poles, turns = lax.axis_size("pole"), lax.axis_size("snode")
    rows = turns // 2
    width = pivot.shape[-1]
    quarter = (width + 8, width // 2)
    mirrored = jax.ShapeDtypeStruct((2,) + quarter, F32)
    parts = jax.ShapeDtypeStruct((4, width, width), BF16)

    def at(pole_index, snode_index):
        return pole_index * turns + snode_index

    def hosts(row, pole):
        return at(pole, 2 * row + 1), at(pole, 2 * row)

    swaps = [(at(p, s), at(p, s ^ 1)) for p in range(poles) for s in range(2, turns)]
    first = [(at(p, 0), at(p, 1)) for p in range(poles)]
    every = [(at(p, s), at(p, s ^ 1)) for p in range(poles) for s in range(turns)]
    raw = jax.ShapeDtypeStruct((2, width, width), F32)
    constants = [parts, mirrored, jax.ShapeDtypeStruct((4,) + quarter, F32), raw]
    factors = [parts, parts, parts, parts, raw]

    scratch = [
        pltpu.VMEM(pivot.shape[1:], F32),
        pltpu.VMEM(factor.shape[2:], F32),
        pltpu.SMEM(live.shape, jnp.int32),
        pltpu.VMEM(weight.shape, F32),
        pltpu.SemaphoreType.DMA((6,)),
    ]
    far = [pltpu.with_memory_space_constraint(a, pltpu.HBM) for a in (live, pivot, factor, weight)]
    made = run(sent_constant_kernel, [], [], constants * 2, scratch, far=far)
    made, second = made[:4], made[4:]
    e_in = lax.ppermute(made[1], AXES, every)
    o_f1s, o_e, o_w, o_f0 = run(first_constant_kernel, [], made, constants, scratch, far=far)
    o_f0s, o_f0t, o_gs, o_gt, o_g = run(
        factor_kernel, [live], [o_f0, o_f1s], factors
    )
    g_in = lax.ppermute(o_g, AXES, swaps)
    made = run(sent_second_kernel, [live], [pivot, factor, weight, o_g, *second], constants)
    e_second = lax.ppermute(made[1], AXES, first)
    m_f1s, m_e, m_w, m_f0 = run(
        second_constant_kernel, [live], [pivot, factor, weight, *made], constants
    )
    m_f0s, m_f0t, m_gs, m_gt, m_g = run(
        factor_kernel, [live], [m_f0, m_f1s], factors
    )
    starts = functools.partial(step_kernel, lambda place: place == 1)
    (wave_even,) = run(starts, [], [o_gs, o_gt, o_e, e_in], [mirrored])
    wave_even = lax.ppermute(wave_even, AXES, [(at(p, 1), at(p, 0)) for p in range(poles)])
    (wave_odd,) = run(starts, [], [m_gs, m_gt, m_e, e_second], [mirrored])
    received = []
    if rows > 1:
        received = [
            lax.ppermute(wave_odd, AXES, [(at(p, 1), at(p, 3)) for p in range(poles)]),
            lax.ppermute(wave_even, AXES, [(at(p, 0), at(p, 2)) for p in range(poles)]),
        ]
    else:
        received = [jnp.zeros(mirrored.shape, F32)]
    fas, fat, ea, ps, pt, ep = run(
        pair_kernel,
        [],
        [m_g, m_e, g_in, e_in, e_second],
        [parts, parts, mirrored, parts, parts, mirrored],
        cost=LONG,
    )
    arrived = list(received)
    for turn in range(1, rows - 1):
        (wave,) = run(
            functools.partial(step_kernel, lambda place, turn=turn: lax.div(place, 2) == turn),
            [],
            [ps, pt, ep] + arrived,
            [mirrored],
        )
        odd, even = (
            [pair for p in range(poles) for pair in [(hosts(turn, p)[c], hosts(turn + 1, p)[c])]]
            for c in range(2)
        )
        if turn < rows - 2:
            arrived = [lax.ppermute(wave, AXES, odd + even)]
        else:
            arrived = [lax.ppermute(wave, AXES, odd), lax.ppermute(wave, AXES, even)]
        received += arrived
    pairs_in_rows = [(at(p, s), at(p, s + 1)) for p in range(poles) for s in range(2, turns, 2)]
    (entered_odd,) = run(sum_kernel, [], received[:1] + received[2:-1], [mirrored])
    shared_even = lax.ppermute(entered_odd, AXES, [(t, s) for s, t in pairs_in_rows])
    own, sent = run(
        share_kernel,
        [],
        [fas, fat, ea] + received,
        [mirrored, mirrored],
        [pltpu.VMEM(mirrored.shape, F32)],
    )
    shared_odd = lax.ppermute(sent, AXES, pairs_in_rows)

    offs = jax.ShapeDtypeStruct((2, 2 * width, width // 2), F32)
    diags = jax.ShapeDtypeStruct((2,) + quarter, F32)
    off, diag = run(density_kernel, [], [weight, own, m_f0s, m_f0t, m_gs, m_gt, m_w, shared_even], [offs, diags])
    off, us, ts = run(
        more_off_kernel,
        [],
        [weight, shared_even, shared_odd, e_in, o_f0s, o_f0t, o_gs, o_w, off],
        [offs, parts, parts],
    )

    def exchanged(value, distance):
        return lax.ppermute(value, "pole", [(p, p ^ distance) for p in range(poles)])

    def summed(parts):
        kept = parts[0] + exchanged(parts[1], 1)
        distance = 2
        while distance < poles:
            kept = kept + exchanged(kept, distance)
            distance *= 2
        return kept, exchanged(kept, 1)

    full = jax.ShapeDtypeStruct((2, width, width), F32)
    off_sums = summed(off)
    (diag,) = run(more_diag_kernel, [], [us, ts, o_f0t, o_gt, o_w, diag], [diags])
    diag_sums = summed(diag)
    done = jax.ShapeDtypeStruct((8, 128), F32)
    density_off, done = run(unpack_off_kernel, [], list(off_sums), [full, done])
    (density_diag,) = run(unpack_diag_kernel, [], [*diag_sums, done], [full])
    return density_diag, density_off


def solution(mesh):
    placed = (
        P("pole", "snode", None, None, None),
        P("pole", "snode", None, None, None),
        P("snode"),
        P("pole", None),
    )
    return jax.shard_map(
        local,
        mesh=mesh,
        in_specs=placed,
        out_specs=(P("snode", None, None), P("snode", None, None)),
        check_vma=False,
    )
```

```python
import functools

import jax
import jax.numpy as jnp
from jax import lax
from jax.experimental import pallas as pl
from jax.experimental.pallas import tpu as pltpu
from jax.sharding import PartitionSpec as P

F32 = jnp.float32
BF16 = jnp.bfloat16
AXES = ("pole", "snode")
VMEM_LIMIT = 16 * 1024 * 1024


def halves(value):
    high = value.astype(BF16)
    return high, (value - high.astype(F32)).astype(BF16)


def split_pair(real, imag):
    (rh, rl), (ih, il) = halves(real), halves(imag)
    return rh, ih, rl, il


def deep_dot(left, right):
    return jnp.dot(
        jnp.concatenate(left, axis=1), jnp.concatenate(right, axis=0), preferred_element_type=F32
    )


def dot(left, right):
    return jnp.dot(left, right, preferred_element_type=F32)


def dot3(lh, ll, rh, rl):
    return dot(lh, rh) + (dot(lh, rl) + dot(ll, rh))


def wide_dot(left, right):
    arh, aih, arl, ail = left
    brh, bih, brl, bil = right
    real = dot3(arh, arl, brh, brl) - dot3(aih, ail, bih, bil)
    imag = dot3(arh, arl, bih, bil) + dot3(aih, ail, brh, brl)
    return real, imag


def complex_dot(left, right):
    arh, aih, arl, ail = left
    brh, bih, brl, bil = right
    blocks = [arh, arh, arl, aih, aih, ail]
    real = deep_dot(blocks, [brh, brl, brh, -bih, -bil, -bih])
    imag = deep_dot(blocks, [bih, bil, bih, brh, brl, brh])
    return real, imag


def rows_columns(size):
    return (
        lax.broadcasted_iota(jnp.int32, (size, size), 0),
        lax.broadcasted_iota(jnp.int32, (size, size), 1),
    )


def packed(block):
    half = block.shape[0] // 2
    row, column = rows_columns(half)
    lower = block[half:, half:]
    mixed = jnp.where(row >= column, block[:half, :half], lower)
    diagonal = jnp.sum(jnp.where(row == column, lower, 0.0), axis=0, keepdims=True)
    return jnp.concatenate(
        [block[:half, half:], mixed, jnp.broadcast_to(diagonal, (8, half))], axis=0
    )


def unpacked(value):
    half = value.shape[1]
    row, column = rows_columns(half)
    right, mixed = value[:half], value[half : 2 * half]
    diagonal = value[2 * half : 2 * half + 1]
    turned = mixed.T
    first = jnp.where(row >= column, mixed, turned)
    last = jnp.where(row < column, mixed, jnp.where(row == column, diagonal, turned))
    return jnp.concatenate(
        [jnp.concatenate([first, right], axis=1), jnp.concatenate([right.T, last], axis=1)], axis=0
    )


def unpacked_split(ref):
    return split_pair(unpacked(ref[0]), unpacked(ref[1]))


def load4(ref):
    return tuple(ref[i] for i in range(4))


def store4(ref, parts):
    for i, part in enumerate(parts):
        ref[i] = part


def whereabouts():
    place = lax.axis_index("snode")
    return place, lax.rem(place, 2), lax.rem(lax.axis_index("pole"), 2)


def hosted_slot():
    place, odd, _ = whereabouts()
    return jnp.where(place < 2, 0, 1 - odd)


def slot_of(hosted):
    return hosted_slot() if hosted else 1 - hosted_slot()


def constants_of(slot, blocks, link, widths, weights, f1s, e, weighted, *_, wait=lambda: None):
    width = blocks.shape[-1]
    row, column = rows_columns(width)
    kept = [column < widths[k] for k in range(2)]
    both = [jnp.logical_and(row < widths[k], kept[k]) for k in range(2)]
    f1 = [jnp.where(kept[1], link[c], 0.0) for c in range(2)]
    s1, t1 = split_pair(*f1), split_pair(f1[0].T, f1[1].T)
    store4(f1s, s1)
    wait()
    d = [[jnp.where(both[k], blocks[k, c], 0.0) for c in range(2)] for k in range(2)]
    br, bi = complex_dot(split_pair(*d[0]), s1)
    tr, ti = complex_dot(t1, split_pair(br, bi))
    er, ei = d[1][0] + tr, d[1][1] + ti
    e[0], e[1] = packed(er), packed(ei)
    w0, w1 = weights[pl.ds(slot, 1), 0:1], weights[pl.ds(slot, 1), 1:2]
    weighted[0] = packed(w1 * d[0][0] + w0 * d[0][1])
    weighted[1] = packed(w1 * er + w0 * ei)
    weighted_b = flat(w1 * br + w0 * bi)
    weighted[2] = weighted_b[: width + 8]
    weighted[3, : width - 8] = weighted_b[width + 8 :]


def fetched_constants(slot, live, pivot, factor, weight, outs, scratch):
    blocks, link, widths, weights, sems = scratch
    first_factor = pltpu.make_async_copy(factor.at[slot, 0], outs[3], sems.at[5])
    copies = [
        pltpu.make_async_copy(live, widths, sems.at[0]),
        pltpu.make_async_copy(factor.at[slot, 1], link, sems.at[1]),
        pltpu.make_async_copy(pivot.at[slot, 0], blocks.at[0], sems.at[2]),
        pltpu.make_async_copy(pivot.at[slot, 1], blocks.at[1], sems.at[3]),
        pltpu.make_async_copy(weight, weights, sems.at[4]),
    ]
    for copy in copies:
        copy.start()
    first_factor.start()
    copies[0].wait()
    copies[1].wait()

    def wait():
        for copy in copies[2:]:
            copy.wait()

    constants_of(slot, blocks, link, widths, weights, *outs, wait=wait)
    first_factor.wait()


def sent_constant_kernel(live, pivot, factor, weight, *refs):
    outs, second, scratch = refs[:4], refs[4:8], refs[8:]
    place, _, core = whereabouts()

    @pl.when(jnp.logical_and(place != 1, core == 0))
    def _():
        fetched_constants(slot_of(True), live, pivot, factor, weight, second, scratch)

    @pl.when(jnp.logical_or(place != 1, core == 0))
    def _():
        fetched_constants(slot_of(False), live, pivot, factor, weight, outs, scratch)


def first_constant_kernel(live, pivot, factor, weight, *refs):
    made, outs, scratch = refs[:4], refs[4:8], refs[8:]
    place, _, core = whereabouts()
    late = jnp.logical_and(place == 1, core == 1)

    @pl.when(jnp.logical_not(late))
    def _():
        for source, target in zip(made, outs):
            target[...] = source[...]

    @pl.when(late)
    def _():
        fetched_constants(slot_of(False), live, pivot, factor, weight, outs, scratch)


def second_constants(live, pivot, factor, weight, f1s, e, weighted, first_factor):
    slot = slot_of(True)
    first_factor[...] = factor[slot, 0]
    constants_of(slot, pivot.at[slot], factor.at[slot, 1], live, weight, f1s, e, weighted)


def sent_second_kernel(live, pivot, factor, weight, _, *refs):
    made, outs = refs[:4], refs[4:]
    place, _, core = whereabouts()

    @pl.when(core == 0)
    def _():
        for source, target in zip(made, outs):
            target[...] = source[...]

    @pl.when(jnp.logical_and(place != 1, core == 1))
    def _():
        second_constants(live, pivot, factor, weight, *outs)


def second_constant_kernel(live, pivot, factor, weight, *refs):
    made, outs = refs[:4], refs[4:]
    place = whereabouts()[0]

    @pl.when(place != 1)
    def _():
        for source, target in zip(made, outs):
            target[...] = source[...]

    @pl.when(place == 1)
    def _():
        second_constants(live, pivot, factor, weight, *outs)


def factor_kernel(live, factor, f1s, f0s, f0t, gs, gt, g):
    _, column = rows_columns(factor.shape[-1])
    f0 = [jnp.where(column < live[0], factor[c], 0.0) for c in range(2)]
    s0 = split_pair(*f0)
    gr, gi = complex_dot(s0, load4(f1s))
    g[0], g[1] = gr, gi
    store4(gs, split_pair(gr, gi))
    store4(gt, split_pair(gr.T, gi.T))
    store4(f0s, s0)
    store4(f0t, split_pair(f0[0].T, f0[1].T))


def fold(x, gs, gt, e, out):
    tr, ti = complex_dot(x, load4(gs))
    yr, yi = complex_dot(load4(gt), split_pair(tr, ti))
    out[0] = e[0] + packed(yr)
    out[1] = e[1] + packed(yi)


def step_kernel(active, gs, gt, e, *refs):
    *received, out = refs

    @pl.when(active(whereabouts()[0]))
    def _():
        value = received[0][...]
        for other in received[1:]:
            value = value + other[...]
        fold(split_pair(unpacked(value[0]), unpacked(value[1])), gs, gt, e, out)


def cross_kernel(gs, gt, e, x, second, out):
    place = whereabouts()[0]

    @pl.when(place == 0)
    def _():
        out[...] = second[...]

    @pl.when(place == 1)
    def _():
        fold(unpacked_split(x), gs, gt, e, out)


def pair_kernel(g, e, g_in, e_in, e_second, fas, fat, ea, ps, pt, ep):
    upper = whereabouts()[0] > 1
    is_odd = whereabouts()[1] == 1
    ga = [jnp.where(is_odd, g_in[c], g[c]) for c in range(2)]
    gb = [jnp.where(is_odd, g[c], g_in[c]) for c in range(2)]
    theirs = [jnp.where(upper, e_in[c], e_second[c]) for c in range(2)]
    low = [jnp.where(is_odd, theirs[c], e[c]) for c in range(2)]
    high = [jnp.where(is_odd, e[c], theirs[c]) for c in range(2)]
    sa, sb = split_pair(*ga), split_pair(*gb)
    store4(fas, sa)
    store4(fat, split_pair(ga[0].T, ga[1].T))
    pr, pi = complex_dot(sa, sb)
    store4(ps, split_pair(pr, pi))
    store4(pt, split_pair(pr.T, pi.T))
    br, bi = complex_dot(split_pair(unpacked(low[0]), unpacked(low[1])), sb)
    tr, ti = complex_dot(split_pair(gb[0].T, gb[1].T), split_pair(br, bi))
    for c, term in enumerate((tr, ti)):
        ea[c] = low[c]
        ep[c] = high[c] + packed(term)


def share_kernel(fas, fat, ea, *refs):
    *received, own, sent, scratch = refs
    value = received[0][...]
    for other in received[1:]:
        value = value + other[...]
    value = jnp.where(whereabouts()[0] > 1, value, 0.0)
    fold(split_pair(unpacked(value[0]), unpacked(value[1])), fas, fat, ea, scratch)
    is_odd = whereabouts()[1] == 1
    own[...] = jnp.where(is_odd, scratch[...], value)
    sent[...] = jnp.where(is_odd, value, scratch[...])


def flat(block):
    half = block.shape[1] // 2
    return jnp.concatenate([block[:, :half], block[:, half:]], axis=0)


def real_dot(left, right):
    return dot3(left[0], left[2], right[0], right[2]) + dot3(left[1], left[3], right[1], right[3])


def off_values(slot, weight, xs, f0s, f0t, gs, weighted):
    width = f0s.shape[-1]
    w0, w1 = weight[pl.ds(slot, 1), 0:1], weight[pl.ds(slot, 1), 1:2]
    qr, qi = wide_dot(xs, load4(gs))
    ts = split_pair(w1 * qr + w0 * qi, w0 * qr - w1 * qi)
    second = real_dot(load4(f0t), ts)
    pr, pi = wide_dot(xs, load4(f0s))
    u = w1 * pr + w0 * pi
    us = split_pair(u, w0 * pr - w1 * pi)
    constant = jnp.concatenate([weighted[2], weighted[3, : width - 8]], axis=0)
    return -flat(u), -(flat(second) + constant), us, ts


def diag_values(us, ts, f0t, gt, weighted):
    return (
        weighted[0] + packed(real_dot(load4(f0t), us)),
        weighted[1] + packed(real_dot(load4(gt), ts)),
    )


def density_kernel(weight, x, f0s, f0t, gs, gt, weighted, off, diag):
    core = whereabouts()[2]
    first, second, us, ts = off_values(slot_of(True), weight, unpacked_split(x), f0s, f0t, gs, weighted)
    off[core], off[1 - core] = first, second
    diag[core], diag[1 - core] = diag_values(us, ts, f0t, gt, weighted)


def more_off_kernel(weight, x, x_first, f0s, f0t, gs, weighted, before, off, us_out, ts_out):
    core = whereabouts()[2]
    place = whereabouts()[0]
    x = [
        jnp.where(place > 1, x[c], jnp.where(place == 1, x_first[c], 0.0)) for c in range(2)
    ]
    xs = split_pair(unpacked(x[0]), unpacked(x[1]))
    first, second, us, ts = off_values(slot_of(False), weight, xs, f0s, f0t, gs, weighted)
    off[core] = first + before[core]
    off[1 - core] = second + before[1 - core]
    store4(us_out, us)
    store4(ts_out, ts)


def more_diag_kernel(us, ts, f0t, gt, weighted, before, diag):
    core = whereabouts()[2]
    first, second = diag_values(load4(us), load4(ts), f0t, gt, weighted)
    diag[core] = first + before[core]
    diag[1 - core] = second + before[1 - core]


def unpack_off_kernel(mine, theirs, off, done):
    core = whereabouts()[2]
    width = off.shape[-1]
    half = width // 2
    for source, entry in ((mine, core), (theirs, 1 - core)):
        off[entry, :, :half] = source[:width]
        off[entry, :, half:] = source[width:]
    done[...] = jnp.zeros_like(done)


def unpack_diag_kernel(mine, theirs, _, diag):
    core = whereabouts()[2]
    for source, entry in ((mine, core), (theirs, 1 - core)):
        diag[entry] = unpacked(source[...])


SCALAR = pl.BlockSpec(memory_space=pltpu.SMEM)
WHOLE = pl.BlockSpec(memory_space=pltpu.VMEM)


COST = pl.CostEstimate(flops=1, bytes_accessed=1, transcendentals=0)


LONG = pl.CostEstimate(flops=10**11, bytes_accessed=1, transcendentals=0)


def run(kernel, scalars, arrays, shapes, scratch=(), cost=COST, far=()):
    return pl.pallas_call(
        kernel,
        out_shape=shapes,
        in_specs=[SCALAR] * len(scalars)
        + [pl.BlockSpec(memory_space=pltpu.HBM)] * len(far)
        + [WHOLE] * len(arrays),
        out_specs=[WHOLE] * len(shapes),
        scratch_shapes=list(scratch),
        compiler_params=pltpu.CompilerParams(vmem_limit_bytes=VMEM_LIMIT),
        cost_estimate=cost,
    )(*scalars, *far, *arrays)


def local(pivot, factor, live, weight):
    poles, turns = lax.axis_size("pole"), lax.axis_size("snode")
    rows = turns // 2
    width = pivot.shape[-1]
    quarter = (width + 8, width // 2)
    mirrored = jax.ShapeDtypeStruct((2,) + quarter, F32)
    parts = jax.ShapeDtypeStruct((4, width, width), BF16)

    def at(pole_index, snode_index):
        return pole_index * turns + snode_index

    def hosts(row, pole):
        return at(pole, 2 * row + 1), at(pole, 2 * row)

    swaps = [(at(p, s), at(p, s ^ 1)) for p in range(poles) for s in range(2, turns)]
    first = [(at(p, 0), at(p, 1)) for p in range(poles)]
    every = [(at(p, s), at(p, s ^ 1)) for p in range(poles) for s in range(turns)]
    raw = jax.ShapeDtypeStruct((2, width, width), F32)
    constants = [parts, mirrored, jax.ShapeDtypeStruct((4,) + quarter, F32), raw]
    factors = [parts, parts, parts, parts, raw]

    scratch = [
        pltpu.VMEM(pivot.shape[1:], F32),
        pltpu.VMEM(factor.shape[2:], F32),
        pltpu.SMEM(live.shape, jnp.int32),
        pltpu.VMEM(weight.shape, F32),
        pltpu.SemaphoreType.DMA((6,)),
    ]
    far = [pltpu.with_memory_space_constraint(a, pltpu.HBM) for a in (live, pivot, factor, weight)]
    made = run(sent_constant_kernel, [], [], constants * 2, scratch, far=far)
    made, second = made[:4], made[4:]
    e_in = lax.ppermute(made[1], AXES, every)
    o_f1s, o_e, o_w, o_f0 = run(first_constant_kernel, [], made, constants, scratch, far=far)
    o_f0s, o_f0t, o_gs, o_gt, o_g = run(
        factor_kernel, [live], [o_f0, o_f1s], factors
    )
    g_in = lax.ppermute(o_g, AXES, swaps)
    made = run(sent_second_kernel, [live], [pivot, factor, weight, o_g, *second], constants)
    (wave_even,) = run(cross_kernel, [], [o_gs, o_gt, o_e, e_in, made[1]], [mirrored])
    crossed = lax.ppermute(
        wave_even, AXES, first + [(at(p, 1), at(p, 0)) for p in range(poles)]
    )
    m_f1s, m_e, m_w, m_f0 = run(
        second_constant_kernel, [live], [pivot, factor, weight, *made], constants
    )
    m_f0s, m_f0t, m_gs, m_gt, m_g = run(
        factor_kernel, [live], [m_f0, m_f1s], factors
    )
    starts = functools.partial(step_kernel, lambda place: place == 1)
    (wave_odd,) = run(starts, [], [m_gs, m_gt, m_e, crossed], [mirrored])
    received = []
    if rows > 1:
        received = [
            lax.ppermute(wave_odd, AXES, [(at(p, 1), at(p, 3)) for p in range(poles)]),
            lax.ppermute(crossed, AXES, [(at(p, 0), at(p, 2)) for p in range(poles)]),
        ]
    else:
        received = [jnp.zeros(mirrored.shape, F32)]
    fas, fat, ea, ps, pt, ep = run(
        pair_kernel,
        [],
        [m_g, m_e, g_in, e_in, crossed],
        [parts, parts, mirrored, parts, parts, mirrored],
        cost=LONG,
    )
    arrived = list(received)
    for turn in range(1, rows - 1):
        active = functools.partial(step_kernel, lambda place, turn=turn: lax.div(place, 2) == turn)
        (wave,) = run(active, [], [ps, pt, ep] + arrived, [mirrored])
        up = [pair for p in range(poles) for pair in zip(hosts(turn, p), hosts(turn + 1, p))]
        arrived = [lax.ppermute(wave, AXES, up)]
        received += arrived
    own, sent = run(
        share_kernel,
        [],
        [fas, fat, ea] + received,
        [mirrored, mirrored],
        [pltpu.VMEM(mirrored.shape, F32)],
    )
    shared = lax.ppermute(sent, AXES, every)

    offs = jax.ShapeDtypeStruct((2, 2 * width, width // 2), F32)
    diags = jax.ShapeDtypeStruct((2,) + quarter, F32)
    off, diag = run(density_kernel, [], [weight, own, m_f0s, m_f0t, m_gs, m_gt, m_w], [offs, diags])
    off, us, ts = run(
        more_off_kernel,
        [],
        [weight, shared, e_in, o_f0s, o_f0t, o_gs, o_w, off],
        [offs, parts, parts],
    )

    def exchanged(value, distance):
        return lax.ppermute(value, "pole", [(p, p ^ distance) for p in range(poles)])

    def summed(parts):
        kept = parts[0] + exchanged(parts[1], 1)
        distance = 2
        while distance < poles:
            kept = kept + exchanged(kept, distance)
            distance *= 2
        return kept, exchanged(kept, 1)

    full = jax.ShapeDtypeStruct((2, width, width), F32)
    off_sums = summed(off)
    (diag,) = run(more_diag_kernel, [], [us, ts, o_f0t, o_gt, o_w, diag], [diags])
    diag_sums = summed(diag)
    done = jax.ShapeDtypeStruct((8, 128), F32)
    density_off, done = run(unpack_off_kernel, [], list(off_sums), [full, done])
    (density_diag,) = run(unpack_diag_kernel, [], [*diag_sums, done], [full])
    return density_diag, density_off


def solution(mesh):
    placed = (
        P("pole", "snode", None, None, None),
        P("pole", "snode", None, None, None),
        P("snode"),
        P("pole", None),
    )
    return jax.shard_map(
        local,
        mesh=mesh,
        in_specs=placed,
        out_specs=(P("snode", None, None), P("snode", None, None)),
        check_vma=False,
    )
```

```python
import functools

import jax
import jax.numpy as jnp
from jax import lax
from jax.experimental import pallas as pl
from jax.experimental.pallas import tpu as pltpu
from jax.sharding import PartitionSpec as P

F32 = jnp.float32
BF16 = jnp.bfloat16
AXES = ("pole", "snode")
VMEM_LIMIT = 16 * 1024 * 1024


def halves(value):
    high = value.astype(BF16)
    return high, (value - high.astype(F32)).astype(BF16)


def split_pair(real, imag):
    (rh, rl), (ih, il) = halves(real), halves(imag)
    return rh, ih, rl, il


def deep_dot(left, right):
    return jnp.dot(
        jnp.concatenate(left, axis=1), jnp.concatenate(right, axis=0), preferred_element_type=F32
    )


def dot(left, right):
    return jnp.dot(left, right, preferred_element_type=F32)


def dot3(lh, ll, rh, rl):
    return dot(lh, rh) + (dot(lh, rl) + dot(ll, rh))


def wide_dot(left, right):
    arh, aih, arl, ail = left
    brh, bih, brl, bil = right
    real = dot3(arh, arl, brh, brl) - dot3(aih, ail, bih, bil)
    imag = dot3(arh, arl, bih, bil) + dot3(aih, ail, brh, brl)
    return real, imag


def complex_dot(left, right):
    arh, aih, arl, ail = left
    brh, bih, brl, bil = right
    blocks = [arh, arh, arl, aih, aih, ail]
    real = deep_dot(blocks, [brh, brl, brh, -bih, -bil, -bih])
    imag = deep_dot(blocks, [bih, bil, bih, brh, brl, brh])
    return real, imag


def rows_columns(size):
    return (
        lax.broadcasted_iota(jnp.int32, (size, size), 0),
        lax.broadcasted_iota(jnp.int32, (size, size), 1),
    )


def packed(block):
    half = block.shape[0] // 2
    row, column = rows_columns(half)
    lower = block[half:, half:]
    mixed = jnp.where(row >= column, block[:half, :half], lower)
    diagonal = jnp.sum(jnp.where(row == column, lower, 0.0), axis=0, keepdims=True)
    return jnp.concatenate(
        [block[:half, half:], mixed, jnp.broadcast_to(diagonal, (8, half))], axis=0
    )


def unpacked(value):
    half = value.shape[1]
    row, column = rows_columns(half)
    right, mixed = value[:half], value[half : 2 * half]
    diagonal = value[2 * half : 2 * half + 1]
    turned = mixed.T
    first = jnp.where(row >= column, mixed, turned)
    last = jnp.where(row < column, mixed, jnp.where(row == column, diagonal, turned))
    return jnp.concatenate(
        [jnp.concatenate([first, right], axis=1), jnp.concatenate([right.T, last], axis=1)], axis=0
    )


def unpacked_split(ref):
    return split_pair(unpacked(ref[0]), unpacked(ref[1]))


def load4(ref):
    return tuple(ref[i] for i in range(4))


def store4(ref, parts):
    for i, part in enumerate(parts):
        ref[i] = part


def whereabouts():
    place = lax.axis_index("snode")
    return place, lax.rem(place, 2), lax.rem(lax.axis_index("pole"), 2)


def hosted_slot():
    place, odd, _ = whereabouts()
    return jnp.where(place < 2, 0, 1 - odd)


def slot_of(hosted):
    return hosted_slot() if hosted else 1 - hosted_slot()


def constants_of(slot, blocks, link, widths, weights, f1s, e, weighted, *_, wait=lambda: None):
    width = blocks.shape[-1]
    row, column = rows_columns(width)
    kept = [column < widths[k] for k in range(2)]
    both = [jnp.logical_and(row < widths[k], kept[k]) for k in range(2)]
    f1 = [jnp.where(kept[1], link[c], 0.0) for c in range(2)]
    s1, t1 = split_pair(*f1), split_pair(f1[0].T, f1[1].T)
    store4(f1s, s1)
    wait()
    d = [[jnp.where(both[k], blocks[k, c], 0.0) for c in range(2)] for k in range(2)]
    br, bi = complex_dot(split_pair(*d[0]), s1)
    tr, ti = complex_dot(t1, split_pair(br, bi))
    er, ei = d[1][0] + tr, d[1][1] + ti
    e[0], e[1] = packed(er), packed(ei)
    w0, w1 = weights[pl.ds(slot, 1), 0:1], weights[pl.ds(slot, 1), 1:2]
    weighted[0] = packed(w1 * d[0][0] + w0 * d[0][1])
    weighted[1] = packed(w1 * er + w0 * ei)
    weighted_b = flat(w1 * br + w0 * bi)
    weighted[2] = weighted_b[: width + 8]
    weighted[3, : width - 8] = weighted_b[width + 8 :]


def fetched_constants(slot, live, pivot, factor, weight, outs, scratch):
    blocks, link, widths, weights, sems = scratch
    first_factor = pltpu.make_async_copy(factor.at[slot, 0], outs[3], sems.at[5])
    copies = [
        pltpu.make_async_copy(live, widths, sems.at[0]),
        pltpu.make_async_copy(factor.at[slot, 1], link, sems.at[1]),
        pltpu.make_async_copy(pivot.at[slot, 0], blocks.at[0], sems.at[2]),
        pltpu.make_async_copy(pivot.at[slot, 1], blocks.at[1], sems.at[3]),
        pltpu.make_async_copy(weight, weights, sems.at[4]),
    ]
    for copy in copies:
        copy.start()
    first_factor.start()
    copies[0].wait()
    copies[1].wait()

    def wait():
        for copy in copies[2:]:
            copy.wait()

    constants_of(slot, blocks, link, widths, weights, *outs, wait=wait)
    first_factor.wait()


def sent_constant_kernel(live, pivot, factor, weight, *refs):
    outs, second, scratch = refs[:4], refs[4:8], refs[8:]
    place, _, core = whereabouts()

    @pl.when(jnp.logical_and(place != 1, core == 0))
    def _():
        fetched_constants(slot_of(True), live, pivot, factor, weight, second, scratch)

    @pl.when(jnp.logical_or(place != 1, core == 0))
    def _():
        fetched_constants(slot_of(False), live, pivot, factor, weight, outs, scratch)


def first_constant_kernel(live, pivot, factor, weight, *refs):
    made, outs, scratch = refs[:4], refs[4:8], refs[8:]
    place, _, core = whereabouts()
    late = jnp.logical_and(place == 1, core == 1)

    @pl.when(jnp.logical_not(late))
    def _():
        for source, target in zip(made, outs):
            target[...] = source[...]

    @pl.when(late)
    def _():
        fetched_constants(slot_of(False), live, pivot, factor, weight, outs, scratch)


def second_constants(live, pivot, factor, weight, f1s, e, weighted, first_factor):
    slot = slot_of(True)
    first_factor[...] = factor[slot, 0]
    constants_of(slot, pivot.at[slot], factor.at[slot, 1], live, weight, f1s, e, weighted)


def sent_second_kernel(live, pivot, factor, weight, _, *refs):
    made, outs = refs[:4], refs[4:]
    place, _, core = whereabouts()

    @pl.when(core == 0)
    def _():
        for source, target in zip(made, outs):
            target[...] = source[...]

    @pl.when(jnp.logical_and(place != 1, core == 1))
    def _():
        second_constants(live, pivot, factor, weight, *outs)


def second_constant_kernel(live, pivot, factor, weight, *refs):
    made, outs = refs[:4], refs[4:]
    place = whereabouts()[0]

    @pl.when(place != 1)
    def _():
        for source, target in zip(made, outs):
            target[...] = source[...]

    @pl.when(place == 1)
    def _():
        second_constants(live, pivot, factor, weight, *outs)


def factor_kernel(live, factor, f1s, f0s, f0t, gs, gt, g):
    _, column = rows_columns(factor.shape[-1])
    f0 = [jnp.where(column < live[0], factor[c], 0.0) for c in range(2)]
    s0 = split_pair(*f0)
    gr, gi = complex_dot(s0, load4(f1s))
    g[0], g[1] = gr, gi
    store4(gs, split_pair(gr, gi))
    store4(gt, split_pair(gr.T, gi.T))
    store4(f0s, s0)
    store4(f0t, split_pair(f0[0].T, f0[1].T))


def fold(x, gs, gt, e, out):
    tr, ti = complex_dot(x, load4(gs))
    yr, yi = complex_dot(load4(gt), split_pair(tr, ti))
    out[0] = e[0] + packed(yr)
    out[1] = e[1] + packed(yi)


def step_kernel(active, gs, gt, e, *refs):
    *received, out = refs

    @pl.when(active(whereabouts()[0]))
    def _():
        value = received[0][...]
        for other in received[1:]:
            value = value + other[...]
        fold(split_pair(unpacked(value[0]), unpacked(value[1])), gs, gt, e, out)


def cross_kernel(gs, gt, e, x, second, out):
    place = whereabouts()[0]

    @pl.when(place == 0)
    def _():
        out[...] = second[...]

    @pl.when(place == 1)
    def _():
        fold(unpacked_split(x), gs, gt, e, out)


def pair_kernel(g, e, g_in, e_in, e_second, fas, fat, ea, ps, pt, ep):
    upper = whereabouts()[0] > 1
    is_odd = whereabouts()[1] == 1
    ga = [jnp.where(is_odd, g_in[c], g[c]) for c in range(2)]
    gb = [jnp.where(is_odd, g[c], g_in[c]) for c in range(2)]
    theirs = [jnp.where(upper, e_in[c], e_second[c]) for c in range(2)]
    low = [jnp.where(is_odd, theirs[c], e[c]) for c in range(2)]
    high = [jnp.where(is_odd, e[c], theirs[c]) for c in range(2)]
    sa, sb = split_pair(*ga), split_pair(*gb)
    store4(fas, sa)
    store4(fat, split_pair(ga[0].T, ga[1].T))
    pr, pi = complex_dot(sa, sb)
    store4(ps, split_pair(pr, pi))
    store4(pt, split_pair(pr.T, pi.T))
    br, bi = complex_dot(split_pair(unpacked(low[0]), unpacked(low[1])), sb)
    tr, ti = complex_dot(split_pair(gb[0].T, gb[1].T), split_pair(br, bi))
    for c, term in enumerate((tr, ti)):
        ea[c] = low[c]
        ep[c] = high[c] + packed(term)


def share_kernel(fas, fat, ea, *refs):
    *received, own, sent, scratch = refs
    value = received[0][...]
    for other in received[1:]:
        value = value + other[...]
    value = jnp.where(whereabouts()[0] > 1, value, 0.0)
    fold(split_pair(unpacked(value[0]), unpacked(value[1])), fas, fat, ea, scratch)
    is_odd = whereabouts()[1] == 1
    own[...] = jnp.where(is_odd, scratch[...], value)
    sent[...] = jnp.where(is_odd, value, scratch[...])


def flat(block):
    half = block.shape[1] // 2
    return jnp.concatenate([block[:, :half], block[:, half:]], axis=0)


def real_dot(left, right):
    return dot3(left[0], left[2], right[0], right[2]) + dot3(left[1], left[3], right[1], right[3])


def weights_of(wave_slot, weight):
    return weight[pl.ds(wave_slot, 1), 0:1], weight[pl.ds(wave_slot, 1), 1:2]


def first_off(weights, xs, f0s):
    w0, w1 = weights
    pr, pi = wide_dot(xs, load4(f0s))
    u = w1 * pr + w0 * pi
    return -flat(u), split_pair(u, w0 * pr - w1 * pi)


def second_off(weights, xs, f0t, gs, weighted):
    width = f0t.shape[-1]
    w0, w1 = weights
    qr, qi = wide_dot(xs, load4(gs))
    ts = split_pair(w1 * qr + w0 * qi, w0 * qr - w1 * qi)
    constant = jnp.concatenate([weighted[2], weighted[3, : width - 8]], axis=0)
    return -(flat(real_dot(load4(f0t), ts)) + constant), ts


def diag_values(us, ts, f0t, gt, weighted):
    return (
        weighted[0] + packed(real_dot(load4(f0t), us)),
        weighted[1] + packed(real_dot(load4(gt), ts)),
    )


def density_kernel(weight, x, f0s, f0t, gs, gt, weighted, off, diag):
    core = whereabouts()[2]
    xs, weights = unpacked_split(x), weights_of(slot_of(True), weight)
    second, ts = second_off(weights, xs, f0t, gs, weighted)
    first, us = first_off(weights, xs, f0s)
    off[core], off[1 - core] = first, second
    diag[core], diag[1 - core] = diag_values(us, ts, f0t, gt, weighted)


def more_off_kernel(sent, weight, x, x_first, f0s, f0t, gs, weighted, before, out, split):
    place, _, core = whereabouts()
    for first in (False, True):

        @pl.when(core == (1 if first == sent else 0))
        def _():
            value = [
                jnp.where(place > 1, x[c], jnp.where(place == 1, x_first[c], 0.0)) for c in range(2)
            ]
            xs = split_pair(unpacked(value[0]), unpacked(value[1]))
            weights = weights_of(slot_of(False), weight)
            if first:
                block, parts = first_off(weights, xs, f0s)
            else:
                block, parts = second_off(weights, xs, f0t, gs, weighted)
            out[...] = block + before[1 if sent else 0]
            store4(split, parts)


def more_diag_kernel(kept, sent, f0t, gt, weighted, before, diag):
    core = whereabouts()[2]
    for here, us, ts in ((0, kept, sent), (1, sent, kept)):

        @pl.when(core == here)
        def _():
            first, second = diag_values(load4(us), load4(ts), f0t, gt, weighted)
            diag[here] = first + before[here]
            diag[1 - here] = second + before[1 - here]


def unpack_off_kernel(mine, theirs, off, done):
    core = whereabouts()[2]
    width = off.shape[-1]
    half = width // 2
    for source, entry in ((mine, core), (theirs, 1 - core)):
        off[entry, :, :half] = source[:width]
        off[entry, :, half:] = source[width:]
    done[...] = jnp.zeros_like(done)


def unpack_diag_kernel(mine, theirs, _, diag):
    core = whereabouts()[2]
    for source, entry in ((mine, core), (theirs, 1 - core)):
        diag[entry] = unpacked(source[...])


SCALAR = pl.BlockSpec(memory_space=pltpu.SMEM)
WHOLE = pl.BlockSpec(memory_space=pltpu.VMEM)


COST = pl.CostEstimate(flops=1, bytes_accessed=1, transcendentals=0)


LONG = pl.CostEstimate(flops=10**11, bytes_accessed=1, transcendentals=0)


def run(kernel, scalars, arrays, shapes, scratch=(), cost=COST, far=()):
    return pl.pallas_call(
        kernel,
        out_shape=shapes,
        in_specs=[SCALAR] * len(scalars)
        + [pl.BlockSpec(memory_space=pltpu.HBM)] * len(far)
        + [WHOLE] * len(arrays),
        out_specs=[WHOLE] * len(shapes),
        scratch_shapes=list(scratch),
        compiler_params=pltpu.CompilerParams(vmem_limit_bytes=VMEM_LIMIT),
        cost_estimate=cost,
    )(*scalars, *far, *arrays)


def local(pivot, factor, live, weight):
    poles, turns = lax.axis_size("pole"), lax.axis_size("snode")
    rows = turns // 2
    width = pivot.shape[-1]
    quarter = (width + 8, width // 2)
    mirrored = jax.ShapeDtypeStruct((2,) + quarter, F32)
    parts = jax.ShapeDtypeStruct((4, width, width), BF16)

    def at(pole_index, snode_index):
        return pole_index * turns + snode_index

    def hosts(row, pole):
        return at(pole, 2 * row + 1), at(pole, 2 * row)

    swaps = [(at(p, s), at(p, s ^ 1)) for p in range(poles) for s in range(2, turns)]
    first = [(at(p, 0), at(p, 1)) for p in range(poles)]
    every = [(at(p, s), at(p, s ^ 1)) for p in range(poles) for s in range(turns)]
    raw = jax.ShapeDtypeStruct((2, width, width), F32)
    constants = [parts, mirrored, jax.ShapeDtypeStruct((4,) + quarter, F32), raw]
    factors = [parts, parts, parts, parts, raw]

    scratch = [
        pltpu.VMEM(pivot.shape[1:], F32),
        pltpu.VMEM(factor.shape[2:], F32),
        pltpu.SMEM(live.shape, jnp.int32),
        pltpu.VMEM(weight.shape, F32),
        pltpu.SemaphoreType.DMA((6,)),
    ]
    far = [pltpu.with_memory_space_constraint(a, pltpu.HBM) for a in (live, pivot, factor, weight)]
    made = run(sent_constant_kernel, [], [], constants * 2, scratch, far=far)
    made, second = made[:4], made[4:]
    e_in = lax.ppermute(made[1], AXES, every)
    o_f1s, o_e, o_w, o_f0 = run(first_constant_kernel, [], made, constants, scratch, far=far)
    o_f0s, o_f0t, o_gs, o_gt, o_g = run(
        factor_kernel, [live], [o_f0, o_f1s], factors
    )
    g_in = lax.ppermute(o_g, AXES, swaps)
    made = run(sent_second_kernel, [live], [pivot, factor, weight, o_g, *second], constants)
    (wave_even,) = run(cross_kernel, [], [o_gs, o_gt, o_e, e_in, made[1]], [mirrored])
    crossed = lax.ppermute(
        wave_even, AXES, first + [(at(p, 1), at(p, 0)) for p in range(poles)]
    )
    m_f1s, m_e, m_w, m_f0 = run(
        second_constant_kernel, [live], [pivot, factor, weight, *made], constants
    )
    m_f0s, m_f0t, m_gs, m_gt, m_g = run(
        factor_kernel, [live], [m_f0, m_f1s], factors
    )
    starts = functools.partial(step_kernel, lambda place: place == 1)
    (wave_odd,) = run(starts, [], [m_gs, m_gt, m_e, crossed], [mirrored])
    received = []
    if rows > 1:
        received = [
            lax.ppermute(wave_odd, AXES, [(at(p, 1), at(p, 3)) for p in range(poles)]),
            lax.ppermute(crossed, AXES, [(at(p, 0), at(p, 2)) for p in range(poles)]),
        ]
    else:
        received = [jnp.zeros(mirrored.shape, F32)]
    fas, fat, ea, ps, pt, ep = run(
        pair_kernel,
        [],
        [m_g, m_e, g_in, e_in, crossed],
        [parts, parts, mirrored, parts, parts, mirrored],
        cost=LONG,
    )
    arrived = list(received)
    for turn in range(1, rows - 1):
        active = functools.partial(step_kernel, lambda place, turn=turn: lax.div(place, 2) == turn)
        (wave,) = run(active, [], [ps, pt, ep] + arrived, [mirrored])
        up = [pair for p in range(poles) for pair in zip(hosts(turn, p), hosts(turn + 1, p))]
        arrived = [lax.ppermute(wave, AXES, up)]
        received += arrived
    own, sent = run(
        share_kernel,
        [],
        [fas, fat, ea] + received,
        [mirrored, mirrored],
        [pltpu.VMEM(mirrored.shape, F32)],
    )
    shared = lax.ppermute(sent, AXES, every)

    offs = jax.ShapeDtypeStruct((2, 2 * width, width // 2), F32)
    diags = jax.ShapeDtypeStruct((2,) + quarter, F32)
    off, diag = run(density_kernel, [], [weight, own, m_f0s, m_f0t, m_gs, m_gt, m_w], [offs, diags])
    flat_off = jax.ShapeDtypeStruct(offs.shape[1:], F32)
    arrays = [weight, shared, e_in, o_f0s, o_f0t, o_gs, o_w, off]
    off_sent, sent_split = run(
        functools.partial(more_off_kernel, True), [], arrays, [flat_off, parts]
    )
    off_kept, kept_split = run(
        functools.partial(more_off_kernel, False), [], arrays, [flat_off, parts]
    )

    def exchanged(value, distance):
        return lax.ppermute(value, "pole", [(p, p ^ distance) for p in range(poles)])

    def summed(kept, sent):
        kept = kept + exchanged(sent, 1)
        distance = 2
        while distance < poles:
            kept = kept + exchanged(kept, distance)
            distance *= 2
        return kept, exchanged(kept, 1)

    full = jax.ShapeDtypeStruct((2, width, width), F32)
    off_sums = summed(off_kept, off_sent)
    (diag,) = run(
        more_diag_kernel, [], [kept_split, sent_split, o_f0t, o_gt, o_w, diag], [diags]
    )
    diag_sums = summed(diag[0], diag[1])
    done = jax.ShapeDtypeStruct((8, 128), F32)
    density_off, done = run(unpack_off_kernel, [], list(off_sums), [full, done])
    (density_diag,) = run(unpack_diag_kernel, [], [*diag_sums, done], [full])
    return density_diag, density_off


def solution(mesh):
    placed = (
        P("pole", "snode", None, None, None),
        P("pole", "snode", None, None, None),
        P("snode"),
        P("pole", None),
    )
    return jax.shard_map(
        local,
        mesh=mesh,
        in_specs=placed,
        out_specs=(P("snode", None, None), P("snode", None, None)),
        check_vma=False,
    )
```

```python
import functools

import jax
import jax.numpy as jnp
from jax import lax
from jax.experimental import pallas as pl
from jax.experimental.pallas import tpu as pltpu
from jax.sharding import PartitionSpec as P

F32 = jnp.float32
BF16 = jnp.bfloat16
AXES = ("pole", "snode")
VMEM_LIMIT = 16 * 1024 * 1024


def halves(value):
    high = value.astype(BF16)
    return high, (value - high.astype(F32)).astype(BF16)


def split_pair(real, imag):
    (rh, rl), (ih, il) = halves(real), halves(imag)
    return rh, ih, rl, il


def deep_dot(left, right):
    return jnp.dot(
        jnp.concatenate(left, axis=1), jnp.concatenate(right, axis=0), preferred_element_type=F32
    )


def dot(left, right):
    return jnp.dot(left, right, preferred_element_type=F32)


def dot3(lh, ll, rh, rl):
    return dot(lh, rh) + (dot(lh, rl) + dot(ll, rh))


def wide_dot(left, right):
    arh, aih, arl, ail = left
    brh, bih, brl, bil = right
    real = dot3(arh, arl, brh, brl) - dot3(aih, ail, bih, bil)
    imag = dot3(arh, arl, bih, bil) + dot3(aih, ail, brh, brl)
    return real, imag


def complex_dot(left, right):
    arh, aih, arl, ail = left
    brh, bih, brl, bil = right
    blocks = [arh, arh, arl, aih, aih, ail]
    real = deep_dot(blocks, [brh, brl, brh, -bih, -bil, -bih])
    imag = deep_dot(blocks, [bih, bil, bih, brh, brl, brh])
    return real, imag


def rows_columns(size):
    return (
        lax.broadcasted_iota(jnp.int32, (size, size), 0),
        lax.broadcasted_iota(jnp.int32, (size, size), 1),
    )


def packed(block):
    half = block.shape[0] // 2
    row, column = rows_columns(half)
    lower = block[half:, half:]
    mixed = jnp.where(row >= column, block[:half, :half], lower)
    diagonal = jnp.sum(jnp.where(row == column, lower, 0.0), axis=0, keepdims=True)
    return jnp.concatenate(
        [block[:half, half:], mixed, jnp.broadcast_to(diagonal, (8, half))], axis=0
    )


def unpacked(value):
    half = value.shape[1]
    row, column = rows_columns(half)
    right, mixed = value[:half], value[half : 2 * half]
    diagonal = value[2 * half : 2 * half + 1]
    turned = mixed.T
    first = jnp.where(row >= column, mixed, turned)
    last = jnp.where(row < column, mixed, jnp.where(row == column, diagonal, turned))
    return jnp.concatenate(
        [jnp.concatenate([first, right], axis=1), jnp.concatenate([right.T, last], axis=1)], axis=0
    )


def unpacked_split(ref):
    return split_pair(unpacked(ref[0]), unpacked(ref[1]))


def load4(ref):
    return tuple(ref[i] for i in range(4))


def store4(ref, parts):
    for i, part in enumerate(parts):
        ref[i] = part


def whereabouts():
    place = lax.axis_index("snode")
    return place, lax.rem(place, 2), lax.rem(lax.axis_index("pole"), 2)


def hosted_slot():
    place, odd, _ = whereabouts()
    return jnp.where(place < 2, 0, 1 - odd)


def slot_of(hosted):
    return hosted_slot() if hosted else 1 - hosted_slot()


def constants_of(slot, blocks, link, widths, weights, f1s, e, weighted, *_, wait=lambda: None):
    width = blocks.shape[-1]
    row, column = rows_columns(width)
    kept = [column < widths[k] for k in range(2)]
    both = [jnp.logical_and(row < widths[k], kept[k]) for k in range(2)]
    f1 = [jnp.where(kept[1], link[c], 0.0) for c in range(2)]
    s1, t1 = split_pair(*f1), split_pair(f1[0].T, f1[1].T)
    store4(f1s, s1)
    wait()
    d = [[jnp.where(both[k], blocks[k, c], 0.0) for c in range(2)] for k in range(2)]
    br, bi = complex_dot(split_pair(*d[0]), s1)
    tr, ti = complex_dot(t1, split_pair(br, bi))
    er, ei = d[1][0] + tr, d[1][1] + ti
    e[0], e[1] = packed(er), packed(ei)
    w0, w1 = weights[pl.ds(slot, 1), 0:1], weights[pl.ds(slot, 1), 1:2]
    weighted[0] = packed(w1 * d[0][0] + w0 * d[0][1])
    weighted[1] = packed(w1 * er + w0 * ei)
    weighted_b = flat(w1 * br + w0 * bi)
    weighted[2] = weighted_b[: width + 8]
    weighted[3, : width - 8] = weighted_b[width + 8 :]


def fetches(slot, live, pivot, factor, weight, outs, scratch):
    blocks, link, widths, weights, sems = scratch
    return [
        pltpu.make_async_copy(live, widths, sems.at[0]),
        pltpu.make_async_copy(factor.at[slot, 1], link, sems.at[1]),
        pltpu.make_async_copy(pivot.at[slot, 0], blocks.at[0], sems.at[2]),
        pltpu.make_async_copy(pivot.at[slot, 1], blocks.at[1], sems.at[3]),
        pltpu.make_async_copy(weight, weights, sems.at[4]),
        pltpu.make_async_copy(factor.at[slot, 0], outs[3], sems.at[5]),
    ]


def fetched_constants(slot, live, pivot, factor, weight, outs, scratch):
    blocks, link, widths, weights, _ = scratch
    copies = fetches(slot, live, pivot, factor, weight, outs, scratch)
    copies[0].wait()
    copies[1].wait()

    def wait():
        for copy in copies[2:]:
            copy.wait()

    constants_of(slot, blocks, link, widths, weights, *outs, wait=wait)


def sent_constant_kernel(live, pivot, factor, weight, *refs):
    outs, second, scratch, second_scratch = refs[:4], refs[4:8], refs[8:13], refs[13:]
    place, _, core = whereabouts()
    makes = jnp.logical_or(place != 1, core == 0)
    makes_second = jnp.logical_and(place != 1, core == 0)
    sources = live, pivot, factor, weight

    @pl.when(makes_second)
    def _():
        for copy in fetches(slot_of(True), *sources, second, second_scratch):
            copy.start()

    @pl.when(makes)
    def _():
        for copy in fetches(slot_of(False), *sources, outs, scratch):
            copy.start()

    @pl.when(makes_second)
    def _():
        fetched_constants(slot_of(True), *sources, second, second_scratch)

    @pl.when(makes)
    def _():
        fetched_constants(slot_of(False), *sources, outs, scratch)


def first_constant_kernel(live, pivot, factor, weight, *refs):
    made, outs, scratch = refs[:4], refs[4:8], refs[8:]
    place, _, core = whereabouts()
    late = jnp.logical_and(place == 1, core == 1)

    @pl.when(jnp.logical_not(late))
    def _():
        for source, target in zip(made, outs):
            target[...] = source[...]

    @pl.when(late)
    def _():
        for copy in fetches(slot_of(False), live, pivot, factor, weight, outs, scratch):
            copy.start()
        fetched_constants(slot_of(False), live, pivot, factor, weight, outs, scratch)


def second_constants(live, pivot, factor, weight, f1s, e, weighted, first_factor):
    slot = slot_of(True)
    first_factor[...] = factor[slot, 0]
    constants_of(slot, pivot.at[slot], factor.at[slot, 1], live, weight, f1s, e, weighted)


def sent_second_kernel(live, pivot, factor, weight, _, *refs):
    made, outs = refs[:4], refs[4:]
    place, _, core = whereabouts()

    @pl.when(core == 0)
    def _():
        for source, target in zip(made, outs):
            target[...] = source[...]

    @pl.when(jnp.logical_and(place != 1, core == 1))
    def _():
        second_constants(live, pivot, factor, weight, *outs)


def second_constant_kernel(live, pivot, factor, weight, *refs):
    made, outs = refs[:4], refs[4:]
    place = whereabouts()[0]

    @pl.when(place != 1)
    def _():
        for source, target in zip(made, outs):
            target[...] = source[...]

    @pl.when(place == 1)
    def _():
        second_constants(live, pivot, factor, weight, *outs)


def factor_kernel(live, factor, f1s, f0s, f0t, gs, gt, g):
    _, column = rows_columns(factor.shape[-1])
    f0 = [jnp.where(column < live[0], factor[c], 0.0) for c in range(2)]
    s0 = split_pair(*f0)
    gr, gi = complex_dot(s0, load4(f1s))
    g[0], g[1] = gr, gi
    store4(gs, split_pair(gr, gi))
    store4(gt, split_pair(gr.T, gi.T))
    store4(f0s, s0)
    store4(f0t, split_pair(f0[0].T, f0[1].T))


def fold(x, gs, gt, e, out):
    tr, ti = complex_dot(x, load4(gs))
    yr, yi = complex_dot(load4(gt), split_pair(tr, ti))
    out[0] = e[0] + packed(yr)
    out[1] = e[1] + packed(yi)


def step_kernel(active, gs, gt, e, *refs):
    *received, out = refs

    @pl.when(active(whereabouts()[0]))
    def _():
        value = received[0][...]
        for other in received[1:]:
            value = value + other[...]
        fold(split_pair(unpacked(value[0]), unpacked(value[1])), gs, gt, e, out)


def cross_kernel(gs, gt, e, x, second, out):
    place = whereabouts()[0]

    @pl.when(place == 0)
    def _():
        out[...] = second[...]

    @pl.when(place == 1)
    def _():
        fold(unpacked_split(x), gs, gt, e, out)


def pair_kernel(g, e, g_in, e_in, e_second, fas, fat, ea, ps, pt, ep):
    upper = whereabouts()[0] > 1
    is_odd = whereabouts()[1] == 1
    ga = [jnp.where(is_odd, g_in[c], g[c]) for c in range(2)]
    gb = [jnp.where(is_odd, g[c], g_in[c]) for c in range(2)]
    theirs = [jnp.where(upper, e_in[c], e_second[c]) for c in range(2)]
    low = [jnp.where(is_odd, theirs[c], e[c]) for c in range(2)]
    high = [jnp.where(is_odd, e[c], theirs[c]) for c in range(2)]
    sa, sb = split_pair(*ga), split_pair(*gb)
    store4(fas, sa)
    store4(fat, split_pair(ga[0].T, ga[1].T))
    pr, pi = complex_dot(sa, sb)
    store4(ps, split_pair(pr, pi))
    store4(pt, split_pair(pr.T, pi.T))
    br, bi = complex_dot(split_pair(unpacked(low[0]), unpacked(low[1])), sb)
    tr, ti = complex_dot(split_pair(gb[0].T, gb[1].T), split_pair(br, bi))
    for c, term in enumerate((tr, ti)):
        ea[c] = low[c]
        ep[c] = high[c] + packed(term)


def share_kernel(fas, fat, ea, *refs):
    *received, own, sent, scratch = refs
    value = received[0][...]
    for other in received[1:]:
        value = value + other[...]
    value = jnp.where(whereabouts()[0] > 1, value, 0.0)
    fold(split_pair(unpacked(value[0]), unpacked(value[1])), fas, fat, ea, scratch)
    is_odd = whereabouts()[1] == 1
    own[...] = jnp.where(is_odd, scratch[...], value)
    sent[...] = jnp.where(is_odd, value, scratch[...])


def flat(block):
    half = block.shape[1] // 2
    return jnp.concatenate([block[:, :half], block[:, half:]], axis=0)


def real_dot(left, right):
    return dot3(left[0], left[2], right[0], right[2]) + dot3(left[1], left[3], right[1], right[3])


def off_values(slot, weight, xs, f0s, f0t, gs, weighted):
    width = f0s.shape[-1]
    w0, w1 = weight[pl.ds(slot, 1), 0:1], weight[pl.ds(slot, 1), 1:2]
    qr, qi = wide_dot(xs, load4(gs))
    ts = split_pair(w1 * qr + w0 * qi, w0 * qr - w1 * qi)
    second = real_dot(load4(f0t), ts)
    pr, pi = wide_dot(xs, load4(f0s))
    u = w1 * pr + w0 * pi
    us = split_pair(u, w0 * pr - w1 * pi)
    constant = jnp.concatenate([weighted[2], weighted[3, : width - 8]], axis=0)
    return -flat(u), -(flat(second) + constant), us, ts


def diag_values(us, ts, f0t, gt, weighted):
    return (
        weighted[0] + packed(real_dot(load4(f0t), us)),
        weighted[1] + packed(real_dot(load4(gt), ts)),
    )


def density_kernel(weight, x, f0s, f0t, gs, gt, weighted, off, diag):
    core = whereabouts()[2]
    first, second, us, ts = off_values(slot_of(True), weight, unpacked_split(x), f0s, f0t, gs, weighted)
    off[core], off[1 - core] = first, second
    diag[core], diag[1 - core] = diag_values(us, ts, f0t, gt, weighted)


def more_off_kernel(weight, x, x_first, f0s, f0t, gs, weighted, before, off, us_out, ts_out):
    core = whereabouts()[2]
    place = whereabouts()[0]
    x = [
        jnp.where(place > 1, x[c], jnp.where(place == 1, x_first[c], 0.0)) for c in range(2)
    ]
    xs = split_pair(unpacked(x[0]), unpacked(x[1]))
    first, second, us, ts = off_values(slot_of(False), weight, xs, f0s, f0t, gs, weighted)
    off[core] = first + before[core]
    off[1 - core] = second + before[1 - core]
    store4(us_out, us)
    store4(ts_out, ts)


def more_diag_kernel(us, ts, f0t, gt, weighted, before, diag):
    core = whereabouts()[2]
    first, second = diag_values(load4(us), load4(ts), f0t, gt, weighted)
    diag[core] = first + before[core]
    diag[1 - core] = second + before[1 - core]


def unpack_off_kernel(mine, theirs, off, done):
    core = whereabouts()[2]
    width = off.shape[-1]
    half = width // 2
    for source, entry in ((mine, core), (theirs, 1 - core)):
        off[entry, :, :half] = source[:width]
        off[entry, :, half:] = source[width:]
    done[...] = jnp.zeros_like(done)


def unpack_diag_kernel(mine, theirs, _, diag):
    core = whereabouts()[2]
    for source, entry in ((mine, core), (theirs, 1 - core)):
        diag[entry] = unpacked(source[...])


SCALAR = pl.BlockSpec(memory_space=pltpu.SMEM)
WHOLE = pl.BlockSpec(memory_space=pltpu.VMEM)


COST = pl.CostEstimate(flops=1, bytes_accessed=1, transcendentals=0)


LONG = pl.CostEstimate(flops=10**11, bytes_accessed=1, transcendentals=0)


def run(kernel, scalars, arrays, shapes, scratch=(), cost=COST, far=()):
    return pl.pallas_call(
        kernel,
        out_shape=shapes,
        in_specs=[SCALAR] * len(scalars)
        + [pl.BlockSpec(memory_space=pltpu.HBM)] * len(far)
        + [WHOLE] * len(arrays),
        out_specs=[WHOLE] * len(shapes),
        scratch_shapes=list(scratch),
        compiler_params=pltpu.CompilerParams(vmem_limit_bytes=VMEM_LIMIT),
        cost_estimate=cost,
    )(*scalars, *far, *arrays)


def local(pivot, factor, live, weight):
    poles, turns = lax.axis_size("pole"), lax.axis_size("snode")
    rows = turns // 2
    width = pivot.shape[-1]
    quarter = (width + 8, width // 2)
    mirrored = jax.ShapeDtypeStruct((2,) + quarter, F32)
    parts = jax.ShapeDtypeStruct((4, width, width), BF16)

    def at(pole_index, snode_index):
        return pole_index * turns + snode_index

    def hosts(row, pole):
        return at(pole, 2 * row + 1), at(pole, 2 * row)

    swaps = [(at(p, s), at(p, s ^ 1)) for p in range(poles) for s in range(2, turns)]
    first = [(at(p, 0), at(p, 1)) for p in range(poles)]
    every = [(at(p, s), at(p, s ^ 1)) for p in range(poles) for s in range(turns)]
    raw = jax.ShapeDtypeStruct((2, width, width), F32)
    constants = [parts, mirrored, jax.ShapeDtypeStruct((4,) + quarter, F32), raw]
    factors = [parts, parts, parts, parts, raw]

    scratch = [
        pltpu.VMEM(pivot.shape[1:], F32),
        pltpu.VMEM(factor.shape[2:], F32),
        pltpu.SMEM(live.shape, jnp.int32),
        pltpu.VMEM(weight.shape, F32),
        pltpu.SemaphoreType.DMA((6,)),
    ]
    far = [pltpu.with_memory_space_constraint(a, pltpu.HBM) for a in (live, pivot, factor, weight)]
    made = run(sent_constant_kernel, [], [], constants * 2, scratch * 2, far=far)
    made, second = made[:4], made[4:]
    e_in = lax.ppermute(made[1], AXES, every)
    o_f1s, o_e, o_w, o_f0 = run(first_constant_kernel, [], made, constants, scratch, far=far)
    o_f0s, o_f0t, o_gs, o_gt, o_g = run(
        factor_kernel, [live], [o_f0, o_f1s], factors
    )
    g_in = lax.ppermute(o_g, AXES, swaps)
    made = run(sent_second_kernel, [live], [pivot, factor, weight, o_g, *second], constants)
    (wave_even,) = run(cross_kernel, [], [o_gs, o_gt, o_e, e_in, made[1]], [mirrored])
    crossed = lax.ppermute(
        wave_even, AXES, first + [(at(p, 1), at(p, 0)) for p in range(poles)]
    )
    m_f1s, m_e, m_w, m_f0 = run(
        second_constant_kernel, [live], [pivot, factor, weight, *made], constants
    )
    m_f0s, m_f0t, m_gs, m_gt, m_g = run(
        factor_kernel, [live], [m_f0, m_f1s], factors
    )
    starts = functools.partial(step_kernel, lambda place: place == 1)
    (wave_odd,) = run(starts, [], [m_gs, m_gt, m_e, crossed], [mirrored])
    received = []
    if rows > 1:
        received = [
            lax.ppermute(wave_odd, AXES, [(at(p, 1), at(p, 3)) for p in range(poles)]),
            lax.ppermute(crossed, AXES, [(at(p, 0), at(p, 2)) for p in range(poles)]),
        ]
    else:
        received = [jnp.zeros(mirrored.shape, F32)]
    fas, fat, ea, ps, pt, ep = run(
        pair_kernel,
        [],
        [m_g, m_e, g_in, e_in, crossed],
        [parts, parts, mirrored, parts, parts, mirrored],
        cost=LONG,
    )
    arrived = list(received)
    for turn in range(1, rows - 1):
        active = functools.partial(step_kernel, lambda place, turn=turn: lax.div(place, 2) == turn)
        (wave,) = run(active, [], [ps, pt, ep] + arrived, [mirrored])
        up = [pair for p in range(poles) for pair in zip(hosts(turn, p), hosts(turn + 1, p))]
        arrived = [lax.ppermute(wave, AXES, up)]
        received += arrived
    own, sent = run(
        share_kernel,
        [],
        [fas, fat, ea] + received,
        [mirrored, mirrored],
        [pltpu.VMEM(mirrored.shape, F32)],
    )
    shared = lax.ppermute(sent, AXES, every)

    offs = jax.ShapeDtypeStruct((2, 2 * width, width // 2), F32)
    diags = jax.ShapeDtypeStruct((2,) + quarter, F32)
    off, diag = run(density_kernel, [], [weight, own, m_f0s, m_f0t, m_gs, m_gt, m_w], [offs, diags])
    off, us, ts = run(
        more_off_kernel,
        [],
        [weight, shared, e_in, o_f0s, o_f0t, o_gs, o_w, off],
        [offs, parts, parts],
    )

    def exchanged(value, distance):
        return lax.ppermute(value, "pole", [(p, p ^ distance) for p in range(poles)])

    def summed(parts):
        kept = parts[0] + exchanged(parts[1], 1)
        distance = 2
        while distance < poles:
            kept = kept + exchanged(kept, distance)
            distance *= 2
        return kept, exchanged(kept, 1)

    full = jax.ShapeDtypeStruct((2, width, width), F32)
    off_sums = summed(off)
    (diag,) = run(more_diag_kernel, [], [us, ts, o_f0t, o_gt, o_w, diag], [diags])
    diag_sums = summed(diag)
    done = jax.ShapeDtypeStruct((8, 128), F32)
    density_off, done = run(unpack_off_kernel, [], list(off_sums), [full, done])
    (density_diag,) = run(unpack_diag_kernel, [], [*diag_sums, done], [full])
    return density_diag, density_off


def solution(mesh):
    placed = (
        P("pole", "snode", None, None, None),
        P("pole", "snode", None, None, None),
        P("snode"),
        P("pole", None),
    )
    return jax.shard_map(
        local,
        mesh=mesh,
        in_specs=placed,
        out_specs=(P("snode", None, None), P("snode", None, None)),
        check_vma=False,
    )
```

```python
import functools

import jax
import jax.numpy as jnp
from jax import lax
from jax.experimental import pallas as pl
from jax.experimental.pallas import tpu as pltpu
from jax.sharding import PartitionSpec as P

F32 = jnp.float32
BF16 = jnp.bfloat16
AXES = ("pole", "snode")
VMEM_LIMIT = 16 * 1024 * 1024


def halves(value):
    high = value.astype(BF16)
    return high, (value - high.astype(F32)).astype(BF16)


def split_pair(real, imag):
    (rh, rl), (ih, il) = halves(real), halves(imag)
    return rh, ih, rl, il


def deep_dot(left, right):
    return jnp.dot(
        jnp.concatenate(left, axis=1), jnp.concatenate(right, axis=0), preferred_element_type=F32
    )


def dot(left, right):
    return jnp.dot(left, right, preferred_element_type=F32)


def dot3(lh, ll, rh, rl):
    return dot(lh, rh) + (dot(lh, rl) + dot(ll, rh))


def wide_dot(left, right):
    arh, aih, arl, ail = left
    brh, bih, brl, bil = right
    real = dot3(arh, arl, brh, brl) - dot3(aih, ail, bih, bil)
    imag = dot3(arh, arl, bih, bil) + dot3(aih, ail, brh, brl)
    return real, imag


def complex_dot(left, right):
    arh, aih, arl, ail = left
    brh, bih, brl, bil = right
    blocks = [arh, arh, arl, aih, aih, ail]
    real = deep_dot(blocks, [brh, brl, brh, -bih, -bil, -bih])
    imag = deep_dot(blocks, [bih, bil, bih, brh, brl, brh])
    return real, imag


def rows_columns(size):
    return (
        lax.broadcasted_iota(jnp.int32, (size, size), 0),
        lax.broadcasted_iota(jnp.int32, (size, size), 1),
    )


def packed(block):
    half = block.shape[0] // 2
    row, column = rows_columns(half)
    lower = block[half:, half:]
    mixed = jnp.where(row >= column, block[:half, :half], lower)
    diagonal = jnp.sum(jnp.where(row == column, lower, 0.0), axis=0, keepdims=True)
    return jnp.concatenate(
        [block[:half, half:], mixed, jnp.broadcast_to(diagonal, (8, half))], axis=0
    )


def unpacked(value):
    half = value.shape[1]
    row, column = rows_columns(half)
    right, mixed = value[:half], value[half : 2 * half]
    diagonal = value[2 * half : 2 * half + 1]
    turned = mixed.T
    first = jnp.where(row >= column, mixed, turned)
    last = jnp.where(row < column, mixed, jnp.where(row == column, diagonal, turned))
    return jnp.concatenate(
        [jnp.concatenate([first, right], axis=1), jnp.concatenate([right.T, last], axis=1)], axis=0
    )


def unpacked_split(ref):
    return split_pair(unpacked(ref[0]), unpacked(ref[1]))


def load4(ref):
    return tuple(ref[i] for i in range(4))


def store4(ref, parts):
    for i, part in enumerate(parts):
        ref[i] = part


def whereabouts():
    place = lax.axis_index("snode")
    return place, lax.rem(place, 2), lax.rem(lax.axis_index("pole"), 2)


def hosted_slot():
    place, odd, _ = whereabouts()
    return jnp.where(place < 2, 0, 1 - odd)


def slot_of(hosted):
    return hosted_slot() if hosted else 1 - hosted_slot()


def constants_of(slot, blocks, link, widths, weights, f1s, e, weighted, *_, wait=lambda: None):
    width = blocks.shape[-1]
    row, column = rows_columns(width)
    kept = [column < widths[k] for k in range(2)]
    both = [jnp.logical_and(row < widths[k], kept[k]) for k in range(2)]
    f1 = [jnp.where(kept[1], link[c], 0.0) for c in range(2)]
    s1, t1 = split_pair(*f1), split_pair(f1[0].T, f1[1].T)
    store4(f1s, s1)
    wait()
    d = [[jnp.where(both[k], blocks[k, c], 0.0) for c in range(2)] for k in range(2)]
    br, bi = complex_dot(split_pair(*d[0]), s1)
    tr, ti = complex_dot(t1, split_pair(br, bi))
    er, ei = d[1][0] + tr, d[1][1] + ti
    e[0], e[1] = packed(er), packed(ei)
    w0, w1 = weights[pl.ds(slot, 1), 0:1], weights[pl.ds(slot, 1), 1:2]
    weighted[0] = packed(w1 * d[0][0] + w0 * d[0][1])
    weighted[1] = packed(w1 * er + w0 * ei)
    weighted_b = flat(w1 * br + w0 * bi)
    weighted[2] = weighted_b[: width + 8]
    weighted[3, : width - 8] = weighted_b[width + 8 :]


def fetched_constants(slot, live, pivot, factor, weight, outs, scratch):
    blocks, link, widths, weights, sems = scratch
    first_factor = pltpu.make_async_copy(factor.at[slot, 0], outs[3], sems.at[5])
    copies = [
        pltpu.make_async_copy(live, widths, sems.at[0]),
        pltpu.make_async_copy(factor.at[slot, 1], link, sems.at[1]),
        pltpu.make_async_copy(pivot.at[slot, 0], blocks.at[0], sems.at[2]),
        pltpu.make_async_copy(pivot.at[slot, 1], blocks.at[1], sems.at[3]),
        pltpu.make_async_copy(weight, weights, sems.at[4]),
    ]
    for copy in copies:
        copy.start()
    first_factor.start()
    copies[0].wait()
    copies[1].wait()

    def wait():
        for copy in copies[2:]:
            copy.wait()

    constants_of(slot, blocks, link, widths, weights, *outs, wait=wait)
    first_factor.wait()


def sent_constant_kernel(live, pivot, factor, weight, *refs):
    outs, second, scratch = refs[:4], refs[4:8], refs[8:]
    place, _, core = whereabouts()

    @pl.when(jnp.logical_and(place != 1, core == 1))
    def _():
        fetched_constants(slot_of(True), live, pivot, factor, weight, second, scratch)

    @pl.when(jnp.logical_or(place != 1, core == 1))
    def _():
        fetched_constants(slot_of(False), live, pivot, factor, weight, outs, scratch)


def first_constant_kernel(live, pivot, factor, weight, *refs):
    made, outs, scratch = refs[:4], refs[4:8], refs[8:]
    place, _, core = whereabouts()
    late = jnp.logical_and(place == 1, core == 0)

    @pl.when(jnp.logical_not(late))
    def _():
        for source, target in zip(made, outs):
            target[...] = source[...]

    @pl.when(late)
    def _():
        fetched_constants(slot_of(False), live, pivot, factor, weight, outs, scratch)


def second_constants(live, pivot, factor, weight, f1s, e, weighted, first_factor):
    slot = slot_of(True)
    first_factor[...] = factor[slot, 0]
    constants_of(slot, pivot.at[slot], factor.at[slot, 1], live, weight, f1s, e, weighted)


def sent_second_kernel(live, pivot, factor, weight, _, *refs):
    made, outs = refs[:4], refs[4:]
    place, _, core = whereabouts()

    @pl.when(core == 1)
    def _():
        for source, target in zip(made, outs):
            target[...] = source[...]

    @pl.when(jnp.logical_and(place != 1, core == 0))
    def _():
        second_constants(live, pivot, factor, weight, *outs)


def second_constant_kernel(live, pivot, factor, weight, *refs):
    made, outs = refs[:4], refs[4:]
    place = whereabouts()[0]

    @pl.when(place != 1)
    def _():
        for source, target in zip(made, outs):
            target[...] = source[...]

    @pl.when(place == 1)
    def _():
        second_constants(live, pivot, factor, weight, *outs)


def factor_kernel(live, factor, f1s, f0s, f0t, gs, gt, g):
    _, column = rows_columns(factor.shape[-1])
    f0 = [jnp.where(column < live[0], factor[c], 0.0) for c in range(2)]
    s0 = split_pair(*f0)
    gr, gi = complex_dot(s0, load4(f1s))
    g[0], g[1] = gr, gi
    store4(gs, split_pair(gr, gi))
    store4(gt, split_pair(gr.T, gi.T))
    store4(f0s, s0)
    store4(f0t, split_pair(f0[0].T, f0[1].T))


def fold(x, gs, gt, e, out):
    tr, ti = complex_dot(x, load4(gs))
    yr, yi = complex_dot(load4(gt), split_pair(tr, ti))
    out[0] = e[0] + packed(yr)
    out[1] = e[1] + packed(yi)


def step_kernel(active, gs, gt, e, *refs):
    *received, out = refs

    @pl.when(active(whereabouts()[0]))
    def _():
        value = received[0][...]
        for other in received[1:]:
            value = value + other[...]
        fold(split_pair(unpacked(value[0]), unpacked(value[1])), gs, gt, e, out)


def cross_kernel(gs, gt, e, x, second, out):
    place = whereabouts()[0]

    @pl.when(place == 0)
    def _():
        out[...] = second[...]

    @pl.when(place == 1)
    def _():
        fold(unpacked_split(x), gs, gt, e, out)


def pair_kernel(g, e, g_in, e_in, e_second, fas, fat, ea, ps, pt, ep):
    upper = whereabouts()[0] > 1
    is_odd = whereabouts()[1] == 1
    ga = [jnp.where(is_odd, g_in[c], g[c]) for c in range(2)]
    gb = [jnp.where(is_odd, g[c], g_in[c]) for c in range(2)]
    theirs = [jnp.where(upper, e_in[c], e_second[c]) for c in range(2)]
    low = [jnp.where(is_odd, theirs[c], e[c]) for c in range(2)]
    high = [jnp.where(is_odd, e[c], theirs[c]) for c in range(2)]
    sa, sb = split_pair(*ga), split_pair(*gb)
    store4(fas, sa)
    store4(fat, split_pair(ga[0].T, ga[1].T))
    pr, pi = complex_dot(sa, sb)
    store4(ps, split_pair(pr, pi))
    store4(pt, split_pair(pr.T, pi.T))
    br, bi = complex_dot(split_pair(unpacked(low[0]), unpacked(low[1])), sb)
    tr, ti = complex_dot(split_pair(gb[0].T, gb[1].T), split_pair(br, bi))
    for c, term in enumerate((tr, ti)):
        ea[c] = low[c]
        ep[c] = high[c] + packed(term)


def share_kernel(fas, fat, ea, *refs):
    *received, own, sent, scratch = refs
    value = received[0][...]
    for other in received[1:]:
        value = value + other[...]
    value = jnp.where(whereabouts()[0] > 1, value, 0.0)
    fold(split_pair(unpacked(value[0]), unpacked(value[1])), fas, fat, ea, scratch)
    is_odd = whereabouts()[1] == 1
    own[...] = jnp.where(is_odd, scratch[...], value)
    sent[...] = jnp.where(is_odd, value, scratch[...])


def flat(block):
    half = block.shape[1] // 2
    return jnp.concatenate([block[:, :half], block[:, half:]], axis=0)


def real_dot(left, right):
    return dot3(left[0], left[2], right[0], right[2]) + dot3(left[1], left[3], right[1], right[3])


def off_values(slot, weight, xs, f0s, f0t, gs, weighted):
    width = f0s.shape[-1]
    w0, w1 = weight[pl.ds(slot, 1), 0:1], weight[pl.ds(slot, 1), 1:2]
    qr, qi = wide_dot(xs, load4(gs))
    ts = split_pair(w1 * qr + w0 * qi, w0 * qr - w1 * qi)
    second = real_dot(load4(f0t), ts)
    pr, pi = wide_dot(xs, load4(f0s))
    u = w1 * pr + w0 * pi
    us = split_pair(u, w0 * pr - w1 * pi)
    constant = jnp.concatenate([weighted[2], weighted[3, : width - 8]], axis=0)
    return -flat(u), -(flat(second) + constant), us, ts


def diag_values(us, ts, f0t, gt, weighted):
    return (
        weighted[0] + packed(real_dot(load4(f0t), us)),
        weighted[1] + packed(real_dot(load4(gt), ts)),
    )


def density_kernel(weight, x, f0s, f0t, gs, gt, weighted, off, diag):
    core = whereabouts()[2]
    first, second, us, ts = off_values(slot_of(True), weight, unpacked_split(x), f0s, f0t, gs, weighted)
    off[core], off[1 - core] = first, second
    diag[core], diag[1 - core] = diag_values(us, ts, f0t, gt, weighted)


def more_off_kernel(weight, x, x_first, f0s, f0t, gs, weighted, before, off, us_out, ts_out):
    core = whereabouts()[2]
    place = whereabouts()[0]
    x = [
        jnp.where(place > 1, x[c], jnp.where(place == 1, x_first[c], 0.0)) for c in range(2)
    ]
    xs = split_pair(unpacked(x[0]), unpacked(x[1]))
    first, second, us, ts = off_values(slot_of(False), weight, xs, f0s, f0t, gs, weighted)
    off[core] = first + before[core]
    off[1 - core] = second + before[1 - core]
    store4(us_out, us)
    store4(ts_out, ts)


def more_diag_kernel(us, ts, f0t, gt, weighted, before, diag):
    core = whereabouts()[2]
    first, second = diag_values(load4(us), load4(ts), f0t, gt, weighted)
    diag[core] = first + before[core]
    diag[1 - core] = second + before[1 - core]


def unpack_off_kernel(mine, theirs, off, done):
    core = whereabouts()[2]
    width = off.shape[-1]
    half = width // 2
    for source, entry in ((mine, core), (theirs, 1 - core)):
        off[entry, :, :half] = source[:width]
        off[entry, :, half:] = source[width:]
    done[...] = jnp.zeros_like(done)


def unpack_diag_kernel(mine, theirs, _, diag):
    core = whereabouts()[2]
    for source, entry in ((mine, core), (theirs, 1 - core)):
        diag[entry] = unpacked(source[...])


SCALAR = pl.BlockSpec(memory_space=pltpu.SMEM)
WHOLE = pl.BlockSpec(memory_space=pltpu.VMEM)


COST = pl.CostEstimate(flops=1, bytes_accessed=1, transcendentals=0)


LONG = pl.CostEstimate(flops=10**11, bytes_accessed=1, transcendentals=0)


def run(kernel, scalars, arrays, shapes, scratch=(), cost=COST, far=()):
    return pl.pallas_call(
        kernel,
        out_shape=shapes,
        in_specs=[SCALAR] * len(scalars)
        + [pl.BlockSpec(memory_space=pltpu.HBM)] * len(far)
        + [WHOLE] * len(arrays),
        out_specs=[WHOLE] * len(shapes),
        scratch_shapes=list(scratch),
        compiler_params=pltpu.CompilerParams(vmem_limit_bytes=VMEM_LIMIT),
        cost_estimate=cost,
    )(*scalars, *far, *arrays)


def local(pivot, factor, live, weight):
    poles, turns = lax.axis_size("pole"), lax.axis_size("snode")
    rows = turns // 2
    width = pivot.shape[-1]
    quarter = (width + 8, width // 2)
    mirrored = jax.ShapeDtypeStruct((2,) + quarter, F32)
    parts = jax.ShapeDtypeStruct((4, width, width), BF16)

    def at(pole_index, snode_index):
        return pole_index * turns + snode_index

    def hosts(row, pole):
        return at(pole, 2 * row + 1), at(pole, 2 * row)

    swaps = [(at(p, s), at(p, s ^ 1)) for p in range(poles) for s in range(2, turns)]
    first = [(at(p, 0), at(p, 1)) for p in range(poles)]
    every = [(at(p, s), at(p, s ^ 1)) for p in range(poles) for s in range(turns)]
    raw = jax.ShapeDtypeStruct((2, width, width), F32)
    constants = [parts, mirrored, jax.ShapeDtypeStruct((4,) + quarter, F32), raw]
    factors = [parts, parts, parts, parts, raw]

    scratch = [
        pltpu.VMEM(pivot.shape[1:], F32),
        pltpu.VMEM(factor.shape[2:], F32),
        pltpu.SMEM(live.shape, jnp.int32),
        pltpu.VMEM(weight.shape, F32),
        pltpu.SemaphoreType.DMA((6,)),
    ]
    far = [pltpu.with_memory_space_constraint(a, pltpu.HBM) for a in (live, pivot, factor, weight)]
    made = run(sent_constant_kernel, [], [], constants * 2, scratch, far=far)
    made, second = made[:4], made[4:]
    e_in = lax.ppermute(made[1], AXES, every)
    o_f1s, o_e, o_w, o_f0 = run(first_constant_kernel, [], made, constants, scratch, far=far)
    o_f0s, o_f0t, o_gs, o_gt, o_g = run(
        factor_kernel, [live], [o_f0, o_f1s], factors
    )
    g_in = lax.ppermute(o_g, AXES, swaps)
    made = run(sent_second_kernel, [live], [pivot, factor, weight, o_g, *second], constants)
    (wave_even,) = run(cross_kernel, [], [o_gs, o_gt, o_e, e_in, made[1]], [mirrored])
    crossed = lax.ppermute(
        wave_even, AXES, first + [(at(p, 1), at(p, 0)) for p in range(poles)]
    )
    m_f1s, m_e, m_w, m_f0 = run(
        second_constant_kernel, [live], [pivot, factor, weight, *made], constants
    )
    m_f0s, m_f0t, m_gs, m_gt, m_g = run(
        factor_kernel, [live], [m_f0, m_f1s], factors
    )
    starts = functools.partial(step_kernel, lambda place: place == 1)
    (wave_odd,) = run(starts, [], [m_gs, m_gt, m_e, crossed], [mirrored])
    received = []
    if rows > 1:
        received = [
            lax.ppermute(wave_odd, AXES, [(at(p, 1), at(p, 3)) for p in range(poles)]),
            lax.ppermute(crossed, AXES, [(at(p, 0), at(p, 2)) for p in range(poles)]),
        ]
    else:
        received = [jnp.zeros(mirrored.shape, F32)]
    fas, fat, ea, ps, pt, ep = run(
        pair_kernel,
        [],
        [m_g, m_e, g_in, e_in, crossed],
        [parts, parts, mirrored, parts, parts, mirrored],
        cost=LONG,
    )
    arrived = list(received)
    for turn in range(1, rows - 1):
        active = functools.partial(step_kernel, lambda place, turn=turn: lax.div(place, 2) == turn)
        (wave,) = run(active, [], [ps, pt, ep] + arrived, [mirrored])
        up = [pair for p in range(poles) for pair in zip(hosts(turn, p), hosts(turn + 1, p))]
        arrived = [lax.ppermute(wave, AXES, up)]
        received += arrived
    own, sent = run(
        share_kernel,
        [],
        [fas, fat, ea] + received,
        [mirrored, mirrored],
        [pltpu.VMEM(mirrored.shape, F32)],
    )
    shared = lax.ppermute(sent, AXES, every)

    offs = jax.ShapeDtypeStruct((2, 2 * width, width // 2), F32)
    diags = jax.ShapeDtypeStruct((2,) + quarter, F32)
    off, diag = run(density_kernel, [], [weight, own, m_f0s, m_f0t, m_gs, m_gt, m_w], [offs, diags])
    off, us, ts = run(
        more_off_kernel,
        [],
        [weight, shared, e_in, o_f0s, o_f0t, o_gs, o_w, off],
        [offs, parts, parts],
    )

    def exchanged(value, distance):
        return lax.ppermute(value, "pole", [(p, p ^ distance) for p in range(poles)])

    def summed(parts):
        kept = parts[0] + exchanged(parts[1], 1)
        distance = 2
        while distance < poles:
            kept = kept + exchanged(kept, distance)
            distance *= 2
        return kept, exchanged(kept, 1)

    full = jax.ShapeDtypeStruct((2, width, width), F32)
    off_sums = summed(off)
    (diag,) = run(more_diag_kernel, [], [us, ts, o_f0t, o_gt, o_w, diag], [diags])
    diag_sums = summed(diag)
    done = jax.ShapeDtypeStruct((8, 128), F32)
    density_off, done = run(unpack_off_kernel, [], list(off_sums), [full, done])
    (density_diag,) = run(unpack_diag_kernel, [], [*diag_sums, done], [full])
    return density_diag, density_off


def solution(mesh):
    placed = (
        P("pole", "snode", None, None, None),
        P("pole", "snode", None, None, None),
        P("snode"),
        P("pole", None),
    )
    return jax.shard_map(
        local,
        mesh=mesh,
        in_specs=placed,
        out_specs=(P("snode", None, None), P("snode", None, None)),
        check_vma=False,
    )
```

```python
import functools

import jax
import jax.numpy as jnp
from jax import lax
from jax.experimental import pallas as pl
from jax.experimental.pallas import tpu as pltpu
from jax.sharding import PartitionSpec as P

F32 = jnp.float32
BF16 = jnp.bfloat16
AXES = ("pole", "snode")
VMEM_LIMIT = 16 * 1024 * 1024


def halves(value):
    high = value.astype(BF16)
    return high, (value - high.astype(F32)).astype(BF16)


def split_pair(real, imag):
    (rh, rl), (ih, il) = halves(real), halves(imag)
    return rh, ih, rl, il


def deep_dot(left, right):
    return jnp.dot(
        jnp.concatenate(left, axis=1), jnp.concatenate(right, axis=0), preferred_element_type=F32
    )


def dot(left, right):
    return jnp.dot(left, right, preferred_element_type=F32)


def dot3(lh, ll, rh, rl):
    return dot(lh, rh) + (dot(lh, rl) + dot(ll, rh))


def wide_dot(left, right):
    arh, aih, arl, ail = left
    brh, bih, brl, bil = right
    real = dot3(arh, arl, brh, brl) - dot3(aih, ail, bih, bil)
    imag = dot3(arh, arl, bih, bil) + dot3(aih, ail, brh, brl)
    return real, imag


def complex_dot(left, right):
    arh, aih, arl, ail = left
    brh, bih, brl, bil = right
    blocks = [arh, arh, arl, aih, aih, ail]
    real = deep_dot(blocks, [brh, brl, brh, -bih, -bil, -bih])
    imag = deep_dot(blocks, [bih, bil, bih, brh, brl, brh])
    return real, imag


def rows_columns(size):
    return (
        lax.broadcasted_iota(jnp.int32, (size, size), 0),
        lax.broadcasted_iota(jnp.int32, (size, size), 1),
    )


def packed(block):
    half = block.shape[0] // 2
    row, column = rows_columns(half)
    lower = block[half:, half:]
    mixed = jnp.where(row >= column, block[:half, :half], lower)
    diagonal = jnp.sum(jnp.where(row == column, lower, 0.0), axis=0, keepdims=True)
    return jnp.concatenate(
        [block[:half, half:], mixed, jnp.broadcast_to(diagonal, (8, half))], axis=0
    )


def unpacked(value):
    half = value.shape[1]
    row, column = rows_columns(half)
    right, mixed = value[:half], value[half : 2 * half]
    diagonal = value[2 * half : 2 * half + 1]
    turned = mixed.T
    first = jnp.where(row >= column, mixed, turned)
    last = jnp.where(row < column, mixed, jnp.where(row == column, diagonal, turned))
    return jnp.concatenate(
        [jnp.concatenate([first, right], axis=1), jnp.concatenate([right.T, last], axis=1)], axis=0
    )


def unpacked_split(ref):
    return split_pair(unpacked(ref[0]), unpacked(ref[1]))


def load4(ref):
    return tuple(ref[i] for i in range(4))


def store4(ref, parts):
    for i, part in enumerate(parts):
        ref[i] = part


def whereabouts():
    place = lax.axis_index("snode")
    return place, lax.rem(place, 2), lax.rem(lax.axis_index("pole"), 2)


def hosted_slot():
    place, odd, _ = whereabouts()
    return jnp.where(place < 2, 0, 1 - odd)


def slot_of(hosted):
    return hosted_slot() if hosted else 1 - hosted_slot()


def constants_of(slot, blocks, link, widths, weights, f1s, e, weighted, *_, wait=lambda: None):
    width = blocks.shape[-1]
    row, column = rows_columns(width)
    kept = [column < widths[k] for k in range(2)]
    both = [jnp.logical_and(row < widths[k], kept[k]) for k in range(2)]
    f1 = [jnp.where(kept[1], link[c], 0.0) for c in range(2)]
    s1, t1 = split_pair(*f1), split_pair(f1[0].T, f1[1].T)
    store4(f1s, s1)
    wait()
    d = [[jnp.where(both[k], blocks[k, c], 0.0) for c in range(2)] for k in range(2)]
    br, bi = complex_dot(split_pair(*d[0]), s1)
    tr, ti = complex_dot(t1, split_pair(br, bi))
    er, ei = d[1][0] + tr, d[1][1] + ti
    e[0], e[1] = packed(er), packed(ei)
    w0, w1 = weights[pl.ds(slot, 1), 0:1], weights[pl.ds(slot, 1), 1:2]
    weighted[0] = packed(w1 * d[0][0] + w0 * d[0][1])
    weighted[1] = packed(w1 * er + w0 * ei)
    weighted_b = flat(w1 * br + w0 * bi)
    weighted[2] = weighted_b[: width + 8]
    weighted[3, : width - 8] = weighted_b[width + 8 :]


def fetched_constants(slot, live, pivot, factor, weight, outs, scratch):
    blocks, link, widths, weights, sems = scratch
    first_factor = pltpu.make_async_copy(factor.at[slot, 0], outs[3], sems.at[5])
    copies = [
        pltpu.make_async_copy(live, widths, sems.at[0]),
        pltpu.make_async_copy(factor.at[slot, 1], link, sems.at[1]),
        pltpu.make_async_copy(pivot.at[slot, 0], blocks.at[0], sems.at[2]),
        pltpu.make_async_copy(pivot.at[slot, 1], blocks.at[1], sems.at[3]),
        pltpu.make_async_copy(weight, weights, sems.at[4]),
    ]
    for copy in copies:
        copy.start()
    first_factor.start()
    copies[0].wait()
    copies[1].wait()

    def wait():
        for copy in copies[2:]:
            copy.wait()

    constants_of(slot, blocks, link, widths, weights, *outs, wait=wait)
    first_factor.wait()


def sent_constant_kernel(live, pivot, factor, weight, *refs):
    outs, second, scratch = refs[:4], refs[4:8], refs[8:]
    place, _, core = whereabouts()

    @pl.when(jnp.logical_and(place != 1, core == 0))
    def _():
        fetched_constants(slot_of(True), live, pivot, factor, weight, second, scratch)

    @pl.when(jnp.logical_or(place != 1, core == 0))
    def _():
        fetched_constants(slot_of(False), live, pivot, factor, weight, outs, scratch)


def first_constant_kernel(live, pivot, factor, weight, *refs):
    made, outs, scratch = refs[:4], refs[4:8], refs[8:]
    place, _, core = whereabouts()
    late = jnp.logical_and(place == 1, core == 1)

    @pl.when(jnp.logical_not(late))
    def _():
        for source, target in zip(made, outs):
            target[...] = source[...]

    @pl.when(late)
    def _():
        fetched_constants(slot_of(False), live, pivot, factor, weight, outs, scratch)


def second_constants(live, pivot, factor, weight, f1s, e, weighted, first_factor):
    slot = slot_of(True)
    first_factor[...] = factor[slot, 0]
    constants_of(slot, pivot.at[slot], factor.at[slot, 1], live, weight, f1s, e, weighted)


def sent_second_kernel(live, pivot, factor, weight, _, *refs):
    made, outs = refs[:4], refs[4:]
    place, _, core = whereabouts()

    @pl.when(core == 0)
    def _():
        for source, target in zip(made, outs):
            target[...] = source[...]

    @pl.when(jnp.logical_and(place != 1, core == 1))
    def _():
        second_constants(live, pivot, factor, weight, *outs)


def second_constant_kernel(live, pivot, factor, weight, *refs):
    made, outs = refs[:4], refs[4:]
    place = whereabouts()[0]

    @pl.when(place != 1)
    def _():
        for source, target in zip(made, outs):
            target[...] = source[...]

    @pl.when(place == 1)
    def _():
        second_constants(live, pivot, factor, weight, *outs)


def factor_kernel(live, factor, f1s, f0s, f0t, gs, gt, g):
    _, column = rows_columns(factor.shape[-1])
    f0 = [jnp.where(column < live[0], factor[c], 0.0) for c in range(2)]
    s0 = split_pair(*f0)
    gr, gi = complex_dot(s0, load4(f1s))
    g[0], g[1] = gr, gi
    store4(gs, split_pair(gr, gi))
    store4(gt, split_pair(gr.T, gi.T))
    store4(f0s, s0)
    store4(f0t, split_pair(f0[0].T, f0[1].T))


def fold(x, gs, gt, e, out):
    tr, ti = complex_dot(x, load4(gs))
    yr, yi = complex_dot(load4(gt), split_pair(tr, ti))
    out[0] = e[0] + packed(yr)
    out[1] = e[1] + packed(yi)


def step_kernel(active, gs, gt, e, *refs):
    *received, out = refs

    @pl.when(active(whereabouts()[0]))
    def _():
        value = received[0][...]
        for other in received[1:]:
            value = value + other[...]
        fold(split_pair(unpacked(value[0]), unpacked(value[1])), gs, gt, e, out)


def cross_kernel(gs, gt, e, x, second, out):
    place = whereabouts()[0]

    @pl.when(place == 0)
    def _():
        out[...] = second[...]

    @pl.when(place == 1)
    def _():
        fold(unpacked_split(x), gs, gt, e, out)


def pair_kernel(g, e, g_in, e_in, e_second, fas, fat, ea, ps, pt, ep):
    upper = whereabouts()[0] > 1
    is_odd = whereabouts()[1] == 1
    ga = [jnp.where(is_odd, g_in[c], g[c]) for c in range(2)]
    gb = [jnp.where(is_odd, g[c], g_in[c]) for c in range(2)]
    theirs = [jnp.where(upper, e_in[c], e_second[c]) for c in range(2)]
    low = [jnp.where(is_odd, theirs[c], e[c]) for c in range(2)]
    high = [jnp.where(is_odd, e[c], theirs[c]) for c in range(2)]
    sa, sb = split_pair(*ga), split_pair(*gb)
    store4(fas, sa)
    store4(fat, split_pair(ga[0].T, ga[1].T))
    pr, pi = complex_dot(sa, sb)
    store4(ps, split_pair(pr, pi))
    store4(pt, split_pair(pr.T, pi.T))
    br, bi = complex_dot(split_pair(unpacked(low[0]), unpacked(low[1])), sb)
    tr, ti = complex_dot(split_pair(gb[0].T, gb[1].T), split_pair(br, bi))
    for c, term in enumerate((tr, ti)):
        ea[c] = low[c]
        ep[c] = high[c] + packed(term)


def share_kernel(fas, fat, ea, *refs):
    *received, own, sent, scratch = refs
    value = received[0][...]
    for other in received[1:]:
        value = value + other[...]
    value = jnp.where(whereabouts()[0] > 1, value, 0.0)
    fold(split_pair(unpacked(value[0]), unpacked(value[1])), fas, fat, ea, scratch)
    is_odd = whereabouts()[1] == 1
    own[...] = jnp.where(is_odd, scratch[...], value)
    sent[...] = jnp.where(is_odd, value, scratch[...])


def flat(block):
    half = block.shape[1] // 2
    return jnp.concatenate([block[:, :half], block[:, half:]], axis=0)


def real_dot(left, right):
    return dot3(left[0], left[2], right[0], right[2]) + dot3(left[1], left[3], right[1], right[3])


def off_values(slot, weight, xs, f0s, f0t, gs, weighted):
    width = f0s.shape[-1]
    w0, w1 = weight[pl.ds(slot, 1), 0:1], weight[pl.ds(slot, 1), 1:2]
    qr, qi = wide_dot(xs, load4(gs))
    ts = split_pair(w1 * qr + w0 * qi, w0 * qr - w1 * qi)
    second = real_dot(load4(f0t), ts)
    pr, pi = wide_dot(xs, load4(f0s))
    u = w1 * pr + w0 * pi
    us = split_pair(u, w0 * pr - w1 * pi)
    constant = jnp.concatenate([weighted[2], weighted[3, : width - 8]], axis=0)
    return -flat(u), -(flat(second) + constant), us, ts


def diag_values(us, ts, f0t, gt, weighted):
    return (
        weighted[0] + packed(real_dot(load4(f0t), us)),
        weighted[1] + packed(real_dot(load4(gt), ts)),
    )


def density_kernel(weight, x, f0s, f0t, gs, gt, weighted, off, diag):
    core = whereabouts()[2]
    first, second, us, ts = off_values(slot_of(True), weight, unpacked_split(x), f0s, f0t, gs, weighted)
    off[core], off[1 - core] = first, second
    diag[core], diag[1 - core] = diag_values(us, ts, f0t, gt, weighted)


def more_off_kernel(weight, x, x_first, f0s, f0t, gs, weighted, before, off, us_out, ts_out):
    core = whereabouts()[2]
    place = whereabouts()[0]
    x = [
        jnp.where(place > 1, x[c], jnp.where(place == 1, x_first[c], 0.0)) for c in range(2)
    ]
    xs = split_pair(unpacked(x[0]), unpacked(x[1]))
    first, second, us, ts = off_values(slot_of(False), weight, xs, f0s, f0t, gs, weighted)
    off[core] = first + before[core]
    off[1 - core] = second + before[1 - core]
    store4(us_out, us)
    store4(ts_out, ts)


def more_diag_kernel(us, ts, f0t, gt, weighted, _, before, diag):
    core = whereabouts()[2]
    first, second = diag_values(load4(us), load4(ts), f0t, gt, weighted)
    diag[core] = first + before[core]
    diag[1 - core] = second + before[1 - core]


def unpack_off_kernel(mine, theirs, off, done):
    core = whereabouts()[2]
    width = off.shape[-1]
    half = width // 2
    for source, entry in ((mine, core), (theirs, 1 - core)):
        off[entry, :, :half] = source[:width]
        off[entry, :, half:] = source[width:]
    done[...] = jnp.zeros_like(done)


def unpack_diag_kernel(mine, theirs, _, diag):
    core = whereabouts()[2]
    for source, entry in ((mine, core), (theirs, 1 - core)):
        diag[entry] = unpacked(source[...])


SCALAR = pl.BlockSpec(memory_space=pltpu.SMEM)
WHOLE = pl.BlockSpec(memory_space=pltpu.VMEM)


COST = pl.CostEstimate(flops=1, bytes_accessed=1, transcendentals=0)


LONG = pl.CostEstimate(flops=10**11, bytes_accessed=1, transcendentals=0)


def run(kernel, scalars, arrays, shapes, scratch=(), cost=COST, far=()):
    return pl.pallas_call(
        kernel,
        out_shape=shapes,
        in_specs=[SCALAR] * len(scalars)
        + [pl.BlockSpec(memory_space=pltpu.HBM)] * len(far)
        + [WHOLE] * len(arrays),
        out_specs=[WHOLE] * len(shapes),
        scratch_shapes=list(scratch),
        compiler_params=pltpu.CompilerParams(vmem_limit_bytes=VMEM_LIMIT),
        cost_estimate=cost,
    )(*scalars, *far, *arrays)


def local(pivot, factor, live, weight):
    poles, turns = lax.axis_size("pole"), lax.axis_size("snode")
    rows = turns // 2
    width = pivot.shape[-1]
    quarter = (width + 8, width // 2)
    mirrored = jax.ShapeDtypeStruct((2,) + quarter, F32)
    parts = jax.ShapeDtypeStruct((4, width, width), BF16)

    def at(pole_index, snode_index):
        return pole_index * turns + snode_index

    def hosts(row, pole):
        return at(pole, 2 * row + 1), at(pole, 2 * row)

    swaps = [(at(p, s), at(p, s ^ 1)) for p in range(poles) for s in range(2, turns)]
    first = [(at(p, 0), at(p, 1)) for p in range(poles)]
    every = [(at(p, s), at(p, s ^ 1)) for p in range(poles) for s in range(turns)]
    raw = jax.ShapeDtypeStruct((2, width, width), F32)
    constants = [parts, mirrored, jax.ShapeDtypeStruct((4,) + quarter, F32), raw]
    factors = [parts, parts, parts, parts, raw]

    scratch = [
        pltpu.VMEM(pivot.shape[1:], F32),
        pltpu.VMEM(factor.shape[2:], F32),
        pltpu.SMEM(live.shape, jnp.int32),
        pltpu.VMEM(weight.shape, F32),
        pltpu.SemaphoreType.DMA((6,)),
    ]
    far = [pltpu.with_memory_space_constraint(a, pltpu.HBM) for a in (live, pivot, factor, weight)]
    made = run(sent_constant_kernel, [], [], constants * 2, scratch, far=far)
    made, second = made[:4], made[4:]
    e_in = lax.ppermute(made[1], AXES, every)
    o_f1s, o_e, o_w, o_f0 = run(first_constant_kernel, [], made, constants, scratch, far=far)
    o_f0s, o_f0t, o_gs, o_gt, o_g = run(
        factor_kernel, [live], [o_f0, o_f1s], factors
    )
    g_in = lax.ppermute(o_g, AXES, swaps)
    made = run(sent_second_kernel, [live], [pivot, factor, weight, o_g, *second], constants)
    (wave_even,) = run(cross_kernel, [], [o_gs, o_gt, o_e, e_in, made[1]], [mirrored])
    crossed = lax.ppermute(
        wave_even, AXES, first + [(at(p, 1), at(p, 0)) for p in range(poles)]
    )
    m_f1s, m_e, m_w, m_f0 = run(
        second_constant_kernel, [live], [pivot, factor, weight, *made], constants
    )
    m_f0s, m_f0t, m_gs, m_gt, m_g = run(
        factor_kernel, [live], [m_f0, m_f1s], factors
    )
    starts = functools.partial(step_kernel, lambda place: place == 1)
    (wave_odd,) = run(starts, [], [m_gs, m_gt, m_e, crossed], [mirrored])
    received = []
    if rows > 1:
        received = [
            lax.ppermute(wave_odd, AXES, [(at(p, 1), at(p, 3)) for p in range(poles)]),
            lax.ppermute(crossed, AXES, [(at(p, 0), at(p, 2)) for p in range(poles)]),
        ]
    else:
        received = [jnp.zeros(mirrored.shape, F32)]
    fas, fat, ea, ps, pt, ep = run(
        pair_kernel,
        [],
        [m_g, m_e, g_in, e_in, crossed],
        [parts, parts, mirrored, parts, parts, mirrored],
        cost=LONG,
    )
    arrived = list(received)
    for turn in range(1, rows - 1):
        active = functools.partial(step_kernel, lambda place, turn=turn: lax.div(place, 2) == turn)
        (wave,) = run(active, [], [ps, pt, ep] + arrived, [mirrored])
        up = [pair for p in range(poles) for pair in zip(hosts(turn, p), hosts(turn + 1, p))]
        arrived = [lax.ppermute(wave, AXES, up)]
        received += arrived
    own, sent = run(
        share_kernel,
        [],
        [fas, fat, ea] + received,
        [mirrored, mirrored],
        [pltpu.VMEM(mirrored.shape, F32)],
    )
    shared = lax.ppermute(sent, AXES, every)

    offs = jax.ShapeDtypeStruct((2, 2 * width, width // 2), F32)
    diags = jax.ShapeDtypeStruct((2,) + quarter, F32)
    off, diag = run(density_kernel, [], [weight, own, m_f0s, m_f0t, m_gs, m_gt, m_w], [offs, diags])
    off, us, ts = run(
        more_off_kernel,
        [],
        [weight, shared, e_in, o_f0s, o_f0t, o_gs, o_w, off],
        [offs, parts, parts],
    )

    def exchanged(value, distance):
        return lax.ppermute(value, "pole", [(p, p ^ distance) for p in range(poles)])

    def over_cores(parts):
        return parts[0] + exchanged(parts[1], 1)

    def over_chips(kept):
        distance = 2
        while distance < poles:
            kept = kept + exchanged(kept, distance)
            distance *= 2
        return kept, exchanged(kept, 1)

    full = jax.ShapeDtypeStruct((2, width, width), F32)
    off = over_cores(off)
    (diag,) = run(more_diag_kernel, [], [us, ts, o_f0t, o_gt, o_w, off, diag], [diags])
    off_sums = over_chips(off)
    diag_sums = over_chips(over_cores(diag))
    done = jax.ShapeDtypeStruct((8, 128), F32)
    density_off, done = run(unpack_off_kernel, [], list(off_sums), [full, done])
    (density_diag,) = run(unpack_diag_kernel, [], [*diag_sums, done], [full])
    return density_diag, density_off


def solution(mesh):
    placed = (
        P("pole", "snode", None, None, None),
        P("pole", "snode", None, None, None),
        P("snode"),
        P("pole", None),
    )
    return jax.shard_map(
        local,
        mesh=mesh,
        in_specs=placed,
        out_specs=(P("snode", None, None), P("snode", None, None)),
        check_vma=False,
    )
```

```python
import functools

import jax
import jax.numpy as jnp
from jax import lax
from jax.experimental import pallas as pl
from jax.experimental.pallas import tpu as pltpu
from jax.sharding import PartitionSpec as P

F32 = jnp.float32
BF16 = jnp.bfloat16
AXES = ("pole", "snode")
VMEM_LIMIT = 16 * 1024 * 1024


def halves(value):
    high = value.astype(BF16)
    return high, (value - high.astype(F32)).astype(BF16)


def split_pair(real, imag):
    (rh, rl), (ih, il) = halves(real), halves(imag)
    return rh, ih, rl, il


def deep_dot(left, right):
    return jnp.dot(
        jnp.concatenate(left, axis=1), jnp.concatenate(right, axis=0), preferred_element_type=F32
    )


def dot(left, right):
    return jnp.dot(left, right, preferred_element_type=F32)


def dot3(lh, ll, rh, rl):
    return dot(lh, rh) + (dot(lh, rl) + dot(ll, rh))


def wide_dot(left, right):
    arh, aih, arl, ail = left
    brh, bih, brl, bil = right
    real = dot3(arh, arl, brh, brl) - dot3(aih, ail, bih, bil)
    imag = dot3(arh, arl, bih, bil) + dot3(aih, ail, brh, brl)
    return real, imag


def complex_dot(left, right):
    arh, aih, arl, ail = left
    brh, bih, brl, bil = right
    blocks = [arh, arh, arl, aih, aih, ail]
    real = deep_dot(blocks, [brh, brl, brh, -bih, -bil, -bih])
    imag = deep_dot(blocks, [bih, bil, bih, brh, brl, brh])
    return real, imag


def rows_columns(size):
    return (
        lax.broadcasted_iota(jnp.int32, (size, size), 0),
        lax.broadcasted_iota(jnp.int32, (size, size), 1),
    )


def packed(block):
    half = block.shape[0] // 2
    row, column = rows_columns(half)
    lower = block[half:, half:]
    mixed = jnp.where(row >= column, block[:half, :half], lower)
    diagonal = jnp.sum(jnp.where(row == column, lower, 0.0), axis=0, keepdims=True)
    return jnp.concatenate(
        [block[:half, half:], mixed, jnp.broadcast_to(diagonal, (8, half))], axis=0
    )


def unpacked(value):
    half = value.shape[1]
    row, column = rows_columns(half)
    right, mixed = value[:half], value[half : 2 * half]
    diagonal = value[2 * half : 2 * half + 1]
    turned = mixed.T
    first = jnp.where(row >= column, mixed, turned)
    last = jnp.where(row < column, mixed, jnp.where(row == column, diagonal, turned))
    return jnp.concatenate(
        [jnp.concatenate([first, right], axis=1), jnp.concatenate([right.T, last], axis=1)], axis=0
    )


def unpacked_split(ref):
    return split_pair(unpacked(ref[0]), unpacked(ref[1]))


def load4(ref):
    return tuple(ref[i] for i in range(4))


def store4(ref, parts):
    for i, part in enumerate(parts):
        ref[i] = part


def whereabouts():
    place = lax.axis_index("snode")
    return place, lax.rem(place, 2), lax.rem(lax.axis_index("pole"), 2)


def hosted_slot():
    place, odd, _ = whereabouts()
    return jnp.where(place < 2, 0, 1 - odd)


def slot_of(hosted):
    return hosted_slot() if hosted else 1 - hosted_slot()


def constants_of(slot, blocks, link, widths, weights, f1s, e, weighted, *_, wait=lambda: None):
    width = blocks.shape[-1]
    row, column = rows_columns(width)
    kept = [column < widths[k] for k in range(2)]
    both = [jnp.logical_and(row < widths[k], kept[k]) for k in range(2)]
    f1 = [jnp.where(kept[1], link[c], 0.0) for c in range(2)]
    s1, t1 = split_pair(*f1), split_pair(f1[0].T, f1[1].T)
    store4(f1s, s1)
    wait()
    d = [[jnp.where(both[k], blocks[k, c], 0.0) for c in range(2)] for k in range(2)]
    br, bi = complex_dot(split_pair(*d[0]), s1)
    tr, ti = complex_dot(t1, split_pair(br, bi))
    er, ei = d[1][0] + tr, d[1][1] + ti
    e[0], e[1] = packed(er), packed(ei)
    w0, w1 = weights[pl.ds(slot, 1), 0:1], weights[pl.ds(slot, 1), 1:2]
    weighted[0] = packed(w1 * d[0][0] + w0 * d[0][1])
    weighted[1] = packed(w1 * er + w0 * ei)
    weighted_b = flat(w1 * br + w0 * bi)
    weighted[2] = weighted_b[: width + 8]
    weighted[3, : width - 8] = weighted_b[width + 8 :]


def fetched_constants(slot, live, pivot, factor, weight, outs, scratch):
    blocks, link, widths, weights, sems = scratch
    first_factor = pltpu.make_async_copy(factor.at[slot, 0], outs[3], sems.at[5])
    copies = [
        pltpu.make_async_copy(live, widths, sems.at[0]),
        pltpu.make_async_copy(factor.at[slot, 1], link, sems.at[1]),
        pltpu.make_async_copy(pivot.at[slot, 0], blocks.at[0], sems.at[2]),
        pltpu.make_async_copy(pivot.at[slot, 1], blocks.at[1], sems.at[3]),
        pltpu.make_async_copy(weight, weights, sems.at[4]),
    ]
    for copy in copies:
        copy.start()
    first_factor.start()
    copies[0].wait()
    copies[1].wait()

    def wait():
        for copy in copies[2:]:
            copy.wait()

    constants_of(slot, blocks, link, widths, weights, *outs, wait=wait)
    first_factor.wait()
    _, column = rows_columns(blocks.shape[-1])
    for c in range(2):
        outs[3][c] = jnp.where(column < widths[0], outs[3][c], 0.0)


def sent_constant_kernel(live, pivot, factor, weight, *refs):
    outs, second, scratch = refs[:4], refs[4:8], refs[8:]
    place, _, core = whereabouts()

    @pl.when(jnp.logical_and(place != 1, core == 0))
    def _():
        fetched_constants(slot_of(True), live, pivot, factor, weight, second, scratch)

    @pl.when(jnp.logical_or(place != 1, core == 0))
    def _():
        fetched_constants(slot_of(False), live, pivot, factor, weight, outs, scratch)


def first_constant_kernel(live, pivot, factor, weight, *refs):
    made, outs, scratch = refs[:4], refs[4:8], refs[8:]
    place, _, core = whereabouts()
    late = jnp.logical_and(place == 1, core == 1)

    @pl.when(jnp.logical_not(late))
    def _():
        for source, target in zip(made, outs):
            target[...] = source[...]

    @pl.when(late)
    def _():
        fetched_constants(slot_of(False), live, pivot, factor, weight, outs, scratch)


def second_constants(live, pivot, factor, weight, f1s, e, weighted, first_factor):
    slot = slot_of(True)
    _, column = rows_columns(factor.shape[-1])
    for c in range(2):
        first_factor[c] = jnp.where(column < live[0], factor[slot, 0, c], 0.0)
    constants_of(slot, pivot.at[slot], factor.at[slot, 1], live, weight, f1s, e, weighted)


def sent_second_kernel(live, pivot, factor, weight, _, *refs):
    made, outs = refs[:4], refs[4:]
    place, _, core = whereabouts()

    @pl.when(core == 0)
    def _():
        for source, target in zip(made, outs):
            target[...] = source[...]

    @pl.when(jnp.logical_and(place != 1, core == 1))
    def _():
        second_constants(live, pivot, factor, weight, *outs)


def second_constant_kernel(live, pivot, factor, weight, *refs):
    made, outs = refs[:4], refs[4:]
    place = whereabouts()[0]

    @pl.when(place != 1)
    def _():
        for source, target in zip(made, outs):
            target[...] = source[...]

    @pl.when(place == 1)
    def _():
        second_constants(live, pivot, factor, weight, *outs)


def factor_kernel(factor, f1s, f0s, f0t, gs, gt, g):
    f0 = [factor[c] for c in range(2)]
    s0 = split_pair(*f0)
    gr, gi = complex_dot(s0, load4(f1s))
    g[0], g[1] = gr, gi
    store4(gs, split_pair(gr, gi))
    store4(gt, split_pair(gr.T, gi.T))
    store4(f0s, s0)
    store4(f0t, split_pair(f0[0].T, f0[1].T))


def fold(x, gs, gt, e, out):
    tr, ti = complex_dot(x, load4(gs))
    yr, yi = complex_dot(load4(gt), split_pair(tr, ti))
    out[0] = e[0] + packed(yr)
    out[1] = e[1] + packed(yi)


def step_kernel(active, gs, gt, e, *refs):
    *received, out = refs

    @pl.when(active(whereabouts()[0]))
    def _():
        value = received[0][...]
        for other in received[1:]:
            value = value + other[...]
        fold(split_pair(unpacked(value[0]), unpacked(value[1])), gs, gt, e, out)


def cross_kernel(gs, gt, e, x, second, out):
    place = whereabouts()[0]

    @pl.when(place == 0)
    def _():
        out[...] = second[...]

    @pl.when(place == 1)
    def _():
        fold(unpacked_split(x), gs, gt, e, out)


def pair_kernel(g, e, g_in, e_in, e_second, fas, fat, ea, ps, pt, ep):
    upper = whereabouts()[0] > 1
    is_odd = whereabouts()[1] == 1
    ga = [jnp.where(is_odd, g_in[c], g[c]) for c in range(2)]
    gb = [jnp.where(is_odd, g[c], g_in[c]) for c in range(2)]
    theirs = [jnp.where(upper, e_in[c], e_second[c]) for c in range(2)]
    low = [jnp.where(is_odd, theirs[c], e[c]) for c in range(2)]
    high = [jnp.where(is_odd, e[c], theirs[c]) for c in range(2)]
    sa, sb = split_pair(*ga), split_pair(*gb)
    store4(fas, sa)
    store4(fat, split_pair(ga[0].T, ga[1].T))
    pr, pi = complex_dot(sa, sb)
    store4(ps, split_pair(pr, pi))
    store4(pt, split_pair(pr.T, pi.T))
    br, bi = complex_dot(split_pair(unpacked(low[0]), unpacked(low[1])), sb)
    tr, ti = complex_dot(split_pair(gb[0].T, gb[1].T), split_pair(br, bi))
    for c, term in enumerate((tr, ti)):
        ea[c] = low[c]
        ep[c] = high[c] + packed(term)


def share_kernel(fas, fat, ea, *refs):
    *received, own, sent, scratch = refs
    value = received[0][...]
    for other in received[1:]:
        value = value + other[...]
    value = jnp.where(whereabouts()[0] > 1, value, 0.0)
    fold(split_pair(unpacked(value[0]), unpacked(value[1])), fas, fat, ea, scratch)
    is_odd = whereabouts()[1] == 1
    own[...] = jnp.where(is_odd, scratch[...], value)
    sent[...] = jnp.where(is_odd, value, scratch[...])


def flat(block):
    half = block.shape[1] // 2
    return jnp.concatenate([block[:, :half], block[:, half:]], axis=0)


def real_dot(left, right):
    return dot3(left[0], left[2], right[0], right[2]) + dot3(left[1], left[3], right[1], right[3])


def off_values(slot, weight, xs, f0s, f0t, gs, weighted):
    width = f0s.shape[-1]
    w0, w1 = weight[pl.ds(slot, 1), 0:1], weight[pl.ds(slot, 1), 1:2]
    qr, qi = wide_dot(xs, load4(gs))
    ts = split_pair(w1 * qr + w0 * qi, w0 * qr - w1 * qi)
    second = real_dot(load4(f0t), ts)
    pr, pi = wide_dot(xs, load4(f0s))
    u = w1 * pr + w0 * pi
    us = split_pair(u, w0 * pr - w1 * pi)
    constant = jnp.concatenate([weighted[2], weighted[3, : width - 8]], axis=0)
    return -flat(u), -(flat(second) + constant), us, ts


def diag_values(us, ts, f0t, gt, weighted):
    return (
        weighted[0] + packed(real_dot(load4(f0t), us)),
        weighted[1] + packed(real_dot(load4(gt), ts)),
    )


def density_kernel(weight, x, f0s, f0t, gs, gt, weighted, off, diag):
    core = whereabouts()[2]
    first, second, us, ts = off_values(slot_of(True), weight, unpacked_split(x), f0s, f0t, gs, weighted)
    off[core], off[1 - core] = first, second
    diag[core], diag[1 - core] = diag_values(us, ts, f0t, gt, weighted)


def more_off_kernel(weight, x, x_first, f0s, f0t, gs, weighted, before, off, us_out, ts_out):
    core = whereabouts()[2]
    place = whereabouts()[0]
    x = [
        jnp.where(place > 1, x[c], jnp.where(place == 1, x_first[c], 0.0)) for c in range(2)
    ]
    xs = split_pair(unpacked(x[0]), unpacked(x[1]))
    first, second, us, ts = off_values(slot_of(False), weight, xs, f0s, f0t, gs, weighted)
    off[core] = first + before[core]
    off[1 - core] = second + before[1 - core]
    store4(us_out, us)
    store4(ts_out, ts)


def more_diag_kernel(us, ts, f0t, gt, weighted, before, diag):
    core = whereabouts()[2]
    first, second = diag_values(load4(us), load4(ts), f0t, gt, weighted)
    diag[core] = first + before[core]
    diag[1 - core] = second + before[1 - core]


def unpack_off_kernel(mine, theirs, off, done):
    core = whereabouts()[2]
    width = off.shape[-1]
    half = width // 2
    for source, entry in ((mine, core), (theirs, 1 - core)):
        off[entry, :, :half] = source[:width]
        off[entry, :, half:] = source[width:]
    done[...] = jnp.zeros_like(done)


def unpack_diag_kernel(mine, theirs, _, diag):
    core = whereabouts()[2]
    for source, entry in ((mine, core), (theirs, 1 - core)):
        diag[entry] = unpacked(source[...])


SCALAR = pl.BlockSpec(memory_space=pltpu.SMEM)
WHOLE = pl.BlockSpec(memory_space=pltpu.VMEM)


COST = pl.CostEstimate(flops=1, bytes_accessed=1, transcendentals=0)


LONG = pl.CostEstimate(flops=10**11, bytes_accessed=1, transcendentals=0)


def run(kernel, scalars, arrays, shapes, scratch=(), cost=COST, far=()):
    return pl.pallas_call(
        kernel,
        out_shape=shapes,
        in_specs=[SCALAR] * len(scalars)
        + [pl.BlockSpec(memory_space=pltpu.HBM)] * len(far)
        + [WHOLE] * len(arrays),
        out_specs=[WHOLE] * len(shapes),
        scratch_shapes=list(scratch),
        compiler_params=pltpu.CompilerParams(vmem_limit_bytes=VMEM_LIMIT),
        cost_estimate=cost,
    )(*scalars, *far, *arrays)


def local(pivot, factor, live, weight):
    poles, turns = lax.axis_size("pole"), lax.axis_size("snode")
    rows = turns // 2
    width = pivot.shape[-1]
    quarter = (width + 8, width // 2)
    mirrored = jax.ShapeDtypeStruct((2,) + quarter, F32)
    parts = jax.ShapeDtypeStruct((4, width, width), BF16)

    def at(pole_index, snode_index):
        return pole_index * turns + snode_index

    def hosts(row, pole):
        return at(pole, 2 * row + 1), at(pole, 2 * row)

    swaps = [(at(p, s), at(p, s ^ 1)) for p in range(poles) for s in range(2, turns)]
    first = [(at(p, 0), at(p, 1)) for p in range(poles)]
    every = [(at(p, s), at(p, s ^ 1)) for p in range(poles) for s in range(turns)]
    raw = jax.ShapeDtypeStruct((2, width, width), F32)
    constants = [parts, mirrored, jax.ShapeDtypeStruct((4,) + quarter, F32), raw]
    factors = [parts, parts, parts, parts, raw]

    scratch = [
        pltpu.VMEM(pivot.shape[1:], F32),
        pltpu.VMEM(factor.shape[2:], F32),
        pltpu.SMEM(live.shape, jnp.int32),
        pltpu.VMEM(weight.shape, F32),
        pltpu.SemaphoreType.DMA((6,)),
    ]
    far = [pltpu.with_memory_space_constraint(a, pltpu.HBM) for a in (live, pivot, factor, weight)]
    made = run(sent_constant_kernel, [], [], constants * 2, scratch, far=far)
    made, second = made[:4], made[4:]
    e_in = lax.ppermute(made[1], AXES, every)
    o_f1s, o_e, o_w, o_f0 = run(first_constant_kernel, [], made, constants, scratch, far=far)
    o_f0s, o_f0t, o_gs, o_gt, o_g = run(
        factor_kernel, [], [o_f0, o_f1s], factors
    )
    g_in = lax.ppermute(o_g, AXES, swaps)
    made = run(sent_second_kernel, [live], [pivot, factor, weight, o_g, *second], constants)
    (wave_even,) = run(cross_kernel, [], [o_gs, o_gt, o_e, e_in, made[1]], [mirrored])
    crossed = lax.ppermute(
        wave_even, AXES, first + [(at(p, 1), at(p, 0)) for p in range(poles)]
    )
    m_f1s, m_e, m_w, m_f0 = run(
        second_constant_kernel, [live], [pivot, factor, weight, *made], constants
    )
    m_f0s, m_f0t, m_gs, m_gt, m_g = run(
        factor_kernel, [], [m_f0, m_f1s], factors
    )
    starts = functools.partial(step_kernel, lambda place: place == 1)
    (wave_odd,) = run(starts, [], [m_gs, m_gt, m_e, crossed], [mirrored])
    received = []
    if rows > 1:
        received = [
            lax.ppermute(wave_odd, AXES, [(at(p, 1), at(p, 3)) for p in range(poles)]),
            lax.ppermute(crossed, AXES, [(at(p, 0), at(p, 2)) for p in range(poles)]),
        ]
    else:
        received = [jnp.zeros(mirrored.shape, F32)]
    fas, fat, ea, ps, pt, ep = run(
        pair_kernel,
        [],
        [m_g, m_e, g_in, e_in, crossed],
        [parts, parts, mirrored, parts, parts, mirrored],
        cost=LONG,
    )
    arrived = list(received)
    for turn in range(1, rows - 1):
        active = functools.partial(step_kernel, lambda place, turn=turn: lax.div(place, 2) == turn)
        (wave,) = run(active, [], [ps, pt, ep] + arrived, [mirrored])
        up = [pair for p in range(poles) for pair in zip(hosts(turn, p), hosts(turn + 1, p))]
        arrived = [lax.ppermute(wave, AXES, up)]
        received += arrived
    own, sent = run(
        share_kernel,
        [],
        [fas, fat, ea] + received,
        [mirrored, mirrored],
        [pltpu.VMEM(mirrored.shape, F32)],
    )
    shared = lax.ppermute(sent, AXES, every)

    offs = jax.ShapeDtypeStruct((2, 2 * width, width // 2), F32)
    diags = jax.ShapeDtypeStruct((2,) + quarter, F32)
    off, diag = run(density_kernel, [], [weight, own, m_f0s, m_f0t, m_gs, m_gt, m_w], [offs, diags])
    off, us, ts = run(
        more_off_kernel,
        [],
        [weight, shared, e_in, o_f0s, o_f0t, o_gs, o_w, off],
        [offs, parts, parts],
    )

    def exchanged(value, distance):
        return lax.ppermute(value, "pole", [(p, p ^ distance) for p in range(poles)])

    def summed(parts):
        kept = parts[0] + exchanged(parts[1], 1)
        distance = 2
        while distance < poles:
            kept = kept + exchanged(kept, distance)
            distance *= 2
        return kept, exchanged(kept, 1)

    full = jax.ShapeDtypeStruct((2, width, width), F32)
    off_sums = summed(off)
    (diag,) = run(more_diag_kernel, [], [us, ts, o_f0t, o_gt, o_w, diag], [diags])
    diag_sums = summed(diag)
    done = jax.ShapeDtypeStruct((8, 128), F32)
    density_off, done = run(unpack_off_kernel, [], list(off_sums), [full, done])
    (density_diag,) = run(unpack_diag_kernel, [], [*diag_sums, done], [full])
    return density_diag, density_off


def solution(mesh):
    placed = (
        P("pole", "snode", None, None, None),
        P("pole", "snode", None, None, None),
        P("snode"),
        P("pole", None),
    )
    return jax.shard_map(
        local,
        mesh=mesh,
        in_specs=placed,
        out_specs=(P("snode", None, None), P("snode", None, None)),
        check_vma=False,
    )
```
